128 devices in a mesh: expert: 8 (over y, core), rows: 4 (over x), hid: 4 (over z).
Axes of the slice: x: 4, y: 4, z: 4, core: 2. Of those that a mesh axis runs over, the one named last changes fastest.
Arguments:
- tokens: bfloat16 [16384, 1152], P(('expert', 'rows', 'hid')), may hold values from -40 to 40
- resets: int32 [16384], P(('expert', 'rows', 'hid')), may hold values from 0 to 1, as said below
- routes: int32 [16384, 1], P(('expert', 'rows', 'hid')), may hold values from 0 to 7; in each aligned block of 128 rows (0 to 127, 128 to 255, ...) at most 24 rows name the same one
- cotangent: bfloat16 [16384, 1152], P(('expert', 'rows', 'hid')), may hold values from -6 to 6
- mixer_gain: bfloat16 [1152], P(('expert', 'rows', 'hid')), may hold values from 0.5 to 1.5
- in_proj: bfloat16 [1152, 2, 2304], P(None, None, ('expert', 'rows', 'hid')), may hold values from -0.1875 to 0.1875
- conv_kernel: bfloat16 [4, 2304], P(None, ('expert', 'rows', 'hid')), may hold values from -3 to 3
- conv_bias: bfloat16 [2304], P(('expert', 'rows', 'hid')), may hold values from -3 to 3
- x_proj: bfloat16 [104, 2304], P(None, ('expert', 'rows', 'hid')), may hold values from -0.125 to 0.125
- dt_proj: bfloat16 [72, 2304], P(None, ('expert', 'rows', 'hid')), may hold values from -0.75 to 0.75
- dt_bias: bfloat16 [2304], P(('expert', 'rows', 'hid')), may hold values from -7 to -2.5
- log_decay: bfloat16 [16, 2304], P(None, ('expert', 'rows', 'hid')), may hold values from -3 to 1.5
- skip_gain: bfloat16 [2304], P(('expert', 'rows', 'hid')), may hold values from 0.5 to 1.5
- out_proj: bfloat16 [2304, 1152], P(('expert', 'rows', 'hid')), may hold values from -0.375 to 0.375
- moe_gain: bfloat16 [1152], P(('expert', 'rows', 'hid')), may hold values from 0.5 to 1.5
- router: bfloat16 [1152, 8], P(('expert', 'rows', 'hid')), may hold values from -0.125 to 0.125
- up_proj: bfloat16 [8, 1152, 3072], P('expert', None, 'hid'), may hold values from -0.1875 to 0.1875
- down_proj: bfloat16 [8, 3072, 1152], P('expert', 'hid'), may hold values from -0.875 to 0.875
Outputs:
- output: bfloat16 [16384, 1152], P(('expert', 'rows', 'hid'))
- grad_tokens: float32 [16384, 1152], P(('expert', 'rows', 'hid'))
- grad_mixer_gain: float32 [1152], P(('expert', 'rows', 'hid'))
- grad_in_proj: float32 [1152, 2, 2304], P(None, None, ('expert', 'rows', 'hid'))
- grad_conv_kernel: float32 [4, 2304], P(None, ('expert', 'rows', 'hid'))
- grad_conv_bias: float32 [2304], P(('expert', 'rows', 'hid'))
- grad_x_proj: float32 [104, 2304], P(None, ('expert', 'rows', 'hid'))
- grad_dt_proj: float32 [72, 2304], P(None, ('expert', 'rows', 'hid'))
- grad_dt_bias: float32 [2304], P(('expert', 'rows', 'hid'))
- grad_log_decay: float32 [16, 2304], P(None, ('expert', 'rows', 'hid'))
- grad_skip_gain: float32 [2304], P(('expert', 'rows', 'hid'))
- grad_out_proj: float32 [2304, 1152], P(('expert', 'rows', 'hid'))
- grad_moe_gain: float32 [1152], P(('expert', 'rows', 'hid'))
- grad_router: float32 [1152, 8], P(('expert', 'rows', 'hid'))
- grad_up_proj: float32 [8, 1152, 3072], P('expert', None, 'hid')
- grad_down_proj: float32 [8, 3072, 1152], P('expert', 'hid')
The draws below stay inside these ranges and needn't reach their ends.
Inputs may be any that keep to these rules, and one draw needn't show every extreme that they name: `resets`: 1 marks a document's first token; the first token of every sequence of 512 tokens is marked. `routes`: the 128 rows of one device name one expert at most 24 times.
All inputs are finite; a program needn't handle non-finite values.
Results may differ from the reference program's by a relative error of at most 0.025.
Values may be sent and summed in bfloat16 or wider, within the bound.
A program may use at most 192 MiB of HBM per device.

```python
import math
from functools import partial
import jax
import jax.numpy as jnp
import numpy as np
from jax import lax

D = 1152
DI = 2304
NS = 16
DTR = 72
KCONV = 4
FF = 3072
TOK_DEV = 128
BLK = 32
EXPERTS = 8
SEQ = 512
TOKENS = 16384
CAP = 24
N_EXPERT = 8
N_ROWS = 4
N_HID = 4


def draw_tokens(key, part):
    key = jax.random.fold_in(key, 5)
    first_key, second_key = jax.random.split(key, 2)
    base = jax.random.normal(first_key, (TOKENS, D), jnp.float32)
    scales = jnp.exp(jax.random.uniform(second_key, (TOKENS, 1), jnp.float32, -0.693, 1.386))
    return (base * scales).astype(jnp.bfloat16)


def draw_resets(key, part):
    key = jax.random.fold_in(key, 11)
    first_key, second_key, third_key = jax.random.split(key, 3)
    seq_count = TOKENS // SEQ
    half_dev = max(TOK_DEV // 2, 2)
    opening = jax.random.randint(first_key, (seq_count, 1), 1, half_dev)
    closing = jax.random.randint(second_key, (seq_count, 1), SEQ - half_dev, SEQ)
    extra = jax.random.randint(third_key, (seq_count, SEQ), 0, 16) == 0
    places = jnp.arange(SEQ, dtype=jnp.int32)[None, :]
    outside = (places < opening) | (places > closing)
    marked = (places == 0) | (places == opening) | (places == closing) | outside & extra
    return marked.astype(jnp.int32).reshape(TOKENS)


def block_levels(stream_key, dims, cuts, smallest, top_value):
    def one(axis_at, parts):
        draws = jax.random.uniform(jax.random.fold_in(jax.random.fold_in(stream_key, 6), axis_at), (parts,), jnp.float32, smallest / len(cuts), top_value / len(cuts))
        return jnp.repeat(jnp.exp(draws), dims[axis_at] // parts).reshape((-1,) + (1,) * (len(dims) - axis_at - 1))

    level = one(*cuts[0])
    for cut in cuts[1:]:
        level = level * one(*cut)
    return level


def deal_out(stream_key, own, number, rows, amount, top, reach, skew):
    ranking = jax.random.permutation(stream_key, amount)
    crowded, ordinary = load_shares(amount, rows * top, reach, skew, True), load_shares(amount, rows * top, reach, skew, False)
    places = jnp.arange(amount)

    def named(tallies, turn):
        used = int((tallies > 0).sum())
        fixed = max(1, used // 4)
        shifted = fixed + (places - fixed + turn * (used - fixed)) % max(1, amount - fixed)
        return jnp.zeros((amount,), jnp.int32).at[ranking[jnp.where(places < fixed, places, shifted)]].set(jnp.asarray(tallies, jnp.int32))

    tallies = jnp.where(number % 4 == 0, named(crowded, number // 4), named(ordinary, number - number // 4 - 1))
    mixed = jax.random.permutation(jax.random.fold_in(own, 3), amount)
    donor, sink = mixed[0:amount // 2 * 2:2], mixed[1:amount // 2 * 2:2]
    room = jnp.minimum(tallies[donor] - 1, reach - tallies[sink]) // 2
    room = jnp.where((donor == ranking[0]) | (sink == ranking[0]) | (tallies[sink] == 0), 0, jnp.maximum(room, 0))
    shifted = jax.random.randint(jax.random.fold_in(own, 4), (amount // 2,), 0, 1 << 20) % (room + 1)
    tallies = tallies.at[donor].add(-shifted).at[sink].add(shifted)
    labels = jnp.searchsorted(jnp.cumsum(tallies), jnp.arange(rows * top), side="right").astype(jnp.int32)
    listing = labels.reshape(top, rows).T
    listing = listing[jax.random.permutation(jax.random.fold_in(own, 1), rows)]
    turn = jax.random.randint(jax.random.fold_in(own, 2), (rows, 1), 0, top)
    return jnp.take_along_axis(listing, (jnp.arange(top)[None, :] + turn) % top, axis=1)


def load_shares(count, total, reach, skew, full):
    loads = [(1 << 20) // math.isqrt(standing ** skew) + 1 for standing in range(1, count + 1)]
    largest = reach if full else min(reach, max(-(-total // count), total * loads[0] // sum(loads)))
    least = 1 if total - largest >= count - 1 else 0
    given, rest = [largest] + [least] * (count - 1), total - largest - least * (count - 1)
    while rest > 0:
        free = [i for i in range(1, count) if given[i] < largest] or [i for i in range(1, count) if given[i] < reach]
        pool, budget = sum([loads[i] for i in free]), rest
        for i in free:
            addition = min(reach - given[i], max(1, budget * loads[i] // pool), rest)
            given[i] = given[i] + addition
            rest = rest - addition
    return np.array(given)


def normal_values(stream_key, extent, width, limit, cuts=(), kind=jnp.bfloat16):
    values = width * jax.random.normal(stream_key, extent, jnp.float32)
    if cuts:
        values = values * block_levels(stream_key, extent, cuts, -0.22, 0.18)
    return jnp.clip(values, -limit, limit).astype(kind)


def setup_inputs(seed: int = 0) -> dict:
    splits = jax.random.split(jax.random.key(seed), 19)
    tokens = draw_tokens(jax.random.fold_in(splits[18], 71), 0)
    resets = draw_resets(jax.random.fold_in(splits[18], 71), 0)
    routes_keys = jax.random.split(jax.random.fold_in(splits[2], 1), TOKENS // TOK_DEV)
    routes_turns = jax.random.permutation(jax.random.fold_in(splits[2], 3), TOKENS // TOK_DEV)
    routes = jax.vmap(lambda own, number: deal_out(jax.random.fold_in(splits[2], 2), own, number, TOK_DEV, EXPERTS, 1, CAP, 2))(routes_keys, routes_turns).reshape((TOKENS, 1))
    cotangent = normal_values(splits[3], (TOKENS, D), 1.0, 6.0, ((0, 128),))
    mixer_gain = jnp.clip(1.0 + 0.1 * jax.random.normal(splits[4], (D,), jnp.float32), 0.5, 1.5).astype(jnp.bfloat16)
    in_proj = normal_values(splits[5], (D, 2, DI), D ** -0.5, 0.1875, ((2, 128),))
    conv_kernel = normal_values(splits[6], (KCONV, DI), KCONV ** -0.5, 3.0, ((1, 128),))
    conv_bias = normal_values(splits[7], (DI,), 0.5, 3.0, ((0, 128),))
    x_proj = normal_values(splits[8], (DTR + 2 * NS, DI), DI ** -0.5, 0.125, ((1, 128),))
    dt_proj = normal_values(splits[9], (DTR, DI), DTR ** -0.5, 0.75, ((1, 128),))
    dt_bias = jnp.clip(-7.0 + 4.5 * jax.random.uniform(splits[10], (DI,), jnp.float32) ** block_levels(splits[10], (DI,), ((0, 128),), -0.2, 0.2), -7.0, -2.5).astype(jnp.bfloat16)
    log_decay = jnp.clip(-3.0 + 4.5 * jax.random.uniform(splits[11], (NS, DI), jnp.float32) ** block_levels(splits[11], (NS, DI), ((1, 128),), -0.2, 0.2), -3.0, 1.5).astype(jnp.bfloat16)
    skip_gain = jnp.clip(0.5 + 1.0 * jax.random.uniform(splits[12], (DI,), jnp.float32) ** block_levels(splits[12], (DI,), ((0, 128),), -0.2, 0.2), 0.5, 1.5).astype(jnp.bfloat16)
    out_proj = normal_values(splits[13], (DI, D), (DI // 8) ** -0.5, 0.375, ((0, 128),))
    moe_gain = jnp.clip(1.0 + 0.1 * jax.random.normal(splits[14], (D,), jnp.float32), 0.5, 1.5).astype(jnp.bfloat16)
    router = normal_values(splits[15], (D, EXPERTS), (2 * D) ** -0.5, 0.125, ((0, 128),))
    up_proj = normal_values(splits[16], (EXPERTS, D, FF), D ** -0.5, 0.1875, ((0, 8), (2, 4)))
    down_proj = normal_values(splits[17], (EXPERTS, FF, D), (FF // 64) ** -0.5, 0.875, ((0, 8), (1, 4)))
    return dict(tokens=tokens, resets=resets, routes=routes, cotangent=cotangent, mixer_gain=mixer_gain, in_proj=in_proj, conv_kernel=conv_kernel, conv_bias=conv_bias, x_proj=x_proj, dt_proj=dt_proj, dt_bias=dt_bias, log_decay=log_decay, skip_gain=skip_gain, out_proj=out_proj, moe_gain=moe_gain, router=router, up_proj=up_proj, down_proj=down_proj)


@jax.custom_vjp
def low(v):
    return lax.optimization_barrier(v.astype(jnp.bfloat16)).astype(jnp.float32)

@jax.custom_vjp
def low_back(v):
    return v

def low_keep(v):
    return (low(v), None)

def low_pass(kept, grad):
    return (grad,)

def back_keep(v):
    return (v, None)

def back_low(kept, grad):
    return (low(grad),)
low.defvjp(low_keep, low_pass)
low_back.defvjp(back_keep, back_low)
EPS = 1e-05

def matmul(first_op, second_op):
    return jnp.dot(first_op, second_op, precision=lax.Precision.HIGHEST, preferred_element_type=jnp.float32)

def rms_norm(values, gain):
    return values * lax.rsqrt(lax.optimization_barrier(jnp.mean(values * values, axis=-1, keepdims=True)) + EPS) * gain

def join(first, second):
    return (first[0] * second[0], second[0] * first[1] + second[1])

def scan_block(a_neg, carry, pieces):
    state, product = carry
    dt_part, b_part, c_part, x_part, r_part = pieces
    decay = jnp.exp(dt_part[:, None, :] * a_neg[None]) * (1.0 - r_part)[:, None, None]
    inject = b_part[:, :, None] * (dt_part * x_part)[:, None, :]
    cum_decay, cum_inject = lax.associative_scan(join, (decay, inject))
    states = cum_decay * state[None] + cum_inject
    outputs = lax.optimization_barrier(jnp.sum(c_part[:, :, None] * states, axis=1))
    return ((states[-1], product * cum_decay[-1]), outputs)

def scan_states(dt, b_mat, c_mat, xs_in, marks, a_neg, h_start):
    blocks = dt.shape[0] // BLK
    pieces = tuple((value.reshape((blocks, BLK) + value.shape[1:]) for value in (dt, b_mat, c_mat, xs_in, marks)))
    (h_end, product), outputs = lax.scan(jax.checkpoint(partial(scan_block, a_neg)), (h_start, jnp.ones_like(h_start)), pieces)
    return (outputs.reshape(dt.shape), h_end, product)

def convolve(ids_ext, extended, kernel, bias):
    margin = kernel.shape[0] - 1
    length = extended.shape[0] - margin
    own_ids = ids_ext[margin:]
    total = jnp.broadcast_to(bias[None, :], (length, bias.shape[0]))
    for offset in range(kernel.shape[0]):
        same = (ids_ext[offset:offset + length] == own_ids)[:, None]
        total = total + jnp.where(same, kernel[offset][None, :] * extended[offset:offset + length], 0.0)
    return jax.nn.silu(total)

def mixer(weights, pieces):
    in_proj, conv_kernel, conv_bias, x_proj, dt_proj, dt_bias, log_decay, skip_gain, out_proj = weights
    normed, marks = pieces
    inner = dt_proj.shape[1]
    rank_dt = dt_proj.shape[0]
    state_size = log_decay.shape[0]
    margin = conv_kernel.shape[0] - 1
    mixed_in = low_back(matmul(low(normed), in_proj))
    x_low = low(mixed_in[:, :inner])
    gate_z = mixed_in[:, inner:]
    doc_ids = jnp.cumsum(marks).astype(jnp.int32)
    ids_ext = jnp.concatenate([jnp.full((margin,), -1, jnp.int32), doc_ids])
    extended = jnp.concatenate([jnp.zeros((margin, inner), x_low.dtype), x_low])
    conv_out = convolve(ids_ext, extended, conv_kernel, conv_bias)
    projected = low_back(matmul(low(conv_out), x_proj.T))
    dtr = low(projected[:, :rank_dt])
    b_mat = projected[:, rank_dt:rank_dt + state_size]
    c_mat = projected[:, rank_dt + state_size:]
    dt = jax.nn.softplus(low_back(matmul(dtr, dt_proj)) + dt_bias)
    zero_state = jnp.zeros((state_size, inner), conv_out.dtype)
    scanned, h_end, product = scan_states(dt, b_mat, c_mat, conv_out, marks.astype(conv_out.dtype), -jnp.exp(log_decay), zero_state)
    gated = (scanned + skip_gain * conv_out) * jax.nn.silu(gate_z)
    return low_back(matmul(low(gated), out_proj))

def forward(route, resets, inputs, mixer_gain, in_proj, conv_kernel, conv_bias, x_proj, dt_proj, dt_bias, log_decay, skip_gain, out_proj, moe_gain, router, up_proj, down_proj):
    normed_one = rms_norm(inputs, mixer_gain)
    seq_count = inputs.shape[0] // SEQ
    in_flat = in_proj.reshape(in_proj.shape[0], -1)
    weights = (in_flat, conv_kernel, conv_bias, x_proj, dt_proj, dt_bias, log_decay, skip_gain, out_proj)
    branch = lax.map(jax.checkpoint(partial(mixer, weights)), (normed_one.reshape(seq_count, SEQ, -1), resets.reshape(seq_count, SEQ)))
    hidden_one = inputs + branch.reshape(inputs.shape)
    moe_low = low(rms_norm(hidden_one, moe_gain))
    logits = low_back(matmul(moe_low, router))
    probs = jax.nn.softmax(logits, axis=-1)
    experts = router.shape[1]
    picked = route[:, None] == jnp.arange(experts, dtype=jnp.int32)[None, :]
    gate = lax.optimization_barrier(jnp.sum(probs * picked.astype(probs.dtype), axis=-1))
    order = jnp.argsort(route, stable=True).astype(jnp.int32)
    counts = lax.optimization_barrier(jnp.sum(picked.astype(jnp.int32), axis=0)).astype(jnp.int32)
    starts = (jnp.cumsum(counts) - counts).astype(jnp.int32)
    most = N_EXPERT * N_ROWS * N_HID * CAP
    padded = jnp.concatenate([moe_low[order], jnp.zeros((most, moe_low.shape[1]), moe_low.dtype)])

    def expert_rows(pieces):
        up_one, down_one, start = pieces
        chosen = lax.dynamic_slice_in_dim(padded, start, most, 0)
        pre_act = low_back(matmul(chosen, up_one))
        hidden_act = low(jax.nn.gelu(pre_act, approximate=True))
        return low_back(matmul(hidden_act, down_one))
    results = lax.map(jax.checkpoint(expert_rows), (up_proj, down_proj, starts))
    sorted_route = route[order]
    position = (jnp.arange(inputs.shape[0], dtype=jnp.int32) - starts[sorted_route]).astype(jnp.int32)
    expert_out = results[sorted_route, position][jnp.argsort(order).astype(jnp.int32)]
    return hidden_one + gate[:, None] * expert_out

def reference(tokens, resets, routes, cotangent, mixer_gain, in_proj, conv_kernel, conv_bias, x_proj, dt_proj, dt_bias, log_decay, skip_gain, out_proj, moe_gain, router, up_proj, down_proj):
    floats = tuple((value.astype(jnp.float32) for value in (tokens, mixer_gain, in_proj, conv_kernel, conv_bias, x_proj, dt_proj, dt_bias, log_decay, skip_gain, out_proj, moe_gain, router, up_proj, down_proj)))
    output, pullback = jax.vjp(partial(forward, routes[:, 0], resets), *floats)
    grads = pullback(cotangent.astype(jnp.float32))
    return (output.astype(jnp.bfloat16), grads[0], grads[1], grads[2], grads[3], grads[4], grads[5], grads[6], grads[7], grads[8], grads[9], grads[10], grads[11], grads[12], grads[13], grads[14])
```

```python
from functools import partial

import jax
import jax.numpy as jnp
from jax import lax
from jax.experimental import pallas as pl
from jax.experimental.pallas import tpu as pltpu
from jax.sharding import PartitionSpec as P

EPS = 1e-05
LOG2E = 1.4426950408889634
STOP = 1e6
STEP = 16
F32 = jnp.float32
BF16 = jnp.bfloat16


def matmul(first_op, second_op):
    return jnp.dot(first_op, second_op, preferred_element_type=F32)


def inner_rows(first_op, second_op):
    return lax.dot_general(
        first_op, second_op, (((0,), (0,)), ((), ())), preferred_element_type=F32
    )


def outer_cols(first_op, second_op):
    return lax.dot_general(
        first_op, second_op, (((1,), (1,)), ((), ())), preferred_element_type=F32
    )


def rms_norm(values, gain):
    return values * lax.rsqrt(jnp.mean(values * values, axis=-1, keepdims=True) + EPS) * gain


def scan_forward_kernel(a_ref, dtm, dtx, b_cols, c_cols, y, starts, parts):
    a = a_ref[...]
    states, inner = a.shape
    half = states // 2

    def chunk(i, h):
        starts[i] = h
        for j in range(STEP):
            t = i * STEP + j
            if j % 8 == 0:
                b_now, c_now = b_cols[2 * i + j // 8], c_cols[2 * i + j // 8]
            at = j % 8
            decay = jnp.exp2(a * dtm[pl.ds(t, 1), :])
            h = decay * h + b_now[:, at : at + 1] * dtx[pl.ds(t, 1), :]
            p = c_now[:, at : at + 1] * h
            parts[j * half : (j + 1) * half, :] = p[:half] + p[half:]
        rows = pl.ds(pl.multiple_of(i * STEP, STEP), STEP)
        y[rows, :] = parts[...].reshape(STEP, half, inner).sum(axis=1)
        return h

    lax.fori_loop(0, dtm.shape[0] // STEP, chunk, jnp.zeros((states, inner), F32))


def scan_forward(a, dtm, dtx, b_cols, c_cols):
    (tokens, inner), states = dtm.shape, a.shape[0]
    return pl.pallas_call(
        scan_forward_kernel,
        out_shape=(
            jax.ShapeDtypeStruct((tokens, inner), F32),
            jax.ShapeDtypeStruct((tokens // STEP, states, inner), F32),
        ),
        scratch_shapes=[pltpu.VMEM((STEP * states // 2, inner), F32)],
        compiler_params=pltpu.CompilerParams(vmem_limit_bytes=32 << 20),
        name="scan_forward",
    )(a, dtm, dtx, b_cols, c_cols)


def over_lanes(v):
    whole = v.shape[1] // 128
    total = v[:, :128]
    for k in range(1, whole):
        total = total + v[:, k * 128 : (k + 1) * 128]
    rest = v.shape[1] - whole * 128
    if rest:
        blank = jnp.zeros((v.shape[0], 128 - rest), F32)
        total = total + jnp.concatenate([v[:, whole * 128 :], blank], axis=1)
    return total


def scan_backward_kernel(
    a_ref, dt, dtm, dtx, gy, b_cols, c_cols, starts, s1, s2, gb, gc, g_rate,
    held, decays, parts_1, parts_2, lanes_b, lanes_c,
):
    a = a_ref[...]
    states, inner = a.shape
    half = states // 2
    g_rate[...] = jnp.zeros_like(g_rate)
    row_at = lax.broadcasted_iota(jnp.int32, (STEP, STEP * half), 0)
    col_at = lax.broadcasted_iota(jnp.int32, (STEP, STEP * half), 1)
    picks = (col_at // half == row_at).astype(BF16)
    ones = jnp.ones((8, 128), BF16)
    chunks = dt.shape[0] // STEP

    def chunk(k, u):
        i = chunks - 1 - k
        h = starts[i]
        held[0] = h
        for j in range(STEP):
            t = i * STEP + j
            if j % 8 == 0:
                b_now = b_cols[2 * i + j // 8]
            at = j % 8
            decay = jnp.exp2(a * dtm[pl.ds(t, 1), :])
            h = decay * h + b_now[:, at : at + 1] * dtx[pl.ds(t, 1), :]
            decays[j] = decay
            held[j + 1] = h
        for j in range(STEP - 1, -1, -1):
            t = i * STEP + j
            if j % 8 == 7:
                b_now, c_now = b_cols[2 * i + j // 8], c_cols[2 * i + j // 8]
            at = j % 8
            gy_row = gy[pl.ds(t, 1), :]
            g = c_now[:, at : at + 1] * gy_row + u
            u = decays[j] * g
            q = u * held[j]
            g_rate[...] += q * dt[pl.ds(t, 1), :]
            w = q * a
            parts_2[j * half : (j + 1) * half, :] = w[:half] + w[half:]
            w = g * b_now[:, at : at + 1]
            parts_1[j * half : (j + 1) * half, :] = w[:half] + w[half:]
            lanes_b[j * states : (j + 1) * states, :] = over_lanes(g * dtx[pl.ds(t, 1), :])
            lanes_c[j * states : (j + 1) * states, :] = over_lanes(held[j + 1] * gy_row)
        rows = pl.ds(pl.multiple_of(i * STEP, STEP), STEP)
        s1[rows, :] = matmul(picks, parts_1[...].astype(BF16))
        s2[rows, :] = matmul(picks, parts_2[...].astype(BF16))
        gb[i] = outer_cols(ones, lanes_b[...].astype(BF16))
        gc[i] = outer_cols(ones, lanes_c[...].astype(BF16))
        return u

    lax.fori_loop(0, chunks, chunk, jnp.zeros((states, inner), F32))


def scan_backward(a, dt, dtm, dtx, gy, b_cols, c_cols, starts):
    (tokens, inner), states = dtm.shape, a.shape[0]
    line = jax.ShapeDtypeStruct((tokens, inner), F32)
    small = jax.ShapeDtypeStruct((tokens // STEP, 8, STEP * states), F32)
    return pl.pallas_call(
        scan_backward_kernel,
        out_shape=(line, line, small, small, jax.ShapeDtypeStruct((states, inner), F32)),
        scratch_shapes=[
            pltpu.VMEM((STEP + 1, states, inner), F32),
            pltpu.VMEM((STEP, states, inner), F32),
            pltpu.VMEM((STEP * states // 2, inner), F32),
            pltpu.VMEM((STEP * states // 2, inner), F32),
            pltpu.VMEM((STEP * states, 128), F32),
            pltpu.VMEM((STEP * states, 128), F32),
        ],
        compiler_params=pltpu.CompilerParams(vmem_limit_bytes=40 << 20),
        name="scan_backward",
    )(a, dt, dtm, dtx, gy, b_cols, c_cols, starts)


def columns_by_eight(values):
    tokens, states = values.shape
    return values.reshape(tokens // 8, 8, states).transpose(0, 2, 1)


def convolve(ids_ext, extended, kernel, bias):
    margin = kernel.shape[0] - 1
    length = extended.shape[0] - margin
    own_ids = ids_ext[margin:]
    total = jnp.broadcast_to(bias[None, :], (length, bias.shape[0]))
    for offset in range(kernel.shape[0]):
        same = (ids_ext[offset : offset + length] == own_ids)[:, None]
        total = total + jnp.where(
            same, kernel[offset][None, :] * extended[offset : offset + length], 0.0
        )
    return jax.nn.silu(total)


def gathered_hid(shard):
    return lax.all_gather(shard, "hid", axis=0, tiled=False)


def shares_summed(partial_rows, count):
    parts = partial_rows.astype(BF16).reshape(count, -1, partial_rows.shape[1])
    back = lax.all_to_all(parts, "hid", split_axis=0, concat_axis=0, tiled=True)
    return jnp.sum(back.astype(F32), axis=0)


def shards(
    tokens, resets, routes, cotangent, mixer_gain, in_proj, conv_kernel, conv_bias, x_proj, dt_proj,
    dt_bias, log_decay, skip_gain, out_proj, moe_gain, router, up_proj, down_proj,
):
    rows_dev, model = tokens.shape
    own = conv_bias.shape[0]
    experts = router.shape[1]
    rank, states, taps = dt_proj.shape[0], log_decay.shape[0], conv_kernel.shape[0]
    wide = rank + 2 * states
    owners = lax.axis_size("expert") * lax.axis_size("rows")
    hids = lax.axis_size("hid")
    capacity = 3 * rows_dev // (2 * experts)
    inner = owners * own
    mixer_axes = ("expert", "rows")

    in_lines = in_proj.transpose(2, 1, 0)
    norm_pack = jnp.concatenate([mixer_gain[:, None], moe_gain[:, None], router], axis=1)
    norm_cols = norm_pack.size // own
    small = jnp.concatenate(
        [
            x_proj.T, dt_proj.T, conv_kernel.T, conv_bias[:, None], dt_bias[:, None], log_decay.T,
            skip_gain[:, None], norm_pack.reshape(own, norm_cols),
        ],
        axis=1,
    )
    small_used = small.shape[1]
    small_width = -(-small_used // 128) * 128
    small = jnp.pad(small, ((0, 0), (0, small_width - small_used)))
    pack = jnp.concatenate([in_lines[:, 0], in_lines[:, 1], out_proj, small], axis=1)
    width = pack.shape[1]
    whole = lax.all_gather(pack, mixer_axes, axis=0, tiled=False)
    tokens_reset = jnp.concatenate(
        [tokens, jnp.broadcast_to(resets[:, None].astype(BF16), (rows_dev, 128))], axis=1
    )
    sequence = gathered_hid(tokens_reset).reshape(hids * rows_dev, -1)

    whole = whole.reshape(inner, width)
    in_x, in_gate = whole[:, :model], whole[:, model : 2 * model]
    out_full, small_full = whole[:, 2 * model : 3 * model], whole[:, 3 * model :]
    cuts = [rank + 2 * states, rank, taps, 1, 1, states, 1, norm_cols]
    pieces, at = [], 0
    for cut in cuts:
        pieces.append(small_full[:, at : at + cut])
        at += cut
    xp, dtp, kernel_t, conv_shift, dt_shift, decay_t, skip, norm_part = pieces
    norm_rows = gathered_hid(norm_part.reshape(owners, -1))
    norm_rows = norm_rows.transpose(1, 0, 2).reshape(model, 2 + experts)
    gain_one = norm_rows[:, 0].astype(F32)
    gain_two = norm_rows[:, 1].astype(F32)
    router_full = norm_rows[:, 2:]

    marks = sequence[:, model].astype(F32)
    all_rows = sequence[:, :model].astype(F32)
    normed_low = rms_norm(all_rows, gain_one).astype(BF16)
    inputs = tokens.astype(F32)

    x_low = outer_cols(normed_low, in_x).astype(BF16)
    gate_z = outer_cols(normed_low, in_gate)
    doc_ids = jnp.cumsum(marks.astype(jnp.int32))
    margin = taps - 1
    ids_ext = jnp.concatenate([jnp.full((margin,), -1, jnp.int32), doc_ids])
    extended = jnp.concatenate([jnp.zeros((margin, inner), F32), x_low.astype(F32)])
    conv_out, conv_back = jax.vjp(
        partial(convolve, ids_ext), extended, kernel_t.T.astype(F32), conv_shift[:, 0].astype(F32)
    )
    conv_low = conv_out.astype(BF16)
    projected = matmul(conv_low, xp)
    projected = jnp.sum(gathered_hid(projected.astype(BF16)).astype(F32), axis=0)
    dtr_low = projected[:, :rank].astype(BF16)
    b_cols = columns_by_eight(projected[:, rank : rank + states])
    c_cols = columns_by_eight(projected[:, rank + states :])
    dt_lin = outer_cols(dtr_low, dtp) + dt_shift[:, 0].astype(F32)[None, :]
    dt = jax.nn.softplus(dt_lin)
    dtm = dt + STOP * marks[:, None]
    dtx = dt * conv_out
    rate = jnp.exp(decay_t.T.astype(F32))
    a = rate * (-LOG2E)
    scanned, starts = scan_forward(a, dtm, dtx, b_cols, c_cols)
    skip_row = skip[:, 0].astype(F32)[None, :]
    y = scanned + skip_row * conv_out
    sig_z = jax.nn.sigmoid(gate_z)
    silu_z = gate_z * sig_z
    gated_low = (y * silu_z).astype(BF16)
    hidden_one = inputs + shares_summed(matmul(gated_low, out_full), hids)

    normed_two, norm_two_back = jax.vjp(rms_norm, hidden_one, gain_two)
    moe_low = normed_two.astype(BF16)
    probs = jax.nn.softmax(matmul(moe_low, router_full), axis=-1)
    picked = routes == jnp.arange(experts, dtype=jnp.int32)[None, :]
    onehot = picked.astype(F32)
    gate = jnp.sum(probs * onehot, axis=-1)
    picked_int = picked.astype(jnp.int32)
    within = jnp.sum(picked_int * (jnp.cumsum(picked_int, axis=0) - 1), axis=1)
    slot_index = routes[:, 0] * capacity + within
    selector = (
        jnp.arange(experts * capacity, dtype=jnp.int32)[:, None] == slot_index[None, :]
    ).astype(BF16)
    grad_output = cotangent.astype(F32)
    grad_eo = (gate[:, None] * grad_output).astype(BF16)
    up_local, down_local = up_proj[0], down_proj[0]

    def sent(rows):
        slots = matmul(selector, rows).astype(BF16).reshape(experts, 1, capacity, model)
        slots = jnp.broadcast_to(slots, (experts, hids, capacity, model))
        slots = slots.reshape(experts * hids, capacity, model)
        return lax.all_to_all(
            slots, ("expert", "hid"), split_axis=0, concat_axis=0, tiled=True
        ).reshape(-1, model)

    def returned(rows):
        back = lax.all_to_all(
            rows.astype(BF16).reshape(experts * hids, capacity, model),
            ("expert", "hid"), split_axis=0, concat_axis=0, tiled=True,
        )
        sums = jnp.sum(back.astype(F32).reshape(experts, hids, capacity, model), axis=1)
        return inner_rows(selector, sums.reshape(experts * capacity, model).astype(BF16))

    arrived = sent(moe_low)
    grad_arrived = sent(grad_eo)
    pre_act = matmul(arrived, up_local)
    hidden_act, gelu_back = jax.vjp(partial(jax.nn.gelu, approximate=True), pre_act)
    hidden_low = hidden_act.astype(BF16)
    expert_out = returned(matmul(hidden_low, down_local))
    grad_pre = gelu_back(outer_cols(grad_arrived, down_local))[0].astype(BF16)
    grad_rows = returned(outer_cols(grad_pre, up_local))
    grad_up = inner_rows(arrived, grad_pre).astype(BF16)
    grad_down = inner_rows(hidden_low, grad_arrived).astype(BF16)

    def over_rows(shard):
        mine = lax.psum_scatter(shard, "rows", scatter_dimension=0, tiled=True)
        return lax.all_gather(mine, "rows", axis=0, tiled=True).astype(F32)

    grad_up_sum, grad_down_sum = over_rows(grad_up), over_rows(grad_down)
    output = (hidden_one + gate[:, None] * expert_out).astype(BF16)
    grad_gate = jnp.sum(grad_output * expert_out, axis=-1)
    grad_logits = ((gate * grad_gate)[:, None] * (onehot - probs)).astype(BF16)
    grad_router = inner_rows(moe_low, grad_logits)
    grad_moe = grad_rows + outer_cols(grad_logits, router_full)
    grad_hidden_more, grad_gain_two = norm_two_back(grad_moe)
    grad_hidden = grad_output + grad_hidden_more

    grad_seq = gathered_hid(grad_hidden.astype(BF16)).reshape(hids * rows_dev, model)
    grad_out_proj = inner_rows(gated_low, grad_seq)
    grad_gated = outer_cols(grad_seq, out_full)
    grad_y = grad_gated * silu_z
    grad_gate_z = grad_gated * y * (sig_z * (1.0 + gate_z * (1.0 - sig_z)))
    s1, s2, gb, gc, g_rate = scan_backward(a, dt, dtm, dtx, grad_y, b_cols, c_cols, starts)
    grad_dt_lin = jax.nn.sigmoid(dt_lin) * (conv_out * s1 + s2 * (1.0 / LOG2E))
    grad_log_decay = -rate * g_rate
    grad_skip = jnp.sum(grad_y * conv_out, axis=0)
    grad_dt_bias = jnp.sum(grad_dt_lin, axis=0)
    grad_scan_x = skip_row * grad_y + dt * s1
    grad_dt_low = grad_dt_lin.astype(BF16)
    grad_b = gb[:, 0].reshape(-1, states)
    grad_c = gc[:, 0].reshape(-1, states)
    grad_proj = jnp.concatenate([matmul(grad_dt_low, dtp), grad_b, grad_c], axis=1)
    grad_proj = jnp.sum(gathered_hid(grad_proj.astype(BF16)).astype(F32), axis=0).astype(BF16)
    grad_dt_proj = inner_rows(grad_dt_low, dtr_low)
    grad_x_proj = inner_rows(conv_low, grad_proj)
    grad_conv_out = grad_scan_x + outer_cols(grad_proj, xp)
    grad_ext, grad_kernel, grad_conv_bias = conv_back(grad_conv_out)
    grad_x_low = grad_ext[margin:].astype(BF16)
    grad_gate_low = grad_gate_z.astype(BF16)
    grad_in_x = inner_rows(grad_x_low, normed_low)
    grad_in_gate = inner_rows(grad_gate_low, normed_low)
    grad_normed = shares_summed(matmul(grad_x_low, in_x) + matmul(grad_gate_low, in_gate), hids)
    unused, norm_one_back = jax.vjp(rms_norm, inputs, gain_one)
    grad_more, grad_gain_one = norm_one_back(grad_normed)
    grad_tokens = grad_hidden + grad_more

    norm_grads = jnp.concatenate([grad_gain_one[:, None], grad_gain_two[:, None], grad_router], axis=1)
    norm_grads = norm_grads.reshape(owners, hids, -1).transpose(1, 0, 2)
    norm_grads = lax.psum_scatter(norm_grads, "hid", scatter_dimension=0, tiled=True)
    grad_small = jnp.concatenate(
        [
            grad_x_proj, grad_dt_proj, grad_kernel.T, grad_conv_bias[:, None], grad_dt_bias[:, None],
            grad_log_decay.T, grad_skip[:, None], norm_grads.reshape(inner, norm_cols),
        ],
        axis=1,
    )
    grad_small = jnp.pad(grad_small, ((0, 0), (0, small_width - small_used)))

    def to_owners(grads):
        back = lax.all_to_all(
            grads.astype(BF16).reshape(owners, own, -1),
            mixer_axes, split_axis=0, concat_axis=0, tiled=True,
        )
        return jnp.sum(back.astype(F32), axis=0)

    out_part = to_owners(grad_out_proj)
    rest = to_owners(jnp.concatenate([grad_in_x, grad_in_gate, grad_small], axis=1))
    grad_in = jnp.stack([rest[:, :model], rest[:, model : 2 * model]], axis=1).transpose(2, 1, 0)
    small_sum = rest[:, 2 * model :]
    done, at = [], 0
    for cut in cuts:
        done.append(small_sum[:, at : at + cut])
        at += cut
    norm_sum = done[7].reshape(model // (owners * hids), 2 + experts)
    return (
        output,
        grad_tokens,
        norm_sum[:, 0],
        grad_in,
        done[2].T,
        done[3][:, 0],
        done[0].T,
        done[1].T,
        done[4][:, 0],
        done[5].T,
        done[6][:, 0],
        out_part,
        norm_sum[:, 1],
        norm_sum[:, 2:],
        grad_up_sum[None],
        grad_down_sum[None],
    )


def solution(mesh):
    every = ("expert", "rows", "hid")
    in_specs = (
        P(every, None), P(every), P(every, None), P(every, None), P(every), P(None, None, every),
        P(None, every), P(every), P(None, every), P(None, every), P(every), P(None, every), P(every),
        P(every, None), P(every), P(every, None), P("expert", None, "hid"), P("expert", "hid", None),
    )
    out_specs = (
        P(every, None), P(every, None), P(every), P(None, None, every), P(None, every), P(every),
        P(None, every), P(None, every), P(every), P(None, every), P(every), P(every, None), P(every),
        P(every, None), P("expert", None, "hid"), P("expert", "hid", None),
    )
    return jax.shard_map(shards, mesh=mesh, in_specs=in_specs, out_specs=out_specs, check_vma=False)
```

```python
from functools import partial

import jax
import jax.numpy as jnp
from jax import lax
from jax.experimental import pallas as pl
from jax.experimental.pallas import tpu as pltpu
from jax.sharding import PartitionSpec as P

EPS = 1e-05
LOG2E = 1.4426950408889634
STOP = 1e6
STEP = 16
MAIN = 16
EXTRA = 512
GELU_C = 0.7978845608028654
F32 = jnp.float32
BF16 = jnp.bfloat16


def matmul(first_op, second_op):
    return jnp.dot(first_op, second_op, preferred_element_type=F32)


def inner_rows(first_op, second_op):
    return lax.dot_general(
        first_op, second_op, (((0,), (0,)), ((), ())), preferred_element_type=F32
    )


def outer_cols(first_op, second_op):
    return lax.dot_general(
        first_op, second_op, (((1,), (1,)), ((), ())), preferred_element_type=F32
    )


def rms_norm(values, gain):
    return values * lax.rsqrt(jnp.mean(values * values, axis=-1, keepdims=True) + EPS) * gain


def scan_forward_kernel(a_ref, dtm, dtx, b_cols, c_cols, y, starts, parts):
    a = a_ref[...]
    states, inner = a.shape
    half = states // 2

    def chunk(i, h):
        starts[i] = h
        for j in range(STEP):
            t = i * STEP + j
            if j % 8 == 0:
                b_now, c_now = b_cols[2 * i + j // 8], c_cols[2 * i + j // 8]
            at = j % 8
            decay = jnp.exp2(a * dtm[pl.ds(t, 1), :])
            h = decay * h + b_now[:, at : at + 1] * dtx[pl.ds(t, 1), :]
            p = c_now[:, at : at + 1] * h
            parts[j * half : (j + 1) * half, :] = p[:half] + p[half:]
        rows = pl.ds(pl.multiple_of(i * STEP, STEP), STEP)
        y[rows, :] = parts[...].reshape(STEP, half, inner).sum(axis=1)
        return h

    lax.fori_loop(0, dtm.shape[0] // STEP, chunk, jnp.zeros((states, inner), F32))


def scan_forward(a, dtm, dtx, b_cols, c_cols):
    (tokens, inner), states = dtm.shape, a.shape[0]
    return pl.pallas_call(
        scan_forward_kernel,
        out_shape=(
            jax.ShapeDtypeStruct((tokens, inner), F32),
            jax.ShapeDtypeStruct((tokens // STEP, states, inner), F32),
        ),
        scratch_shapes=[pltpu.VMEM((STEP * states // 2, inner), F32)],
        compiler_params=pltpu.CompilerParams(vmem_limit_bytes=32 << 20),
        name="scan_forward",
    )(a, dtm, dtx, b_cols, c_cols)


def over_lanes(v):
    whole = v.shape[1] // 128
    total = v[:, :128]
    for k in range(1, whole):
        total = total + v[:, k * 128 : (k + 1) * 128]
    rest = v.shape[1] - whole * 128
    if rest:
        blank = jnp.zeros((v.shape[0], 128 - rest), F32)
        total = total + jnp.concatenate([v[:, whole * 128 :], blank], axis=1)
    return total


def scan_backward_kernel(
    a_ref, dt, dtm, dtx, gy, b_cols, c_cols, starts, s1, s2, gb, gc, g_rate,
    held, decays, parts_1, parts_2, lanes_b, lanes_c,
):
    a = a_ref[...]
    states, inner = a.shape
    half = states // 2
    g_rate[...] = jnp.zeros_like(g_rate)
    row_at = lax.broadcasted_iota(jnp.int32, (STEP, STEP * half), 0)
    col_at = lax.broadcasted_iota(jnp.int32, (STEP, STEP * half), 1)
    picks = (col_at // half == row_at).astype(BF16)
    ones = jnp.ones((8, 128), BF16)
    chunks = dt.shape[0] // STEP

    def chunk(k, u):
        i = chunks - 1 - k
        h = starts[i]
        held[0] = h
        for j in range(STEP):
            t = i * STEP + j
            if j % 8 == 0:
                b_now = b_cols[2 * i + j // 8]
            at = j % 8
            decay = jnp.exp2(a * dtm[pl.ds(t, 1), :])
            h = decay * h + b_now[:, at : at + 1] * dtx[pl.ds(t, 1), :]
            decays[j] = decay
            held[j + 1] = h
        for j in range(STEP - 1, -1, -1):
            t = i * STEP + j
            if j % 8 == 7:
                b_now, c_now = b_cols[2 * i + j // 8], c_cols[2 * i + j // 8]
            at = j % 8
            gy_row = gy[pl.ds(t, 1), :]
            g = c_now[:, at : at + 1] * gy_row + u
            u = decays[j] * g
            q = u * held[j]
            g_rate[...] += q * dt[pl.ds(t, 1), :]
            w = q * a
            parts_2[j * half : (j + 1) * half, :] = w[:half] + w[half:]
            w = g * b_now[:, at : at + 1]
            parts_1[j * half : (j + 1) * half, :] = w[:half] + w[half:]
            lanes_b[j * states : (j + 1) * states, :] = over_lanes(g * dtx[pl.ds(t, 1), :])
            lanes_c[j * states : (j + 1) * states, :] = over_lanes(held[j + 1] * gy_row)
        rows = pl.ds(pl.multiple_of(i * STEP, STEP), STEP)
        s1[rows, :] = matmul(picks, parts_1[...].astype(BF16))
        s2[rows, :] = matmul(picks, parts_2[...].astype(BF16))
        gb[i] = outer_cols(ones, lanes_b[...].astype(BF16))
        gc[i] = outer_cols(ones, lanes_c[...].astype(BF16))
        return u

    lax.fori_loop(0, chunks, chunk, jnp.zeros((states, inner), F32))


def scan_backward(a, dt, dtm, dtx, gy, b_cols, c_cols, starts):
    (tokens, inner), states = dtm.shape, a.shape[0]
    line = jax.ShapeDtypeStruct((tokens, inner), F32)
    small = jax.ShapeDtypeStruct((tokens // STEP, 8, STEP * states), F32)
    return pl.pallas_call(
        scan_backward_kernel,
        out_shape=(line, line, small, small, jax.ShapeDtypeStruct((states, inner), F32)),
        scratch_shapes=[
            pltpu.VMEM((STEP + 1, states, inner), F32),
            pltpu.VMEM((STEP, states, inner), F32),
            pltpu.VMEM((STEP * states // 2, inner), F32),
            pltpu.VMEM((STEP * states // 2, inner), F32),
            pltpu.VMEM((STEP * states, 128), F32),
            pltpu.VMEM((STEP * states, 128), F32),
        ],
        compiler_params=pltpu.CompilerParams(vmem_limit_bytes=40 << 20),
        name="scan_backward",
    )(a, dt, dtm, dtx, gy, b_cols, c_cols, starts)


def columns_by_eight(values):
    tokens, states = values.shape
    return values.reshape(tokens // 8, 8, states).transpose(0, 2, 1)


def convolve(ids_ext, extended, kernel, bias):
    margin = kernel.shape[0] - 1
    length = extended.shape[0] - margin
    own_ids = ids_ext[margin:]
    total = jnp.broadcast_to(bias[None, :], (length, bias.shape[0]))
    for offset in range(kernel.shape[0]):
        same = (ids_ext[offset : offset + length] == own_ids)[:, None]
        total = total + jnp.where(
            same, kernel[offset][None, :] * extended[offset : offset + length], 0.0
        )
    return jax.nn.silu(total)


MESH = pl.DeviceIdType.MESH
ANY = pl.BlockSpec(memory_space=pl.ANY)
IN_VMEM = pl.BlockSpec(memory_space=pltpu.VMEM)
DMA = pltpu.SemaphoreType.DMA


def places():
    return lax.axis_index("expert"), lax.axis_index("rows"), lax.axis_index("hid")


def greet(peers):
    barrier = pltpu.get_barrier_semaphore()
    for peer in peers:
        pl.semaphore_signal(barrier, inc=1, device_id=peer, device_id_type=MESH)
    pl.semaphore_wait(barrier, len(peers))


def remote(src, dst, send_sem, recv_sem, peer):
    return pltpu.make_async_remote_copy(
        src_ref=src, dst_ref=dst, send_sem=send_sem, recv_sem=recv_sem, device_id=peer,
        device_id_type=MESH,
    )


def hid_peers():
    e, r, h = places()
    return [(e, r, lax.rem(h + k, 4)) for k in (1, 2, 3)]


def mixer_peers():
    e, r, h = places()
    c = lax.rem(e, 2)
    mate = (e + 1 - 2 * c, r, h)
    first = [(lax.rem(e + 2 * k * (1 - c), 8), lax.rem(r + k * c, 4), h) for k in (1, 2, 3)]
    second = [(lax.rem(e + 2 * k * c, 8), lax.rem(r + k * (1 - c), 4), h) for k in (1, 2, 3)]
    return mate, first, second


def block_at(c, f, s):
    y = f * (1 - c) + s * c
    x = s * (1 - c) + f * c
    return (2 * y + c) * 4 + x


def gather_kernel(
    pack, norm, line, whole, norms, sequence, tiles, total, local_sems, z_send, z_recv, n_send, n_recv,
    w_send, w_recv, v_send, v_recv,
):
    e, r, h = places()
    c = lax.rem(e, 2)
    y = e // 2
    f0 = y * (1 - c) + r * c
    s0 = r * (1 - c) + y * c
    mate, first, second = mixer_peers()
    z_peers = hid_peers()
    own = e * 4 + r
    greet([mate] + first + second + z_peers)
    n_copies = [
        remote(norm, tiles.at[k], n_send.at[k], n_recv.at[k], z_peers[k]) for k in range(3)
    ]
    for copy in n_copies:
        copy.start()
    w_one = [remote(pack, whole.at[own], w_send.at[k], w_recv.at[k], first[k]) for k in range(3)]
    w_two = [[remote(pack, whole.at[own], w_send.at[3 + k], w_recv.at[3 + k], second[k]) for k in range(3)]]
    w_mate = [remote(pack, whole.at[own], w_send.at[15], w_recv.at[15], mate)]
    for k in (1, 0, 2):
        w_one[k].start()
    for k in (1, 0, 2):
        w_two[0][k].start()
    z_copies = [remote(line, sequence.at[h], z_send.at[k], z_recv.at[k], z_peers[k]) for k in range(3)]
    for k in (1, 0, 2):
        z_copies[k].start()
    w_mate[0].start()
    mine = [
        pltpu.make_async_copy(pack, whole.at[own], local_sems.at[0]),
        pltpu.make_async_copy(line, sequence.at[h], local_sems.at[1]),
    ]
    for copy in mine:
        copy.start()
    for copy in n_copies:
        copy.wait_recv()
    total[...] = norm[...] + tiles[0] + tiles[1] + tiles[2]
    v_one = [remote(total, norms.at[own], v_send.at[k], v_recv.at[k], first[k]) for k in range(3)]
    v_two = [[remote(total, norms.at[own], v_send.at[3 + k], v_recv.at[3 + k], second[k]) for k in range(3)]]
    v_mate = [remote(total, norms.at[own], v_send.at[15], v_recv.at[15], mate)]
    for copy in v_one + v_two[0] + v_mate:
        copy.start()
    mine.append(pltpu.make_async_copy(total, norms.at[own], local_sems.at[2]))
    mine[2].start()
    for k in range(3):
        came = block_at(c, lax.rem(f0 + 3 - k, 4), s0)
        for buf, one, send, recv, two, other in (
            (whole, w_one, w_send, w_recv, w_two, w_mate), (norms, v_one, v_send, v_recv, v_two, v_mate)
        ):
            one[k].wait_recv()
            block = buf.at[came]
            two.append([remote(block, block, send.at[6 + 3 * k + j], recv.at[6 + 3 * k + j], second[j]) for j in range(3)])
            for j in (1, 0, 2):
                two[1 + k][j].start()
            other.append(remote(block, block, send.at[16 + k], recv.at[16 + k], mate))
            other[-1].start()
    for k in range(4):
        for j in range(3):
            came = block_at(c, lax.rem(f0 + 4 - k, 4), lax.rem(s0 + 3 - j, 4))
            for buf, send, recv, two, other in (
                (whole, w_send, w_recv, w_two, w_mate), (norms, v_send, v_recv, v_two, v_mate)
            ):
                two[k][j].wait_recv()
                block = buf.at[came]
                at = 19 + 3 * k + j
                other.append(remote(block, block, send.at[at], recv.at[at], mate))
                other[-1].start()
    for copy in w_mate + v_mate:
        copy.wait_recv()
    for copy in z_copies:
        copy.wait_recv()
    for copy in n_copies + w_one + sum(w_two, []) + w_mate + v_one + sum(v_two, []) + v_mate + z_copies:
        copy.wait_send()
    for copy in mine:
        copy.wait()


def gather_start(pack, norm, line):
    return pl.pallas_call(
        gather_kernel,
        out_shape=(
            jax.ShapeDtypeStruct((32, *pack.shape), BF16),
            jax.ShapeDtypeStruct((32, *norm.shape), BF16),
            jax.ShapeDtypeStruct((4, *line.shape), BF16),
        ),
        in_specs=[IN_VMEM] * 3,
        out_specs=(ANY, ANY, ANY),
        scratch_shapes=[
            pltpu.VMEM((3, *norm.shape), BF16),
            pltpu.VMEM(norm.shape, BF16),
            DMA((3,)), DMA((3,)), DMA((3,)), DMA((3,)), DMA((3,)), DMA((31,)), DMA((31,)), DMA((31,)), DMA((31,)),
        ],
        compiler_params=pltpu.CompilerParams(
            collective_id=1, has_side_effects=True, vmem_limit_bytes=32 << 20
        ),
        name="gather_start",
    )(pack, norm, line)


def hid_kernel(mode, src, dst, *scratch):
    e, r, h = places()
    peers = hid_peers()
    landing, send, recv = (dst, *scratch) if mode == 0 else scratch
    greet(peers)
    copies = []
    for k in (1, 0, 2):
        part = src.at[lax.rem(h + 1 + k, 4)] if mode == 2 else src
        place = landing.at[h] if mode == 0 else landing.at[k]
        copies.append(remote(part, place, send.at[k], recv.at[k], peers[k]))
        copies[-1].start()
    if mode == 0:
        dst[h] = src[...]
    for copy in copies:
        copy.wait_recv()
    if mode != 0:
        mine = src[h] if mode == 2 else src[...]
        dst[...] = (
            mine.astype(F32) + landing[0].astype(F32) + landing[1].astype(F32) + landing[2].astype(F32)
        )
    for copy in copies:
        copy.wait_send()


def over_hid(mode, values, number):
    part = values.shape[1:] if mode == 2 else values.shape
    out = jax.ShapeDtypeStruct((4, *part) if mode == 0 else part, BF16 if mode == 0 else F32)
    landing = [] if mode == 0 else [pltpu.VMEM((3, *part), BF16)]
    return pl.pallas_call(
        partial(hid_kernel, mode),
        out_shape=out,
        in_specs=[IN_VMEM],
        out_specs=IN_VMEM,
        scratch_shapes=[*landing, DMA((3,)), DMA((3,))],
        compiler_params=pltpu.CompilerParams(
            collective_id=number, has_side_effects=True, vmem_limit_bytes=32 << 20
        ),
        name=f"over_hid_{number}",
    )(values)


def return_kernel(
    grads, summed, tile_sum, pairs, halves, lines, fours, ends, own_tile, tiles, m_send, m_recv, s_send, s_recv,
    f_send, f_recv, z_send, z_recv,
):
    e, r, h = places()
    c = lax.rem(e, 2)
    y = e // 2
    f0 = y * (1 - c) + r * c
    s0 = r * (1 - c) + y * c
    mate, first, second = mixer_peers()
    z_peers = hid_peers()
    width = grads.shape[2]
    greet([mate] + first + second + z_peers)
    other = 1 - c
    mate_s0 = r * (1 - other) + y * other
    m_copies = []
    for n, k in enumerate((2, 1, 3, 0)):
        for f in range(4):
            s = lax.rem(mate_s0 + k, 4)
            m_copies.append(
                remote(grads.at[block_at(other, f, s)], pairs.at[n, f], m_send.at[n * 4 + f], m_recv.at[n * 4 + f], mate)
            )
            m_copies[-1].start()
    s_copies = []
    for n, k in enumerate((2, 1, 3, 0)):
        s = lax.rem(s0 + k, 4)
        for f in range(4):
            m_copies[n * 4 + f].wait_recv()
            block = block_at(c, f, s)
            halves[n, f] = (grads[block].astype(F32) + pairs[n, f].astype(F32)).astype(BF16)
        if k:
            s_copies.append(remote(halves.at[n], fours.at[n], s_send.at[n], s_recv.at[n], second[k - 1]))
            s_copies[-1].start()
    for copy in s_copies:
        copy.wait_recv()
    f_copies = []
    for n, k in enumerate((2, 1, 3, 0)):
        f = lax.rem(f0 + k, 4)
        line = (
            halves[3, f].astype(F32) + fours[0, f].astype(F32) + fours[1, f].astype(F32) + fours[2, f].astype(F32)
        )
        if k:
            lines[n] = line.astype(BF16)
            f_copies.append(remote(lines.at[n], ends.at[n], f_send.at[n], f_recv.at[n], first[k - 1]))
            f_copies[-1].start()
        else:
            for copy in f_copies:
                copy.wait_recv()
            line = line + ends[0].astype(F32) + ends[1].astype(F32) + ends[2].astype(F32)
            summed[...] = line
            own_tile[...] = line[:, width - 128 :].astype(BF16)
    z_copies = [remote(own_tile, tiles.at[k], z_send.at[k], z_recv.at[k], z_peers[k]) for k in range(3)]
    for copy in z_copies:
        copy.start()
    for copy in z_copies:
        copy.wait_recv()
    tile_sum[...] = (
        summed[:, width - 128 :] + tiles[0].astype(F32) + tiles[1].astype(F32) + tiles[2].astype(F32)
    )
    for copy in m_copies + s_copies + f_copies + z_copies:
        copy.wait_send()


def return_grads(grads):
    owners, rows, width = grads.shape
    return pl.pallas_call(
        return_kernel,
        out_shape=(jax.ShapeDtypeStruct((rows, width), F32), jax.ShapeDtypeStruct((rows, 128), F32)),
        in_specs=[IN_VMEM],
        out_specs=(IN_VMEM, IN_VMEM),
        scratch_shapes=[
            pltpu.VMEM((4, 4, rows, width), BF16),
            pltpu.VMEM((4, 4, rows, width), BF16),
            pltpu.VMEM((3, rows, width), BF16),
            pltpu.VMEM((3, 4, rows, width), BF16),
            pltpu.VMEM((3, rows, width), BF16),
            pltpu.VMEM((rows, 128), BF16),
            pltpu.VMEM((3, rows, 128), BF16),
            DMA((16,)), DMA((16,)), DMA((3,)), DMA((3,)), DMA((3,)), DMA((3,)), DMA((3,)), DMA((3,)),
        ],
        compiler_params=pltpu.CompilerParams(
            collective_id=2, has_side_effects=True, vmem_limit_bytes=40 << 20
        ),
        name="return_grads",
    )(grads)


def gelu_pair(pre, grad):
    square = pre * pre
    t = jnp.tanh(GELU_C * pre * (1.0 + 0.044715 * square))
    up = 0.5 * (1.0 + t)
    slope = up + 0.5 * pre * (1.0 - t * t) * (GELU_C * (1.0 + 3 * 0.044715 * square))
    return pre * up, slope * grad


def expert_kernel(
    slots, up, down, back, g_up, g_down, held, results, hid_out, pre_out, hid_w, pre_w, from_left, from_right,
    half_left, half_right, sums, d_send, d_recv, r_send, r_recv, l_send, l_recv, f_send, f_recv, c_send, c_recv,
    k_send, k_recv, h_send, h_recv, b_send, b_recv,
):
    e, r, h = places()
    model, hidden = up.shape
    right, left, across = lax.rem(h + 1, 4), lax.rem(h + 3, 4), lax.rem(h + 2, 4)
    to_right, to_left = (e, r, right), (e, r, left)
    to_expert = [(lax.rem(e + k, 8), r, h) for k in range(8)]
    source = [lax.rem(e + 8 - k, 8) for k in range(8)]
    greet(to_expert[1:] + [to_right, to_left])

    d_copies = [None]
    for k in range(1, 8):
        d_copies.append(
            remote(slots.at[lax.rem(e + k, 8)], held.at[h, e], d_send.at[k], d_recv.at[k], to_expert[k])
        )
        d_copies[k].start()
    held[h, e] = slots[e]

    def along(buf, where, k, send, recv, peer):
        block = buf.at[where, source[k]]
        copy = remote(block, block, send.at[k], recv.at[k], peer)
        copy.start()
        return copy

    r_copies, l_copies = [None] * 8, [None] * 8
    for k in range(8):
        if k:
            d_copies[k].wait_recv()
        r_copies[k] = along(held, h, k, r_send, r_recv, to_right)
        if k >= 4:
            l_copies[k] = along(held, h, k, l_send, l_recv, to_left)
    for k in range(4):
        l_copies[k] = along(held, h, k, l_send, l_recv, to_left)

    half = 128

    def worked(where):
        lines = held[where]
        main_x = lines[:, :, :model].reshape(half, model)
        main_g = lines[:, :, model : 2 * model].reshape(half, model)
        extra = lines[:, :, 2 * model :].reshape(half, model)
        rows_x = jnp.concatenate([main_x, extra], axis=0)
        rows_g = jnp.concatenate([main_g, extra], axis=0)

        def first_layer(i, carry):
            cols = pl.ds(pl.multiple_of(i * 256, 256), 256)
            pre = matmul(rows_x, up[:, cols])
            grad = outer_cols(rows_g, down[cols, :])
            hid_m, pre_m = gelu_pair(pre[:half], grad[:half])
            pre_e = pre[half:].reshape(8, 2, 8, 256)[:, 0]
            grad_e = grad[half:].reshape(8, 2, 8, 256)[:, 1]
            hid_e, gpre_e = gelu_pair(pre_e, grad_e)
            none = jnp.zeros_like(hid_e)

            def stacked(a, b):
                return jnp.stack([a, b], axis=1).reshape(half, 256).astype(BF16)

            hid_m, pre_m = hid_m.astype(BF16), pre_m.astype(BF16)
            hid_out[:half, cols] = hid_m
            pre_out[:half, cols] = pre_m
            hid_w[where, :half, cols] = hid_m
            pre_w[where, :half, cols] = pre_m
            hid_out[half:, cols] = stacked(hid_e, none)
            pre_out[half:, cols] = stacked(none, gpre_e)
            hid_w[where, half:, cols] = stacked(none, hid_e)
            pre_w[where, half:, cols] = stacked(gpre_e, none)
            return carry

        lax.fori_loop(0, hidden // 256, first_layer, 0)

        def second_layer(i, carry):
            at = pl.multiple_of(i * 384, 384)
            cols = pl.ds(at, 384)
            share = matmul(hid_out[...], down[:, cols])
            grad = outer_cols(pre_out[...], up[cols, :])
            shape = (8, 16, 384)
            results[where, :, :, cols] = share[:half].astype(BF16).reshape(shape)
            results[where, :, :, pl.ds(model + at, 384)] = grad[:half].astype(BF16).reshape(shape)
            results[where, :, :, pl.ds(2 * model + at, 384)] = (share[half:] + grad[half:]).astype(BF16).reshape(shape)
            return carry

        lax.fori_loop(0, model // 384, second_layer, 0)

    worked(h)
    f_copies = [None] * 8
    for k in range(4):
        r_copies[k].wait_recv()
        f_copies[k] = along(held, left, k, f_send, f_recv, to_right)
        l_copies[4 + k].wait_recv()
        f_copies[4 + k] = along(held, right, 4 + k, f_send, f_recv, to_left)
    for k in range(4, 8):
        r_copies[k].wait_recv()
    worked(left)
    c_copies = [None] * 8
    k_copies = [None] * 8

    def toward_right(k):
        block = results.at[right, source[k]]
        c_copies[k] = remote(block, from_left.at[k], c_send.at[k], c_recv.at[k], to_right)
        c_copies[k].start()

    def toward_left(k):
        block = results.at[left, source[k]]
        k_copies[k] = remote(block, from_right.at[k], k_send.at[k], k_recv.at[k], to_left)
        k_copies[k].start()

    for k in range(4):
        toward_left(k)
    for k in range(4):
        l_copies[k].wait_recv()
    worked(right)
    for k in range(4, 8):
        toward_right(k)
    for k in range(8):
        f_copies[k].wait_recv()
    worked(across)
    h_copies = []
    for k in range(4):
        for at, landing, peer in ((k, half_left, to_right), (4 + k, half_right, to_left)):
            block = results.at[across, source[at]]
            copy = remote(block, landing.at[k], h_send.at[at], h_recv.at[at], peer)
            copy.start()
            h_copies.append(copy)

    def weight_grads(i, carry):
        cols = pl.ds(pl.multiple_of(i * 128, 128), 128)
        total = jnp.zeros((128, hidden), F32)
        for lanes, kept, out in ((0, pre_w, g_up),):
            x_main = held[:, :, :, pl.ds(pl.multiple_of(i * 128, 128), 128)].reshape(4, half, 128)
            x_extra = held[:, :, :, pl.ds(pl.multiple_of(2 * model + i * 128, 128), 128)].reshape(4, half, 128)
            rows = jnp.concatenate([x_main, x_extra], axis=1).reshape(8 * half, 128)
            total = inner_rows(rows, kept[...].reshape(8 * half, hidden))
            out[cols, :] = total.astype(BF16)
        g_main = held[:, :, :, pl.ds(pl.multiple_of(model + i * 128, 128), 128)].reshape(4, half, 128)
        rows = jnp.concatenate([g_main, x_extra], axis=1).reshape(8 * half, 128)
        g_down[:, cols] = inner_rows(hid_w[...].reshape(8 * half, hidden), rows).astype(BF16)
        return carry

    lax.fori_loop(0, model // 128, weight_grads, 0)

    for k in range(4):
        h_copies[2 * k].wait_recv()
        block = source[k]
        results[right, block] = (results[right, block].astype(F32) + half_left[k].astype(F32)).astype(BF16)
        toward_right(k)
        h_copies[2 * k + 1].wait_recv()
        block = source[4 + k]
        results[left, block] = (results[left, block].astype(F32) + half_right[k].astype(F32)).astype(BF16)
        toward_left(4 + k)
    b_copies = []
    for k in (4, 5, 6, 7, 3, 2, 1, 0):
        c_copies[k].wait_recv()
        k_copies[k].wait_recv()
        total = results[h, source[k]].astype(F32) + from_left[k].astype(F32) + from_right[k].astype(F32)
        if k:
            sums[k] = total.astype(BF16)
            copy = remote(sums.at[k], back.at[e], b_send.at[k], b_recv.at[k], to_expert[8 - k])
            copy.start()
            b_copies.append(copy)
        else:
            back[e] = total.astype(BF16)
    for copy in b_copies:
        copy.wait_recv()
    for copy in d_copies[1:] + r_copies + l_copies + f_copies + c_copies + k_copies + h_copies + b_copies:
        copy.wait_send()


def experts_both_ways(slots, up, down):
    count, lines, width = slots.shape
    model, hidden = up.shape
    eight = DMA((8,))
    return pl.pallas_call(
        expert_kernel,
        out_shape=(
            jax.ShapeDtypeStruct(slots.shape, BF16),
            jax.ShapeDtypeStruct(up.shape, BF16),
            jax.ShapeDtypeStruct(down.shape, BF16),
        ),
        in_specs=[IN_VMEM] * 3,
        out_specs=(IN_VMEM,) * 3,
        scratch_shapes=[
            pltpu.VMEM((4, count, lines, width), BF16),
            pltpu.VMEM((4, count, lines, width), BF16),
            pltpu.VMEM((256, hidden), BF16),
            pltpu.VMEM((256, hidden), BF16),
            pltpu.VMEM((4, 256, hidden), BF16),
            pltpu.VMEM((4, 256, hidden), BF16),
            pltpu.VMEM((8, lines, width), BF16),
            pltpu.VMEM((8, lines, width), BF16),
            pltpu.VMEM((4, lines, width), BF16),
            pltpu.VMEM((4, lines, width), BF16),
            pltpu.VMEM((8, lines, width), BF16),
            *[eight] * 16,
        ],
        compiler_params=pltpu.CompilerParams(
            collective_id=8, has_side_effects=True, vmem_limit_bytes=48 << 20
        ),
        name="experts",
    )(slots, up, down)


def spread_extra(lines):
    count, rows, width = lines.shape
    lines = jnp.pad(lines, ((0, 0), (0, 0), (0, MAIN * EXTRA // rows - width)))
    return lines.reshape(count, MAIN, EXTRA)


def gathered_extra(tiles, width):
    count = tiles.shape[0]
    return tiles.reshape(count, 2, MAIN * EXTRA // 2)[:, :, :width]


def joined_channels(whole, width):
    extra = gathered_extra(whole[:, :, width:], width).reshape(-1, width)
    return jnp.concatenate([whole[:, :, :width].reshape(-1, width), extra], axis=0)


def shards(
    tokens, resets, routes, cotangent, mixer_gain, in_proj, conv_kernel, conv_bias, x_proj, dt_proj,
    dt_bias, log_decay, skip_gain, out_proj, moe_gain, router, up_proj, down_proj,
):
    rows_dev, model = tokens.shape
    own = conv_bias.shape[0]
    experts = router.shape[1]
    rank, states, taps = dt_proj.shape[0], log_decay.shape[0], conv_kernel.shape[0]
    wide = rank + 2 * states
    owners = lax.axis_size("expert") * lax.axis_size("rows")
    hids = lax.axis_size("hid")
    inner = owners * own
    mixer_axes = ("expert", "rows")

    in_lines = in_proj.transpose(2, 1, 0)
    norm_pack = jnp.concatenate([mixer_gain[:, None], moe_gain[:, None], router], axis=1)
    small = jnp.concatenate(
        [
            x_proj.T, dt_proj.T, conv_kernel.T, conv_bias[:, None], dt_bias[:, None], log_decay.T,
            skip_gain[:, None],
        ],
        axis=1,
    )
    small_used = small.shape[1]
    small_width = -(-small_used // 128) * 128
    small = jnp.pad(small, ((0, 0), (0, small_width - small_used)))
    pack = jnp.concatenate([in_lines[:, 0], in_lines[:, 1], out_proj, small], axis=1)
    width = pack.shape[1]
    tokens_reset = jnp.concatenate(
        [tokens, jnp.broadcast_to(resets[:, None].astype(BF16), (rows_dev, 128))], axis=1
    )
    hid_at = lax.axis_index("hid")
    pack = jnp.concatenate([pack[:MAIN], spread_extra(pack[None, MAIN:])[0]], axis=1)
    norm_tile = jnp.pad(norm_pack.reshape(1, -1), ((0, 0), (0, 96 - norm_pack.size))).reshape(MAIN, 6)
    norm_tile = jnp.pad(norm_tile, ((0, 0), (0, 26)))[:, None, :]
    norm_tile = jnp.where(jnp.arange(hids)[None, :, None] == hid_at, norm_tile, 0).reshape(MAIN, 128)
    whole, norms, sequence = gather_start(pack, norm_tile, tokens_reset)
    whole = joined_channels(whole, width)
    sequence = sequence.reshape(hids * rows_dev, -1)
    norm_rows = norms.reshape(owners, MAIN, hids, 32)[..., :6].transpose(0, 2, 1, 3)
    norm_rows = norm_rows.reshape(owners, hids, 96)[:, :, : norm_pack.size].reshape(model, 2 + experts)

    in_x, in_gate = whole[:, :model], whole[:, model : 2 * model]
    out_full, small_full = whole[:, 2 * model : 3 * model], whole[:, 3 * model :]
    cuts = [rank + 2 * states, rank, taps, 1, 1, states, 1]
    pieces, at = [], 0
    for cut in cuts:
        pieces.append(small_full[:, at : at + cut])
        at += cut
    xp, dtp, kernel_t, conv_shift, dt_shift, decay_t, skip = pieces
    gain_one = norm_rows[:, 0].astype(F32)
    gain_two = norm_rows[:, 1].astype(F32)
    router_full = norm_rows[:, 2:]

    marks = sequence[:, model].astype(F32)
    all_rows = sequence[:, :model].astype(F32)
    normed_low = rms_norm(all_rows, gain_one).astype(BF16)
    inputs = tokens.astype(F32)

    x_low = outer_cols(normed_low, in_x).astype(BF16)
    gate_z = outer_cols(normed_low, in_gate)
    doc_ids = jnp.cumsum(marks.astype(jnp.int32))
    margin = taps - 1
    ids_ext = jnp.concatenate([jnp.full((margin,), -1, jnp.int32), doc_ids])
    extended = jnp.concatenate([jnp.zeros((margin, inner), F32), x_low.astype(F32)])
    conv_out, conv_back = jax.vjp(
        partial(convolve, ids_ext), extended, kernel_t.T.astype(F32), conv_shift[:, 0].astype(F32)
    )
    conv_low = conv_out.astype(BF16)
    projected = matmul(conv_low, xp)
    projected = over_hid(1, projected.astype(BF16), 3)
    dtr_low = projected[:, :rank].astype(BF16)
    b_cols = columns_by_eight(projected[:, rank : rank + states])
    c_cols = columns_by_eight(projected[:, rank + states :])
    dt_lin = outer_cols(dtr_low, dtp) + dt_shift[:, 0].astype(F32)[None, :]
    dt = jax.nn.softplus(dt_lin)
    dtm = dt + STOP * marks[:, None]
    dtx = dt * conv_out
    rate = jnp.exp(decay_t.T.astype(F32))
    a = rate * (-LOG2E)
    scanned, starts = scan_forward(a, dtm, dtx, b_cols, c_cols)
    skip_row = skip[:, 0].astype(F32)[None, :]
    y = scanned + skip_row * conv_out
    sig_z = jax.nn.sigmoid(gate_z)
    silu_z = gate_z * sig_z
    gated_low = (y * silu_z).astype(BF16)
    branch = matmul(gated_low, out_full).astype(BF16).reshape(hids, rows_dev, model)
    hidden_one = inputs + over_hid(2, branch, 4)

    normed_two, norm_two_back = jax.vjp(rms_norm, hidden_one, gain_two)
    moe_low = normed_two.astype(BF16)
    probs = jax.nn.softmax(matmul(moe_low, router_full), axis=-1)
    picked = routes == jnp.arange(experts, dtype=jnp.int32)[None, :]
    onehot = picked.astype(F32)
    gate = jnp.sum(probs * onehot, axis=-1)
    picked_int = picked.astype(jnp.int32)
    within = jnp.sum(picked_int * (jnp.cumsum(picked_int, axis=0) - 1), axis=1)
    grad_output = cotangent.astype(F32)
    grad_eo = (gate[:, None] * grad_output).astype(BF16)
    slot = jnp.arange(experts * MAIN, dtype=jnp.int32)[:, None]
    line, expert_at = slot % MAIN, slot // MAIN
    here = expert_at == routes[:, 0][None, :]
    place_of = within[None, :]
    pick_main = (here & (place_of == line)).astype(BF16)
    pick_top = (here & (line < 8) & (place_of == line + 16)).astype(BF16)
    pick_low = (here & (line >= 8) & (place_of == line + 8)).astype(BF16)
    main = matmul(pick_main, jnp.concatenate([moe_low, grad_eo], axis=1))
    extra = matmul(pick_top, moe_low) + matmul(pick_low, grad_eo)
    slots = jnp.concatenate([main, extra], axis=1).astype(BF16).reshape(experts, MAIN, 3 * model)
    back, grad_up, grad_down = experts_both_ways(slots, up_proj[0], down_proj[0])
    back = back.reshape(experts * MAIN, 3 * model)
    expert_out = inner_rows(pick_main, back[:, :model]) + inner_rows(pick_top, back[:, 2 * model :])
    grad_rows = inner_rows(pick_main, back[:, model : 2 * model]) + inner_rows(pick_low, back[:, 2 * model :])

    def over_rows(shard):
        mine = lax.psum_scatter(shard, "rows", scatter_dimension=0, tiled=True)
        return lax.all_gather(mine, "rows", axis=0, tiled=True).astype(F32)

    grad_up_sum, grad_down_sum = over_rows(grad_up), over_rows(grad_down)
    output = (hidden_one + gate[:, None] * expert_out).astype(BF16)
    grad_gate = jnp.sum(grad_output * expert_out, axis=-1)
    grad_logits = ((gate * grad_gate)[:, None] * (onehot - probs)).astype(BF16)
    grad_router = inner_rows(moe_low, grad_logits)
    grad_moe = grad_rows + outer_cols(grad_logits, router_full)
    grad_hidden_more, grad_gain_two = norm_two_back(grad_moe)
    grad_hidden = grad_output + grad_hidden_more

    grad_seq = over_hid(0, grad_hidden.astype(BF16), 5).reshape(hids * rows_dev, model)
    grad_out_proj = inner_rows(gated_low, grad_seq)
    grad_gated = outer_cols(grad_seq, out_full)
    grad_y = grad_gated * silu_z
    grad_gate_z = grad_gated * y * (sig_z * (1.0 + gate_z * (1.0 - sig_z)))
    s1, s2, gb, gc, g_rate = scan_backward(a, dt, dtm, dtx, grad_y, b_cols, c_cols, starts)
    grad_dt_lin = jax.nn.sigmoid(dt_lin) * (conv_out * s1 + s2 * (1.0 / LOG2E))
    grad_log_decay = -rate * g_rate
    grad_skip = jnp.sum(grad_y * conv_out, axis=0)
    grad_dt_bias = jnp.sum(grad_dt_lin, axis=0)
    grad_scan_x = skip_row * grad_y + dt * s1
    grad_dt_low = grad_dt_lin.astype(BF16)
    grad_b = gb[:, 0].reshape(-1, states)
    grad_c = gc[:, 0].reshape(-1, states)
    grad_proj = jnp.concatenate([matmul(grad_dt_low, dtp), grad_b, grad_c], axis=1)
    grad_proj = over_hid(1, grad_proj.astype(BF16), 6).astype(BF16)
    grad_dt_proj = inner_rows(grad_dt_low, dtr_low)
    grad_x_proj = inner_rows(conv_low, grad_proj)
    grad_conv_out = grad_scan_x + outer_cols(grad_proj, xp)
    grad_ext, grad_kernel, grad_conv_bias = conv_back(grad_conv_out)
    grad_x_low = grad_ext[margin:].astype(BF16)
    grad_gate_low = grad_gate_z.astype(BF16)
    grad_in_x = inner_rows(grad_x_low, normed_low)
    grad_in_gate = inner_rows(grad_gate_low, normed_low)
    grad_normed = matmul(grad_x_low, in_x) + matmul(grad_gate_low, in_gate)
    grad_normed = over_hid(2, grad_normed.astype(BF16).reshape(hids, rows_dev, model), 7)
    unused, norm_one_back = jax.vjp(rms_norm, inputs, gain_one)
    grad_more, grad_gain_one = norm_one_back(grad_normed)
    grad_tokens = grad_hidden + grad_more

    norm_grads = jnp.concatenate([grad_gain_one[:, None], grad_gain_two[:, None], grad_router], axis=1)
    norm_grads = jnp.pad(norm_grads.reshape(owners, hids, -1), ((0, 0), (0, 0), (0, 96 - norm_pack.size)))
    norm_grads = norm_grads.reshape(owners, hids, MAIN, 6).transpose(0, 2, 1, 3)
    norm_grads = jnp.pad(norm_grads, ((0, 0), (0, 0), (0, 0), (0, 26))).reshape(owners, MAIN, 128)
    grad_small = jnp.concatenate(
        [
            grad_x_proj, grad_dt_proj, grad_kernel.T, grad_conv_bias[:, None], grad_dt_bias[:, None],
            grad_log_decay.T, grad_skip[:, None],
        ],
        axis=1,
    )
    grad_small = jnp.pad(grad_small, ((0, 0), (0, small_width - small_used)))
    grads = jnp.concatenate([grad_in_x, grad_in_gate, grad_out_proj, grad_small], axis=1).astype(BF16)
    split = owners * MAIN
    extra = spread_extra(grads[split:].reshape(owners, own - MAIN, width))
    grads = jnp.concatenate(
        [grads[:split].reshape(owners, MAIN, width), extra, norm_grads.astype(BF16)], axis=2
    )
    summed, norm_sum = return_grads(grads)
    rest = jnp.concatenate([summed[:, :width], gathered_extra(summed[None, :, width : width + EXTRA], width)[0]], axis=0)
    grad_in = jnp.stack([rest[:, :model], rest[:, model : 2 * model]], axis=1).transpose(2, 1, 0)
    out_part = rest[:, 2 * model : 3 * model]
    small_sum = rest[:, 3 * model :]
    done, at = [], 0
    for cut in cuts:
        done.append(small_sum[:, at : at + cut])
        at += cut
    norm_sum = lax.dynamic_slice_in_dim(norm_sum, hid_at * 32, 32, axis=1)[:, :6]
    norm_sum = norm_sum.reshape(96)[: norm_pack.size].reshape(model // (owners * hids), 2 + experts)
    return (
        output,
        grad_tokens,
        norm_sum[:, 0],
        grad_in,
        done[2].T,
        done[3][:, 0],
        done[0].T,
        done[1].T,
        done[4][:, 0],
        done[5].T,
        done[6][:, 0],
        out_part,
        norm_sum[:, 1],
        norm_sum[:, 2:],
        grad_up_sum[None],
        grad_down_sum[None],
    )


def solution(mesh):
    every = ("expert", "rows", "hid")
    in_specs = (
        P(every, None), P(every), P(every, None), P(every, None), P(every), P(None, None, every),
        P(None, every), P(every), P(None, every), P(None, every), P(every), P(None, every), P(every),
        P(every, None), P(every), P(every, None), P("expert", None, "hid"), P("expert", "hid", None),
    )
    out_specs = (
        P(every, None), P(every, None), P(every), P(None, None, every), P(None, every), P(every),
        P(None, every), P(None, every), P(every), P(None, every), P(every), P(every, None), P(every),
        P(every, None), P("expert", None, "hid"), P("expert", "hid", None),
    )
    return jax.shard_map(shards, mesh=mesh, in_specs=in_specs, out_specs=out_specs, check_vma=False)
```

```python
from functools import partial

import jax
import jax.numpy as jnp
from jax import lax
from jax.experimental import pallas as pl
from jax.experimental.pallas import tpu as pltpu
from jax.sharding import PartitionSpec as P

EPS = 1e-05
LOG2E = 1.4426950408889634
STOP = 1e6
STEP = 16
MAIN = 16
EXTRA = 512
GELU_C = 0.7978845608028654
F32 = jnp.float32
BF16 = jnp.bfloat16


def matmul(first_op, second_op):
    return jnp.dot(first_op, second_op, preferred_element_type=F32)


def inner_rows(first_op, second_op):
    return lax.dot_general(
        first_op, second_op, (((0,), (0,)), ((), ())), preferred_element_type=F32
    )


def outer_cols(first_op, second_op):
    return lax.dot_general(
        first_op, second_op, (((1,), (1,)), ((), ())), preferred_element_type=F32
    )


def rms_norm(values, gain):
    return values * lax.rsqrt(jnp.mean(values * values, axis=-1, keepdims=True) + EPS) * gain


def over_lanes(v):
    whole = v.shape[1] // 128
    total = v[:, :128]
    for k in range(1, whole):
        total = total + v[:, k * 128 : (k + 1) * 128]
    rest = v.shape[1] - whole * 128
    if rest:
        blank = jnp.zeros((v.shape[0], 128 - rest), F32)
        total = total + jnp.concatenate([v[:, whole * 128 :], blank], axis=1)
    return total


MESH = pl.DeviceIdType.MESH
ANY = pl.BlockSpec(memory_space=pl.ANY)
IN_VMEM = pl.BlockSpec(memory_space=pltpu.VMEM)
DMA = pltpu.SemaphoreType.DMA


def places():
    return lax.axis_index("expert"), lax.axis_index("rows"), lax.axis_index("hid")


def greet(peers):
    barrier = pltpu.get_barrier_semaphore()
    for peer in peers:
        pl.semaphore_signal(barrier, inc=1, device_id=peer, device_id_type=MESH)
    pl.semaphore_wait(barrier, len(peers))


def remote(src, dst, send_sem, recv_sem, peer):
    return pltpu.make_async_remote_copy(
        src_ref=src, dst_ref=dst, send_sem=send_sem, recv_sem=recv_sem, device_id=peer,
        device_id_type=MESH,
    )


def hid_peers():
    e, r, h = places()
    return [(e, r, lax.rem(h + k, 4)) for k in (1, 2, 3)]


def mixer_peers():
    e, r, h = places()
    c = lax.rem(e, 2)
    mate = (e + 1 - 2 * c, r, h)
    first = [(lax.rem(e + 2 * k * (1 - c), 8), lax.rem(r + k * c, 4), h) for k in (1, 2, 3)]
    second = [(lax.rem(e + 2 * k * c, 8), lax.rem(r + k * (1 - c), 4), h) for k in (1, 2, 3)]
    return mate, first, second


def block_at(c, f, s):
    y = f * (1 - c) + s * c
    x = s * (1 - c) + f * c
    return (2 * y + c) * 4 + x


def gather_kernel(
    pack, norm, line, whole, norms, sequence, tiles, total, local_sems, z_send, z_recv, n_send, n_recv,
    w_send, w_recv, v_send, v_recv,
):
    e, r, h = places()
    c = lax.rem(e, 2)
    y = e // 2
    f0 = y * (1 - c) + r * c
    s0 = r * (1 - c) + y * c
    mate, first, second = mixer_peers()
    z_peers = hid_peers()
    own = e * 4 + r
    greet([mate] + first + second + z_peers)
    n_copies = [
        remote(norm, tiles.at[k], n_send.at[k], n_recv.at[k], z_peers[k]) for k in range(3)
    ]
    for copy in n_copies:
        copy.start()
    w_one = [remote(pack, whole.at[own], w_send.at[k], w_recv.at[k], first[k]) for k in range(3)]
    w_two = [[remote(pack, whole.at[own], w_send.at[3 + k], w_recv.at[3 + k], second[k]) for k in range(3)]]
    w_mate = [remote(pack, whole.at[own], w_send.at[15], w_recv.at[15], mate)]
    for k in (1, 0, 2):
        w_one[k].start()
    for k in (1, 0, 2):
        w_two[0][k].start()
    z_copies = [remote(line, sequence.at[h], z_send.at[k], z_recv.at[k], z_peers[k]) for k in range(3)]
    for k in (1, 0, 2):
        z_copies[k].start()
    w_mate[0].start()
    mine = [
        pltpu.make_async_copy(pack, whole.at[own], local_sems.at[0]),
        pltpu.make_async_copy(line, sequence.at[h], local_sems.at[1]),
    ]
    for copy in mine:
        copy.start()
    for copy in n_copies:
        copy.wait_recv()
    total[...] = norm[...] + tiles[0] + tiles[1] + tiles[2]
    v_one = [remote(total, norms.at[own], v_send.at[k], v_recv.at[k], first[k]) for k in range(3)]
    v_two = [[remote(total, norms.at[own], v_send.at[3 + k], v_recv.at[3 + k], second[k]) for k in range(3)]]
    v_mate = [remote(total, norms.at[own], v_send.at[15], v_recv.at[15], mate)]
    for copy in v_one + v_two[0] + v_mate:
        copy.start()
    mine.append(pltpu.make_async_copy(total, norms.at[own], local_sems.at[2]))
    mine[2].start()
    for k in range(3):
        came = block_at(c, lax.rem(f0 + 3 - k, 4), s0)
        for buf, one, send, recv, two, other in (
            (whole, w_one, w_send, w_recv, w_two, w_mate), (norms, v_one, v_send, v_recv, v_two, v_mate)
        ):
            one[k].wait_recv()
            block = buf.at[came]
            two.append([remote(block, block, send.at[6 + 3 * k + j], recv.at[6 + 3 * k + j], second[j]) for j in range(3)])
            for j in (1, 0, 2):
                two[1 + k][j].start()
            other.append(remote(block, block, send.at[16 + k], recv.at[16 + k], mate))
            other[-1].start()
    for k in range(4):
        for j in range(3):
            came = block_at(c, lax.rem(f0 + 4 - k, 4), lax.rem(s0 + 3 - j, 4))
            for buf, send, recv, two, other in (
                (whole, w_send, w_recv, w_two, w_mate), (norms, v_send, v_recv, v_two, v_mate)
            ):
                two[k][j].wait_recv()
                block = buf.at[came]
                at = 19 + 3 * k + j
                other.append(remote(block, block, send.at[at], recv.at[at], mate))
                other[-1].start()
    for copy in w_mate + v_mate:
        copy.wait_recv()
    for copy in z_copies:
        copy.wait_recv()
    for copy in n_copies + w_one + sum(w_two, []) + w_mate + v_one + sum(v_two, []) + v_mate + z_copies:
        copy.wait_send()
    for copy in mine:
        copy.wait()


def gather_start(pack, norm, line):
    return pl.pallas_call(
        gather_kernel,
        out_shape=(
            jax.ShapeDtypeStruct((32, *pack.shape), BF16),
            jax.ShapeDtypeStruct((32, *norm.shape), BF16),
            jax.ShapeDtypeStruct((4, *line.shape), BF16),
        ),
        in_specs=[IN_VMEM] * 3,
        out_specs=(ANY, ANY, ANY),
        scratch_shapes=[
            pltpu.VMEM((3, *norm.shape), BF16),
            pltpu.VMEM(norm.shape, BF16),
            DMA((3,)), DMA((3,)), DMA((3,)), DMA((3,)), DMA((3,)), DMA((31,)), DMA((31,)), DMA((31,)), DMA((31,)),
        ],
        compiler_params=pltpu.CompilerParams(
            collective_id=1, has_side_effects=True, vmem_limit_bytes=32 << 20
        ),
        name="gather_start",
    )(pack, norm, line)


def return_kernel(
    grads, low_up, low_down, summed, tile_sum, wide_up, wide_down, in_up, in_down, out_up, out_down, c_sems, pairs, halves, lines, fours, ends, own_tile, tiles, m_send, m_recv, s_send, s_recv,
    f_send, f_recv, z_send, z_recv,
):
    e, r, h = places()
    c = lax.rem(e, 2)
    y = e // 2
    f0 = y * (1 - c) + r * c
    s0 = r * (1 - c) + y * c
    mate, first, second = mixer_peers()
    z_peers = hid_peers()
    width = grads.shape[2]
    greet([mate] + first + second + z_peers)
    moved = [
        pltpu.make_async_copy(low_up, in_up, c_sems.at[0]),
        pltpu.make_async_copy(low_down, in_down, c_sems.at[1]),
        pltpu.make_async_copy(out_up, wide_up, c_sems.at[2]),
        pltpu.make_async_copy(out_down, wide_down, c_sems.at[3]),
    ]
    moved[0].start()
    moved[1].start()
    other = 1 - c
    mate_s0 = r * (1 - other) + y * other
    m_copies = []
    for n, k in enumerate((2, 1, 3, 0)):
        for f in range(4):
            s = lax.rem(mate_s0 + k, 4)
            m_copies.append(
                remote(grads.at[block_at(other, f, s)], pairs.at[n, f], m_send.at[n * 4 + f], m_recv.at[n * 4 + f], mate)
            )
            m_copies[-1].start()
    s_copies = []
    for n, k in enumerate((2, 1, 3, 0)):
        s = lax.rem(s0 + k, 4)
        for f in range(4):
            m_copies[n * 4 + f].wait_recv()
            block = block_at(c, f, s)
            halves[n, f] = (grads[block].astype(F32) + pairs[n, f].astype(F32)).astype(BF16)
        if k:
            s_copies.append(remote(halves.at[n], fours.at[n], s_send.at[n], s_recv.at[n], second[k - 1]))
            s_copies[-1].start()
    for n, (kept, wide) in enumerate(((in_up, out_up), (in_down, out_down))):
        moved[n].wait()
        wide[...] = kept[...].astype(F32)
        moved[2 + n].start()
    for copy in s_copies:
        copy.wait_recv()
    f_copies = []
    for n, k in enumerate((2, 1, 3, 0)):
        f = lax.rem(f0 + k, 4)
        line = (
            halves[3, f].astype(F32) + fours[0, f].astype(F32) + fours[1, f].astype(F32) + fours[2, f].astype(F32)
        )
        if k:
            lines[n] = line.astype(BF16)
            f_copies.append(remote(lines.at[n], ends.at[n], f_send.at[n], f_recv.at[n], first[k - 1]))
            f_copies[-1].start()
        else:
            for copy in f_copies:
                copy.wait_recv()
            line = line + ends[0].astype(F32) + ends[1].astype(F32) + ends[2].astype(F32)
            summed[...] = line
            own_tile[...] = line[:, width - 128 :].astype(BF16)
    z_copies = [remote(own_tile, tiles.at[k], z_send.at[k], z_recv.at[k], z_peers[k]) for k in range(3)]
    for copy in z_copies:
        copy.start()
    for copy in z_copies:
        copy.wait_recv()
    tile_sum[...] = (
        summed[:, width - 128 :] + tiles[0].astype(F32) + tiles[1].astype(F32) + tiles[2].astype(F32)
    )
    for copy in m_copies + s_copies + f_copies + z_copies:
        copy.wait_send()
    moved[2].wait()
    moved[3].wait()


def return_grads(grads, low_up, low_down):
    owners, rows, width = grads.shape
    return pl.pallas_call(
        return_kernel,
        out_shape=(
            jax.ShapeDtypeStruct((rows, width), F32),
            jax.ShapeDtypeStruct((rows, 128), F32),
            jax.ShapeDtypeStruct(low_up.shape, F32),
            jax.ShapeDtypeStruct(low_down.shape, F32),
        ),
        in_specs=[IN_VMEM, ANY, ANY],
        out_specs=(IN_VMEM, IN_VMEM, ANY, ANY),
        scratch_shapes=[
            pltpu.VMEM(low_up.shape, BF16),
            pltpu.VMEM(low_down.shape, BF16),
            pltpu.VMEM(low_up.shape, F32),
            pltpu.VMEM(low_down.shape, F32),
            DMA((4,)),
            pltpu.VMEM((4, 4, rows, width), BF16),
            pltpu.VMEM((4, 4, rows, width), BF16),
            pltpu.VMEM((3, rows, width), BF16),
            pltpu.VMEM((3, 4, rows, width), BF16),
            pltpu.VMEM((3, rows, width), BF16),
            pltpu.VMEM((rows, 128), BF16),
            pltpu.VMEM((3, rows, 128), BF16),
            DMA((16,)), DMA((16,)), DMA((3,)), DMA((3,)), DMA((3,)), DMA((3,)), DMA((3,)), DMA((3,)),
        ],
        compiler_params=pltpu.CompilerParams(
            collective_id=2, has_side_effects=True, vmem_limit_bytes=40 << 20
        ),
        name="return_grads",
    )(grads, low_up, low_down)


def gelu_pair(pre, grad):
    square = pre * pre
    t = jnp.tanh(GELU_C * pre * (1.0 + 0.044715 * square))
    up = 0.5 * (1.0 + t)
    slope = up + 0.5 * pre * (1.0 - t * t) * (GELU_C * (1.0 + 3 * 0.044715 * square))
    return pre * up, slope * grad


def expert_kernel(
    slots, up, down, back, g_up, g_down, held, results, hid_out, pre_out, hid_w, pre_w, from_left, from_right,
    half_left, half_right, sums, d_send, d_recv, r_send, r_recv, l_send, l_recv, f_send, f_recv, c_send, c_recv,
    k_send, k_recv, h_send, h_recv, b_send, b_recv,
):
    e, r, h = places()
    model, hidden = up.shape
    right, left, across = lax.rem(h + 1, 4), lax.rem(h + 3, 4), lax.rem(h + 2, 4)
    to_right, to_left = (e, r, right), (e, r, left)
    to_expert = [(lax.rem(e + k, 8), r, h) for k in range(8)]
    source = [lax.rem(e + 8 - k, 8) for k in range(8)]
    greet(to_expert[1:] + [to_right, to_left])

    d_copies = [None]
    for k in range(1, 8):
        d_copies.append(
            remote(slots.at[lax.rem(e + k, 8)], held.at[h, e], d_send.at[k], d_recv.at[k], to_expert[k])
        )
        d_copies[k].start()
    held[h, e] = slots[e]

    def along(buf, where, k, send, recv, peer):
        block = buf.at[where, source[k]]
        copy = remote(block, block, send.at[k], recv.at[k], peer)
        copy.start()
        return copy

    r_copies, l_copies = [None] * 8, [None] * 8
    for k in range(8):
        if k:
            d_copies[k].wait_recv()
        r_copies[k] = along(held, h, k, r_send, r_recv, to_right)
        if k >= 4:
            l_copies[k] = along(held, h, k, l_send, l_recv, to_left)
    for k in range(4):
        l_copies[k] = along(held, h, k, l_send, l_recv, to_left)

    half = 128

    def worked(where):
        lines = held[where]
        main_x = lines[:, :, :model].reshape(half, model)
        main_g = lines[:, :, model : 2 * model].reshape(half, model)
        extra = lines[:, :, 2 * model :].reshape(half, model)
        rows_x = jnp.concatenate([main_x, extra], axis=0)
        rows_g = jnp.concatenate([main_g, extra], axis=0)

        def first_layer(i, carry):
            cols = pl.ds(pl.multiple_of(i * 256, 256), 256)
            pre = matmul(rows_x, up[:, cols])
            grad = outer_cols(rows_g, down[cols, :])
            hid_m, pre_m = gelu_pair(pre[:half], grad[:half])
            pre_e = pre[half:].reshape(8, 2, 8, 256)[:, 0]
            grad_e = grad[half:].reshape(8, 2, 8, 256)[:, 1]
            hid_e, gpre_e = gelu_pair(pre_e, grad_e)
            none = jnp.zeros_like(hid_e)

            def stacked(a, b):
                return jnp.stack([a, b], axis=1).reshape(half, 256).astype(BF16)

            hid_m, pre_m = hid_m.astype(BF16), pre_m.astype(BF16)
            hid_out[:half, cols] = hid_m
            pre_out[:half, cols] = pre_m
            hid_w[where, :half, cols] = hid_m
            pre_w[where, :half, cols] = pre_m
            hid_out[half:, cols] = stacked(hid_e, none)
            pre_out[half:, cols] = stacked(none, gpre_e)
            hid_w[where, half:, cols] = stacked(none, hid_e)
            pre_w[where, half:, cols] = stacked(gpre_e, none)
            return carry

        lax.fori_loop(0, hidden // 256, first_layer, 0)

        def second_layer(i, carry):
            at = pl.multiple_of(i * 384, 384)
            cols = pl.ds(at, 384)
            share = matmul(hid_out[...], down[:, cols])
            grad = outer_cols(pre_out[...], up[cols, :])
            shape = (8, 16, 384)
            results[where, :, :, cols] = share[:half].astype(BF16).reshape(shape)
            results[where, :, :, pl.ds(model + at, 384)] = grad[:half].astype(BF16).reshape(shape)
            results[where, :, :, pl.ds(2 * model + at, 384)] = (share[half:] + grad[half:]).astype(BF16).reshape(shape)
            return carry

        lax.fori_loop(0, model // 384, second_layer, 0)

    worked(h)
    f_copies = [None] * 8
    for k in range(4):
        r_copies[k].wait_recv()
        f_copies[k] = along(held, left, k, f_send, f_recv, to_right)
        l_copies[4 + k].wait_recv()
        f_copies[4 + k] = along(held, right, 4 + k, f_send, f_recv, to_left)
    for k in range(4, 8):
        r_copies[k].wait_recv()
    worked(left)
    c_copies = [None] * 8
    k_copies = [None] * 8

    def toward_right(k):
        block = results.at[right, source[k]]
        c_copies[k] = remote(block, from_left.at[k], c_send.at[k], c_recv.at[k], to_right)
        c_copies[k].start()

    def toward_left(k):
        block = results.at[left, source[k]]
        k_copies[k] = remote(block, from_right.at[k], k_send.at[k], k_recv.at[k], to_left)
        k_copies[k].start()

    for k in range(4):
        toward_left(k)
    for k in range(4):
        l_copies[k].wait_recv()
    worked(right)
    for k in range(4, 8):
        toward_right(k)
    for k in range(8):
        f_copies[k].wait_recv()
    worked(across)
    h_copies = []
    for k in range(4):
        for at, landing, peer in ((k, half_left, to_right), (4 + k, half_right, to_left)):
            block = results.at[across, source[at]]
            copy = remote(block, landing.at[k], h_send.at[at], h_recv.at[at], peer)
            copy.start()
            h_copies.append(copy)

    def weight_grads(i, carry):
        cols = pl.ds(pl.multiple_of(i * 128, 128), 128)
        total = jnp.zeros((128, hidden), F32)
        for lanes, kept, out in ((0, pre_w, g_up),):
            x_main = held[:, :, :, pl.ds(pl.multiple_of(i * 128, 128), 128)].reshape(4, half, 128)
            x_extra = held[:, :, :, pl.ds(pl.multiple_of(2 * model + i * 128, 128), 128)].reshape(4, half, 128)
            rows = jnp.concatenate([x_main, x_extra], axis=1).reshape(8 * half, 128)
            total = inner_rows(rows, kept[...].reshape(8 * half, hidden))
            out[cols, :] = total.astype(BF16)
        g_main = held[:, :, :, pl.ds(pl.multiple_of(model + i * 128, 128), 128)].reshape(4, half, 128)
        rows = jnp.concatenate([g_main, x_extra], axis=1).reshape(8 * half, 128)
        g_down[:, cols] = inner_rows(hid_w[...].reshape(8 * half, hidden), rows).astype(BF16)
        return carry

    lax.fori_loop(0, model // 128, weight_grads, 0)

    for k in range(4):
        h_copies[2 * k].wait_recv()
        block = source[k]
        results[right, block] = (results[right, block].astype(F32) + half_left[k].astype(F32)).astype(BF16)
        toward_right(k)
        h_copies[2 * k + 1].wait_recv()
        block = source[4 + k]
        results[left, block] = (results[left, block].astype(F32) + half_right[k].astype(F32)).astype(BF16)
        toward_left(4 + k)
    b_copies = []
    for k in (4, 5, 6, 7, 3, 2, 1, 0):
        c_copies[k].wait_recv()
        k_copies[k].wait_recv()
        total = results[h, source[k]].astype(F32) + from_left[k].astype(F32) + from_right[k].astype(F32)
        if k:
            sums[k] = total.astype(BF16)
            copy = remote(sums.at[k], back.at[e], b_send.at[k], b_recv.at[k], to_expert[8 - k])
            copy.start()
            b_copies.append(copy)
        else:
            back[e] = total.astype(BF16)
    for copy in b_copies:
        copy.wait_recv()
    for copy in d_copies[1:] + r_copies + l_copies + f_copies + c_copies + k_copies + h_copies + b_copies:
        copy.wait_send()


def experts_both_ways(slots, up, down):
    count, lines, width = slots.shape
    model, hidden = up.shape
    eight = DMA((8,))
    return pl.pallas_call(
        expert_kernel,
        out_shape=(
            jax.ShapeDtypeStruct(slots.shape, BF16),
            jax.ShapeDtypeStruct(up.shape, BF16),
            jax.ShapeDtypeStruct(down.shape, BF16),
        ),
        in_specs=[IN_VMEM] * 3,
        out_specs=(IN_VMEM,) * 3,
        scratch_shapes=[
            pltpu.VMEM((4, count, lines, width), BF16),
            pltpu.VMEM((4, count, lines, width), BF16),
            pltpu.VMEM((256, hidden), BF16),
            pltpu.VMEM((256, hidden), BF16),
            pltpu.VMEM((4, 256, hidden), BF16),
            pltpu.VMEM((4, 256, hidden), BF16),
            pltpu.VMEM((8, lines, width), BF16),
            pltpu.VMEM((8, lines, width), BF16),
            pltpu.VMEM((4, lines, width), BF16),
            pltpu.VMEM((4, lines, width), BF16),
            pltpu.VMEM((8, lines, width), BF16),
            *[eight] * 16,
        ],
        compiler_params=pltpu.CompilerParams(
            collective_id=8, has_side_effects=True, vmem_limit_bytes=48 << 20
        ),
        name="experts",
    )(slots, up, down)


def across(tile, width):
    whole = width // 128
    return jnp.concatenate([tile] * whole + [tile[:, : width - 128 * whole]], axis=1)


def eye(size):
    at = [lax.broadcasted_iota(jnp.int32, (size, size), axis) for axis in (0, 1)]
    return (at[0] == at[1]).astype(BF16)


def both_cols(lines, main, extra):
    return jnp.concatenate([outer_cols(lines, main), outer_cols(lines, extra)], axis=1)


def mixer_kernel(
    seq, whole, gains, normed, x_low, u_out, gate_z, proj, dt_lin, y_out, gated, starts, hidden, params, extra,
    xs, marks, conv, dtm, dtx, parts, own, landing, branch, came, p_send, p_recv, b_send, b_recv,
):
    e, r, h = places()
    model = normed.shape[1]
    inner, states, block = u_out.shape[1], starts.shape[1], hidden.shape[0]
    lines = block // STEP
    small = 3 * model
    z_peers = hid_peers()
    greet(z_peers)
    row = lax.broadcasted_iota(jnp.int32, (512, 512), 0)
    col = lax.broadcasted_iota(jnp.int32, (512, 512), 1)
    wanted = (row % 64 // 2) * MAIN + (row % 2) * 8 + row // 64
    moved = matmul((wanted == col).astype(BF16), whole[:, small + 256 :]).astype(BF16)
    for k in range(8):
        extra[:, k * 512 : (k + 1) * 512] = moved[k * 64 : (k + 1) * 64]
    params[...] = both_cols(eye(128), whole[:, small : small + 128], extra[:, small : small + 128])
    xs[0:8] = jnp.zeros((8, inner), F32)
    marks[0:8] = jnp.zeros((8, 128), F32)
    gain = gains[0:1, :]

    def proj_copy(b, k):
        at = k * 4 + b
        return remote(own.at[b], landing.at[k, b], p_send.at[at], p_recv.at[at], z_peers[k])

    def stage_one(b, carry):
        start = pl.multiple_of(b * block, block)
        rows = pl.ds(start, block)
        values = seq[rows, :model].astype(F32)
        scale = lax.rsqrt(jnp.mean(values * values, axis=-1, keepdims=True) + EPS)
        low = (values * scale * gain).astype(BF16)
        normed[rows, :] = low
        gate_z[rows, :] = both_cols(low, whole[:, model : 2 * model], extra[:, model : 2 * model])
        x = both_cols(low, whole[:, :model], extra[:, :model]).astype(BF16)
        x_low[rows, :] = x
        after = pl.ds(pl.multiple_of(8 + start, 8), block)
        xs[after, :] = x.astype(F32)
        now = seq[rows, model:].astype(F32)
        marks[after, :] = now
        lines_x, lines_m = xs[pl.ds(start, block + 8), :], marks[pl.ds(start, block + 8), :]
        mask = 1.0 - now
        total = params[124:125, :] + params[123:124, :] * x.astype(F32)
        for back in (1, 2, 3):
            past = lines_x[8 - back : 8 - back + block]
            total = total + params[123 - back : 124 - back, :] * past * across(mask, inner)
            if back < 3:
                mask = mask * (1.0 - lines_m[8 - back : 8 - back + block])
        u_out[rows, :] = total
        convolved = total * jax.nn.sigmoid(total)
        conv[rows, :] = convolved
        conv_low = convolved.astype(BF16)
        share = matmul(conv_low[:, :512], whole[:, small : small + 128]) + matmul(
            conv_low[:, 512:], extra[:, small : small + 128]
        )
        own[b] = share.astype(BF16)
        for k in (1, 0, 2):
            proj_copy(b, k).start()
        return carry

    lax.fori_loop(0, 4, stage_one, 0)
    a = jnp.exp(params[104:120, :]) * (-LOG2E)
    half = states // 2

    def branch_copy(b, sender):
        return remote(branch.at[b], came.at[sender], b_send.at[b], b_recv.at[sender], (e, r, b))

    def stage_two(b, state):
        start = pl.multiple_of(b * block, block)
        rows = pl.ds(start, block)
        for k in range(3):
            proj_copy(b, k).wait_recv()
        sums = (
            own[b].astype(F32) + landing[0, b].astype(F32) + landing[1, b].astype(F32) + landing[2, b].astype(F32)
        )
        proj[rows, :] = sums
        lin = both_cols(sums.astype(BF16), whole[:, small + 128 : small + 256], extra[:, small + 128 : small + 256])
        lin = lin + params[125:126, :]
        dt_lin[rows, :] = lin
        dt = jax.nn.softplus(lin)
        convolved = conv[rows, :]
        dtm[...] = dt + across(STOP * marks[pl.ds(pl.multiple_of(8 + start, 8), block), :], inner)
        dtx[...] = dt * convolved
        turned = sums.T
        b_all, c_all = turned[72:88], turned[88:104]

        def chunk(i, h_now):
            starts[b * lines + i] = h_now
            shift = lax.rem(block - i * STEP, block)
            b_now, c_now = pltpu.roll(b_all, shift, 1), pltpu.roll(c_all, shift, 1)
            for j in range(STEP):
                t = pl.ds(i * STEP + j, 1)
                decay = jnp.exp2(a * dtm[t, :])
                h_now = decay * h_now + b_now[:, j : j + 1] * dtx[t, :]
                p = c_now[:, j : j + 1] * h_now
                parts[j * half : (j + 1) * half, :] = p[:half] + p[half:]
            here = pl.ds(pl.multiple_of(start + i * STEP, STEP), STEP)
            y_out[here, :] = parts[...].reshape(STEP, half, inner).sum(axis=1)
            return h_now

        state = lax.fori_loop(0, lines, chunk, state)
        y = y_out[rows, :] + params[126:127, :] * convolved
        y_out[rows, :] = y
        z = gate_z[rows, :]
        low = (y * z * jax.nn.sigmoid(z)).astype(BF16)
        gated[rows, :] = low
        out = matmul(low[:, :512], whole[:, 2 * model : small]) + matmul(low[:, 512:], extra[:, 2 * model : small])
        branch[b] = out.astype(BF16)

        @pl.when(b != h)
        def send():
            branch_copy(b, lax.rem(h - b + 4, 4) - 1).start()

        return state

    lax.fori_loop(0, 4, stage_two, jnp.zeros((states, inner), F32))
    for k in range(3):
        branch_copy(0, k).wait_recv()
    mine = pl.ds(pl.multiple_of(h * block, block), block)
    hidden[...] = (
        seq[mine, :model].astype(F32) + branch[h].astype(F32) + came[0].astype(F32) + came[1].astype(F32)
        + came[2].astype(F32)
    )
    for b in range(4):
        for k in range(3):
            proj_copy(b, k).wait_send()

        @pl.when(b != h)
        def sent():
            branch_copy(b, 0).wait_send()


def mixer_forward(seq, whole, gains, inner, states):
    tokens, model = seq.shape[0], gains.shape[1]
    block = tokens // 4
    S = jax.ShapeDtypeStruct
    outs = (
        S((tokens, model), BF16), S((tokens, inner), BF16), S((tokens, inner), F32), S((tokens, inner), F32),
        S((tokens, 128), F32), S((tokens, inner), F32), S((tokens, inner), F32), S((tokens, inner), BF16),
        S((tokens // STEP, states, inner), F32), S((block, model), F32), S((128, inner), F32),
        S((64, 4096), BF16),
    )
    return pl.pallas_call(
        mixer_kernel,
        out_shape=outs,
        in_specs=[IN_VMEM] * 3,
        out_specs=(IN_VMEM,) * len(outs),
        scratch_shapes=[
            pltpu.VMEM((tokens + 8, inner), F32),
            pltpu.VMEM((tokens + 8, 128), F32),
            pltpu.VMEM((tokens, inner), F32),
            pltpu.VMEM((block, inner), F32),
            pltpu.VMEM((block, inner), F32),
            pltpu.VMEM((STEP * states // 2, inner), F32),
            pltpu.VMEM((4, block, 128), BF16),
            pltpu.VMEM((3, 4, block, 128), BF16),
            pltpu.VMEM((4, block, model), BF16),
            pltpu.VMEM((3, block, model), BF16),
            DMA((12,)), DMA((12,)), DMA((4,)), DMA((3,)),
        ],
        compiler_params=pltpu.CompilerParams(
            collective_id=3, has_side_effects=True, vmem_limit_bytes=52 << 20
        ),
        name="mixer_forward",
    )(seq, whole, gains)


class RowsRing:
    def __init__(self, source, target, slots, total, send, recv, local):
        self.source, self.target, self.slots, self.total = source, target, slots, total
        self.send, self.recv, self.local = send, recv, local
        self.size = slots.shape[1]
        e, r, h = places()
        self.r = r
        self.right, self.left = lax.rem(r + 1, 4), lax.rem(r + 3, 4)
        self.to_right, self.to_left = (e, self.right, h), (e, self.left, h)

    def peers(self):
        return [self.to_right, self.to_left]

    def rows(self, quarter, part):
        return pl.ds(pl.multiple_of((2 * quarter + part) * self.size, self.size), self.size)

    def copy(self, n):
        across = lax.rem(self.r + 2, 4)
        src, out, slots, total = self.source, self.target, self.slots, self.total
        plan = [
            (src.at[self.rows(across, 0)], slots.at[0], self.to_right),
            (src.at[self.rows(across, 1)], slots.at[1], self.to_left),
            (src.at[self.rows(self.right, 1)], slots.at[7], self.to_right),
            (src.at[self.rows(self.left, 0)], slots.at[8], self.to_left),
            (slots.at[4], slots.at[6], self.to_right),
            (slots.at[5], slots.at[9], self.to_left),
            (total.at[0], out.at[self.rows(self.r, 0)], self.to_right),
            (total.at[1], out.at[self.rows(self.r, 1)], self.to_right),
            (total.at[0], out.at[self.rows(self.r, 0)], self.to_left),
            (total.at[1], out.at[self.rows(self.r, 1)], self.to_left),
            (out.at[self.rows(self.left, 0)], out.at[self.rows(self.left, 0)], self.to_right),
            (out.at[self.rows(self.right, 1)], out.at[self.rows(self.right, 1)], self.to_left),
        ]
        a, b, peer = plan[n]
        return remote(a, b, self.send.at[n], self.recv.at[n], peer)

    def own_copy(self, n):
        src, slots = self.source, self.slots
        plan = [
            (src.at[self.rows(self.right, 0)], slots.at[2]),
            (src.at[self.rows(self.left, 1)], slots.at[3]),
            (src.at[self.rows(self.r, 0)], slots.at[10]),
            (src.at[self.rows(self.r, 1)], slots.at[11]),
            (self.total.at[0], self.target.at[self.rows(self.r, 0)]),
            (self.total.at[1], self.target.at[self.rows(self.r, 1)]),
        ]
        a, b = plan[n]
        return pltpu.make_async_copy(a, b, self.local.at[n])

    def begin(self):
        for n in range(4):
            self.copy(n).start()
        for n in range(4):
            self.own_copy(n).start()

    def pass_on(self):
        slots = self.slots
        for n in (0, 1):
            self.own_copy(n).wait()
            self.copy(n).wait_recv()
            slots[4 + n] = (slots[n].astype(F32) + slots[2 + n].astype(F32)).astype(BF16)
            self.copy(4 + n).start()

    def finish(self):
        slots = self.slots
        for n in (2, 3):
            self.own_copy(n).wait()
        for n in (2, 3, 4, 5):
            self.copy(n).wait_recv()
        for n in (0, 1):
            total = slots[10 + n].astype(F32) + slots[6 + n].astype(F32) + slots[8 + n].astype(F32)
            self.total[n] = total.astype(BF16)
        for n in (6, 9, 7, 8):
            self.copy(n).start()
        for n in (4, 5):
            self.own_copy(n).start()

    def forward(self):
        for n, after in ((6, 10), (9, 11)):
            self.copy(n).wait_recv()
            self.copy(after).start()

    def end(self):
        for n in (7, 8, 10, 11):
            self.copy(n).wait_recv()
        for n in (4, 5):
            self.own_copy(n).wait()
        for n in range(12):
            self.copy(n).wait_send()


def mixer_back_kernel(
    grad_hidden, seq, whole, gains, norm_in, normed, x_low, u_in, gate_z, proj, dt_lin, y_in, gated, starts, params,
    extra, g_up, g_down, grads, grad_tokens, all_up, all_down, ghs, gus, marks, gy, dts, dtm, dtx, conv, s1, s2, gsx, gdl, ggate, gx, gp_all,
    conv_low, held, decays, parts_1, parts_2, lanes_b, lanes_c, state, g_rate, rows_sum, own, landing, branch, came,
    a_send, a_recv, p_send, p_recv, b_send, b_recv, ring_up, ring_down, total_up, total_down, x_send, x_recv, x_local,
):
    e, r, h = places()
    model = normed.shape[1]
    inner, states, block = u_in.shape[1], starts.shape[1], grad_hidden.shape[0]
    lines, half, small = block // STEP, states // 2, 3 * model
    z_peers = hid_peers()
    rings = [
        RowsRing(g_up, all_up, ring_up, total_up, x_send.at[0], x_recv.at[0], x_local.at[0]),
        RowsRing(g_down, all_down, ring_down, total_down, x_send.at[1], x_recv.at[1], x_local.at[1]),
    ]
    greet(z_peers + rings[0].peers())
    ghs[h] = grad_hidden[...].astype(BF16)
    gh_copies = [remote(ghs.at[h], ghs.at[h], a_send.at[k], a_recv.at[k], z_peers[k]) for k in range(3)]
    for k in (1, 0, 2):
        gh_copies[k].start()
    for ring in rings:
        ring.begin()
    state[...] = jnp.zeros_like(state)
    g_rate[...] = jnp.zeros_like(g_rate)
    rows_sum[...] = jnp.zeros_like(rows_sum)
    gus[512:520] = jnp.zeros((8, inner), F32)
    marks[0:512] = seq[:, model:].astype(F32)
    marks[512:520] = jnp.zeros((8, 128), F32)
    a = jnp.exp(params[104:120, :]) * (-LOG2E)

    def spots(shape, axis):
        return lax.broadcasted_iota(jnp.int32, shape, axis)

    picks = (spots((STEP, STEP * half), 1) // half == spots((STEP, STEP * half), 0)).astype(BF16)
    tall = (block * states, 128)
    chosen = (spots(tall, 1) - 72 == spots(tall, 0) % states)
    chosen_c = (spots(tall, 1) - 88 == spots(tall, 0) % states)
    gather_rows = (spots((block, block * states), 1) // states == spots((block, block * states), 0)).astype(BF16)
    ones = jnp.ones((128, 128), BF16)

    def gh_wait(b):
        at = lax.rem(h - b + 4, 4) - 1
        remote(ghs.at[h], ghs.at[h], a_send.at[at], a_recv.at[at], z_peers[0]).wait_recv()

    def proj_copy(b, k):
        at = k * 4 + b
        return remote(own.at[b], landing.at[k, b], p_send.at[at], p_recv.at[at], z_peers[k])

    def branch_copy(b, sender):
        return remote(branch.at[b], came.at[sender], b_send.at[b], b_recv.at[sender], (e, r, b))

    def stage_a(b):
        start = pl.multiple_of(b * block, block)
        rows = pl.ds(start, block)
        lin = dt_lin[rows, :]
        dt = jax.nn.softplus(lin)
        u_now = u_in[rows, :]
        convolved = u_now * jax.nn.sigmoid(u_now)
        conv[...] = convolved
        conv_low[rows, :] = convolved.astype(BF16)
        dts[...] = dt
        dtm[...] = dt + across(STOP * marks[rows, :], inner)
        dtx[...] = dt * convolved
        z = gate_z[rows, :]
        sig = jax.nn.sigmoid(z)
        turned = proj[rows, :].T
        b_all, c_all = turned[72:88], turned[88:104]

        @pl.when(b != h)
        def arrived():
            gh_wait(b)

        gg = both_cols(ghs[b], whole[:, 2 * model : small], extra[:, 2 * model : small])
        gy_now = gg * z * sig
        gy[...] = gy_now
        ggate[rows, :] = (gg * y_in[rows, :] * (sig * (1.0 + z * (1.0 - sig)))).astype(BF16)

        def chunk(step, carry):
            u, rate = carry
            i = lines - 1 - step
            hh = starts[b * lines + i]
            held[0] = hh
            shift = lax.rem(block - i * STEP, block)
            b_now, c_now = pltpu.roll(b_all, shift, 1), pltpu.roll(c_all, shift, 1)
            for j in range(STEP):
                t = pl.ds(i * STEP + j, 1)
                decay = jnp.exp2(a * dtm[t, :])
                hh = decay * hh + b_now[:, j : j + 1] * dtx[t, :]
                decays[j] = decay
                held[j + 1] = hh
            for j in range(STEP - 1, -1, -1):
                t = pl.ds(i * STEP + j, 1)
                gy_row = gy[t, :]
                g = c_now[:, j : j + 1] * gy_row + u
                u = decays[j] * g
                q = u * held[j]
                g_rate[...] += q * dts[t, :]
                w = q * a
                parts_2[j * half : (j + 1) * half, :] = w[:half] + w[half:]
                w = g * b_now[:, j : j + 1]
                parts_1[j * half : (j + 1) * half, :] = w[:half] + w[half:]
                at = pl.ds(pl.multiple_of((i * STEP + j) * states, states), states)
                lanes_b[at, :] = over_lanes(g * dtx[t, :]).astype(BF16)
                lanes_c[at, :] = over_lanes(held[j + 1] * gy_row).astype(BF16)
            here = pl.ds(pl.multiple_of(i * STEP, STEP), STEP)
            s1[here, :] = matmul(picks, parts_1[...].astype(BF16))
            s2[here, :] = matmul(picks, parts_2[...].astype(BF16))
            return u, rate

        u_end, unused = lax.fori_loop(0, lines, chunk, (state[...], 0))
        state[...] = u_end
        grad_lin = jax.nn.sigmoid(lin) * (convolved * s1[...] + s2[...] * (1.0 / LOG2E))
        low = grad_lin.astype(BF16)
        gdl[rows, :] = low
        rows_sum[5:6, :] += jnp.sum(grad_lin, axis=0, keepdims=True)
        rows_sum[6:7, :] += jnp.sum(gy_now * convolved, axis=0, keepdims=True)
        gsx[rows, :] = params[126:127, :] * gy_now + dt * s1[...]
        spread = jnp.where(chosen, matmul(lanes_b[...], ones), 0.0) + jnp.where(
            chosen_c, matmul(lanes_c[...], ones), 0.0
        )
        share = matmul(gather_rows, spread.astype(BF16))
        share = share + matmul(low[:, :512], whole[:, small + 128 : small + 256])
        share = share + matmul(low[:, 512:], extra[:, small + 128 : small + 256])
        own[b] = share.astype(BF16)
        for k in (1, 0, 2):
            proj_copy(b, k).start()

    def stage_b(b):
        start = pl.multiple_of(b * block, block)
        rows = pl.ds(start, block)
        for k in range(3):
            proj_copy(b, k).wait_recv()
        gp = (
            own[b].astype(F32) + landing[0, b].astype(F32) + landing[1, b].astype(F32) + landing[2, b].astype(F32)
        ).astype(BF16)
        gp_all[rows, :] = gp
        u_now = u_in[rows, :]
        sig = jax.nn.sigmoid(u_now)
        gu = gsx[rows, :] + both_cols(gp, whole[:, small : small + 128], extra[:, small : small + 128])
        gu = gu * (sig * (1.0 + u_now * (1.0 - sig)))
        gus[rows, :] = gu
        lines_g, lines_m = gus[pl.ds(start, block + 8), :], marks[pl.ds(start, block + 8), :]
        x = x_low[rows, :].astype(F32)
        total = params[123:124, :] * gu
        rows_sum[3:4, :] += jnp.sum(gu * x, axis=0, keepdims=True)
        rows_sum[4:5, :] += jnp.sum(gu, axis=0, keepdims=True)
        mask = jnp.ones((block, 128), F32)
        for ahead in (1, 2, 3):
            mask = mask * (1.0 - lines_m[ahead : ahead + block])
            moved = lines_g[ahead : ahead + block] * across(mask, inner)
            total = total + params[123 - ahead : 124 - ahead, :] * moved
            rows_sum[3 - ahead : 4 - ahead, :] += jnp.sum(moved * x, axis=0, keepdims=True)
        low = total.astype(BF16)
        gx[rows, :] = low
        gate = ggate[rows, :]
        out = (
            matmul(low[:, :512], whole[:, :model])
            + matmul(low[:, 512:], extra[:, :model])
            + matmul(gate[:, :512], whole[:, model : 2 * model])
            + matmul(gate[:, 512:], extra[:, model : 2 * model])
        )
        branch[b] = out.astype(BF16)

        @pl.when(b != h)
        def send():
            branch_copy(b, lax.rem(h - b + 4, 4) - 1).start()

    def step(n, carry):
        stage_a(3 - n)

        @pl.when(n > 0)
        def later():
            stage_b(4 - n)

        @pl.when(n == 0)
        def pass_on():
            for ring in rings:
                ring.pass_on()

        @pl.when(n == 1)
        def finish():
            for ring in rings:
                ring.finish()

        return carry

    lax.fori_loop(0, 4, step, 0)

    owners = grads.shape[0]
    extras = []

    def weight(left, right, at, size):
        main = inner_rows(left[:, :512], right)
        grads[:, :, at : at + size] = main.astype(BF16).reshape(owners, MAIN, size)
        extras.append(inner_rows(left[:, 512:], right).astype(BF16))

    for ring in rings:
        ring.forward()
    weight(gated[...], ghs[...].reshape(4 * block, model), 2 * model, model)
    stage_b(0)
    gx_rows, gate_rows, low_norm = gx[...], ggate[...], normed[...]
    weight(gx_rows, low_norm, 0, model)
    weight(gate_rows, low_norm, model, model)
    weight(gdl[...], proj[...].astype(BF16), small + 128, 128)
    ends = jnp.concatenate(
        [
            jnp.zeros((104, inner), F32), g_rate[...] * (a * (1.0 / LOG2E)), rows_sum[...],
        ],
        axis=0,
    ).astype(BF16)
    low_conv, low_gp, unit = conv_low[...], gp_all[...], eye(128)
    main = inner_rows(low_conv[:, :512], low_gp) + inner_rows(ends[:, :512], unit)
    grads[:, :, small : small + 128] = main.astype(BF16).reshape(owners, MAIN, 128)
    last = (inner_rows(low_conv[:, 512:], low_gp) + inner_rows(ends[:, 512:], unit)).astype(BF16)
    lines_e = jnp.concatenate(
        [extras[1], extras[2], extras[0], last, extras[3], jnp.zeros((64, 4096 - small - 256), BF16)], axis=1
    )
    stacked = jnp.concatenate([lines_e[:, k * 512 : (k + 1) * 512] for k in range(8)], axis=0)
    row, col = spots((512, 512), 0), spots((512, 512), 1)
    wanted = (col % 64 // 2) * MAIN + (col % 2) * 8 + col // 64
    grads[:, :, small + 256 : small + 768] = (
        matmul((wanted == row).astype(BF16), stacked).astype(BF16).reshape(owners, MAIN, 512)
    )
    for k in range(3):
        branch_copy(0, k).wait_recv()
    mine = pl.ds(pl.multiple_of(h * block, block), block)
    grad_n = branch[h].astype(F32) + came[0].astype(F32) + came[1].astype(F32) + came[2].astype(F32)
    values = seq[mine, :model].astype(F32)
    scale = lax.rsqrt(jnp.mean(values * values, axis=-1, keepdims=True) + EPS)
    scaled = grad_n * gains[0:1, :]
    inside = jnp.mean(scaled * values, axis=-1, keepdims=True)
    grad_tokens[...] = grad_hidden[...] + scale * scaled - values * (scale * scale * scale * inside)
    first = jnp.sum(grad_n * values * scale, axis=0, keepdims=True)
    tile = norm_in[...] + jnp.where(spots(norm_in.shape, 0) == 0, first, 0.0)
    span = model // owners
    for n in range(owners):
        piece = tile[:, n * span : (n + 1) * span]
        grads[n, :, small + 768 :] = jnp.concatenate([piece, jnp.zeros((MAIN, 128 - span), F32)], axis=1).astype(BF16)
    for ring in rings:
        ring.end()
    for copy in gh_copies:
        copy.wait_send()
    for b in range(4):
        for k in range(3):
            proj_copy(b, k).wait_send()

        @pl.when(b != h)
        def sent():
            branch_copy(b, 0).wait_send()


def mixer_backward(grad_hidden, seq, whole, gains, norm_in, saved, owners, g_up, g_down):
    normed, x_low, u, gate_z, proj, dt_lin, y, gated, starts, params, extra = saved
    block, model = grad_hidden.shape
    tokens, inner = u.shape
    states = starts.shape[1]
    line, low = pltpu.VMEM((block, inner), F32), pltpu.VMEM((tokens, inner), BF16)
    return pl.pallas_call(
        mixer_back_kernel,
        out_shape=(
            jax.ShapeDtypeStruct((owners, MAIN, 3 * model + 896), BF16),
            jax.ShapeDtypeStruct((block, model), F32),
            jax.ShapeDtypeStruct(g_up.shape, BF16),
            jax.ShapeDtypeStruct(g_down.shape, BF16),
        ),
        in_specs=[IN_VMEM] * 16 + [ANY] * 2,
        out_specs=(IN_VMEM, IN_VMEM, ANY, ANY),
        scratch_shapes=[
            pltpu.VMEM((4, block, model), BF16),
            pltpu.VMEM((tokens + 8, inner), F32),
            pltpu.VMEM((tokens + 8, 128), F32),
            line, line, line, line, line, line, line,
            pltpu.VMEM((tokens, inner), F32),
            low, low, low,
            pltpu.VMEM((tokens, 128), BF16),
            low,
            pltpu.VMEM((STEP + 1, states, inner), F32),
            pltpu.VMEM((STEP, states, inner), F32),
            pltpu.VMEM((STEP * states // 2, inner), F32),
            pltpu.VMEM((STEP * states // 2, inner), F32),
            pltpu.VMEM((block * states, 128), BF16),
            pltpu.VMEM((block * states, 128), BF16),
            pltpu.VMEM((states, inner), F32),
            pltpu.VMEM((states, inner), F32),
            pltpu.VMEM((8, inner), F32),
            pltpu.VMEM((4, block, 128), BF16),
            pltpu.VMEM((3, 4, block, 128), BF16),
            pltpu.VMEM((4, block, model), BF16),
            pltpu.VMEM((3, block, model), BF16),
            DMA((3,)), DMA((3,)), DMA((12,)), DMA((12,)), DMA((4,)), DMA((3,)),
            pltpu.VMEM((12, g_up.shape[0] // 8, g_up.shape[1]), BF16),
            pltpu.VMEM((12, g_down.shape[0] // 8, g_down.shape[1]), BF16),
            pltpu.VMEM((2, g_up.shape[0] // 8, g_up.shape[1]), BF16),
            pltpu.VMEM((2, g_down.shape[0] // 8, g_down.shape[1]), BF16),
            DMA((2, 12)), DMA((2, 12)), DMA((2, 6)),
        ],
        compiler_params=pltpu.CompilerParams(
            collective_id=5, has_side_effects=True, vmem_limit_bytes=58 << 20
        ),
        name="mixer_backward",
    )(
        grad_hidden, seq, whole, gains, norm_in, normed, x_low, u, gate_z, proj, dt_lin, y, gated, starts, params, extra,
        g_up, g_down,
    )


def spread_extra(lines):
    count, rows, width = lines.shape
    lines = jnp.pad(lines, ((0, 0), (0, 0), (0, MAIN * EXTRA // rows - width)))
    return lines.reshape(count, MAIN, EXTRA)


def gathered_extra(tiles, width):
    count = tiles.shape[0]
    return tiles.reshape(count, 2, MAIN * EXTRA // 2)[:, :, :width]


def shards(
    tokens, resets, routes, cotangent, mixer_gain, in_proj, conv_kernel, conv_bias, x_proj, dt_proj,
    dt_bias, log_decay, skip_gain, out_proj, moe_gain, router, up_proj, down_proj,
):
    rows_dev, model = tokens.shape
    own = conv_bias.shape[0]
    experts = router.shape[1]
    rank, states, taps = dt_proj.shape[0], log_decay.shape[0], conv_kernel.shape[0]
    wide = rank + 2 * states
    owners = lax.axis_size("expert") * lax.axis_size("rows")
    hids = lax.axis_size("hid")
    inner = owners * own
    mixer_axes = ("expert", "rows")

    in_lines = in_proj.transpose(2, 1, 0)
    small = jnp.concatenate(
        [
            x_proj.T, log_decay.T, conv_kernel.T, conv_bias[:, None], dt_bias[:, None], skip_gain[:, None],
            jnp.zeros((own, 1), BF16), dt_proj.T, jnp.zeros((own, 128 - rank), BF16),
        ],
        axis=1,
    )
    pack = jnp.concatenate([in_lines[:, 0], in_lines[:, 1], out_proj, small], axis=1)
    width = pack.shape[1]
    tokens_reset = jnp.concatenate(
        [tokens, jnp.broadcast_to(resets[:, None].astype(BF16), (rows_dev, 128))], axis=1
    )
    hid_at = lax.axis_index("hid")
    pack = jnp.concatenate([pack[:MAIN], spread_extra(pack[None, MAIN:])[0]], axis=1)
    norm_tile = jnp.concatenate([mixer_gain[None], moe_gain[None], router.T], axis=0)
    norm_lines, share = norm_tile.shape
    norm_tile = jnp.pad(norm_tile, ((0, MAIN - norm_lines), (0, 0)))
    norm_tile = jnp.where(jnp.arange(hids)[None, :, None] == hid_at, norm_tile[:, None, :], 0)
    norm_tile = jnp.pad(norm_tile.reshape(MAIN, hids * share), ((0, 0), (0, 128 - hids * share)))
    whole, norms, sequence = gather_start(pack, norm_tile, tokens_reset)
    sequence = sequence.reshape(hids * rows_dev, -1)
    gains = norms[:, :, : hids * share].transpose(1, 0, 2).reshape(MAIN, model)
    gains_float = gains.astype(F32)
    gain_one, gain_two = gains_float[0], gains_float[1]
    router_t = gains[2 : 2 + experts]
    packed = whole.reshape(owners * MAIN, -1)
    *saved, hidden_one, params, extra = mixer_forward(sequence, packed, gains_float, inner, states)
    normed_two, norm_two_back = jax.vjp(rms_norm, hidden_one, gain_two)
    moe_low = normed_two.astype(BF16)
    probs = jax.nn.softmax(outer_cols(moe_low, router_t), axis=-1)
    picked = routes == jnp.arange(experts, dtype=jnp.int32)[None, :]
    onehot = picked.astype(F32)
    gate = jnp.sum(probs * onehot, axis=-1)
    picked_int = picked.astype(jnp.int32)
    within = jnp.sum(picked_int * (jnp.cumsum(picked_int, axis=0) - 1), axis=1)
    grad_output = cotangent.astype(F32)
    grad_eo = (gate[:, None] * grad_output).astype(BF16)
    slot = jnp.arange(experts * MAIN, dtype=jnp.int32)[:, None]
    line, expert_at = slot % MAIN, slot // MAIN
    here = expert_at == routes[:, 0][None, :]
    place_of = within[None, :]
    pick_main = (here & (place_of == line)).astype(BF16)
    pick_top = (here & (line < 8) & (place_of == line + 16)).astype(BF16)
    pick_low = (here & (line >= 8) & (place_of == line + 8)).astype(BF16)
    main = matmul(pick_main, jnp.concatenate([moe_low, grad_eo], axis=1))
    folded = matmul(pick_top, moe_low) + matmul(pick_low, grad_eo)
    slots = jnp.concatenate([main, folded], axis=1).astype(BF16).reshape(experts, MAIN, 3 * model)
    back, grad_up, grad_down = experts_both_ways(slots, up_proj[0], down_proj[0])
    back = back.reshape(experts * MAIN, 3 * model)
    expert_out = inner_rows(pick_main, back[:, :model]) + inner_rows(pick_top, back[:, 2 * model :])
    grad_rows = inner_rows(pick_main, back[:, model : 2 * model]) + inner_rows(pick_low, back[:, 2 * model :])

    output = (hidden_one + gate[:, None] * expert_out).astype(BF16)
    grad_gate = jnp.sum(grad_output * expert_out, axis=-1)
    grad_logits = ((gate * grad_gate)[:, None] * (onehot - probs)).astype(BF16)
    grad_router = inner_rows(moe_low, grad_logits)
    grad_moe = grad_rows + matmul(grad_logits, router_t)
    grad_hidden_more, grad_gain_two = norm_two_back(grad_moe)
    grad_hidden = grad_output + grad_hidden_more

    norm_grads = jnp.concatenate([jnp.zeros((1, model), F32), grad_gain_two[None], grad_router.T], axis=0)
    norm_grads = jnp.pad(norm_grads, ((0, MAIN - norm_lines), (0, 0)))
    grads, grad_tokens, all_up, all_down = mixer_backward(
        grad_hidden, sequence, packed, gains_float, norm_grads, (*saved, params, extra), owners, grad_up, grad_down
    )
    summed, norm_sum, grad_up_sum, grad_down_sum = return_grads(grads, all_up, all_down)
    rest = jnp.concatenate([summed[:, :width], gathered_extra(summed[None, :, width : width + EXTRA], width)[0]], axis=0)
    grad_in = jnp.stack([rest[:, :model], rest[:, model : 2 * model]], axis=1).transpose(2, 1, 0)
    out_part = rest[:, 2 * model : 3 * model]
    small_sum = rest[:, 3 * model :]
    done, at = [], 0
    for cut in (wide, states, taps, 1, 1, 1, 1, rank):
        done.append(small_sum[:, at : at + cut])
        at += cut
    norm_sum = lax.dynamic_slice_in_dim(norm_sum, hid_at * share, share, axis=1)
    return (
        output,
        grad_tokens,
        norm_sum[0],
        grad_in,
        done[2].T,
        done[3][:, 0],
        done[0].T,
        done[7].T,
        done[4][:, 0],
        done[1].T,
        done[5][:, 0],
        out_part,
        norm_sum[1],
        norm_sum[2 : 2 + experts].T,
        grad_up_sum[None],
        grad_down_sum[None],
    )


def solution(mesh):
    every = ("expert", "rows", "hid")
    in_specs = (
        P(every, None), P(every), P(every, None), P(every, None), P(every), P(None, None, every),
        P(None, every), P(every), P(None, every), P(None, every), P(every), P(None, every), P(every),
        P(every, None), P(every), P(every, None), P("expert", None, "hid"), P("expert", "hid", None),
    )
    out_specs = (
        P(every, None), P(every, None), P(every), P(None, None, every), P(None, every), P(every),
        P(None, every), P(None, every), P(every), P(None, every), P(every), P(every, None), P(every),
        P(every, None), P("expert", None, "hid"), P("expert", "hid", None),
    )
    return jax.shard_map(shards, mesh=mesh, in_specs=in_specs, out_specs=out_specs, check_vma=False)
```

```python
from functools import partial

import jax
import jax.numpy as jnp
from jax import lax
from jax.experimental import pallas as pl
from jax.experimental.pallas import tpu as pltpu
from jax.sharding import PartitionSpec as P

EPS = 1e-05
LOG2E = 1.4426950408889634
STOP = 1e6
STEP = 16
MAIN = 16
EXTRA = 512
GELU_C = 0.7978845608028654
F32 = jnp.float32
BF16 = jnp.bfloat16


def matmul(first_op, second_op):
    return jnp.dot(first_op, second_op, preferred_element_type=F32)


def inner_rows(first_op, second_op):
    return lax.dot_general(
        first_op, second_op, (((0,), (0,)), ((), ())), preferred_element_type=F32
    )


def outer_cols(first_op, second_op):
    return lax.dot_general(
        first_op, second_op, (((1,), (1,)), ((), ())), preferred_element_type=F32
    )


def rms_norm(values, gain):
    return values * lax.rsqrt(jnp.mean(values * values, axis=-1, keepdims=True) + EPS) * gain


def over_lanes(v):
    whole = v.shape[1] // 128
    total = v[:, :128]
    for k in range(1, whole):
        total = total + v[:, k * 128 : (k + 1) * 128]
    rest = v.shape[1] - whole * 128
    if rest:
        blank = jnp.zeros((v.shape[0], 128 - rest), F32)
        total = total + jnp.concatenate([v[:, whole * 128 :], blank], axis=1)
    return total


MESH = pl.DeviceIdType.MESH
ANY = pl.BlockSpec(memory_space=pl.ANY)
IN_VMEM = pl.BlockSpec(memory_space=pltpu.VMEM)
DMA = pltpu.SemaphoreType.DMA


def places():
    return lax.axis_index("expert"), lax.axis_index("rows"), lax.axis_index("hid")


def greet(peers):
    barrier = pltpu.get_barrier_semaphore()
    for peer in peers:
        pl.semaphore_signal(barrier, inc=1, device_id=peer, device_id_type=MESH)
    pl.semaphore_wait(barrier, len(peers))


def remote(src, dst, send_sem, recv_sem, peer):
    return pltpu.make_async_remote_copy(
        src_ref=src, dst_ref=dst, send_sem=send_sem, recv_sem=recv_sem, device_id=peer,
        device_id_type=MESH,
    )


def hid_peers():
    e, r, h = places()
    return [(e, r, lax.rem(h + k, 4)) for k in (1, 2, 3)]


def mixer_peers():
    e, r, h = places()
    c = lax.rem(e, 2)
    mate = (e + 1 - 2 * c, r, h)
    first = [(lax.rem(e + 2 * k * (1 - c), 8), lax.rem(r + k * c, 4), h) for k in (1, 2, 3)]
    second = [(lax.rem(e + 2 * k * c, 8), lax.rem(r + k * (1 - c), 4), h) for k in (1, 2, 3)]
    return mate, first, second


def block_at(c, f, s):
    y = f * (1 - c) + s * c
    x = s * (1 - c) + f * c
    return (2 * y + c) * 4 + x


def gelu_pair(pre, grad):
    square = pre * pre
    t = jnp.tanh(GELU_C * pre * (1.0 + 0.044715 * square))
    up = 0.5 * (1.0 + t)
    slope = up + 0.5 * pre * (1.0 - t * t) * (GELU_C * (1.0 + 3 * 0.044715 * square))
    return pre * up, slope * grad


def expert_kernel(
    slots, up, down, hid_in, cotangent, moe_low, probs, routes, gains, output, grad_hidden, norm_out, g_up, g_down, back, held, results, hid_out, pre_out, hid_w, pre_w, from_left, from_right,
    half_left, half_right, sums, d_send, d_recv, r_send, r_recv, l_send, l_recv, f_send, f_recv, c_send, c_recv,
    k_send, k_recv, h_send, h_recv, b_send, b_recv,
):
    e, r, h = places()
    model, hidden = up.shape
    right, left, across = lax.rem(h + 1, 4), lax.rem(h + 3, 4), lax.rem(h + 2, 4)
    to_right, to_left = (e, r, right), (e, r, left)
    to_expert = [(lax.rem(e + k, 8), r, h) for k in range(8)]
    source = [lax.rem(e + 8 - k, 8) for k in range(8)]
    greet(to_expert[1:] + [to_right, to_left])

    d_copies = [None]
    for k in range(1, 8):
        d_copies.append(
            remote(slots.at[lax.rem(e + k, 8)], held.at[h, e], d_send.at[k], d_recv.at[k], to_expert[k])
        )
        d_copies[k].start()
    held[h, e] = slots[e]

    def along(buf, where, k, send, recv, peer):
        block = buf.at[where, source[k]]
        copy = remote(block, block, send.at[k], recv.at[k], peer)
        copy.start()
        return copy

    r_copies, l_copies = [None] * 8, [None] * 8
    for k in range(8):
        if k:
            d_copies[k].wait_recv()
        r_copies[k] = along(held, h, k, r_send, r_recv, to_right)
        if k >= 4:
            l_copies[k] = along(held, h, k, l_send, l_recv, to_left)
    for k in range(4):
        l_copies[k] = along(held, h, k, l_send, l_recv, to_left)

    half = 128

    def worked(where):
        lines = held[where]
        main_x = lines[:, :, :model].reshape(half, model)
        main_g = lines[:, :, model : 2 * model].reshape(half, model)
        extra = lines[:, :, 2 * model :].reshape(half, model)
        rows_x = jnp.concatenate([main_x, extra], axis=0)
        rows_g = jnp.concatenate([main_g, extra], axis=0)

        def first_layer(i, carry):
            cols = pl.ds(pl.multiple_of(i * 256, 256), 256)
            pre = matmul(rows_x, up[:, cols])
            grad = outer_cols(rows_g, down[cols, :])
            hid_m, pre_m = gelu_pair(pre[:half], grad[:half])
            pre_e = pre[half:].reshape(8, 2, 8, 256)[:, 0]
            grad_e = grad[half:].reshape(8, 2, 8, 256)[:, 1]
            hid_e, gpre_e = gelu_pair(pre_e, grad_e)
            none = jnp.zeros_like(hid_e)

            def stacked(a, b):
                return jnp.stack([a, b], axis=1).reshape(half, 256).astype(BF16)

            hid_m, pre_m = hid_m.astype(BF16), pre_m.astype(BF16)
            hid_out[:half, cols] = hid_m
            pre_out[:half, cols] = pre_m
            hid_w[where, :half, cols] = hid_m
            pre_w[where, :half, cols] = pre_m
            hid_out[half:, cols] = stacked(hid_e, none)
            pre_out[half:, cols] = stacked(none, gpre_e)
            hid_w[where, half:, cols] = stacked(none, hid_e)
            pre_w[where, half:, cols] = stacked(gpre_e, none)
            return carry

        lax.fori_loop(0, hidden // 256, first_layer, 0)

        def second_layer(i, carry):
            at = pl.multiple_of(i * 384, 384)
            cols = pl.ds(at, 384)
            share = matmul(hid_out[...], down[:, cols])
            grad = outer_cols(pre_out[...], up[cols, :])
            shape = (8, 16, 384)
            results[where, :, :, cols] = share[:half].astype(BF16).reshape(shape)
            results[where, :, :, pl.ds(model + at, 384)] = grad[:half].astype(BF16).reshape(shape)
            results[where, :, :, pl.ds(2 * model + at, 384)] = (share[half:] + grad[half:]).astype(BF16).reshape(shape)
            return carry

        lax.fori_loop(0, model // 384, second_layer, 0)

    worked(h)
    f_copies = [None] * 8
    for k in range(4):
        r_copies[k].wait_recv()
        f_copies[k] = along(held, left, k, f_send, f_recv, to_right)
        l_copies[4 + k].wait_recv()
        f_copies[4 + k] = along(held, right, 4 + k, f_send, f_recv, to_left)
    for k in range(4, 8):
        r_copies[k].wait_recv()
    worked(left)
    c_copies = [None] * 8
    k_copies = [None] * 8

    def toward_right(k):
        block = results.at[right, source[k]]
        c_copies[k] = remote(block, from_left.at[k], c_send.at[k], c_recv.at[k], to_right)
        c_copies[k].start()

    def toward_left(k):
        block = results.at[left, source[k]]
        k_copies[k] = remote(block, from_right.at[k], k_send.at[k], k_recv.at[k], to_left)
        k_copies[k].start()

    for k in range(4):
        toward_left(k)
    for k in range(4):
        l_copies[k].wait_recv()
    worked(right)
    for k in range(4, 8):
        toward_right(k)
    for k in range(8):
        f_copies[k].wait_recv()
    worked(across)
    h_copies = []
    for k in range(4):
        for at, landing, peer in ((k, half_left, to_right), (4 + k, half_right, to_left)):
            block = results.at[across, source[at]]
            copy = remote(block, landing.at[k], h_send.at[at], h_recv.at[at], peer)
            copy.start()
            h_copies.append(copy)

    def weight_grads(i, carry):
        cols = pl.ds(pl.multiple_of(i * 128, 128), 128)
        total = jnp.zeros((128, hidden), F32)
        for lanes, kept, out in ((0, pre_w, g_up),):
            x_main = held[:, :, :, pl.ds(pl.multiple_of(i * 128, 128), 128)].reshape(4, half, 128)
            x_extra = held[:, :, :, pl.ds(pl.multiple_of(2 * model + i * 128, 128), 128)].reshape(4, half, 128)
            rows = jnp.concatenate([x_main, x_extra], axis=1).reshape(8 * half, 128)
            total = inner_rows(rows, kept[...].reshape(8 * half, hidden))
            out[cols, :] = total.astype(BF16)
        g_main = held[:, :, :, pl.ds(pl.multiple_of(model + i * 128, 128), 128)].reshape(4, half, 128)
        rows = jnp.concatenate([g_main, x_extra], axis=1).reshape(8 * half, 128)
        g_down[:, cols] = inner_rows(hid_w[...].reshape(8 * half, hidden), rows).astype(BF16)
        return carry

    lax.fori_loop(0, model // 128, weight_grads, 0)

    for k in range(4):
        h_copies[2 * k].wait_recv()
        block = source[k]
        results[right, block] = (results[right, block].astype(F32) + half_left[k].astype(F32)).astype(BF16)
        toward_right(k)
        h_copies[2 * k + 1].wait_recv()
        block = source[4 + k]
        results[left, block] = (results[left, block].astype(F32) + half_right[k].astype(F32)).astype(BF16)
        toward_left(4 + k)
    b_copies = []
    for k in (4, 5, 6, 7, 3, 2, 1, 0):
        c_copies[k].wait_recv()
        k_copies[k].wait_recv()
        total = results[h, source[k]].astype(F32) + from_left[k].astype(F32) + from_right[k].astype(F32)
        if k:
            sums[k] = total.astype(BF16)
            copy = remote(sums.at[k], back.at[e], b_send.at[k], b_recv.at[k], to_expert[8 - k])
            copy.start()
            b_copies.append(copy)
        else:
            back[e] = total.astype(BF16)
    for copy in b_copies:
        copy.wait_recv()
    main, top, low_half, onehot = slot_picks(routes[...], slots.shape[0])
    lines = back[...].reshape(128, 3 * model)
    shares = probs[...]
    gate = jnp.sum(shares * onehot, axis=-1, keepdims=True)
    hid, grad_output, low = hid_in[...], cotangent[...].astype(F32), moe_low[...]
    expert_out = inner_rows(main, lines[:, :model]) + inner_rows(top, lines[:, 2 * model :])
    output[...] = (hid + gate * expert_out).astype(BF16)
    grad_gate = jnp.sum(grad_output * expert_out, axis=-1, keepdims=True)
    grad_logits = (gate * grad_gate * (onehot - shares)).astype(BF16)
    grad_moe = inner_rows(main, lines[:, model : 2 * model]) + inner_rows(low_half, lines[:, 2 * model :])
    grad_moe = grad_moe + matmul(grad_logits, gains[...].astype(BF16))
    scale = lax.rsqrt(jnp.mean(hid * hid, axis=-1, keepdims=True) + EPS)
    scaled = grad_moe * gains[1:2, :]
    inside = jnp.mean(scaled * hid, axis=-1, keepdims=True)
    grad_hidden[...] = grad_output + scale * scaled - hid * (scale * scale * scale * inside)
    grad_gain = jnp.sum(grad_moe * hid * scale, axis=0, keepdims=True)
    at = lax.broadcasted_iota(jnp.int32, norm_out.shape, 0)
    norm_out[...] = inner_rows(grad_logits, low) + jnp.where(at == 1, grad_gain, 0.0)
    for copy in d_copies[1:] + r_copies + l_copies + f_copies + c_copies + k_copies + h_copies + b_copies:
        copy.wait_send()


def experts_both_ways(slots, up, down, *rest):
    count, lines, width = slots.shape
    model, hidden = up.shape
    eight = DMA((8,))
    return pl.pallas_call(
        expert_kernel,
        out_shape=(
            jax.ShapeDtypeStruct(rest[1].shape, BF16),
            jax.ShapeDtypeStruct(rest[0].shape, F32),
            jax.ShapeDtypeStruct(rest[5].shape, F32),
            jax.ShapeDtypeStruct(up.shape, BF16),
            jax.ShapeDtypeStruct(down.shape, BF16),
        ),
        in_specs=[IN_VMEM] * 9,
        out_specs=(IN_VMEM,) * 5,
        scratch_shapes=[
            pltpu.VMEM(slots.shape, BF16),
            pltpu.VMEM((4, count, lines, width), BF16),
            pltpu.VMEM((4, count, lines, width), BF16),
            pltpu.VMEM((256, hidden), BF16),
            pltpu.VMEM((256, hidden), BF16),
            pltpu.VMEM((4, 256, hidden), BF16),
            pltpu.VMEM((4, 256, hidden), BF16),
            pltpu.VMEM((8, lines, width), BF16),
            pltpu.VMEM((8, lines, width), BF16),
            pltpu.VMEM((4, lines, width), BF16),
            pltpu.VMEM((4, lines, width), BF16),
            pltpu.VMEM((8, lines, width), BF16),
            *[eight] * 16,
        ],
        compiler_params=pltpu.CompilerParams(
            collective_id=8, has_side_effects=True, vmem_limit_bytes=62 << 20
        ),
        name="experts",
    )(slots, up, down, *rest)


def across(tile, width):
    whole = width // 128
    return jnp.concatenate([tile] * whole + [tile[:, : width - 128 * whole]], axis=1)


def eye(size):
    at = [lax.broadcasted_iota(jnp.int32, (size, size), axis) for axis in (0, 1)]
    return (at[0] == at[1]).astype(BF16)


def both_cols(lines, main, extra):
    return jnp.concatenate([outer_cols(lines, main), outer_cols(lines, extra)], axis=1)


def gather_all(
    pack, norm, line, whole, norms, sequence, tiles, total, local_sems, z_send, z_recv, n_send, n_recv,
    w_send, w_recv, v_send, v_recv,
):
    e, r, h = places()
    c = lax.rem(e, 2)
    y = e // 2
    f0 = y * (1 - c) + r * c
    s0 = r * (1 - c) + y * c
    mate, first, second = mixer_peers()
    z_peers = hid_peers()
    own = e * 4 + r
    n_copies = [
        remote(norm, tiles.at[k], n_send.at[k], n_recv.at[k], z_peers[k]) for k in range(3)
    ]
    for copy in n_copies:
        copy.start()
    w_one = [remote(pack, whole.at[own], w_send.at[k], w_recv.at[k], first[k]) for k in range(3)]
    w_two = [[remote(pack, whole.at[own], w_send.at[3 + k], w_recv.at[3 + k], second[k]) for k in range(3)]]
    w_mate = [remote(pack, whole.at[own], w_send.at[15], w_recv.at[15], mate)]
    for k in (1, 0, 2):
        w_one[k].start()
    for k in (1, 0, 2):
        w_two[0][k].start()
    z_copies = [remote(line, sequence.at[h], z_send.at[k], z_recv.at[k], z_peers[k]) for k in range(3)]
    for k in (1, 0, 2):
        z_copies[k].start()
    w_mate[0].start()
    mine = [
        pltpu.make_async_copy(pack, whole.at[own], local_sems.at[0]),
        pltpu.make_async_copy(line, sequence.at[h], local_sems.at[1]),
    ]
    for copy in mine:
        copy.start()
    for copy in n_copies:
        copy.wait_recv()
    total[...] = norm[...] + tiles[0] + tiles[1] + tiles[2]
    v_one = [remote(total, norms.at[own], v_send.at[k], v_recv.at[k], first[k]) for k in range(3)]
    v_two = [[remote(total, norms.at[own], v_send.at[3 + k], v_recv.at[3 + k], second[k]) for k in range(3)]]
    v_mate = [remote(total, norms.at[own], v_send.at[15], v_recv.at[15], mate)]
    for copy in v_one + v_two[0] + v_mate:
        copy.start()
    mine.append(pltpu.make_async_copy(total, norms.at[own], local_sems.at[2]))
    mine[2].start()
    for k in range(3):
        came = block_at(c, lax.rem(f0 + 3 - k, 4), s0)
        for buf, one, send, recv, two, other in (
            (whole, w_one, w_send, w_recv, w_two, w_mate), (norms, v_one, v_send, v_recv, v_two, v_mate)
        ):
            one[k].wait_recv()
            block = buf.at[came]
            two.append([remote(block, block, send.at[6 + 3 * k + j], recv.at[6 + 3 * k + j], second[j]) for j in range(3)])
            for j in (1, 0, 2):
                two[1 + k][j].start()
            other.append(remote(block, block, send.at[16 + k], recv.at[16 + k], mate))
            other[-1].start()
    for k in range(4):
        for j in range(3):
            came = block_at(c, lax.rem(f0 + 4 - k, 4), lax.rem(s0 + 3 - j, 4))
            for buf, send, recv, two, other in (
                (whole, w_send, w_recv, w_two, w_mate), (norms, v_send, v_recv, v_two, v_mate)
            ):
                two[k][j].wait_recv()
                block = buf.at[came]
                at = 19 + 3 * k + j
                other.append(remote(block, block, send.at[at], recv.at[at], mate))
                other[-1].start()
    for copy in w_mate + v_mate:
        copy.wait_recv()
    for copy in z_copies:
        copy.wait_recv()
    for copy in n_copies + w_one + sum(w_two, []) + w_mate + v_one + sum(v_two, []) + v_mate + z_copies:
        copy.wait_send()
    for copy in mine:
        copy.wait()


def slot_picks(route, experts, states=16):
    count = route.shape[1]
    line = lax.broadcasted_iota(jnp.int32, (states, count), 0)
    chosen = jnp.where(line - 2 == route, 1.0, 0.0)
    earlier = lax.broadcasted_iota(jnp.int32, (count, count), 0) <= lax.broadcasted_iota(jnp.int32, (count, count), 1)
    counts = matmul(chosen.astype(BF16), jnp.where(earlier, 1.0, 0.0).astype(BF16))
    within = jnp.sum(chosen * (counts - 1.0), axis=0, keepdims=True).astype(jnp.int32)
    slot = lax.broadcasted_iota(jnp.int32, (experts * MAIN, count), 0)
    line, expert = slot % MAIN, slot // MAIN
    here = expert == route

    def of(found):
        return jnp.where(found, 1.0, 0.0).astype(BF16)

    main = of(here & (within == line))
    top = of(here & (line < 8) & (within == line + 16))
    low = of(here & (line >= 8) & (within == line + 8))
    column = jnp.broadcast_to(route.astype(F32), (count, count)).T[:, :states]
    place = lax.broadcasted_iota(jnp.int32, (count, states), 1) - 2
    onehot = jnp.where(place.astype(F32) == column, 1.0, 0.0)
    return main, top, low, onehot


def forward_kernel(*refs):
    (
        x_lines, g_lines, out_lines, x_cols, dt_cols, decay_in, taps_in, conv_bias, dt_bias, skip, gain_one, gain_two,
        router, tokens, resets, routes, cotangent,
        whole_hbm, seq_hbm, extra_hbm, normed_hbm, x_low_hbm, u_hbm, gate_hbm, proj_hbm, lin_hbm, y_hbm, gated_hbm,
        starts_hbm, hidden, params, gains, slots, moe_out, probs,
        pack, norm, line, whole, whole_all, norms, sequence, seq, extra, tiles, total, local_sems, z_send, z_recv, n_send, n_recv,
        w_send, w_recv, v_send, v_recv, k_sems, s_sems,
        normed, x_low, u_out, gate_z, proj, dt_lin, y_out, gated, starts,
        xs, marks, conv, dtm, dtx, parts, own, landing, branch, came, p_send, p_recv, b_send, b_recv,
    ) = refs
    e, r, h = places()
    block, model = tokens.shape
    inner, states, experts = u_out.shape[1], starts.shape[1], router.shape[0]
    lines, small = block // STEP, 3 * model
    channels, share = x_lines.shape[0], gain_one.shape[1]

    def wide(a):
        return a[...].astype(F32)

    line[:, :model] = tokens[...]
    line[:, model:] = jnp.broadcast_to(wide(resets), (block, 128)).T.astype(BF16)
    columns = jnp.concatenate(
        [
            wide(decay_in), wide(taps_in), wide(conv_bias), wide(dt_bias), wide(skip),
            jnp.zeros((105, channels), F32),
        ],
        axis=0,
    )
    columns = jnp.concatenate([columns, jnp.zeros((128, 128 - channels), F32)], axis=1).T[:channels, :24]
    tail = jnp.concatenate(
        [
            jnp.concatenate([wide(x_cols), columns], axis=1),
            jnp.concatenate([wide(dt_cols), jnp.zeros((channels, 128 - dt_cols.shape[1]), F32)], axis=1),
        ],
        axis=1,
    )
    both = jnp.concatenate([wide(x_lines), wide(g_lines), wide(out_lines), tail], axis=1)
    pack[:, : small + 256] = both[:MAIN].astype(BF16)
    last = jnp.concatenate([both[MAIN:], jnp.zeros((channels - MAIN, 4096 - small - 256), F32)], axis=1)
    last = [last[n : n + 1, k * EXTRA : (k + 1) * EXTRA] for n in range(2) for k in range(8)]
    pack[:, small + 256 :] = jnp.concatenate(last, axis=0).astype(BF16)
    tile = jnp.concatenate([wide(gain_one), wide(gain_two), wide(router), jnp.zeros((6, share), F32)], axis=0)
    tile = jnp.concatenate([tile, jnp.zeros((MAIN, 128 - share), F32)], axis=1)
    norm[...] = pltpu.roll(tile, h * share, 1).astype(BF16)
    z_peers = hid_peers()
    mate, first, second = mixer_peers()
    greet([mate] + first + second + z_peers)
    gather_all(
        pack, norm, line, whole, norms, sequence, tiles, total, local_sems, z_send, z_recv, n_send, n_recv,
        w_send, w_recv, v_send, v_recv,
    )
    span = share * 4
    gains[...] = jnp.concatenate([norms[n].astype(F32)[:, :span] for n in range(32)], axis=1)
    whole_all[...] = whole[...].reshape(512, small + 768)
    seq[...] = sequence[...].reshape(4 * block, model + 128)
    row = lax.broadcasted_iota(jnp.int32, (512, 512), 0)
    col = lax.broadcasted_iota(jnp.int32, (512, 512), 1)
    wanted = (row % 64 // 2) * MAIN + (row % 2) * 8 + row // 64
    moved = matmul((wanted == col).astype(BF16), whole_all[:, small + 256 :]).astype(BF16)
    for k in range(8):
        extra[:, k * 512 : (k + 1) * 512] = moved[k * 64 : (k + 1) * 64]
    params[...] = both_cols(eye(128), whole_all[:, small : small + 128], extra[:, small : small + 128])
    kept_copies = [
        pltpu.make_async_copy(kept, out, k_sems.at[n])
        for n, (kept, out) in enumerate(((whole_all, whole_hbm), (seq, seq_hbm), (extra, extra_hbm)))
    ]
    for copy in kept_copies:
        copy.start()
    xs[0:8] = jnp.zeros((8, inner), F32)
    marks[0:8] = jnp.zeros((8, 128), F32)
    gain = gains[0:1, :]

    pairs = (
        (normed, normed_hbm), (x_low, x_low_hbm), (u_out, u_hbm), (gate_z, gate_hbm), (proj, proj_hbm),
        (dt_lin, lin_hbm), (y_out, y_hbm), (gated, gated_hbm), (starts, starts_hbm),
    )

    def saved_copy(n, b):
        kept, out = pairs[n]
        size = kept.shape[0] // 4
        rows = pl.ds(pl.multiple_of(b * size, size), size)
        return pltpu.make_async_copy(kept.at[rows], out.at[rows], s_sems.at[n, b])

    def proj_copy(b, k):
        at = k * 4 + b
        return remote(own.at[b], landing.at[k, b], p_send.at[at], p_recv.at[at], z_peers[k])

    def stage_one(b, carry):
        start = pl.multiple_of(b * block, block)
        rows = pl.ds(start, block)
        values = seq[rows, :model].astype(F32)
        scale = lax.rsqrt(jnp.mean(values * values, axis=-1, keepdims=True) + EPS)
        low = (values * scale * gain).astype(BF16)
        normed[rows, :] = low
        gate_z[rows, :] = both_cols(low, whole_all[:, model : 2 * model], extra[:, model : 2 * model])
        x = both_cols(low, whole_all[:, :model], extra[:, :model]).astype(BF16)
        x_low[rows, :] = x
        after = pl.ds(pl.multiple_of(8 + start, 8), block)
        xs[after, :] = x.astype(F32)
        now = seq[rows, model:].astype(F32)
        marks[after, :] = now
        lines_x, lines_m = xs[pl.ds(start, block + 8), :], marks[pl.ds(start, block + 8), :]
        mask = 1.0 - now
        total = params[124:125, :] + params[123:124, :] * x.astype(F32)
        for back in (1, 2, 3):
            past = lines_x[8 - back : 8 - back + block]
            total = total + params[123 - back : 124 - back, :] * past * across(mask, inner)
            if back < 3:
                mask = mask * (1.0 - lines_m[8 - back : 8 - back + block])
        u_out[rows, :] = total
        convolved = total * jax.nn.sigmoid(total)
        conv[rows, :] = convolved
        conv_low = convolved.astype(BF16)
        share = matmul(conv_low[:, :512], whole_all[:, small : small + 128]) + matmul(
            conv_low[:, 512:], extra[:, small : small + 128]
        )
        own[b] = share.astype(BF16)
        for k in (1, 0, 2):
            proj_copy(b, k).start()
        for n in range(4):
            saved_copy(n, b).start()
        return carry

    lax.fori_loop(0, 4, stage_one, 0)
    a = jnp.exp(params[104:120, :]) * (-LOG2E)
    half = states // 2

    def branch_copy(b, sender):
        return remote(branch.at[b], came.at[sender], b_send.at[b], b_recv.at[sender], (e, r, b))

    def stage_two(b, state):
        start = pl.multiple_of(b * block, block)
        rows = pl.ds(start, block)
        for k in range(3):
            proj_copy(b, k).wait_recv()
        sums = (
            own[b].astype(F32) + landing[0, b].astype(F32) + landing[1, b].astype(F32) + landing[2, b].astype(F32)
        )
        proj[rows, :] = sums
        lin = both_cols(sums.astype(BF16), whole_all[:, small + 128 : small + 256], extra[:, small + 128 : small + 256])
        lin = lin + params[125:126, :]
        dt_lin[rows, :] = lin
        dt = jax.nn.softplus(lin)
        convolved = conv[rows, :]
        dtm[...] = dt + across(STOP * marks[pl.ds(pl.multiple_of(8 + start, 8), block), :], inner)
        dtx[...] = dt * convolved
        turned = sums.T
        b_all, c_all = turned[72:88], turned[88:104]

        def chunk(i, h_now):
            starts[b * lines + i] = h_now
            shift = lax.rem(block - i * STEP, block)
            b_now, c_now = pltpu.roll(b_all, shift, 1), pltpu.roll(c_all, shift, 1)
            for j in range(STEP):
                t = pl.ds(i * STEP + j, 1)
                decay = jnp.exp2(a * dtm[t, :])
                h_now = decay * h_now + b_now[:, j : j + 1] * dtx[t, :]
                p = c_now[:, j : j + 1] * h_now
                parts[j * half : (j + 1) * half, :] = p[:half] + p[half:]
            here = pl.ds(pl.multiple_of(start + i * STEP, STEP), STEP)
            y_out[here, :] = parts[...].reshape(STEP, half, inner).sum(axis=1)
            return h_now

        state = lax.fori_loop(0, lines, chunk, state)
        y = y_out[rows, :] + params[126:127, :] * convolved
        y_out[rows, :] = y
        z = gate_z[rows, :]
        low = (y * z * jax.nn.sigmoid(z)).astype(BF16)
        gated[rows, :] = low
        out = matmul(low[:, :512], whole_all[:, 2 * model : small]) + matmul(low[:, 512:], extra[:, 2 * model : small])
        branch[b] = out.astype(BF16)

        @pl.when(b != h)
        def send():
            branch_copy(b, lax.rem(h - b + 4, 4) - 1).start()

        for n in range(4, 9):
            saved_copy(n, b).start()
        return state

    lax.fori_loop(0, 4, stage_two, jnp.zeros((states, inner), F32))
    for k in range(3):
        branch_copy(0, k).wait_recv()
    mine = pl.ds(pl.multiple_of(h * block, block), block)
    hid = (
        seq[mine, :model].astype(F32) + branch[h].astype(F32) + came[0].astype(F32) + came[1].astype(F32)
        + came[2].astype(F32)
    )
    hidden[...] = hid
    scale = lax.rsqrt(jnp.mean(hid * hid, axis=-1, keepdims=True) + EPS)
    moe_low = (hid * scale * gains[1:2, :]).astype(BF16)
    moe_out[...] = moe_low
    logits = outer_cols(moe_low, gains[...].astype(BF16))
    lane = lax.broadcasted_iota(jnp.int32, logits.shape, 1)
    real = (lane >= 2) & (lane < 2 + experts)
    logits = jnp.where(real, logits, -1e30)
    powers = jnp.exp(logits - jnp.max(logits, axis=-1, keepdims=True))
    shares = powers / jnp.sum(powers, axis=-1, keepdims=True)
    probs[...] = shares
    main, top, low_half, onehot = slot_picks(routes[...], experts)
    gate = jnp.sum(shares * onehot, axis=-1, keepdims=True)
    grad_eo = (gate * cotangent[...].astype(F32)).astype(BF16)
    shape = (experts, MAIN, model)
    slots[:, :, :model] = matmul(main, moe_low).astype(BF16).reshape(shape)
    slots[:, :, model : 2 * model] = matmul(main, grad_eo).astype(BF16).reshape(shape)
    slots[:, :, 2 * model :] = (matmul(top, moe_low) + matmul(low_half, grad_eo)).astype(BF16).reshape(shape)
    for n in range(9):
        for b in range(4):
            saved_copy(n, b).wait()
    for copy in kept_copies:
        copy.wait()
    for b in range(4):
        for k in range(3):
            proj_copy(b, k).wait_send()

        @pl.when(b != h)
        def sent():
            branch_copy(b, 0).wait_send()


def mixer_forward(arrays, inner, states, experts):
    tokens = arrays[13]
    block, model = tokens.shape
    length = 4 * block
    width = 3 * model + 768
    S, V = jax.ShapeDtypeStruct, pltpu.VMEM
    saved = [
        ((length, model), BF16), ((length, inner), BF16), ((length, inner), F32), ((length, inner), F32),
        ((length, 128), F32), ((length, inner), F32), ((length, inner), F32), ((length, inner), BF16),
        ((length // STEP, states, inner), F32),
    ]
    outs = (
        S((512, width), BF16), S((length, model + 128), BF16), S((64, 4096), BF16), *[S(*one) for one in saved],
        S((block, model), F32), S((128, inner), F32), S((MAIN, model), F32), S((experts, MAIN, 3 * model), BF16),
        S((block, model), BF16), S((block, MAIN), F32),
    )
    return pl.pallas_call(
        forward_kernel,
        out_shape=outs,
        in_specs=[IN_VMEM] * len(arrays),
        out_specs=(*[ANY] * 12, *[IN_VMEM] * 6),
        scratch_shapes=[
            V((MAIN, width), BF16), V((MAIN, 128), BF16), V((block, model + 128), BF16), V((32, MAIN, width), BF16),
            V((512, width), BF16),
            V((32, MAIN, 128), BF16), V((4, block, model + 128), BF16), V((length, model + 128), BF16), V((64, 4096), BF16),
            V((3, MAIN, 128), BF16), V((MAIN, 128), BF16),
            DMA((3,)), DMA((3,)), DMA((3,)), DMA((3,)), DMA((3,)), DMA((31,)), DMA((31,)), DMA((31,)), DMA((31,)),
            DMA((3,)), DMA((9, 4)),
            *[V(*one) for one in saved],
            V((length + 8, inner), F32), V((length + 8, 128), F32), V((length, inner), F32), V((block, inner), F32),
            V((block, inner), F32), V((STEP * states // 2, inner), F32), V((4, block, 128), BF16),
            V((3, 4, block, 128), BF16), V((4, block, model), BF16), V((3, block, model), BF16),
            DMA((12,)), DMA((12,)), DMA((4,)), DMA((3,)),
        ],
        compiler_params=pltpu.CompilerParams(
            collective_id=1, has_side_effects=True, vmem_limit_bytes=62 << 20
        ),
        name="mixer_forward",
    )(*arrays)


class Flow:
    ORDER = (2, 1, 3, 0)

    def __init__(self, source, out, pairs, halves, fours, lines, ends, send, recv):
        self.source, self.out, self.pairs, self.halves = source, out, pairs, halves
        self.fours, self.lines, self.ends, self.send, self.recv = fours, lines, ends, send, recv
        e, r, h = places()
        self.c = lax.rem(e, 2)
        y = e // 2
        self.f0 = y * (1 - self.c) + r * self.c
        self.s0 = r * (1 - self.c) + y * self.c
        self.mate_s0 = r * self.c + y * (1 - self.c)
        self.mate, self.first, self.second_peers = mixer_peers()

    def copy(self, src, dst, at, peer):
        return remote(src, dst, self.send.at[at], self.recv.at[at], peer)

    def mate_copy(self, n, f):
        s = lax.rem(self.mate_s0 + self.ORDER[n], 4)
        block = block_at(1 - self.c, f, s)
        return self.copy(self.source.at[block], self.pairs.at[n, f], n * 4 + f, self.mate)

    def second_copy(self, n):
        return self.copy(self.halves.at[n], self.fours.at[n], 16 + n, self.second_peers[self.ORDER[n] - 1])

    def first_copy(self, n):
        return self.copy(self.lines.at[n], self.ends.at[n], 19 + n, self.first[self.ORDER[n] - 1])

    def begin(self):
        for n in range(4):
            for f in range(4):
                self.mate_copy(n, f).start()

    def second(self):
        for n, k in enumerate(self.ORDER):
            s = lax.rem(self.s0 + k, 4)
            for f in range(4):
                self.mate_copy(n, f).wait_recv()
                total = self.source[block_at(self.c, f, s)].astype(F32) + self.pairs[n, f].astype(F32)
                self.halves[n, f] = total.astype(BF16)
            if k:
                self.second_copy(n).start()

    def third(self):
        for n in range(3):
            self.second_copy(n).wait_recv()
        for n, k in enumerate(self.ORDER):
            f = lax.rem(self.f0 + k, 4)
            line = self.halves[3, f].astype(F32)
            for m in range(3):
                line = line + self.fours[m, f].astype(F32)
            if k:
                self.lines[n] = line.astype(BF16)
                self.first_copy(n).start()
            else:
                self.out[...] = line

    def finish(self):
        for n in range(3):
            self.first_copy(n).wait_recv()
        self.out[...] = (
            self.out[...] + self.ends[0].astype(F32) + self.ends[1].astype(F32) + self.ends[2].astype(F32)
        )

    def end(self):
        for n in range(4):
            for f in range(4):
                self.mate_copy(n, f).wait_send()
        for n in range(3):
            self.second_copy(n).wait_send()
            self.first_copy(n).wait_send()


def flow_scratch(width):
    return [
        pltpu.VMEM((32, MAIN, width), BF16), pltpu.VMEM((MAIN, width), F32), pltpu.VMEM((4, 4, MAIN, width), BF16),
        pltpu.VMEM((4, 4, MAIN, width), BF16), pltpu.VMEM((3, 4, MAIN, width), BF16),
        pltpu.VMEM((3, MAIN, width), BF16), pltpu.VMEM((3, MAIN, width), BF16), DMA((22,)), DMA((22,)),
    ]


class RowsRing:
    def __init__(self, source, target, slots, total, send, recv, local):
        self.source, self.target, self.slots, self.total = source, target, slots, total
        self.send, self.recv, self.local = send, recv, local
        self.size = slots.shape[1]
        e, r, h = places()
        self.r = r
        self.right, self.left = lax.rem(r + 1, 4), lax.rem(r + 3, 4)
        self.to_right, self.to_left = (e, self.right, h), (e, self.left, h)

    def peers(self):
        return [self.to_right, self.to_left]

    def rows(self, quarter, part):
        return pl.ds(pl.multiple_of((2 * quarter + part) * self.size, self.size), self.size)

    def copy(self, n):
        across = lax.rem(self.r + 2, 4)
        src, out, slots, total = self.source, self.target, self.slots, self.total
        plan = [
            (src.at[self.rows(across, 0)], slots.at[0], self.to_right),
            (src.at[self.rows(across, 1)], slots.at[1], self.to_left),
            (src.at[self.rows(self.right, 1)], slots.at[7], self.to_right),
            (src.at[self.rows(self.left, 0)], slots.at[8], self.to_left),
            (slots.at[4], slots.at[6], self.to_right),
            (slots.at[5], slots.at[9], self.to_left),
            (total.at[0], out.at[self.rows(self.r, 0)], self.to_right),
            (total.at[1], out.at[self.rows(self.r, 1)], self.to_right),
            (total.at[0], out.at[self.rows(self.r, 0)], self.to_left),
            (total.at[1], out.at[self.rows(self.r, 1)], self.to_left),
            (out.at[self.rows(self.left, 0)], out.at[self.rows(self.left, 0)], self.to_right),
            (out.at[self.rows(self.right, 1)], out.at[self.rows(self.right, 1)], self.to_left),
        ]
        a, b, peer = plan[n]
        return remote(a, b, self.send.at[n], self.recv.at[n], peer)

    def own_copy(self, n):
        src, slots = self.source, self.slots
        plan = [
            (src.at[self.rows(self.right, 0)], slots.at[2]),
            (src.at[self.rows(self.left, 1)], slots.at[3]),
            (src.at[self.rows(self.r, 0)], slots.at[10]),
            (src.at[self.rows(self.r, 1)], slots.at[11]),
            (self.total.at[0], self.target.at[self.rows(self.r, 0)]),
            (self.total.at[1], self.target.at[self.rows(self.r, 1)]),
        ]
        a, b = plan[n]
        return pltpu.make_async_copy(a, b, self.local.at[n])

    def begin(self):
        for n in range(4):
            self.copy(n).start()
        for n in range(4):
            self.own_copy(n).start()

    def pass_on(self):
        slots = self.slots
        for n in (0, 1):
            self.own_copy(n).wait()
            self.copy(n).wait_recv()
            slots[4 + n] = (slots[n].astype(F32) + slots[2 + n].astype(F32)).astype(BF16)
            self.copy(4 + n).start()

    def finish(self):
        slots = self.slots
        for n in (2, 3):
            self.own_copy(n).wait()
        for n in (2, 3, 4, 5):
            self.copy(n).wait_recv()
        for n in (0, 1):
            total = slots[10 + n].astype(F32) + slots[6 + n].astype(F32) + slots[8 + n].astype(F32)
            self.total[n] = total.astype(BF16)
        for n in (6, 9, 7, 8):
            self.copy(n).start()
        for n in (4, 5):
            self.own_copy(n).start()

    def forward(self):
        for n, after in ((6, 10), (9, 11)):
            self.copy(n).wait_recv()
            self.copy(after).start()

    def end(self):
        for n in (7, 8, 10, 11):
            self.copy(n).wait_recv()
        for n in (4, 5):
            self.own_copy(n).wait()
        for n in range(12):
            self.copy(n).wait_send()


def mixer_back_kernel(*refs):
    (
        grad_hidden, seq_all, whole_in, gains, norm_in, normed_in, x_low_in, u_all, gate_all, proj_in, lin_all, y_all,
        gated_in, starts_in, params, extra_in, g_up, g_down,
        grad_tokens, grad_in, grad_out, grad_x, grad_dt, by_channel, by_feature, all_up, all_down,
        seq_own, seq_marks, whole, normed, x_low, u_in, gate_z, proj, dt_lin, y_in, gated, starts, extra, in_sems,
        ghs, gus, marks, gy, dts, dtm, dtx, conv, s1, s2, gdl, ggate, gx, gp_all,
        conv_low, held, decays, parts_1, parts_2, lanes_b, lanes_c, state, g_rate, rows_sum, own, landing, branch, came,
        a_send, a_recv, p_send, p_recv, b_send, b_recv, ring_up, ring_down, total_up, total_down, x_send, x_recv, x_local, own_tile, tiles, z_send, z_recv, *flow_refs, gain_sum,
    ) = refs
    e, r, h = places()
    block, model = grad_hidden.shape
    inner, states = u_in.shape[1], starts.shape[1]
    lines, half, small = block // STEP, states // 2, 3 * model
    owners = 32
    mine = pl.ds(pl.multiple_of(h * block, block), block)
    loads = [
        (lin_all, dt_lin), (u_all, u_in), (gate_all, gate_z), (y_all, y_in), (seq_all.at[:, model:], seq_marks),
        (proj_in, proj), (starts_in, starts), (whole_in, whole), (extra_in, extra), (x_low_in, x_low),
        (gated_in, gated), (normed_in, normed), (seq_all.at[mine, :model], seq_own),
    ]
    loads = [pltpu.make_async_copy(a, b, in_sems.at[n]) for n, (a, b) in enumerate(loads)]
    for copy in loads:
        copy.start()
    z_peers = hid_peers()
    mate, first, second = mixer_peers()
    rings = [
        RowsRing(g_up, all_up, ring_up, total_up, x_send.at[0], x_recv.at[0], x_local.at[0]),
        RowsRing(g_down, all_down, ring_down, total_down, x_send.at[1], x_recv.at[1], x_local.at[1]),
    ]
    ghs[h] = grad_hidden[...].astype(BF16)
    greet([mate] + first + second + z_peers)
    gh_copies = [remote(ghs.at[h], ghs.at[h], a_send.at[k], a_recv.at[k], z_peers[k]) for k in range(3)]
    for k in (1, 0, 2):
        gh_copies[k].start()
    for ring in rings:
        ring.begin()
    flow_early, flow_in, flow_rest = [Flow(*flow_refs[9 * n : 9 * n + 9]) for n in range(3)]
    state[...] = jnp.zeros_like(state)
    g_rate[...] = jnp.zeros_like(g_rate)
    rows_sum[...] = jnp.zeros_like(rows_sum)
    gain_sum[...] = jnp.zeros_like(gain_sum)
    gus[512:520] = jnp.zeros((8, inner), F32)
    a = jnp.exp(params[104:120, :]) * (-LOG2E)
    for copy in loads[:5]:
        copy.wait()
    marks[0:512] = seq_marks[...].astype(F32)
    marks[512:520] = jnp.zeros((8, 128), F32)

    def prepare(b, carry):
        rows = pl.ds(pl.multiple_of(b * block, block), block)
        lin = dt_lin[rows, :]
        dt = jax.nn.softplus(lin)
        dt_lin[rows, :] = jax.nn.sigmoid(lin)
        u_now = u_in[rows, :]
        convolved = u_now * jax.nn.sigmoid(u_now)
        conv[rows, :] = convolved
        conv_low[rows, :] = convolved.astype(BF16)
        dts[rows, :] = dt
        dtm[rows, :] = dt + across(STOP * marks[rows, :], inner)
        dtx[rows, :] = dt * convolved
        z = gate_z[rows, :]
        sig = jax.nn.sigmoid(z)
        gate_z[rows, :] = z * sig
        y_in[rows, :] = y_in[rows, :] * (sig * (1.0 + z * (1.0 - sig)))
        return carry

    lax.fori_loop(0, 4, prepare, 0)
    for copy in loads[5:]:
        copy.wait()

    def spots(shape, axis):
        return lax.broadcasted_iota(jnp.int32, shape, axis)

    picks = (spots((STEP, STEP * half), 1) // half == spots((STEP, STEP * half), 0)).astype(BF16)
    tall = (block * states, 128)
    ones = jnp.ones((128, 128), BF16)

    def gh_wait(b):
        at = lax.rem(h - b + 4, 4) - 1
        remote(ghs.at[h], ghs.at[h], a_send.at[at], a_recv.at[at], z_peers[0]).wait_recv()

    def proj_copy(b, k):
        at = k * 4 + b
        return remote(own.at[b], landing.at[k, b], p_send.at[at], p_recv.at[at], z_peers[k])

    def branch_copy(b, sender):
        return remote(branch.at[b], came.at[sender], b_send.at[b], b_recv.at[sender], (e, r, b))

    def stage_a(b):
        start = pl.multiple_of(b * block, block)
        rows = pl.ds(start, block)
        turned = proj[rows, :].T
        b_all, c_all = turned[72:88], turned[88:104]

        @pl.when(b != h)
        def arrived():
            gh_wait(b)

        gg = both_cols(ghs[b], whole[:, 2 * model : small], extra[:, 2 * model : small])
        gy_now = gg * gate_z[rows, :]
        gy[...] = gy_now
        ggate[rows, :] = (gg * y_in[rows, :]).astype(BF16)

        def chunk(step, u):
            i = lines - 1 - step
            hh = starts[b * lines + i]
            held[0] = hh
            shift = lax.rem(block - i * STEP, block)
            b_now, c_now = pltpu.roll(b_all, shift, 1), pltpu.roll(c_all, shift, 1)
            for j in range(STEP):
                t = pl.ds(start + i * STEP + j, 1)
                decay = jnp.exp2(a * dtm[t, :])
                hh = decay * hh + b_now[:, j : j + 1] * dtx[t, :]
                decays[j] = decay
                held[j + 1] = hh
            for j in range(STEP - 1, -1, -1):
                t = pl.ds(start + i * STEP + j, 1)
                gy_row = gy[pl.ds(i * STEP + j, 1), :]
                g = c_now[:, j : j + 1] * gy_row + u
                u = decays[j] * g
                q = u * held[j]
                g_rate[...] += q * dts[t, :]
                w = q * a
                parts_2[j * half : (j + 1) * half, :] = w[:half] + w[half:]
                w = g * b_now[:, j : j + 1]
                parts_1[j * half : (j + 1) * half, :] = w[:half] + w[half:]
                at = pl.ds(pl.multiple_of((i * STEP + j) * states, states), states)
                lanes_b[at, :] = over_lanes(g * dtx[t, :]).astype(BF16)
                lanes_c[at, :] = over_lanes(held[j + 1] * gy_row).astype(BF16)
            here = pl.ds(pl.multiple_of(i * STEP, STEP), STEP)
            s1[here, :] = matmul(picks, parts_1[...].astype(BF16))
            s2[here, :] = matmul(picks, parts_2[...].astype(BF16))
            return u

        state[...] = lax.fori_loop(0, lines, chunk, state[...])
        convolved = conv[rows, :]
        grad_lin = dt_lin[rows, :] * (convolved * s1[...] + s2[...] * (1.0 / LOG2E))
        low = grad_lin.astype(BF16)
        gdl[rows, :] = low
        rows_sum[5:6, :] += jnp.sum(grad_lin, axis=0, keepdims=True)
        rows_sum[6:7, :] += jnp.sum(gy_now * convolved, axis=0, keepdims=True)
        dts[rows, :] = params[126:127, :] * gy_now + dts[rows, :] * s1[...]
        at_state = spots(tall, 0) % states
        spread = jnp.where(spots(tall, 1) - 72 == at_state, matmul(lanes_b[...], ones), 0.0) + jnp.where(
            spots(tall, 1) - 88 == at_state, matmul(lanes_c[...], ones), 0.0
        )
        share = spread.reshape(block, states, 128).sum(axis=1)
        share = share + matmul(low[:, :512], whole[:, small + 128 : small + 256])
        share = share + matmul(low[:, 512:], extra[:, small + 128 : small + 256])
        own[b] = share.astype(BF16)
        for k in (1, 0, 2):
            proj_copy(b, k).start()

    def stage_b(b):
        start = pl.multiple_of(b * block, block)
        rows = pl.ds(start, block)
        for k in range(3):
            proj_copy(b, k).wait_recv()
        gp = (
            own[b].astype(F32) + landing[0, b].astype(F32) + landing[1, b].astype(F32) + landing[2, b].astype(F32)
        ).astype(BF16)
        gp_all[rows, :] = gp
        u_now = u_in[rows, :]
        sig = jax.nn.sigmoid(u_now)
        gu = dts[rows, :] + both_cols(gp, whole[:, small : small + 128], extra[:, small : small + 128])
        gu = gu * (sig * (1.0 + u_now * (1.0 - sig)))
        gus[rows, :] = gu
        lines_g, lines_m = gus[pl.ds(start, block + 8), :], marks[pl.ds(start, block + 8), :]
        x = x_low[rows, :].astype(F32)
        total = params[123:124, :] * gu
        rows_sum[3:4, :] += jnp.sum(gu * x, axis=0, keepdims=True)
        rows_sum[4:5, :] += jnp.sum(gu, axis=0, keepdims=True)
        mask = jnp.ones((block, 128), F32)
        for ahead in (1, 2, 3):
            mask = mask * (1.0 - lines_m[ahead : ahead + block])
            moved = lines_g[ahead : ahead + block] * across(mask, inner)
            total = total + params[123 - ahead : 124 - ahead, :] * moved
            rows_sum[3 - ahead : 4 - ahead, :] += jnp.sum(moved * x, axis=0, keepdims=True)
        low = total.astype(BF16)
        gx[rows, :] = low
        gate = ggate[rows, :]
        out = (
            matmul(low[:, :512], whole[:, :model])
            + matmul(low[:, 512:], extra[:, :model])
            + matmul(gate[:, :512], whole[:, model : 2 * model])
            + matmul(gate[:, 512:], extra[:, model : 2 * model])
        )
        branch[b] = out.astype(BF16)

        @pl.when(b != h)
        def send():
            branch_copy(b, lax.rem(h - b + 4, 4) - 1).start()

        gain_sum[...] += jnp.sum(out * normed[rows, :].astype(F32), axis=0, keepdims=True)

    def step(n, carry):
        stage_a(3 - n)

        @pl.when(n > 0)
        def later():
            stage_b(4 - n)

        @pl.when(n == 0)
        def pass_on():
            for ring in rings:
                ring.pass_on()

        @pl.when(n == 1)
        def finish():
            for ring in rings:
                ring.finish()

        return carry

    lax.fori_loop(0, 4, step, 0)

    extras = []

    def weight(left, right, target, at, size):
        main = inner_rows(left[:, :512], right)
        target[:, :, at : at + size] = main.astype(BF16).reshape(owners, MAIN, size)
        extras.append(inner_rows(left[:, 512:], right).astype(BF16))

    for ring in rings:
        ring.forward()
    low_norm = normed[...]
    weight(gated[...], ghs[...].reshape(4 * block, model), flow_early.source, 0, model)
    weight(ggate[...], low_norm, flow_early.source, model, model)
    flow_early.begin()
    stage_b(0)
    flow_early.second()
    weight(gx[...], low_norm, flow_in.source, 0, model)
    flow_in.begin()
    weight(gdl[...], proj[...].astype(BF16), flow_rest.source, 128, 128)
    ends = jnp.concatenate(
        [jnp.zeros((104, inner), F32), g_rate[...] * (a * (1.0 / LOG2E)), rows_sum[...]], axis=0
    ).astype(BF16)
    low_conv, low_gp, unit = conv_low[...], gp_all[...], eye(128)
    main = inner_rows(low_conv[:, :512], low_gp) + inner_rows(ends[:, :512], unit)
    flow_rest.source[:, :, :128] = main.astype(BF16).reshape(owners, MAIN, 128)
    last = (inner_rows(low_conv[:, 512:], low_gp) + inner_rows(ends[:, 512:], unit)).astype(BF16)
    lines_e = jnp.concatenate(
        [extras[2], extras[1], extras[0], last, extras[3], jnp.zeros((64, 4096 - small - 256), BF16)], axis=1
    )
    stacked = jnp.concatenate([lines_e[:, k * 512 : (k + 1) * 512] for k in range(8)], axis=0)
    row, col = spots((512, 512), 0), spots((512, 512), 1)
    wanted = (col % 64 // 2) * MAIN + (col % 2) * 8 + col // 64
    flow_rest.source[:, :, 256:768] = (
        matmul((wanted == row).astype(BF16), stacked).astype(BF16).reshape(owners, MAIN, 512)
    )
    span = model // owners
    tile = norm_in[...] + jnp.where(spots(norm_in.shape, 0) == 0, gain_sum[...] / gains[0:1, :], 0.0)
    for n in range(owners):
        piece = tile[:, n * span : (n + 1) * span]
        piece = jnp.concatenate([piece, jnp.zeros((MAIN, 128 - span), F32)], axis=1)
        flow_rest.source[n, :, 768:] = piece.astype(BF16)
    flow_rest.begin()
    flow_in.second()
    flow_rest.second()
    flow_early.third()
    for ring in rings:
        ring.end()
    flow_in.third()
    flow_rest.third()
    for k in range(3):
        branch_copy(0, k).wait_recv()
    grad_n = branch[h].astype(F32) + came[0].astype(F32) + came[1].astype(F32) + came[2].astype(F32)
    values = seq_own[...].astype(F32)
    scale = lax.rsqrt(jnp.mean(values * values, axis=-1, keepdims=True) + EPS)
    scaled = grad_n * gains[0:1, :]
    inside = jnp.mean(scaled * values, axis=-1, keepdims=True)
    grad_tokens[...] = grad_hidden[...] + scale * scaled - values * (scale * scale * scale * inside)
    flow_rest.finish()
    rest = flow_rest.out[...]
    own_tile[...] = rest[:, 768:].astype(BF16)
    z_copies = [remote(own_tile, tiles.at[k], z_send.at[k], z_recv.at[k], z_peers[k]) for k in range(3)]
    for copy in z_copies:
        copy.start()
    flow_early.finish()
    flow_in.finish()
    rank, wide = grad_dt.shape[1], grad_x.shape[1]
    extra_rows = [
        jnp.concatenate([rest[n * 8 + k : n * 8 + k + 1, 256:768] for k in range(8)], axis=1) for n in range(2)
    ]

    def full(main, at, size):
        return jnp.concatenate([main, *[line[:, at : at + size] for line in extra_rows]], axis=0)

    grad_in[:, 0, :] = full(flow_in.out[...], 0, model)
    grad_in[:, 1, :] = full(flow_early.out[:, model:], model, model)
    grad_out[...] = full(flow_early.out[:, :model], 2 * model, model)
    small_sum = full(rest[:, :256], small, 256)
    grad_x[...] = small_sum[:, :wide]
    grad_dt[...] = small_sum[:, 128 : 128 + rank]
    channels = jnp.concatenate([small_sum[:, :128], jnp.zeros((110, 128), F32)], axis=0)
    by_channel[...] = channels.T[104:128, : grad_out.shape[0]]
    for copy in z_copies:
        copy.wait_recv()
    tile = rest[:, 768:] + tiles[0].astype(F32) + tiles[1].astype(F32) + tiles[2].astype(F32)
    share = by_feature.shape[1]
    by_feature[...] = pltpu.roll(tile, lax.rem(128 - h * share, 128), 1)[:, :share]
    for flow in (flow_early, flow_in, flow_rest):
        flow.end()
    for copy in gh_copies + z_copies:
        copy.wait_send()
    for b in range(4):
        for k in range(3):
            proj_copy(b, k).wait_send()

        @pl.when(b != h)
        def sent():
            branch_copy(b, 0).wait_send()


def mixer_backward(grad_hidden, seq, whole, gains, norm_in, saved, g_up, g_down, own, wide, rank):
    normed, x_low, u, gate_z, proj, dt_lin, y, gated, starts, params, extra = saved
    block, model = grad_hidden.shape
    tokens, inner = u.shape
    states = starts.shape[1]
    S = jax.ShapeDtypeStruct

    def like(array):
        return pltpu.VMEM(array.shape, array.dtype)

    line, low = pltpu.VMEM((block, inner), F32), pltpu.VMEM((tokens, inner), BF16)
    tall = pltpu.VMEM((tokens, inner), F32)
    eighths = [(g.shape[0] // 8, g.shape[1]) for g in (g_up, g_down)]
    return pl.pallas_call(
        mixer_back_kernel,
        out_shape=(
            S((block, model), F32), S((own, 2, model), F32), S((own, model), F32), S((own, wide), F32),
            S((own, rank), F32), S((24, own), F32), S((MAIN, model // 128), F32), S(g_up.shape, BF16),
            S(g_down.shape, BF16),
        ),
        in_specs=[IN_VMEM, ANY, ANY, IN_VMEM, IN_VMEM, *[ANY] * 9, IN_VMEM, ANY, ANY, ANY],
        out_specs=(*[IN_VMEM] * 7, ANY, ANY),
        scratch_shapes=[
            pltpu.VMEM((block, model), BF16), pltpu.VMEM((tokens, 128), BF16), like(whole), like(normed), like(x_low),
            like(u), like(gate_z), like(proj), like(dt_lin), like(y), like(gated), like(starts), like(extra),
            DMA((13,)),
            pltpu.VMEM((4, block, model), BF16),
            pltpu.VMEM((tokens + 8, inner), F32),
            pltpu.VMEM((tokens + 8, 128), F32),
            line, tall, tall, tall, tall, line, line,
            low, low, low,
            pltpu.VMEM((tokens, 128), BF16),
            low,
            pltpu.VMEM((STEP + 1, states, inner), F32),
            pltpu.VMEM((STEP, states, inner), F32),
            pltpu.VMEM((STEP * states // 2, inner), F32),
            pltpu.VMEM((STEP * states // 2, inner), F32),
            pltpu.VMEM((block * states, 128), BF16),
            pltpu.VMEM((block * states, 128), BF16),
            pltpu.VMEM((states, inner), F32),
            pltpu.VMEM((states, inner), F32),
            pltpu.VMEM((8, inner), F32),
            pltpu.VMEM((4, block, 128), BF16),
            pltpu.VMEM((3, 4, block, 128), BF16),
            pltpu.VMEM((4, block, model), BF16),
            pltpu.VMEM((3, block, model), BF16),
            DMA((3,)), DMA((3,)), DMA((12,)), DMA((12,)), DMA((4,)), DMA((3,)),
            *[pltpu.VMEM((12, *size), BF16) for size in eighths],
            *[pltpu.VMEM((2, *size), BF16) for size in eighths],
            DMA((2, 12)), DMA((2, 12)), DMA((2, 6)),
            pltpu.VMEM((MAIN, 128), BF16), pltpu.VMEM((3, MAIN, 128), BF16), DMA((3,)), DMA((3,)),
            *flow_scratch(2 * model), *flow_scratch(model), *flow_scratch(896),
            pltpu.VMEM((1, model), F32),
        ],
        compiler_params=pltpu.CompilerParams(
            collective_id=5, has_side_effects=True, vmem_limit_bytes=62 << 20
        ),
        name="mixer_backward",
    )(
        grad_hidden, seq, whole, gains, norm_in, normed, x_low, u, gate_z, proj, dt_lin, y, gated, starts, params, extra,
        g_up, g_down,
    )


def finish_kernel(
    channel, feature, result_in, tokens_in, in_in, out_in, x_in, dt_in, up_in, down_in,
    result, tokens, grad_in, grad_out, grad_x, grad_dt, decay, taps, conv_bias, dt_bias, skip, gain_one, gain_two, router, up,
    down, low_up, low_down, high_up, high_down, sems,
):
    loads = []
    for n, (a, b) in enumerate(((up_in, low_up), (down_in, low_down))):
        size = a.shape[0] // 4
        loads.append([])
        for q in range(4):
            rows = pl.ds(q * size, size)
            copy = pltpu.make_async_copy(a.at[rows, :], b.at[rows, :], sems.at[n, q])
            copy.start()
            loads[n].append(copy)
    stores = []
    straight = ((result_in, result), (tokens_in, tokens), (in_in, grad_in), (out_in, grad_out), (x_in, grad_x), (dt_in, grad_dt))
    for a, b in straight:
        b[...] = a[...]
    lines = channel[...]
    decay[...] = lines[0:16]
    taps[...] = lines[16:20]
    conv_bias[...] = lines[20:21]
    dt_bias[...] = lines[21:22]
    skip[...] = lines[22:23]
    lines = feature[...]
    gain_one[...] = lines[0:1]
    gain_two[...] = lines[1:2]
    router[...] = lines[2:10]
    for q in range(4):
        for n, (a, b, c) in enumerate(((low_up, high_up, up), (low_down, high_down, down))):
            size = a.shape[0] // 4
            rows = pl.ds(q * size, size)
            loads[n][q].wait()
            b[rows, :] = a[rows, :].astype(F32)
            copy = pltpu.make_async_copy(b.at[rows, :], c.at[rows, :], sems.at[2 + n, q])
            copy.start()
            stores.append(copy)
    for copy in stores:
        copy.wait()


def finished(output, tokens, grad_in, grad_out, grad_x, grad_dt, channel, feature, low_up, low_down):
    S, own, share = jax.ShapeDtypeStruct, channel.shape[1], feature.shape[1]
    straight = (output, tokens, grad_in, grad_out, grad_x, grad_dt)
    outs = [S(a.shape, a.dtype) for a in straight]
    outs += [S((n, own), F32) for n in (16, 4, 1, 1, 1)] + [S((n, share), F32) for n in (1, 1, 8)]
    outs += [S(low_up.shape, F32), S(low_down.shape, F32)]
    return pl.pallas_call(
        finish_kernel,
        out_shape=outs,
        in_specs=[IN_VMEM] * 8 + [ANY] * 2,
        out_specs=[IN_VMEM] * 14 + [ANY] * 2,
        scratch_shapes=[
            pltpu.VMEM(low_up.shape, BF16), pltpu.VMEM(low_down.shape, BF16), pltpu.VMEM(low_up.shape, F32),
            pltpu.VMEM(low_down.shape, F32), DMA((4, 4)),
        ],
        compiler_params=pltpu.CompilerParams(vmem_limit_bytes=62 << 20),
        name="finish",
    )(channel, feature, *straight, low_up, low_down)


def shards(
    tokens, resets, routes, cotangent, mixer_gain, in_proj, conv_kernel, conv_bias, x_proj, dt_proj,
    dt_bias, log_decay, skip_gain, out_proj, moe_gain, router, up_proj, down_proj,
):
    model, own, experts = tokens.shape[1], conv_bias.shape[0], router.shape[1]
    rank, states = dt_proj.shape[0], log_decay.shape[0]
    inner = lax.axis_size("expert") * lax.axis_size("rows") * own
    in_lines = in_proj.transpose(2, 1, 0)
    route_row = routes.reshape(1, -1)
    arrays = (
        in_lines[:, 0], in_lines[:, 1], out_proj, x_proj.T, dt_proj.T, log_decay, conv_kernel, conv_bias[None],
        dt_bias[None], skip_gain[None], mixer_gain[None], moe_gain[None], router.T, tokens, resets[None], route_row,
        cotangent,
    )
    whole, sequence, extra, *saved, hidden_one, params, gains, slots, moe_low, probs = mixer_forward(
        arrays, inner, states, experts
    )
    output, grad_hidden, norm_grads, grad_up, grad_down = experts_both_ways(
        slots, up_proj[0], down_proj[0], hidden_one, cotangent, moe_low, probs, route_row, gains
    )
    results = mixer_backward(
        grad_hidden, sequence, whole, gains, norm_grads, (*saved, params, extra), grad_up, grad_down, own,
        rank + 2 * states, rank,
    )
    (
        output, grad_tokens, grad_in, grad_out, grad_x, grad_dt, grad_decay, grad_taps, grad_conv_bias, grad_dt_bias,
        grad_skip, grad_gain_one, grad_gain_two, grad_router, grad_up_sum, grad_down_sum,
    ) = finished(output, *results)
    return (
        output,
        grad_tokens,
        grad_gain_one[0],
        grad_in.transpose(2, 1, 0),
        grad_taps,
        grad_conv_bias[0],
        grad_x.T,
        grad_dt.T,
        grad_dt_bias[0],
        grad_decay,
        grad_skip[0],
        grad_out,
        grad_gain_two[0],
        grad_router.T,
        grad_up_sum[None],
        grad_down_sum[None],
    )


def solution(mesh):
    every = ("expert", "rows", "hid")
    in_specs = (
        P(every, None), P(every), P(every, None), P(every, None), P(every), P(None, None, every),
        P(None, every), P(every), P(None, every), P(None, every), P(every), P(None, every), P(every),
        P(every, None), P(every), P(every, None), P("expert", None, "hid"), P("expert", "hid", None),
    )
    out_specs = (
        P(every, None), P(every, None), P(every), P(None, None, every), P(None, every), P(every),
        P(None, every), P(None, every), P(every), P(None, every), P(every), P(every, None), P(every),
        P(every, None), P("expert", None, "hid"), P("expert", "hid", None),
    )
    return jax.shard_map(shards, mesh=mesh, in_specs=in_specs, out_specs=out_specs, check_vma=False)
```

```python
from functools import partial

import jax
import jax.numpy as jnp
from jax import lax
from jax.experimental import pallas as pl
from jax.experimental.pallas import tpu as pltpu
from jax.sharding import PartitionSpec as P

EPS = 1e-05
LOG2E = 1.4426950408889634
STOP = 1e6
STEP = 16
MAIN = 16
EXTRA = 512
GELU_C = 0.7978845608028654
F32 = jnp.float32
BF16 = jnp.bfloat16


def matmul(first_op, second_op):
    return jnp.dot(first_op, second_op, preferred_element_type=F32)


def inner_rows(first_op, second_op):
    return lax.dot_general(
        first_op, second_op, (((0,), (0,)), ((), ())), preferred_element_type=F32
    )


def outer_cols(first_op, second_op):
    return lax.dot_general(
        first_op, second_op, (((1,), (1,)), ((), ())), preferred_element_type=F32
    )


def rms_norm(values, gain):
    return values * lax.rsqrt(jnp.mean(values * values, axis=-1, keepdims=True) + EPS) * gain


def over_lanes(v):
    whole = v.shape[1] // 128
    total = v[:, :128]
    for k in range(1, whole):
        total = total + v[:, k * 128 : (k + 1) * 128]
    rest = v.shape[1] - whole * 128
    if rest:
        blank = jnp.zeros((v.shape[0], 128 - rest), F32)
        total = total + jnp.concatenate([v[:, whole * 128 :], blank], axis=1)
    return total


MESH = pl.DeviceIdType.MESH
ANY = pl.BlockSpec(memory_space=pl.ANY)
IN_VMEM = pl.BlockSpec(memory_space=pltpu.VMEM)
DMA = pltpu.SemaphoreType.DMA


def put_rows(parts, j, values):
    count, width = values.shape
    for k in range(parts.shape[0]):
        size = min(128, width - 128 * k)
        parts[k, j * count : (j + 1) * count, :size] = values[:, 128 * k : 128 * k + size]


def summed_groups(parts, count, width):
    groups = parts.shape[1] // count
    columns = []
    for k in range(parts.shape[0]):
        total = parts[k, pl.ds(0, groups, stride=count), :]
        for n in range(1, count):
            total = total + parts[k, pl.ds(n, groups, stride=count), :]
        columns.append(total[:, : min(128, width - 128 * k)])
    return jnp.concatenate(columns, axis=1)


def places():
    return lax.axis_index("expert"), lax.axis_index("rows"), lax.axis_index("hid")


def greet(peers):
    barrier = pltpu.get_barrier_semaphore()
    for peer in peers:
        pl.semaphore_signal(barrier, inc=1, device_id=peer, device_id_type=MESH)
    pl.semaphore_wait(barrier, len(peers))


def remote(src, dst, send_sem, recv_sem, peer):
    return pltpu.make_async_remote_copy(
        src_ref=src, dst_ref=dst, send_sem=send_sem, recv_sem=recv_sem, device_id=peer,
        device_id_type=MESH,
    )


def hid_peers():
    e, r, h = places()
    return [(e, r, lax.rem(h + k, 4)) for k in (1, 2, 3)]


def mixer_peers(turn=None):
    e, r, h = places()
    c = lax.rem(e, 2)
    t = c if turn is None else turn
    mate = (e + 1 - 2 * c, r, h)
    first = [(lax.rem(e + 2 * k * (1 - t), 8), lax.rem(r + k * t, 4), h) for k in (1, 2, 3)]
    second = [(lax.rem(e + 2 * k * t, 8), lax.rem(r + k * (1 - t), 4), h) for k in (1, 2, 3)]
    return mate, first, second


def block_at(c, f, s, turn=None):
    t = c if turn is None else turn
    y = f * (1 - t) + s * t
    x = s * (1 - t) + f * t
    return (2 * y + c) * 4 + x


class RowsPlace:
    def __init__(self, size):
        e, r, h = places()
        self.r, self.size = r, size
        self.right, self.left, self.across = lax.rem(r + 1, 4), lax.rem(r + 3, 4), lax.rem(r + 2, 4)
        self.to_right, self.to_left = (e, self.right, h), (e, self.left, h)

    def rows(self, quarter, part, parts=1):
        return pl.ds(pl.multiple_of((2 * quarter + part) * self.size, self.size), parts * self.size)


class RowsSpread(RowsPlace):
    def __init__(self, source, slots, send, recv):
        super().__init__(slots.shape[1])
        self.source, self.slots, self.send, self.recv = source, slots, send, recv

    def copy(self, n):
        plan = (
            (self.across, 0, 0, self.to_right),
            (self.across, 1, 1, self.to_left),
            (self.right, 1, 2, self.to_right),
            (self.left, 0, 3, self.to_left),
        )
        quarter, half, at, peer = plan[n]
        part = self.source.at[self.rows(quarter, half)]
        return remote(part, self.slots.at[at], self.send.at[n], self.recv.at[n], peer)

    def begin(self):
        for n in range(4):
            self.copy(n).start()

    def end(self):
        for n in range(4):
            self.copy(n).wait_recv()
            self.copy(n).wait_send()


class RowsSum(RowsPlace):
    def __init__(self, source, came, slots, own, sums, total, send, recv, local):
        super().__init__(sums.shape[1])
        self.source, self.came, self.slots, self.own, self.sums, self.total = source, came, slots, own, sums, total
        self.send, self.recv, self.local = send, recv, local

    def load(self, n):
        if n == 4:
            return pltpu.make_async_copy(self.came, self.slots, self.local.at[4])
        quarter, half = ((self.right, 0), (self.left, 1), (self.r, 0), (self.r, 1))[n]
        return pltpu.make_async_copy(self.source.at[self.rows(quarter, half)], self.own.at[n], self.local.at[n])

    def copy(self, n):
        return remote(
            self.sums.at[n], self.sums.at[2 + n], self.send.at[n], self.recv.at[n], (self.to_right, self.to_left)[n]
        )

    def pass_on(self):
        for n in (4, 0, 1):
            self.load(n).wait()
        for n in (0, 1):
            self.sums[n] = (self.slots[n].astype(F32) + self.own[n].astype(F32)).astype(BF16)
            self.copy(n).start()

    def finish(self):
        for n in (2, 3):
            self.load(n).wait()
        for n in (0, 1):
            self.copy(n).wait_recv()
            total = (
                self.own[2 + n].astype(F32) + self.slots[3 - n].astype(F32) + self.sums[2 + n].astype(F32)
            )
            self.total[n * self.size : (n + 1) * self.size, :] = total.astype(BF16)

    def end(self):
        for n in (0, 1):
            self.copy(n).wait_send()


class RowsGather(RowsPlace):
    def __init__(self, quarter, target, send, recv, local):
        super().__init__(quarter.shape[0] // 2)
        self.quarter, self.target, self.send, self.recv, self.local = quarter, target, send, recv, local

    def copy(self, n):
        out = self.target
        plan = (
            (lambda: self.quarter, self.rows(self.r, 0, 2), self.to_right),
            (lambda: self.quarter, self.rows(self.r, 0, 2), self.to_left),
            (lambda: out.at[self.rows(self.left, 0)], self.rows(self.left, 0), self.to_right),
            (lambda: out.at[self.rows(self.right, 1)], self.rows(self.right, 1), self.to_left),
        )
        part, rows, peer = plan[n]
        return remote(part(), out.at[rows], self.send.at[n], self.recv.at[n], peer)

    def own(self):
        return pltpu.make_async_copy(self.quarter, self.target.at[self.rows(self.r, 0, 2)], self.local)

    def begin(self):
        for n in (0, 1):
            self.copy(n).start()
        self.own().start()

    def forward(self):
        for n in (0, 1):
            self.copy(n).wait_recv()
            self.copy(2 + n).start()

    def end(self):
        for n in (2, 3):
            self.copy(n).wait_recv()
        self.own().wait()
        for n in range(4):
            self.copy(n).wait_send()


def gelu_pair(pre, grad):
    square = pre * pre
    t = jnp.tanh(GELU_C * pre * (1.0 + 0.044715 * square))
    up = 0.5 * (1.0 + t)
    slope = up + 0.5 * pre * (1.0 - t * t) * (GELU_C * (1.0 + 3 * 0.044715 * square))
    return pre * up, slope * grad


def expert_kernel(
    slots, up, down, hid_in, cotangent, moe_low, probs, routes, gains, output, grad_hidden, norm_out, g_up, g_down, ring_up, ring_down, x_send, x_recv, back, held, results, hid_out, pre_out, hid_w, pre_w, from_left, from_right,
    half_left, half_right, sums, d_send, d_recv, r_send, r_recv, l_send, l_recv, f_send, f_recv, c_send, c_recv,
    k_send, k_recv, h_send, h_recv, b_send, b_recv,
):
    e, r, h = places()
    model, hidden = up.shape
    right, left, across = lax.rem(h + 1, 4), lax.rem(h + 3, 4), lax.rem(h + 2, 4)
    to_right, to_left = (e, r, right), (e, r, left)
    y, c = e // 2, lax.rem(e, 2)
    target = [2 * lax.rem(y + k // 2, 4) + lax.rem(c + k, 2) for k in range(8)]
    source = [2 * lax.rem(y + 4 - k // 2, 4) + lax.rem(c + k, 2) for k in range(8)]
    to_expert = [(one, r, h) for one in target]
    to_source = [(one, r, h) for one in source]
    via_right, via_left = (4, 3, 2, 0), (5, 7, 6, 1)
    sums_up = RowsSpread(g_up, ring_up, x_send.at[0], x_recv.at[0])
    sums_down = RowsSpread(g_down, ring_down, x_send.at[1], x_recv.at[1])
    greet(to_expert[1:] + [to_right, to_left, sums_up.to_right, sums_up.to_left])

    held[h, e] = slots[e]
    d_copies = [None] * 8
    for n in (1, 2, 6, 3, 7, 4, 5):
        d_copies[n] = remote(slots.at[target[n]], held.at[h, e], d_send.at[n], d_recv.at[n], to_expert[n])
        d_copies[n].start()

    def along(buf, where, k, send, recv, peer):
        block = buf.at[where, source[k]]
        copy = remote(block, block, send.at[k], recv.at[k], peer)
        copy.start()
        return copy

    r_copies, l_copies = [None] * 8, [None] * 8
    for n in (0, 1, 2, 6, 3, 7, 4, 5):
        if n:
            d_copies[n].wait_recv()
        r_copies[n] = along(held, h, n, r_send, r_recv, to_right)
        l_copies[n] = along(held, h, n, l_send, l_recv, to_left)

    half = 128

    def worked(where):
        lines = held[where]
        main_x = lines[:, :, :model].reshape(half, model)
        main_g = lines[:, :, model : 2 * model].reshape(half, model)
        extra = lines[:, :, 2 * model :].reshape(half, model)
        rows_x = jnp.concatenate([main_x, extra], axis=0)
        rows_g = jnp.concatenate([main_g, extra], axis=0)

        def first_layer(i, carry):
            cols = pl.ds(pl.multiple_of(i * 256, 256), 256)
            pre = matmul(rows_x, up[:, cols])
            grad = outer_cols(rows_g, down[cols, :])
            hid_m, pre_m = gelu_pair(pre[:half], grad[:half])
            pre_e = pre[half:].reshape(8, 2, 8, 256)[:, 0]
            grad_e = grad[half:].reshape(8, 2, 8, 256)[:, 1]
            hid_e, gpre_e = gelu_pair(pre_e, grad_e)
            none = jnp.zeros_like(hid_e)

            def stacked(a, b):
                return jnp.stack([a, b], axis=1).reshape(half, 256).astype(BF16)

            hid_m, pre_m = hid_m.astype(BF16), pre_m.astype(BF16)
            hid_out[:half, cols] = hid_m
            pre_out[:half, cols] = pre_m
            hid_w[where, :half, cols] = hid_m
            pre_w[where, :half, cols] = pre_m
            hid_out[half:, cols] = stacked(hid_e, none)
            pre_out[half:, cols] = stacked(none, gpre_e)
            hid_w[where, half:, cols] = stacked(none, hid_e)
            pre_w[where, half:, cols] = stacked(gpre_e, none)
            return carry

        lax.fori_loop(0, hidden // 256, first_layer, 0)

        def second_layer(i, carry):
            at = pl.multiple_of(i * 384, 384)
            cols = pl.ds(at, 384)
            share = matmul(hid_out[...], down[:, cols])
            grad = outer_cols(pre_out[...], up[cols, :])
            shape = (8, 16, 384)
            results[where, :, :, cols] = share[:half].astype(BF16).reshape(shape)
            results[where, :, :, pl.ds(model + at, 384)] = grad[:half].astype(BF16).reshape(shape)
            results[where, :, :, pl.ds(2 * model + at, 384)] = (share[half:] + grad[half:]).astype(BF16).reshape(shape)
            return carry

        lax.fori_loop(0, model // 384, second_layer, 0)

    worked(h)
    f_copies = [None] * 8
    for a, b in ((0, 1), (2, 6), (3, 7), (4, 5)):
        r_copies[a].wait_recv()
        f_copies[a] = along(held, left, a, f_send, f_recv, to_right)
        l_copies[b].wait_recv()
        f_copies[b] = along(held, right, b, f_send, f_recv, to_left)
    for n in via_left:
        r_copies[n].wait_recv()
    worked(left)
    c_copies = [None] * 8
    k_copies = [None] * 8

    def toward_right(n):
        block = results.at[right, source[n]]
        c_copies[n] = remote(block, from_left.at[n], c_send.at[n], c_recv.at[n], to_right)
        c_copies[n].start()

    def toward_left(n):
        block = results.at[left, source[n]]
        k_copies[n] = remote(block, from_right.at[n], k_send.at[n], k_recv.at[n], to_left)
        k_copies[n].start()

    for n in via_right:
        toward_left(n)
    for n in via_right:
        l_copies[n].wait_recv()
    worked(right)
    for n in via_left:
        toward_right(n)
    for n in range(8):
        f_copies[n].wait_recv()
    worked(across)
    h_copies = [None] * 8
    for at in range(4):
        for n, landing, peer in ((via_right[at], half_left, to_right), (via_left[at], half_right, to_left)):
            block = results.at[across, source[n]]
            h_copies[n] = remote(block, landing.at[at], h_send.at[n], h_recv.at[n], peer)
            h_copies[n].start()

    def weight_grads(i, carry):
        cols = pl.ds(pl.multiple_of(i * 128, 128), 128)
        total = jnp.zeros((128, hidden), F32)
        for lanes, kept, out in ((0, pre_w, g_up),):
            x_main = held[:, :, :, pl.ds(pl.multiple_of(i * 128, 128), 128)].reshape(4, half, 128)
            x_extra = held[:, :, :, pl.ds(pl.multiple_of(2 * model + i * 128, 128), 128)].reshape(4, half, 128)
            rows = jnp.concatenate([x_main, x_extra], axis=1).reshape(8 * half, 128)
            total = inner_rows(rows, kept[...].reshape(8 * half, hidden))
            out[cols, :] = total.astype(BF16)
        g_main = held[:, :, :, pl.ds(pl.multiple_of(model + i * 128, 128), 128)].reshape(4, half, 128)
        rows = jnp.concatenate([g_main, x_extra], axis=1).reshape(8 * half, 128)
        g_down[:, cols] = inner_rows(hid_w[...].reshape(8 * half, hidden), rows).astype(BF16)
        return carry

    lax.fori_loop(0, model // 128, weight_grads, 0)

    for ring in (sums_up, sums_down):
        ring.begin()
    for at in range(4):
        n = via_right[at]
        h_copies[n].wait_recv()
        results[right, source[n]] = (results[right, source[n]].astype(F32) + half_left[at].astype(F32)).astype(BF16)
        toward_right(n)
        n = via_left[at]
        h_copies[n].wait_recv()
        results[left, source[n]] = (results[left, source[n]].astype(F32) + half_right[at].astype(F32)).astype(BF16)
        toward_left(n)
    b_copies = []
    for n in (4, 5, 3, 7, 2, 6, 1, 0):
        c_copies[n].wait_recv()
        k_copies[n].wait_recv()
        total = results[h, source[n]].astype(F32) + from_left[n].astype(F32) + from_right[n].astype(F32)
        if n:
            sums[n] = total.astype(BF16)
            copy = remote(sums.at[n], back.at[e], b_send.at[n], b_recv.at[n], to_source[n])
            copy.start()
            b_copies.append(copy)
        else:
            back[e] = total.astype(BF16)
    for copy in b_copies:
        copy.wait_recv()
    main, top, low_half, onehot = slot_picks(routes[...], slots.shape[0])
    lines = back[...].reshape(128, 3 * model)
    shares = probs[...]
    gate = jnp.sum(shares * onehot, axis=-1, keepdims=True)
    hid, grad_output, low = hid_in[...], cotangent[...].astype(F32), moe_low[...]
    expert_out = inner_rows(main, lines[:, :model]) + inner_rows(top, lines[:, 2 * model :])
    output[...] = (hid + gate * expert_out).astype(BF16)
    grad_gate = jnp.sum(grad_output * expert_out, axis=-1, keepdims=True)
    grad_logits = (gate * grad_gate * (onehot - shares)).astype(BF16)
    grad_moe = inner_rows(main, lines[:, model : 2 * model]) + inner_rows(low_half, lines[:, 2 * model :])
    grad_moe = grad_moe + matmul(grad_logits, gains[...].astype(BF16))
    scale = lax.rsqrt(jnp.mean(hid * hid, axis=-1, keepdims=True) + EPS)
    scaled = grad_moe * gains[1:2, :]
    inside = jnp.mean(scaled * hid, axis=-1, keepdims=True)
    grad_hidden[...] = grad_output + scale * scaled - hid * (scale * scale * scale * inside)
    grad_gain = jnp.sum(grad_moe * hid * scale, axis=0, keepdims=True)
    at = lax.broadcasted_iota(jnp.int32, norm_out.shape, 0)
    norm_out[...] = inner_rows(grad_logits, low) + jnp.where(at == 1, grad_gain, 0.0)
    for ring in (sums_up, sums_down):
        ring.end()
    for copy in d_copies[1:] + r_copies + l_copies + f_copies + c_copies + k_copies + h_copies + b_copies:
        copy.wait_send()


def experts_both_ways(slots, up, down, *rest):
    count, lines, width = slots.shape
    model, hidden = up.shape
    eight = DMA((8,))
    return pl.pallas_call(
        expert_kernel,
        out_shape=(
            jax.ShapeDtypeStruct(rest[1].shape, BF16),
            jax.ShapeDtypeStruct(rest[0].shape, F32),
            jax.ShapeDtypeStruct(rest[5].shape, F32),
            jax.ShapeDtypeStruct(up.shape, BF16),
            jax.ShapeDtypeStruct(down.shape, BF16),
            jax.ShapeDtypeStruct((4, up.shape[0] // 8, up.shape[1]), BF16),
            jax.ShapeDtypeStruct((4, down.shape[0] // 8, down.shape[1]), BF16),
        ),
        in_specs=[IN_VMEM] * 9,
        out_specs=(IN_VMEM,) * 7,
        scratch_shapes=[
            DMA((2, 4)),
            DMA((2, 4)),
            pltpu.VMEM(slots.shape, BF16),
            pltpu.VMEM((4, count, lines, width), BF16),
            pltpu.VMEM((4, count, lines, width), BF16),
            pltpu.VMEM((256, hidden), BF16),
            pltpu.VMEM((256, hidden), BF16),
            pltpu.VMEM((4, 256, hidden), BF16),
            pltpu.VMEM((4, 256, hidden), BF16),
            pltpu.VMEM((8, lines, width), BF16),
            pltpu.VMEM((8, lines, width), BF16),
            pltpu.VMEM((4, lines, width), BF16),
            pltpu.VMEM((4, lines, width), BF16),
            pltpu.VMEM((8, lines, width), BF16),
            *[eight] * 16,
        ],
        compiler_params=pltpu.CompilerParams(
            collective_id=8, has_side_effects=True, vmem_limit_bytes=62 << 20
        ),
        name="experts",
    )(slots, up, down, *rest)


def across(tile, width):
    whole = width // 128
    return jnp.concatenate([tile] * whole + [tile[:, : width - 128 * whole]], axis=1)


def eye(size):
    at = [lax.broadcasted_iota(jnp.int32, (size, size), axis) for axis in (0, 1)]
    return (at[0] == at[1]).astype(BF16)


def both_cols(lines, main, extra):
    return jnp.concatenate([outer_cols(lines, main), outer_cols(lines, extra)], axis=1)


def gather_all(
    pack, norm, line, whole, norms, sequence, tiles, total, local_sems, z_send, z_recv, n_send, n_recv,
    w_send, w_recv, v_send, v_recv,
):
    e, r, h = places()
    c = lax.rem(e, 2)
    y = e // 2
    f0 = y * (1 - c) + r * c
    s0 = r * (1 - c) + y * c
    mate, first, second = mixer_peers()
    z_peers = hid_peers()
    own = e * 4 + r
    n_copies = [
        remote(norm, tiles.at[k], n_send.at[k], n_recv.at[k], z_peers[k]) for k in range(3)
    ]
    for copy in n_copies:
        copy.start()
    w_one = [remote(pack, whole.at[own], w_send.at[k], w_recv.at[k], first[k]) for k in range(3)]
    w_two = [[remote(pack, whole.at[own], w_send.at[3 + k], w_recv.at[3 + k], second[k]) for k in range(3)]]
    w_mate = [remote(pack, whole.at[own], w_send.at[15], w_recv.at[15], mate)]
    for k in (1, 0, 2):
        w_one[k].start()
    for k in (1, 0, 2):
        w_two[0][k].start()
    z_copies = [remote(line, sequence.at[h], z_send.at[k], z_recv.at[k], z_peers[k]) for k in range(3)]
    for k in (1, 0, 2):
        z_copies[k].start()
    w_mate[0].start()
    mine = [
        pltpu.make_async_copy(pack, whole.at[own], local_sems.at[0]),
        pltpu.make_async_copy(line, sequence.at[h], local_sems.at[1]),
    ]
    for copy in mine:
        copy.start()
    for copy in n_copies:
        copy.wait_recv()
    total[...] = norm[...] + tiles[0] + tiles[1] + tiles[2]
    v_one = [remote(total, norms.at[own], v_send.at[k], v_recv.at[k], first[k]) for k in range(3)]
    v_two = [[remote(total, norms.at[own], v_send.at[3 + k], v_recv.at[3 + k], second[k]) for k in range(3)]]
    v_mate = [remote(total, norms.at[own], v_send.at[15], v_recv.at[15], mate)]
    for copy in v_one + v_two[0] + v_mate:
        copy.start()
    mine.append(pltpu.make_async_copy(total, norms.at[own], local_sems.at[2]))
    mine[2].start()
    for k in range(3):
        came = block_at(c, lax.rem(f0 + 3 - k, 4), s0)
        for buf, one, send, recv, two, other in (
            (whole, w_one, w_send, w_recv, w_two, w_mate), (norms, v_one, v_send, v_recv, v_two, v_mate)
        ):
            one[k].wait_recv()
            block = buf.at[came]
            two.append([remote(block, block, send.at[6 + 3 * k + j], recv.at[6 + 3 * k + j], second[j]) for j in range(3)])
            for j in (1, 0, 2):
                two[1 + k][j].start()
            other.append(remote(block, block, send.at[16 + k], recv.at[16 + k], mate))
            other[-1].start()
    for k in range(4):
        for j in range(3):
            came = block_at(c, lax.rem(f0 + 4 - k, 4), lax.rem(s0 + 3 - j, 4))
            for buf, send, recv, two, other in (
                (whole, w_send, w_recv, w_two, w_mate), (norms, v_send, v_recv, v_two, v_mate)
            ):
                two[k][j].wait_recv()
                block = buf.at[came]
                at = 19 + 3 * k + j
                other.append(remote(block, block, send.at[at], recv.at[at], mate))
                other[-1].start()
    for copy in w_mate + v_mate:
        copy.wait_recv()
    for copy in z_copies:
        copy.wait_recv()
    for copy in n_copies + w_one + sum(w_two, []) + w_mate + v_one + sum(v_two, []) + v_mate + z_copies:
        copy.wait_send()
    for copy in mine:
        copy.wait()


def slot_picks(route, experts, states=16):
    count = route.shape[1]
    line = lax.broadcasted_iota(jnp.int32, (states, count), 0)
    chosen = jnp.where(line - 2 == route, 1.0, 0.0)
    earlier = lax.broadcasted_iota(jnp.int32, (count, count), 0) <= lax.broadcasted_iota(jnp.int32, (count, count), 1)
    counts = matmul(chosen.astype(BF16), jnp.where(earlier, 1.0, 0.0).astype(BF16))
    within = jnp.sum(chosen * (counts - 1.0), axis=0, keepdims=True).astype(jnp.int32)
    slot = lax.broadcasted_iota(jnp.int32, (experts * MAIN, count), 0)
    line, expert = slot % MAIN, slot // MAIN
    here = expert == route

    def of(found):
        return jnp.where(found, 1.0, 0.0).astype(BF16)

    main = of(here & (within == line))
    top = of(here & (line < 8) & (within == line + 16))
    low = of(here & (line >= 8) & (within == line + 8))
    column = jnp.broadcast_to(route.astype(F32), (count, count)).T[:, :states]
    place = lax.broadcasted_iota(jnp.int32, (count, states), 1) - 2
    onehot = jnp.where(place.astype(F32) == column, 1.0, 0.0)
    return main, top, low, onehot


def forward_kernel(*refs):
    (
        x_lines, g_lines, out_lines, x_cols, dt_cols, decay_in, taps_in, conv_bias, dt_bias, skip, gain_one, gain_two,
        router, tokens, resets, routes, cotangent,
        whole_hbm, seq_hbm, extra_hbm, normed_hbm, x_low_hbm, u_hbm, gate_hbm, proj_hbm, lin_hbm, y_hbm, gated_hbm,
        starts_hbm, hidden, params, gains, slots, moe_out, probs,
        pack, norm, line, whole, whole_all, norms, sequence, seq, extra, tiles, total, local_sems, z_send, z_recv, n_send, n_recv,
        w_send, w_recv, v_send, v_recv, k_sems, s_sems,
        normed, x_low, u_out, gate_z, proj, dt_lin, y_out, gated, starts,
        xs, marks, conv, dtm, dtx, parts, own, landing, branch, came, p_send, p_recv, b_send, b_recv, quarters, owned, q_send, q_recv,
    ) = refs
    e, r, h = places()
    block, model = tokens.shape
    inner, states, experts = u_out.shape[1], starts.shape[1], router.shape[0]
    lines, small = block // STEP, 3 * model
    channels, share = x_lines.shape[0], gain_one.shape[1]

    def wide(a):
        return a[...].astype(F32)

    line[:, :model] = tokens[...]
    line[:, model:] = jnp.broadcast_to(wide(resets), (block, 128)).T.astype(BF16)
    columns = jnp.concatenate(
        [
            wide(decay_in), wide(taps_in), wide(conv_bias), wide(dt_bias), wide(skip),
            jnp.zeros((105, channels), F32),
        ],
        axis=0,
    )
    columns = jnp.concatenate([columns, jnp.zeros((128, 128 - channels), F32)], axis=1).T[:channels, :24]
    tail = jnp.concatenate(
        [
            jnp.concatenate([wide(x_cols), columns], axis=1),
            jnp.concatenate([wide(dt_cols), jnp.zeros((channels, 128 - dt_cols.shape[1]), F32)], axis=1),
        ],
        axis=1,
    )
    both = jnp.concatenate([wide(x_lines), wide(g_lines), wide(out_lines), tail], axis=1)
    pack[:, : small + 256] = both[:MAIN].astype(BF16)
    last = jnp.concatenate([both[MAIN:], jnp.zeros((channels - MAIN, 4096 - small - 256), F32)], axis=1)
    last = [last[n : n + 1, k * EXTRA : (k + 1) * EXTRA] for n in range(2) for k in range(8)]
    pack[:, small + 256 :] = jnp.concatenate(last, axis=0).astype(BF16)
    tile = jnp.concatenate([wide(gain_one), wide(gain_two), wide(router), jnp.zeros((6, share), F32)], axis=0)
    tile = jnp.concatenate([tile, jnp.zeros((MAIN, 128 - share), F32)], axis=1)
    norm[...] = pltpu.roll(tile, h * share, 1).astype(BF16)
    z_peers = hid_peers()
    mate, first, second = mixer_peers()
    greet([mate] + first + second + z_peers)
    gather_all(
        pack, norm, line, whole, norms, sequence, tiles, total, local_sems, z_send, z_recv, n_send, n_recv,
        w_send, w_recv, v_send, v_recv,
    )
    span = share * 4
    gains[...] = jnp.concatenate([norms[n].astype(F32)[:, :span] for n in range(32)], axis=1)
    whole_all[...] = whole[...].reshape(512, small + 768)
    seq[...] = sequence[...].reshape(4 * block, model + 128)
    row = lax.broadcasted_iota(jnp.int32, (512, 512), 0)
    col = lax.broadcasted_iota(jnp.int32, (512, 512), 1)
    wanted = (row % 64 // 2) * MAIN + (row % 2) * 8 + row // 64
    moved = matmul((wanted == col).astype(BF16), whole_all[:, small + 256 :]).astype(BF16)
    for k in range(8):
        extra[:, k * 512 : (k + 1) * 512] = moved[k * 64 : (k + 1) * 64]
    params[...] = both_cols(eye(128), whole_all[:, small : small + 128], extra[:, small : small + 128])
    kept_copies = [
        pltpu.make_async_copy(kept, out, k_sems.at[n])
        for n, (kept, out) in enumerate(((whole_all, whole_hbm), (seq, seq_hbm), (extra, extra_hbm)))
    ]
    for copy in kept_copies:
        copy.start()
    xs[0:8] = jnp.zeros((8, inner), F32)
    marks[0:8] = jnp.zeros((8, 128), F32)
    gain = gains[0:1, :]

    pairs = (
        (normed, normed_hbm), (x_low, x_low_hbm), (u_out, u_hbm), (gate_z, gate_hbm), (proj, proj_hbm),
        (dt_lin, lin_hbm), (y_out, y_hbm), (gated, gated_hbm), (starts, starts_hbm),
    )

    def saved_copy(n, b):
        kept, out = pairs[n]
        size = kept.shape[0] // 4
        rows = pl.ds(pl.multiple_of(b * size, size), size)
        return pltpu.make_async_copy(kept.at[rows], out.at[rows], s_sems.at[n, b])

    def proj_copy(b, k):
        at = k * 4 + b
        return remote(own.at[b], landing.at[k, b], p_send.at[at], p_recv.at[at], z_peers[k])

    def stage_one(b, carry):
        start = pl.multiple_of(b * block, block)
        rows = pl.ds(start, block)
        values = seq[rows, :model].astype(F32)
        scale = lax.rsqrt(jnp.mean(values * values, axis=-1, keepdims=True) + EPS)
        low = (values * scale * gain).astype(BF16)
        normed[rows, :] = low
        gate_z[rows, :] = both_cols(low, whole_all[:, model : 2 * model], extra[:, model : 2 * model])
        x = both_cols(low, whole_all[:, :model], extra[:, :model]).astype(BF16)
        x_low[rows, :] = x
        after = pl.ds(pl.multiple_of(8 + start, 8), block)
        xs[after, :] = x.astype(F32)
        now = seq[rows, model:].astype(F32)
        marks[after, :] = now
        lines_x, lines_m = xs[pl.ds(start, block + 8), :], marks[pl.ds(start, block + 8), :]
        mask = 1.0 - now
        total = params[124:125, :] + params[123:124, :] * x.astype(F32)
        for back in (1, 2, 3):
            past = lines_x[8 - back : 8 - back + block]
            total = total + params[123 - back : 124 - back, :] * past * across(mask, inner)
            if back < 3:
                mask = mask * (1.0 - lines_m[8 - back : 8 - back + block])
        u_out[rows, :] = total
        convolved = total * jax.nn.sigmoid(total)
        conv[rows, :] = convolved
        conv_low = convolved.astype(BF16)
        share = matmul(conv_low[:, :512], whole_all[:, small : small + 128]) + matmul(
            conv_low[:, 512:], extra[:, small : small + 128]
        )
        own[b] = share.astype(BF16)
        for k in (1, 0, 2):
            proj_copy(b, k).start()
        for n in range(4):
            saved_copy(n, b).start()
        return carry

    lax.fori_loop(0, 4, stage_one, 0)
    a = jnp.exp(params[104:120, :]) * (-LOG2E)
    half = states // 2

    quarter = block // 4

    def part_copy(b, k):
        rows = pl.ds(pl.multiple_of(lax.rem(h + 1 + k, 4) * quarter, quarter), quarter)
        at = k * 4 + b
        return remote(branch.at[b, rows], came.at[k, b], b_send.at[at], b_recv.at[at], z_peers[k])

    def whole_copy(b, sender):
        return remote(quarters.at[b], owned.at[sender], q_send.at[b], q_recv.at[sender], (e, r, b))

    def sum_up(b):
        rows = pl.ds(pl.multiple_of(h * quarter, quarter), quarter)
        for k in range(3):
            part_copy(b, k).wait_recv()
        total = branch[b, rows, :].astype(F32)
        for k in range(3):
            total = total + came[k, b].astype(F32)
        quarters[b] = total.astype(BF16)

        @pl.when(b != h)
        def send():
            whole_copy(b, lax.rem(h - b + 4, 4) - 1).start()

    def stage_two(b, state):
        start = pl.multiple_of(b * block, block)
        rows = pl.ds(start, block)
        for k in range(3):
            proj_copy(b, k).wait_recv()
        sums = (
            own[b].astype(F32) + landing[0, b].astype(F32) + landing[1, b].astype(F32) + landing[2, b].astype(F32)
        )
        proj[rows, :] = sums
        lin = both_cols(sums.astype(BF16), whole_all[:, small + 128 : small + 256], extra[:, small + 128 : small + 256])
        lin = lin + params[125:126, :]
        dt_lin[rows, :] = lin
        dt = jax.nn.softplus(lin)
        convolved = conv[rows, :]
        dtm[...] = dt + across(STOP * marks[pl.ds(pl.multiple_of(8 + start, 8), block), :], inner)
        dtx[...] = dt * convolved
        turned = sums.T
        b_all, c_all = turned[72:88], turned[88:104]

        def chunk(i, h_now):
            starts[b * lines + i] = h_now
            shift = lax.rem(block - i * STEP, block)
            b_now, c_now = pltpu.roll(b_all, shift, 1), pltpu.roll(c_all, shift, 1)
            rows_m, rows_x = (ref[pl.ds(pl.multiple_of(i * STEP, STEP), STEP), :] for ref in (dtm, dtx))
            for j in range(STEP):
                decay = jnp.exp2(a * rows_m[j : j + 1])
                h_now = decay * h_now + b_now[:, j : j + 1] * rows_x[j : j + 1]
                p = c_now[:, j : j + 1] * h_now
                put_rows(parts, j, p[:half] + p[half:])
            here = pl.ds(pl.multiple_of(start + i * STEP, STEP), STEP)
            y_out[here, :] = summed_groups(parts, half, inner)
            return h_now

        state = lax.fori_loop(0, lines, chunk, state)
        y = y_out[rows, :] + params[126:127, :] * convolved
        y_out[rows, :] = y
        z = gate_z[rows, :]
        low = (y * z * jax.nn.sigmoid(z)).astype(BF16)
        gated[rows, :] = low
        out = matmul(low[:, :512], whole_all[:, 2 * model : small]) + matmul(low[:, 512:], extra[:, 2 * model : small])
        branch[b] = out.astype(BF16)

        for k in (1, 0, 2):
            part_copy(b, k).start()

        @pl.when(b > 0)
        def earlier():
            sum_up(b - 1)

        for n in range(4, 9):
            saved_copy(n, b).start()
        return state

    lax.fori_loop(0, 4, stage_two, jnp.zeros((states, inner), F32))
    sum_up(3)
    for k in range(3):
        whole_copy(0, k).wait_recv()
    mine = pl.ds(pl.multiple_of(h * block, block), block)
    hidden[...] = seq[mine, :model].astype(F32)
    for k in range(4):
        rows = pl.ds(pl.multiple_of(lax.rem(h + k, 4) * quarter, quarter), quarter)
        piece = owned[k - 1] if k else quarters[h]
        hidden[rows, :] += piece.astype(F32)
    hid = hidden[...]
    scale = lax.rsqrt(jnp.mean(hid * hid, axis=-1, keepdims=True) + EPS)
    moe_low = (hid * scale * gains[1:2, :]).astype(BF16)
    moe_out[...] = moe_low
    logits = outer_cols(moe_low, gains[...].astype(BF16))
    lane = lax.broadcasted_iota(jnp.int32, logits.shape, 1)
    real = (lane >= 2) & (lane < 2 + experts)
    logits = jnp.where(real, logits, -1e30)
    powers = jnp.exp(logits - jnp.max(logits, axis=-1, keepdims=True))
    shares = powers / jnp.sum(powers, axis=-1, keepdims=True)
    probs[...] = shares
    main, top, low_half, onehot = slot_picks(routes[...], experts)
    gate = jnp.sum(shares * onehot, axis=-1, keepdims=True)
    grad_eo = (gate * cotangent[...].astype(F32)).astype(BF16)
    shape = (experts, MAIN, model)
    slots[:, :, :model] = matmul(main, moe_low).astype(BF16).reshape(shape)
    slots[:, :, model : 2 * model] = matmul(main, grad_eo).astype(BF16).reshape(shape)
    slots[:, :, 2 * model :] = (matmul(top, moe_low) + matmul(low_half, grad_eo)).astype(BF16).reshape(shape)
    for n in range(9):
        for b in range(4):
            saved_copy(n, b).wait()
    for copy in kept_copies:
        copy.wait()
    for b in range(4):
        for k in range(3):
            proj_copy(b, k).wait_send()
            part_copy(b, k).wait_send()

        @pl.when(b != h)
        def sent():
            whole_copy(b, 0).wait_send()


def mixer_forward(arrays, inner, states, experts):
    tokens = arrays[13]
    block, model = tokens.shape
    length = 4 * block
    width = 3 * model + 768
    S, V = jax.ShapeDtypeStruct, pltpu.VMEM
    saved = [
        ((length, model), BF16), ((length, inner), BF16), ((length, inner), F32), ((length, inner), F32),
        ((length, 128), F32), ((length, inner), F32), ((length, inner), F32), ((length, inner), BF16),
        ((length // STEP, states, inner), F32),
    ]
    outs = (
        S((512, width), BF16), S((length, model + 128), BF16), S((64, 4096), BF16), *[S(*one) for one in saved],
        S((block, model), F32), S((128, inner), F32), S((MAIN, model), F32), S((experts, MAIN, 3 * model), BF16),
        S((block, model), BF16), S((block, MAIN), F32),
    )
    return pl.pallas_call(
        forward_kernel,
        out_shape=outs,
        in_specs=[IN_VMEM] * len(arrays),
        out_specs=(*[ANY] * 12, *[IN_VMEM] * 6),
        scratch_shapes=[
            V((MAIN, width), BF16), V((MAIN, 128), BF16), V((block, model + 128), BF16), V((32, MAIN, width), BF16),
            V((512, width), BF16),
            V((32, MAIN, 128), BF16), V((4, block, model + 128), BF16), V((length, model + 128), BF16), V((64, 4096), BF16),
            V((3, MAIN, 128), BF16), V((MAIN, 128), BF16),
            DMA((3,)), DMA((3,)), DMA((3,)), DMA((3,)), DMA((3,)), DMA((31,)), DMA((31,)), DMA((31,)), DMA((31,)),
            DMA((3,)), DMA((9, 4)),
            *[V(*one) for one in saved],
            V((length + 8, inner), F32), V((length + 8, 128), F32), V((length, inner), F32), V((block, inner), F32),
            V((block, inner), F32), V((-(-inner // 128), STEP * states // 2, 128), F32), V((4, block, 128), BF16),
            V((3, 4, block, 128), BF16), V((4, block, model), BF16), V((3, 4, block // 4, model), BF16),
            DMA((12,)), DMA((12,)), DMA((12,)), DMA((12,)), V((4, block // 4, model), BF16),
            V((3, block // 4, model), BF16), DMA((4,)), DMA((3,)),
        ],
        compiler_params=pltpu.CompilerParams(
            collective_id=1, has_side_effects=True, vmem_limit_bytes=62 << 20
        ),
        name="mixer_forward",
    )(*arrays)


class Flow:
    ORDER = (2, 1, 3, 0)

    def __init__(self, turn, source, out, pairs, halves, fours, lines, ends, send, recv):
        self.source, self.out, self.pairs, self.halves = source, out, pairs, halves
        self.fours, self.lines, self.ends, self.send, self.recv = fours, lines, ends, send, recv
        e, r, h = places()
        self.c = lax.rem(e, 2)
        y = e // 2
        self.turn = self.c if turn is None else turn
        self.mate_turn = 1 - self.c if turn is None else turn
        self.f0 = y * (1 - self.turn) + r * self.turn
        self.s0 = r * (1 - self.turn) + y * self.turn
        self.mate_s0 = r * (1 - self.mate_turn) + y * self.mate_turn
        self.mate, self.first, self.second_peers = mixer_peers(self.turn)

    def copy(self, src, dst, at, peer):
        return remote(src, dst, self.send.at[at], self.recv.at[at], peer)

    def mate_copy(self, n, f):
        s = lax.rem(self.mate_s0 + self.ORDER[n], 4)
        block = block_at(1 - self.c, f, s, self.mate_turn)
        return self.copy(self.source.at[block], self.pairs.at[n, f], n * 4 + f, self.mate)

    def second_copy(self, n):
        return self.copy(self.halves.at[n], self.fours.at[n], 16 + n, self.second_peers[self.ORDER[n] - 1])

    def first_copy(self, n):
        return self.copy(self.lines.at[n], self.ends.at[n], 19 + n, self.first[self.ORDER[n] - 1])

    def begin(self):
        for n in range(4):
            for f in range(4):
                self.mate_copy(n, f).start()

    def second(self):
        for n, k in enumerate(self.ORDER):
            s = lax.rem(self.s0 + k, 4)
            for f in range(4):
                self.mate_copy(n, f).wait_recv()
                total = self.source[block_at(self.c, f, s, self.turn)].astype(F32) + self.pairs[n, f].astype(F32)
                self.halves[n, f] = total.astype(BF16)
            if k:
                self.second_copy(n).start()

    def third(self):
        for n in range(3):
            self.second_copy(n).wait_recv()
        for n, k in enumerate(self.ORDER):
            f = lax.rem(self.f0 + k, 4)
            line = self.halves[3, f].astype(F32)
            for m in range(3):
                line = line + self.fours[m, f].astype(F32)
            if k:
                self.lines[n] = line.astype(BF16)
                self.first_copy(n).start()
            else:
                self.out[...] = line

    def finish(self):
        for n in range(3):
            self.first_copy(n).wait_recv()
        self.out[...] = (
            self.out[...] + self.ends[0].astype(F32) + self.ends[1].astype(F32) + self.ends[2].astype(F32)
        )

    def end(self):
        for n in range(4):
            for f in range(4):
                self.mate_copy(n, f).wait_send()
        for n in range(3):
            self.second_copy(n).wait_send()
            self.first_copy(n).wait_send()


def flow_scratch(width):
    return [
        pltpu.VMEM((32, MAIN, width), BF16), pltpu.VMEM((MAIN, width), F32), pltpu.VMEM((4, 4, MAIN, width), BF16),
        pltpu.VMEM((4, 4, MAIN, width), BF16), pltpu.VMEM((3, 4, MAIN, width), BF16),
        pltpu.VMEM((3, MAIN, width), BF16), pltpu.VMEM((3, MAIN, width), BF16), DMA((22,)), DMA((22,)),
    ]


def mixer_back_kernel(*refs):
    (
        grad_hidden, seq_all, whole_in, gains, norm_in, normed_in, x_low_in, u_all, gate_all, proj_in, lin_all, y_all,
        gated_in, starts_in, params, extra_in, g_up, g_down, came_up, came_down,
        grad_tokens, grad_in, grad_out, grad_x, grad_dt, by_channel, by_feature, all_up, all_down,
        seq_own, seq_marks, whole, normed, x_low, u_in, gate_z, proj, dt_lin, y_in, gated, starts, extra, in_sems,
        ghs, gus, marks, dts, dtm, dtx, conv, s1, s2, gdl, ggate, gx, gp_all,
        conv_low, held, decays, parts_1, parts_2, lanes_b, lanes_c, state, g_rate, rows_sum, own, landing, branch, came,
        a_send, a_recv, p_send, p_recv, b_send, b_recv, x_send, x_recv, x_local,
        e_slots_up, e_own_up, e_sums_up, total_up, e_slots_down, e_own_down, e_sums_down, total_down,
        y_send, y_recv, y_local, own_tile, tiles, z_send, z_recv, *flow_refs, gain_sum,
    ) = refs
    e, r, h = places()
    block, model = grad_hidden.shape
    inner, states = u_in.shape[1], starts.shape[1]
    lines, half, small = block // STEP, states // 2, 3 * model
    owners = 32
    mine = pl.ds(pl.multiple_of(h * block, block), block)
    loads = [
        (lin_all, dt_lin), (u_all, u_in), (gate_all, gate_z), (y_all, y_in), (seq_all.at[:, model:], seq_marks),
        (proj_in, proj), (starts_in, starts), (whole_in, whole), (extra_in, extra), (x_low_in, x_low),
        (gated_in, gated), (normed_in, normed), (seq_all.at[mine, :model], seq_own),
    ]
    loads = [pltpu.make_async_copy(a, b, in_sems.at[n]) for n, (a, b) in enumerate(loads)]
    for copy in loads:
        copy.start()
    z_peers = hid_peers()
    mate, first, second = mixer_peers()
    sums = [
        RowsSum(g_up, came_up, e_slots_up, e_own_up, e_sums_up, total_up, y_send.at[0], y_recv.at[0], y_local.at[0]),
        RowsSum(
            g_down, came_down, e_slots_down, e_own_down, e_sums_down, total_down, y_send.at[1], y_recv.at[1], y_local.at[1]
        ),
    ]
    rings = [
        RowsGather(part, whole_grad, x_send.at[n], x_recv.at[n], x_local.at[n])
        for n, (part, whole_grad) in enumerate(((total_up, all_up), (total_down, all_down)))
    ]
    for ring in sums:
        for n in (4, 0, 1, 2, 3):
            ring.load(n).start()
    ghs[h] = grad_hidden[...].astype(BF16)
    greet([mate] + first + second + z_peers)
    gh_copies = [remote(ghs.at[h], ghs.at[h], a_send.at[k], a_recv.at[k], z_peers[k]) for k in range(3)]
    for k in (1, 0, 2):
        gh_copies[k].start()
    for ring in sums:
        ring.pass_on()
    flow_early, flow_in, flow_rest = [
        Flow(None, *flow_refs[9 * n : 9 * n + 9]) for n in range(3)
    ]
    state[...] = jnp.zeros_like(state)
    g_rate[...] = jnp.zeros_like(g_rate)
    rows_sum[...] = jnp.zeros_like(rows_sum)
    gain_sum[...] = jnp.zeros_like(gain_sum)
    gus[512:520] = jnp.zeros((8, inner), F32)
    a = jnp.exp(params[104:120, :]) * (-LOG2E)
    for copy in loads[:5]:
        copy.wait()
    marks[0:512] = seq_marks[...].astype(F32)
    marks[512:520] = jnp.zeros((8, 128), F32)

    def prepare(b, carry):
        rows = pl.ds(pl.multiple_of(b * block, block), block)
        lin = dt_lin[rows, :]
        dt = jax.nn.softplus(lin)
        dt_lin[rows, :] = jax.nn.sigmoid(lin)
        u_now = u_in[rows, :]
        convolved = u_now * jax.nn.sigmoid(u_now)
        conv[rows, :] = convolved
        conv_low[rows, :] = convolved.astype(BF16)
        dts[rows, :] = dt
        dtm[rows, :] = dt + across(STOP * marks[rows, :], inner)
        dtx[rows, :] = dt * convolved
        z = gate_z[rows, :]
        sig = jax.nn.sigmoid(z)
        gate_z[rows, :] = z * sig
        y_in[rows, :] = y_in[rows, :] * (sig * (1.0 + z * (1.0 - sig)))
        return carry

    lax.fori_loop(0, 4, prepare, 0)
    for copy in loads[5:]:
        copy.wait()

    def spots(shape, axis):
        return lax.broadcasted_iota(jnp.int32, shape, axis)

    tall = (block * states, 128)
    ones = jnp.ones((128, 128), BF16)

    extras = []

    def weight(left, right, target, at, size):
        main = inner_rows(left[:, :512], right)
        target[:, :, at : at + size] = main.astype(BF16).reshape(owners, MAIN, size)
        extras.append(inner_rows(left[:, 512:], right).astype(BF16))

    for copy in gh_copies:
        copy.wait_recv()
    gh_rows, low_norm = ghs[...].reshape(4 * block, model), normed[...]
    gg = both_cols(gh_rows, whole[:, 2 * model : small], extra[:, 2 * model : small])
    gate_z[...] = gg * gate_z[...]
    ggate[...] = (gg * y_in[...]).astype(BF16)
    weight(gated[...], gh_rows, flow_early.source, 0, model)
    weight(ggate[...], low_norm, flow_early.source, model, model)
    flow_early.begin()
    for ring, gather in zip(sums, rings):
        ring.finish()
        gather.begin()

    def proj_copy(b, k):
        at = k * 4 + b
        return remote(own.at[b], landing.at[k, b], p_send.at[at], p_recv.at[at], z_peers[k])

    def branch_copy(b, sender):
        return remote(branch.at[b], came.at[sender], b_send.at[b], b_recv.at[sender], (e, r, b))

    def stage_a(b):
        start = pl.multiple_of(b * block, block)
        rows = pl.ds(start, block)
        turned = proj[rows, :].T
        b_all, c_all = turned[72:88], turned[88:104]

        gy_now = gate_z[rows, :]

        def chunk(step, u):
            i = lines - 1 - step
            hh = starts[b * lines + i]
            held[0] = hh
            shift = lax.rem(block - i * STEP, block)
            b_now, c_now = pltpu.roll(b_all, shift, 1), pltpu.roll(c_all, shift, 1)
            there = pl.ds(pl.multiple_of(start + i * STEP, STEP), STEP)
            rows_m, rows_x, rows_g, rows_t = (ref[there, :] for ref in (dtm, dtx, gate_z, dts))
            for j in range(STEP):
                decay = jnp.exp2(a * rows_m[j : j + 1])
                hh = decay * hh + b_now[:, j : j + 1] * rows_x[j : j + 1]
                decays[j] = decay
                held[j + 1] = hh
            for j in range(STEP - 1, -1, -1):
                gy_row = rows_g[j : j + 1]
                g = c_now[:, j : j + 1] * gy_row + u
                u = decays[j] * g
                q = u * held[j]
                g_rate[...] += q * rows_t[j : j + 1]
                w = q * a
                put_rows(parts_2, j, w[:half] + w[half:])
                w = g * b_now[:, j : j + 1]
                put_rows(parts_1, j, w[:half] + w[half:])
                at = pl.ds(pl.multiple_of((i * STEP + j) * states, states), states)
                lanes_b[at, :] = over_lanes(g * rows_x[j : j + 1]).astype(BF16)
                lanes_c[at, :] = over_lanes(held[j + 1] * gy_row).astype(BF16)
            here = pl.ds(pl.multiple_of(i * STEP, STEP), STEP)
            s1[here, :] = summed_groups(parts_1, half, inner)
            s2[here, :] = summed_groups(parts_2, half, inner)
            return u

        state[...] = lax.fori_loop(0, lines, chunk, state[...])
        convolved = conv[rows, :]
        grad_lin = dt_lin[rows, :] * (convolved * s1[...] + s2[...] * (1.0 / LOG2E))
        low = grad_lin.astype(BF16)
        gdl[rows, :] = low
        rows_sum[5:6, :] += jnp.sum(grad_lin, axis=0, keepdims=True)
        rows_sum[6:7, :] += jnp.sum(gy_now * convolved, axis=0, keepdims=True)
        dts[rows, :] = params[126:127, :] * gy_now + dts[rows, :] * s1[...]
        at_state = spots(tall, 0) % states
        spread = jnp.where(spots(tall, 1) - 72 == at_state, matmul(lanes_b[...], ones), 0.0) + jnp.where(
            spots(tall, 1) - 88 == at_state, matmul(lanes_c[...], ones), 0.0
        )
        share = spread.reshape(block, states, 128).sum(axis=1)
        share = share + matmul(low[:, :512], whole[:, small + 128 : small + 256])
        share = share + matmul(low[:, 512:], extra[:, small + 128 : small + 256])
        own[b] = share.astype(BF16)
        for k in (1, 0, 2):
            proj_copy(b, k).start()

    def stage_b(b):
        start = pl.multiple_of(b * block, block)
        rows = pl.ds(start, block)
        for k in range(3):
            proj_copy(b, k).wait_recv()
        gp = (
            own[b].astype(F32) + landing[0, b].astype(F32) + landing[1, b].astype(F32) + landing[2, b].astype(F32)
        ).astype(BF16)
        gp_all[rows, :] = gp
        u_now = u_in[rows, :]
        sig = jax.nn.sigmoid(u_now)
        gu = dts[rows, :] + both_cols(gp, whole[:, small : small + 128], extra[:, small : small + 128])
        gu = gu * (sig * (1.0 + u_now * (1.0 - sig)))
        gus[rows, :] = gu
        lines_g, lines_m = gus[pl.ds(start, block + 8), :], marks[pl.ds(start, block + 8), :]
        x = x_low[rows, :].astype(F32)
        total = params[123:124, :] * gu
        rows_sum[3:4, :] += jnp.sum(gu * x, axis=0, keepdims=True)
        rows_sum[4:5, :] += jnp.sum(gu, axis=0, keepdims=True)
        mask = jnp.ones((block, 128), F32)
        for ahead in (1, 2, 3):
            mask = mask * (1.0 - lines_m[ahead : ahead + block])
            moved = lines_g[ahead : ahead + block] * across(mask, inner)
            total = total + params[123 - ahead : 124 - ahead, :] * moved
            rows_sum[3 - ahead : 4 - ahead, :] += jnp.sum(moved * x, axis=0, keepdims=True)
        low = total.astype(BF16)
        gx[rows, :] = low
        gate = ggate[rows, :]
        out = (
            matmul(low[:, :512], whole[:, :model])
            + matmul(low[:, 512:], extra[:, :model])
            + matmul(gate[:, :512], whole[:, model : 2 * model])
            + matmul(gate[:, 512:], extra[:, model : 2 * model])
        )
        branch[b] = out.astype(BF16)

        @pl.when(b != h)
        def send():
            branch_copy(b, lax.rem(h - b + 4, 4) - 1).start()

        gain_sum[...] += jnp.sum(out * normed[rows, :].astype(F32), axis=0, keepdims=True)

    def step(n, carry):
        stage_a(3 - n)

        @pl.when(n > 0)
        def later():
            stage_b(4 - n)

        @pl.when(n == 0)
        def pass_on():
            flow_early.second()

        @pl.when(n == 2)
        def early():
            for ring in rings:
                ring.forward()
            flow_early.third()

        return carry

    lax.fori_loop(0, 4, step, 0)

    flow_early.finish()
    stage_b(0)
    weight(gx[...], low_norm, flow_in.source, 0, model)
    flow_in.begin()
    weight(gdl[...], proj[...].astype(BF16), flow_rest.source, 128, 128)
    ends = jnp.concatenate(
        [jnp.zeros((104, inner), F32), g_rate[...] * (a * (1.0 / LOG2E)), rows_sum[...]], axis=0
    ).astype(BF16)
    low_conv, low_gp, unit = conv_low[...], gp_all[...], eye(128)
    main = inner_rows(low_conv[:, :512], low_gp) + inner_rows(ends[:, :512], unit)
    flow_rest.source[:, :, :128] = main.astype(BF16).reshape(owners, MAIN, 128)
    last = (inner_rows(low_conv[:, 512:], low_gp) + inner_rows(ends[:, 512:], unit)).astype(BF16)
    lines_e = jnp.concatenate(
        [extras[2], extras[1], extras[0], last, extras[3], jnp.zeros((64, 4096 - small - 256), BF16)], axis=1
    )
    stacked = jnp.concatenate([lines_e[:, k * 512 : (k + 1) * 512] for k in range(8)], axis=0)
    row, col = spots((512, 512), 0), spots((512, 512), 1)
    wanted = (col % 64 // 2) * MAIN + (col % 2) * 8 + col // 64
    flow_rest.source[:, :, 256:768] = (
        matmul((wanted == row).astype(BF16), stacked).astype(BF16).reshape(owners, MAIN, 512)
    )
    span = model // owners
    tile = norm_in[...] + jnp.where(spots(norm_in.shape, 0) == 0, gain_sum[...] / gains[0:1, :], 0.0)
    for n in range(owners):
        piece = tile[:, n * span : (n + 1) * span]
        piece = jnp.concatenate([piece, jnp.zeros((MAIN, 128 - span), F32)], axis=1)
        flow_rest.source[n, :, 768:] = piece.astype(BF16)
    flow_rest.begin()
    flow_in.second()
    flow_rest.second()
    flow_in.third()
    flow_rest.third()
    for ring in sums + rings:
        ring.end()
    for k in range(3):
        branch_copy(0, k).wait_recv()
    grad_n = branch[h].astype(F32) + came[0].astype(F32) + came[1].astype(F32) + came[2].astype(F32)
    values = seq_own[...].astype(F32)
    scale = lax.rsqrt(jnp.mean(values * values, axis=-1, keepdims=True) + EPS)
    scaled = grad_n * gains[0:1, :]
    inside = jnp.mean(scaled * values, axis=-1, keepdims=True)
    grad_tokens[...] = grad_hidden[...] + scale * scaled - values * (scale * scale * scale * inside)
    flow_rest.finish()
    rest = flow_rest.out[...]
    own_tile[...] = rest[:, 768:].astype(BF16)
    z_copies = [remote(own_tile, tiles.at[k], z_send.at[k], z_recv.at[k], z_peers[k]) for k in range(3)]
    for copy in z_copies:
        copy.start()
    flow_in.finish()
    rank, wide = grad_dt.shape[1], grad_x.shape[1]
    extra_rows = [
        jnp.concatenate([rest[n * 8 + k : n * 8 + k + 1, 256:768] for k in range(8)], axis=1) for n in range(2)
    ]

    def full(main, at, size):
        return jnp.concatenate([main, *[line[:, at : at + size] for line in extra_rows]], axis=0)

    grad_in[:, 0, :] = full(flow_in.out[...], 0, model)
    grad_in[:, 1, :] = full(flow_early.out[:, model:], model, model)
    grad_out[...] = full(flow_early.out[:, :model], 2 * model, model)
    small_sum = full(rest[:, :256], small, 256)
    grad_x[...] = small_sum[:, :wide]
    grad_dt[...] = small_sum[:, 128 : 128 + rank]
    channels = jnp.concatenate([small_sum[:, :128], jnp.zeros((110, 128), F32)], axis=0)
    by_channel[...] = channels.T[104:128, : grad_out.shape[0]]
    for copy in z_copies:
        copy.wait_recv()
    tile = rest[:, 768:] + tiles[0].astype(F32) + tiles[1].astype(F32) + tiles[2].astype(F32)
    share = by_feature.shape[1]
    by_feature[...] = pltpu.roll(tile, lax.rem(128 - h * share, 128), 1)[:, :share]
    for flow in (flow_early, flow_in, flow_rest):
        flow.end()
    for copy in gh_copies + z_copies:
        copy.wait_send()
    for b in range(4):
        for k in range(3):
            proj_copy(b, k).wait_send()

        @pl.when(b != h)
        def sent():
            branch_copy(b, 0).wait_send()


def mixer_backward(grad_hidden, seq, whole, gains, norm_in, saved, expert_grads, own, wide, rank):
    normed, x_low, u, gate_z, proj, dt_lin, y, gated, starts, params, extra = saved
    block, model = grad_hidden.shape
    tokens, inner = u.shape
    states = starts.shape[1]
    S = jax.ShapeDtypeStruct
    g_up, g_down, came_up, came_down = expert_grads

    def like(array):
        return pltpu.VMEM(array.shape, array.dtype)

    line, low = pltpu.VMEM((block, inner), F32), pltpu.VMEM((tokens, inner), BF16)
    tall = pltpu.VMEM((tokens, inner), F32)
    return pl.pallas_call(
        mixer_back_kernel,
        out_shape=(
            S((block, model), F32), S((own, 2, model), F32), S((own, model), F32), S((own, wide), F32),
            S((own, rank), F32), S((24, own), F32), S((MAIN, model // 128), F32), S(g_up.shape, BF16),
            S(g_down.shape, BF16),
        ),
        in_specs=[IN_VMEM, ANY, ANY, IN_VMEM, IN_VMEM, *[ANY] * 9, IN_VMEM, *[ANY] * 5],
        out_specs=(*[IN_VMEM] * 7, ANY, ANY),
        scratch_shapes=[
            pltpu.VMEM((block, model), BF16), pltpu.VMEM((tokens, 128), BF16), like(whole), like(normed), like(x_low),
            like(u), like(gate_z), like(proj), like(dt_lin), like(y), like(gated), like(starts), like(extra),
            DMA((13,)),
            pltpu.VMEM((4, block, model), BF16),
            pltpu.VMEM((tokens + 8, inner), F32),
            pltpu.VMEM((tokens + 8, 128), F32),
            tall, tall, tall, tall, line, line,
            low, low, low,
            pltpu.VMEM((tokens, 128), BF16),
            low,
            pltpu.VMEM((STEP + 1, states, inner), F32),
            pltpu.VMEM((STEP, states, inner), F32),
            pltpu.VMEM((-(-inner // 128), STEP * states // 2, 128), F32),
            pltpu.VMEM((-(-inner // 128), STEP * states // 2, 128), F32),
            pltpu.VMEM((block * states, 128), BF16),
            pltpu.VMEM((block * states, 128), BF16),
            pltpu.VMEM((states, inner), F32),
            pltpu.VMEM((states, inner), F32),
            pltpu.VMEM((8, inner), F32),
            pltpu.VMEM((4, block, 128), BF16),
            pltpu.VMEM((3, 4, block, 128), BF16),
            pltpu.VMEM((4, block, model), BF16),
            pltpu.VMEM((3, block, model), BF16),
            DMA((3,)), DMA((3,)), DMA((12,)), DMA((12,)), DMA((4,)), DMA((3,)),
            DMA((2, 4)), DMA((2, 4)), DMA((2,)),
            like(came_up), like(came_up), like(came_up), pltpu.VMEM((g_up.shape[0] // 4, g_up.shape[1]), BF16),
            like(came_down), like(came_down), like(came_down), pltpu.VMEM((g_down.shape[0] // 4, g_down.shape[1]), BF16),
            DMA((2, 2)), DMA((2, 2)), DMA((2, 5)),
            pltpu.VMEM((MAIN, 128), BF16), pltpu.VMEM((3, MAIN, 128), BF16), DMA((3,)), DMA((3,)),
            *flow_scratch(2 * model), *flow_scratch(model), *flow_scratch(896),
            pltpu.VMEM((1, model), F32),
        ],
        compiler_params=pltpu.CompilerParams(
            collective_id=5, has_side_effects=True, vmem_limit_bytes=62 << 20
        ),
        name="mixer_backward",
    )(
        grad_hidden, seq, whole, gains, norm_in, normed, x_low, u, gate_z, proj, dt_lin, y, gated, starts, params, extra,
        g_up, g_down, came_up, came_down,
    )


def finish_kernel(
    channel, feature, result_in, tokens_in, in_in, out_in, x_in, dt_in, up_in, down_in,
    result, tokens, grad_in, grad_out, grad_x, grad_dt, decay, taps, conv_bias, dt_bias, skip, gain_one, gain_two, router, up,
    down, low_up, low_down, high_up, high_down, sems,
):
    loads = []
    for n, (a, b) in enumerate(((up_in, low_up), (down_in, low_down))):
        size = a.shape[0] // 4
        loads.append([])
        for q in range(4):
            rows = pl.ds(q * size, size)
            copy = pltpu.make_async_copy(a.at[rows, :], b.at[rows, :], sems.at[n, q])
            copy.start()
            loads[n].append(copy)
    stores = []
    straight = ((result_in, result), (tokens_in, tokens), (in_in, grad_in), (out_in, grad_out), (x_in, grad_x), (dt_in, grad_dt))
    for a, b in straight:
        b[...] = a[...]
    lines = channel[...]
    decay[...] = lines[0:16]
    taps[...] = lines[16:20]
    conv_bias[...] = lines[20:21]
    dt_bias[...] = lines[21:22]
    skip[...] = lines[22:23]
    lines = feature[...]
    gain_one[...] = lines[0:1]
    gain_two[...] = lines[1:2]
    router[...] = lines[2:10]
    for q in range(4):
        for n, (a, b, c) in enumerate(((low_up, high_up, up), (low_down, high_down, down))):
            size = a.shape[0] // 4
            rows = pl.ds(q * size, size)
            loads[n][q].wait()
            b[rows, :] = a[rows, :].astype(F32)
            copy = pltpu.make_async_copy(b.at[rows, :], c.at[rows, :], sems.at[2 + n, q])
            copy.start()
            stores.append(copy)
    for copy in stores:
        copy.wait()


def finished(output, tokens, grad_in, grad_out, grad_x, grad_dt, channel, feature, low_up, low_down):
    S, own, share = jax.ShapeDtypeStruct, channel.shape[1], feature.shape[1]
    straight = (output, tokens, grad_in, grad_out, grad_x, grad_dt)
    outs = [S(a.shape, a.dtype) for a in straight]
    outs += [S((n, own), F32) for n in (16, 4, 1, 1, 1)] + [S((n, share), F32) for n in (1, 1, 8)]
    outs += [S(low_up.shape, F32), S(low_down.shape, F32)]
    return pl.pallas_call(
        finish_kernel,
        out_shape=outs,
        in_specs=[IN_VMEM] * 8 + [ANY] * 2,
        out_specs=[IN_VMEM] * 14 + [ANY] * 2,
        scratch_shapes=[
            pltpu.VMEM(low_up.shape, BF16), pltpu.VMEM(low_down.shape, BF16), pltpu.VMEM(low_up.shape, F32),
            pltpu.VMEM(low_down.shape, F32), DMA((4, 4)),
        ],
        compiler_params=pltpu.CompilerParams(vmem_limit_bytes=62 << 20),
        name="finish",
    )(channel, feature, *straight, low_up, low_down)


def shards(
    tokens, resets, routes, cotangent, mixer_gain, in_proj, conv_kernel, conv_bias, x_proj, dt_proj,
    dt_bias, log_decay, skip_gain, out_proj, moe_gain, router, up_proj, down_proj,
):
    model, own, experts = tokens.shape[1], conv_bias.shape[0], router.shape[1]
    rank, states = dt_proj.shape[0], log_decay.shape[0]
    inner = lax.axis_size("expert") * lax.axis_size("rows") * own
    in_lines = in_proj.transpose(2, 1, 0)
    route_row = routes.reshape(1, -1)
    arrays = (
        in_lines[:, 0], in_lines[:, 1], out_proj, x_proj.T, dt_proj.T, log_decay, conv_kernel, conv_bias[None],
        dt_bias[None], skip_gain[None], mixer_gain[None], moe_gain[None], router.T, tokens, resets[None], route_row,
        cotangent,
    )
    whole, sequence, extra, *saved, hidden_one, params, gains, slots, moe_low, probs = mixer_forward(
        arrays, inner, states, experts
    )
    output, grad_hidden, norm_grads, *expert_grads = experts_both_ways(
        slots, up_proj[0], down_proj[0], hidden_one, cotangent, moe_low, probs, route_row, gains
    )
    results = mixer_backward(
        grad_hidden, sequence, whole, gains, norm_grads, (*saved, params, extra), expert_grads, own,
        rank + 2 * states, rank,
    )
    (
        output, grad_tokens, grad_in, grad_out, grad_x, grad_dt, grad_decay, grad_taps, grad_conv_bias, grad_dt_bias,
        grad_skip, grad_gain_one, grad_gain_two, grad_router, grad_up_sum, grad_down_sum,
    ) = finished(output, *results)
    return (
        output,
        grad_tokens,
        grad_gain_one[0],
        grad_in.transpose(2, 1, 0),
        grad_taps,
        grad_conv_bias[0],
        grad_x.T,
        grad_dt.T,
        grad_dt_bias[0],
        grad_decay,
        grad_skip[0],
        grad_out,
        grad_gain_two[0],
        grad_router.T,
        grad_up_sum[None],
        grad_down_sum[None],
    )


def solution(mesh):
    every = ("expert", "rows", "hid")
    in_specs = (
        P(every, None), P(every), P(every, None), P(every, None), P(every), P(None, None, every),
        P(None, every), P(every), P(None, every), P(None, every), P(every), P(None, every), P(every),
        P(every, None), P(every), P(every, None), P("expert", None, "hid"), P("expert", "hid", None),
    )
    out_specs = (
        P(every, None), P(every, None), P(every), P(None, None, every), P(None, every), P(every),
        P(None, every), P(None, every), P(every), P(None, every), P(every), P(every, None), P(every),
        P(every, None), P("expert", None, "hid"), P("expert", "hid", None),
    )
    return jax.shard_map(shards, mesh=mesh, in_specs=in_specs, out_specs=out_specs, check_vma=False)
```

```python
from functools import partial

import jax
import jax.numpy as jnp
from jax import lax
from jax.experimental import pallas as pl
from jax.experimental.pallas import tpu as pltpu
from jax.sharding import PartitionSpec as P

EPS = 1e-05
LOG2E = 1.4426950408889634
STOP = 1e6
STEP = 16
FORWARD_SCRATCH = 49
MAIN = 16
EXTRA = 512
GELU_C = 0.7978845608028654
F32 = jnp.float32
BF16 = jnp.bfloat16


def matmul(first_op, second_op):
    return jnp.dot(first_op, second_op, preferred_element_type=F32)


def inner_rows(first_op, second_op):
    return lax.dot_general(
        first_op, second_op, (((0,), (0,)), ((), ())), preferred_element_type=F32
    )


def outer_cols(first_op, second_op):
    return lax.dot_general(
        first_op, second_op, (((1,), (1,)), ((), ())), preferred_element_type=F32
    )


def rms_norm(values, gain):
    return values * lax.rsqrt(jnp.mean(values * values, axis=-1, keepdims=True) + EPS) * gain


def over_lanes(v):
    whole = v.shape[1] // 128
    total = v[:, :128]
    for k in range(1, whole):
        total = total + v[:, k * 128 : (k + 1) * 128]
    rest = v.shape[1] - whole * 128
    if rest:
        blank = jnp.zeros((v.shape[0], 128 - rest), F32)
        total = total + jnp.concatenate([v[:, whole * 128 :], blank], axis=1)
    return total


MESH = pl.DeviceIdType.MESH
ANY = pl.BlockSpec(memory_space=pl.ANY)
IN_VMEM = pl.BlockSpec(memory_space=pltpu.VMEM)
DMA = pltpu.SemaphoreType.DMA


def put_rows(parts, j, values):
    count, width = values.shape
    for k in range(parts.shape[0]):
        size = min(128, width - 128 * k)
        parts[k, j * count : (j + 1) * count, :size] = values[:, 128 * k : 128 * k + size]


def summed_groups(parts, count, width):
    groups = parts.shape[1] // count
    columns = []
    for k in range(parts.shape[0]):
        total = parts[k, pl.ds(0, groups, stride=count), :]
        for n in range(1, count):
            total = total + parts[k, pl.ds(n, groups, stride=count), :]
        columns.append(total[:, : min(128, width - 128 * k)])
    return jnp.concatenate(columns, axis=1)


def places():
    return lax.axis_index("expert"), lax.axis_index("rows"), lax.axis_index("hid")


def hail(peers):
    barrier = pltpu.get_barrier_semaphore()
    for peer in peers:
        pl.semaphore_signal(barrier, inc=1, device_id=peer, device_id_type=MESH)


def greet(peers):
    hail(peers)
    pl.semaphore_wait(pltpu.get_barrier_semaphore(), len(peers))


def remote(src, dst, send_sem, recv_sem, peer):
    return pltpu.make_async_remote_copy(
        src_ref=src, dst_ref=dst, send_sem=send_sem, recv_sem=recv_sem, device_id=peer,
        device_id_type=MESH,
    )


def hid_peers():
    e, r, h = places()
    return [(e, r, lax.rem(h + k, 4)) for k in (1, 2, 3)]


def mixer_peers(turn=None):
    e, r, h = places()
    c = lax.rem(e, 2)
    t = c if turn is None else turn
    mate = (e + 1 - 2 * c, r, h)
    first = [(lax.rem(e + 2 * k * (1 - t), 8), lax.rem(r + k * t, 4), h) for k in (1, 2, 3)]
    second = [(lax.rem(e + 2 * k * t, 8), lax.rem(r + k * (1 - t), 4), h) for k in (1, 2, 3)]
    return mate, first, second


def block_at(c, f, s, turn=None):
    t = c if turn is None else turn
    y = f * (1 - t) + s * t
    x = s * (1 - t) + f * t
    return (2 * y + c) * 4 + x


class RowsPlace:
    def __init__(self, size):
        e, r, h = places()
        self.r, self.size = r, size
        self.right, self.left, self.across = lax.rem(r + 1, 4), lax.rem(r + 3, 4), lax.rem(r + 2, 4)
        self.to_right, self.to_left = (e, self.right, h), (e, self.left, h)

    def rows(self, quarter, part, parts=1):
        return pl.ds(pl.multiple_of((2 * quarter + part) * self.size, self.size), parts * self.size)


class RowsSpread(RowsPlace):
    def __init__(self, source, slots, send, recv):
        super().__init__(slots.shape[1])
        self.source, self.slots, self.send, self.recv = source, slots, send, recv

    def copy(self, n):
        plan = (
            (self.across, 0, 0, self.to_right),
            (self.across, 1, 1, self.to_left),
            (self.right, 1, 2, self.to_right),
            (self.left, 0, 3, self.to_left),
        )
        quarter, half, at, peer = plan[n]
        part = self.source.at[self.rows(quarter, half)]
        return remote(part, self.slots.at[at], self.send.at[n], self.recv.at[n], peer)

    def begin(self):
        for n in range(4):
            self.copy(n).start()

    def end(self):
        for n in range(4):
            self.copy(n).wait_recv()
            self.copy(n).wait_send()


class RowsSum(RowsPlace):
    def __init__(self, source, came, slots, own, sums, total, send, recv, local):
        super().__init__(sums.shape[1])
        self.source, self.came, self.slots, self.own, self.sums, self.total = source, came, slots, own, sums, total
        self.send, self.recv, self.local = send, recv, local

    def load(self, n):
        if n == 4:
            return pltpu.make_async_copy(self.came, self.slots, self.local.at[4])
        quarter, half = ((self.right, 0), (self.left, 1), (self.r, 0), (self.r, 1))[n]
        return pltpu.make_async_copy(self.source.at[self.rows(quarter, half)], self.own.at[n], self.local.at[n])

    def copy(self, n):
        return remote(
            self.sums.at[n], self.sums.at[2 + n], self.send.at[n], self.recv.at[n], (self.to_right, self.to_left)[n]
        )

    def pass_on(self):
        for n in (4, 0, 1):
            self.load(n).wait()
        for n in (0, 1):
            self.sums[n] = (self.slots[n].astype(F32) + self.own[n].astype(F32)).astype(BF16)
            self.copy(n).start()

    def finish(self):
        for n in (2, 3):
            self.load(n).wait()
        for n in (0, 1):
            self.copy(n).wait_recv()
            total = (
                self.own[2 + n].astype(F32) + self.slots[3 - n].astype(F32) + self.sums[2 + n].astype(F32)
            )
            self.total[n * self.size : (n + 1) * self.size, :] = total.astype(BF16)

    def end(self):
        for n in (0, 1):
            self.copy(n).wait_send()


class RowsGather(RowsPlace):
    def __init__(self, quarter, target, send, recv, local):
        super().__init__(quarter.shape[0] // 2)
        self.quarter, self.target, self.send, self.recv, self.local = quarter, target, send, recv, local

    def copy(self, n):
        out = self.target
        plan = (
            (lambda: self.quarter, self.rows(self.r, 0, 2), self.to_right),
            (lambda: self.quarter, self.rows(self.r, 0, 2), self.to_left),
            (lambda: out.at[self.rows(self.left, 0)], self.rows(self.left, 0), self.to_right),
            (lambda: out.at[self.rows(self.right, 1)], self.rows(self.right, 1), self.to_left),
        )
        part, rows, peer = plan[n]
        return remote(part(), out.at[rows], self.send.at[n], self.recv.at[n], peer)

    def own(self):
        return pltpu.make_async_copy(self.quarter, self.target.at[self.rows(self.r, 0, 2)], self.local)

    def begin(self):
        for n in (0, 1):
            self.copy(n).start()
        self.own().start()

    def forward(self):
        for n in (0, 1):
            self.copy(n).wait_recv()
            self.copy(2 + n).start()

    def end(self):
        for n in (2, 3):
            self.copy(n).wait_recv()
        self.own().wait()
        for n in range(4):
            self.copy(n).wait_send()


def gelu_pair(pre, grad):
    square = pre * pre
    t = jnp.tanh(GELU_C * pre * (1.0 + 0.044715 * square))
    up = 0.5 * (1.0 + t)
    slope = up + 0.5 * pre * (1.0 - t * t) * (GELU_C * (1.0 + 3 * 0.044715 * square))
    return pre * up, slope * grad


def expert_part(refs):
    (
        slots, up_in, down_in, hid_in, cotangent, moe_low, probs, routes, gains, output, grad_hidden, norm_out,
        up_out, down_out, ring_up, ring_down, g_up, g_down, up, down, m_sems, x_send, x_recv, back, held, results,
        hid_out, pre_out, hid_w, pre_w, from_left, from_right, half_left, half_right, sums, d_send, d_recv, r_send,
        r_recv, l_send, l_recv, f_send, f_recv, c_send, c_recv, k_send, k_recv, h_send, h_recv, b_send, b_recv,
    ) = refs
    e, r, h = places()
    moves = (
        (up_in, up), (down_in, down), (g_up, up_out), (g_down, down_out),
    )
    moves = [pltpu.make_async_copy(a, b, m_sems.at[n]) for n, (a, b) in enumerate(moves)]
    for move in moves[:2]:
        move.start()
    model, hidden = up.shape
    right, left, across = lax.rem(h + 1, 4), lax.rem(h + 3, 4), lax.rem(h + 2, 4)
    to_right, to_left = (e, r, right), (e, r, left)
    y, c = e // 2, lax.rem(e, 2)
    target = [2 * lax.rem(y + k // 2, 4) + lax.rem(c + k, 2) for k in range(8)]
    source = [2 * lax.rem(y + 4 - k // 2, 4) + lax.rem(c + k, 2) for k in range(8)]
    to_expert = [(one, r, h) for one in target]
    to_source = [(one, r, h) for one in source]
    via_right, via_left = (4, 3, 2, 0), (5, 7, 6, 1)
    sums_up = RowsSpread(g_up, ring_up, x_send.at[0], x_recv.at[0])
    sums_down = RowsSpread(g_down, ring_down, x_send.at[1], x_recv.at[1])

    held[h, e] = slots[e]
    d_copies = [None] * 8
    for n in (1, 2, 6, 3, 7, 4, 5):
        d_copies[n] = remote(slots.at[target[n]], held.at[h, e], d_send.at[n], d_recv.at[n], to_expert[n])
        d_copies[n].start()

    def along(buf, where, k, send, recv, peer):
        block = buf.at[where, source[k]]
        copy = remote(block, block, send.at[k], recv.at[k], peer)
        copy.start()
        return copy

    r_copies, l_copies = [None] * 8, [None] * 8
    for n in (0, 1, 2, 6, 3, 7, 4, 5):
        if n:
            d_copies[n].wait_recv()
        r_copies[n] = along(held, h, n, r_send, r_recv, to_right)
        l_copies[n] = along(held, h, n, l_send, l_recv, to_left)

    half = 128

    def worked(where):
        lines = held[where]
        main_x = lines[:, :, :model].reshape(half, model)
        main_g = lines[:, :, model : 2 * model].reshape(half, model)
        extra = lines[:, :, 2 * model :].reshape(half, model)
        rows_x = jnp.concatenate([main_x, extra], axis=0)
        rows_g = jnp.concatenate([main_g, extra], axis=0)

        def first_layer(i, carry):
            cols = pl.ds(pl.multiple_of(i * 256, 256), 256)
            pre = matmul(rows_x, up[:, cols])
            grad = outer_cols(rows_g, down[cols, :])
            hid_m, pre_m = gelu_pair(pre[:half], grad[:half])
            pre_e = pre[half:].reshape(8, 2, 8, 256)[:, 0]
            grad_e = grad[half:].reshape(8, 2, 8, 256)[:, 1]
            hid_e, gpre_e = gelu_pair(pre_e, grad_e)
            none = jnp.zeros_like(hid_e)

            def stacked(a, b):
                return jnp.stack([a, b], axis=1).reshape(half, 256).astype(BF16)

            hid_m, pre_m = hid_m.astype(BF16), pre_m.astype(BF16)
            hid_out[:half, cols] = hid_m
            pre_out[:half, cols] = pre_m
            hid_w[where, :half, cols] = hid_m
            pre_w[where, :half, cols] = pre_m
            hid_out[half:, cols] = stacked(hid_e, none)
            pre_out[half:, cols] = stacked(none, gpre_e)
            hid_w[where, half:, cols] = stacked(none, hid_e)
            pre_w[where, half:, cols] = stacked(gpre_e, none)
            return carry

        lax.fori_loop(0, hidden // 256, first_layer, 0)

        def second_layer(i, carry):
            at = pl.multiple_of(i * 384, 384)
            cols = pl.ds(at, 384)
            share = matmul(hid_out[...], down[:, cols])
            grad = outer_cols(pre_out[...], up[cols, :])
            shape = (8, 16, 384)
            results[where, :, :, cols] = share[:half].astype(BF16).reshape(shape)
            results[where, :, :, pl.ds(model + at, 384)] = grad[:half].astype(BF16).reshape(shape)
            results[where, :, :, pl.ds(2 * model + at, 384)] = (share[half:] + grad[half:]).astype(BF16).reshape(shape)
            return carry

        lax.fori_loop(0, model // 384, second_layer, 0)

    moves[0].wait()
    moves[1].wait()
    worked(h)
    f_copies = [None] * 8
    for a, b in ((0, 1), (2, 6), (3, 7), (4, 5)):
        r_copies[a].wait_recv()
        f_copies[a] = along(held, left, a, f_send, f_recv, to_right)
        l_copies[b].wait_recv()
        f_copies[b] = along(held, right, b, f_send, f_recv, to_left)
    for n in via_left:
        r_copies[n].wait_recv()
    worked(left)
    c_copies = [None] * 8
    k_copies = [None] * 8

    def toward_right(n):
        block = results.at[right, source[n]]
        c_copies[n] = remote(block, from_left.at[n], c_send.at[n], c_recv.at[n], to_right)
        c_copies[n].start()

    def toward_left(n):
        block = results.at[left, source[n]]
        k_copies[n] = remote(block, from_right.at[n], k_send.at[n], k_recv.at[n], to_left)
        k_copies[n].start()

    for n in via_right:
        toward_left(n)
    for n in via_right:
        l_copies[n].wait_recv()
    worked(right)
    for n in via_left:
        toward_right(n)
    for n in range(8):
        f_copies[n].wait_recv()
    worked(across)
    h_copies = [None] * 8
    for at in range(4):
        for n, landing, peer in ((via_right[at], half_left, to_right), (via_left[at], half_right, to_left)):
            block = results.at[across, source[n]]
            h_copies[n] = remote(block, landing.at[at], h_send.at[n], h_recv.at[n], peer)
            h_copies[n].start()

    def weight_grads(i, carry):
        cols = pl.ds(pl.multiple_of(i * 128, 128), 128)
        total = jnp.zeros((128, hidden), F32)
        for lanes, kept, out in ((0, pre_w, g_up),):
            x_main = held[:, :, :, pl.ds(pl.multiple_of(i * 128, 128), 128)].reshape(4, half, 128)
            x_extra = held[:, :, :, pl.ds(pl.multiple_of(2 * model + i * 128, 128), 128)].reshape(4, half, 128)
            rows = jnp.concatenate([x_main, x_extra], axis=1).reshape(8 * half, 128)
            total = inner_rows(rows, kept[...].reshape(8 * half, hidden))
            out[cols, :] = total.astype(BF16)
        g_main = held[:, :, :, pl.ds(pl.multiple_of(model + i * 128, 128), 128)].reshape(4, half, 128)
        rows = jnp.concatenate([g_main, x_extra], axis=1).reshape(8 * half, 128)
        g_down[:, cols] = inner_rows(hid_w[...].reshape(8 * half, hidden), rows).astype(BF16)
        return carry

    lax.fori_loop(0, model // 128, weight_grads, 0)

    for ring in (sums_up, sums_down):
        ring.begin()
    moves[2].start()
    moves[3].start()
    for at in range(4):
        n = via_right[at]
        h_copies[n].wait_recv()
        results[right, source[n]] = (results[right, source[n]].astype(F32) + half_left[at].astype(F32)).astype(BF16)
        toward_right(n)
        n = via_left[at]
        h_copies[n].wait_recv()
        results[left, source[n]] = (results[left, source[n]].astype(F32) + half_right[at].astype(F32)).astype(BF16)
        toward_left(n)
    b_copies = []
    for n in (4, 5, 3, 7, 2, 6, 1, 0):
        c_copies[n].wait_recv()
        k_copies[n].wait_recv()
        total = results[h, source[n]].astype(F32) + from_left[n].astype(F32) + from_right[n].astype(F32)
        if n:
            sums[n] = total.astype(BF16)
            copy = remote(sums.at[n], back.at[e], b_send.at[n], b_recv.at[n], to_source[n])
            copy.start()
            b_copies.append(copy)
        else:
            back[e] = total.astype(BF16)
    for copy in b_copies:
        copy.wait_recv()
    main, top, low_half, onehot = slot_picks(routes[...], slots.shape[0])
    lines = back[...].reshape(128, 3 * model)
    shares = probs[...]
    gate = jnp.sum(shares * onehot, axis=-1, keepdims=True)
    hid, grad_output, low = hid_in[...], cotangent[...].astype(F32), moe_low[...]
    expert_out = inner_rows(main, lines[:, :model]) + inner_rows(top, lines[:, 2 * model :])
    output[...] = (hid + gate * expert_out).astype(BF16)
    grad_gate = jnp.sum(grad_output * expert_out, axis=-1, keepdims=True)
    grad_logits = (gate * grad_gate * (onehot - shares)).astype(BF16)
    grad_moe = inner_rows(main, lines[:, model : 2 * model]) + inner_rows(low_half, lines[:, 2 * model :])
    grad_moe = grad_moe + matmul(grad_logits, gains[...].astype(BF16))
    scale = lax.rsqrt(jnp.mean(hid * hid, axis=-1, keepdims=True) + EPS)
    scaled = grad_moe * gains[1:2, :]
    inside = jnp.mean(scaled * hid, axis=-1, keepdims=True)
    grad_hidden[...] = grad_output + scale * scaled - hid * (scale * scale * scale * inside)
    grad_gain = jnp.sum(grad_moe * hid * scale, axis=0, keepdims=True)
    at = lax.broadcasted_iota(jnp.int32, norm_out.shape, 0)
    norm_out[...] = inner_rows(grad_logits, low) + jnp.where(at == 1, grad_gain, 0.0)
    for ring in (sums_up, sums_down):
        ring.end()
    moves[2].wait()
    moves[3].wait()
    for copy in d_copies[1:] + r_copies + l_copies + f_copies + c_copies + k_copies + h_copies + b_copies:
        copy.wait_send()


def across(tile, width):
    whole = width // 128
    return jnp.concatenate([tile] * whole + [tile[:, : width - 128 * whole]], axis=1)


def eye(size):
    at = [lax.broadcasted_iota(jnp.int32, (size, size), axis) for axis in (0, 1)]
    return (at[0] == at[1]).astype(BF16)


def both_cols(lines, main, extra):
    return jnp.concatenate([outer_cols(lines, main), outer_cols(lines, extra)], axis=1)


class Gather:
    def __init__(self, source, place, send, recv):
        self.source, self.place, self.send, self.recv = source, place, send, recv
        e, r, h = places()
        self.c = lax.rem(e, 2)
        y = e // 2
        self.f0 = y * (1 - self.c) + r * self.c
        self.s0 = r * (1 - self.c) + y * self.c
        self.own = e * 4 + r
        self.mate, self.first, self.second = mixer_peers()

    def copy(self, at, peer, block=None):
        target = self.place(self.own if block is None else block)
        return remote(self.source if block is None else target, target, self.send.at[at], self.recv.at[at], peer)

    def came(self, k, j=None):
        s = self.s0 if j is None else lax.rem(self.s0 + 3 - j, 4)
        return block_at(self.c, lax.rem(self.f0 + 4 - k, 4), s)

    def begin(self):
        for k in (1, 0, 2):
            self.copy(k, self.first[k]).start()

    def begin_second(self):
        for j in (1, 0, 2):
            self.copy(3 + j, self.second[j]).start()
        self.copy(15, self.mate).start()

    def relay_first(self):
        for k in range(3):
            self.copy(k, self.first[k]).wait_recv()
            block = self.came(k + 1)
            for j in (1, 0, 2):
                self.copy(6 + 3 * k + j, self.second[j], block).start()
            self.copy(16 + k, self.mate, block).start()

    def relay_second(self):
        for k in range(4):
            for j in range(3):
                self.copy(3 + 3 * k + j, self.second[j]).wait_recv()
                self.copy(19 + 3 * k + j, self.mate, self.came(k, j)).start()

    def end(self):
        for at in range(15, 31):
            self.copy(at, self.mate).wait_recv()

    def sent(self):
        for at in range(31):
            self.copy(at, self.mate).wait_send()


def slot_picks(route, experts, states=16):
    count = route.shape[1]
    line = lax.broadcasted_iota(jnp.int32, (states, count), 0)
    chosen = jnp.where(line - 2 == route, 1.0, 0.0)
    earlier = lax.broadcasted_iota(jnp.int32, (count, count), 0) <= lax.broadcasted_iota(jnp.int32, (count, count), 1)
    counts = matmul(chosen.astype(BF16), jnp.where(earlier, 1.0, 0.0).astype(BF16))
    within = jnp.sum(chosen * (counts - 1.0), axis=0, keepdims=True).astype(jnp.int32)
    slot = lax.broadcasted_iota(jnp.int32, (experts * MAIN, count), 0)
    line, expert = slot % MAIN, slot // MAIN
    here = expert == route

    def of(found):
        return jnp.where(found, 1.0, 0.0).astype(BF16)

    main = of(here & (within == line))
    top = of(here & (line < 8) & (within == line + 16))
    low = of(here & (line >= 8) & (within == line + 8))
    column = jnp.broadcast_to(route.astype(F32), (count, count)).T[:, :states]
    place = lax.broadcasted_iota(jnp.int32, (count, states), 1) - 2
    onehot = jnp.where(place.astype(F32) == column, 1.0, 0.0)
    return main, top, low, onehot


def other_core_peers():
    e, r, h = places()
    c = lax.rem(e, 2)
    return [(2 * lax.rem(e // 2 + k, 4) + 1 - c, r, h) for k in (1, 2, 3)]


def forward_part(refs):
    (
        in_lines, out_lines, x_cols, dt_cols, decay_in, taps_in, conv_bias, dt_bias, skip, gain_one, gain_two,
        router, tokens, resets, routes, cotangent,
        whole_hbm, seq_hbm, extra_hbm, normed_hbm, x_low_hbm, u_hbm, gate_hbm, proj_hbm, lin_hbm, y_hbm, gated_hbm,
        starts_hbm, params, gains, hidden, slots, moe_out, probs,
        pack, norm, line, whole_all, norms, seq, extra, tiles, total, local_sems, z_send, z_recv, n_send, n_recv,
        w_send, w_recv, v_send, v_recv, o_send, o_recv, k_sems, s_sems,
        normed, x_low, u_out, gate_z, proj, dt_lin, y_out, gated, starts,
        xs, marks, conv, dtm, dtx, parts, own, landing, branch, came, p_send, p_recv, b_send, b_recv, quarters, owned, q_send, q_recv,
    ) = refs
    e, r, h = places()
    block, model = tokens.shape
    inner, states, experts = u_out.shape[1], starts.shape[1], router.shape[0]
    lines, small = block // STEP, 3 * model
    channels, share = in_lines.shape[0], gain_one.shape[1]

    z_peers = hid_peers()
    mate, first, second = mixer_peers()
    hail([mate] + first + second + z_peers + other_core_peers())

    def wide(a):
        return a[...].astype(F32)

    line[:, :model] = tokens[...]
    line[:, model:] = jnp.broadcast_to(wide(resets), (block, 128)).T.astype(BF16)
    columns = jnp.concatenate(
        [
            wide(decay_in), wide(taps_in), wide(conv_bias), wide(dt_bias), wide(skip),
            jnp.zeros((105, channels), F32),
        ],
        axis=0,
    )
    columns = jnp.concatenate([columns, jnp.zeros((128, 128 - channels), F32)], axis=1).T[:channels, :24]
    tail = jnp.concatenate(
        [
            jnp.concatenate([wide(x_cols), columns], axis=1),
            jnp.concatenate([wide(dt_cols), jnp.zeros((channels, 128 - dt_cols.shape[1]), F32)], axis=1),
        ],
        axis=1,
    )
    in_float = wide(in_lines)
    both = jnp.concatenate([in_float[:, 0], in_float[:, 1], wide(out_lines), tail], axis=1)
    pack[:, : 2 * model] = both[:MAIN, : 2 * model].astype(BF16)
    pack[:, 2 * model : 2 * model + 256] = both[:MAIN, small:].astype(BF16)
    pack[:, 2 * model + 768 :] = both[:MAIN, 2 * model : small].astype(BF16)
    last = jnp.concatenate([both[MAIN:], jnp.zeros((channels - MAIN, 4096 - small - 256), F32)], axis=1)
    last = [last[n : n + 1, k * EXTRA : (k + 1) * EXTRA] for n in range(2) for k in range(8)]
    pack[:, 2 * model + 256 : 2 * model + 768] = jnp.concatenate(last, axis=0).astype(BF16)
    tile = jnp.concatenate([wide(gain_one), wide(gain_two), wide(router), jnp.zeros((6, share), F32)], axis=0)
    tile = jnp.concatenate([tile, jnp.zeros((MAIN, 128 - share), F32)], axis=1)
    norm[...] = pltpu.roll(tile, h * share, 1).astype(BF16)
    pl.semaphore_wait(pltpu.get_barrier_semaphore(), 13)
    mine = pl.ds(pl.multiple_of(h * block, block), block)
    late = 2 * model + 768

    def owner_rows(n):
        return pl.ds(pl.multiple_of(n * MAIN, MAIN), MAIN)

    main = Gather(pack.at[:, :late], lambda n: whole_all.at[owner_rows(n), :late], w_send, w_recv)
    out_part = Gather(pack.at[:, late:], lambda n: whole_all.at[owner_rows(n), late:], o_send, o_recv)
    norm_part = Gather(total, lambda n: norms.at[n], v_send, v_recv)
    n_copies = [remote(norm, tiles.at[k], n_send.at[k], n_recv.at[k], z_peers[k]) for k in range(3)]
    z_copies = [remote(line, seq.at[mine], z_send.at[k], z_recv.at[k], z_peers[k]) for k in range(3)]
    own_copies = [
        pltpu.make_async_copy(pack, whole_all.at[owner_rows(main.own)], local_sems.at[0]),
        pltpu.make_async_copy(line, seq.at[mine], local_sems.at[1]),
    ]
    for copy in n_copies:
        copy.start()
    main.begin()
    main.begin_second()
    for n in (1, 0, 2):
        z_copies[n].start()
    for copy in own_copies:
        copy.start()
    for copy in n_copies:
        copy.wait_recv()
    total[...] = norm[...] + tiles[0] + tiles[1] + tiles[2]
    norms[main.own] = total[...]
    norm_part.begin()
    norm_part.begin_second()
    main.relay_first()
    norm_part.relay_first()
    out_part.begin()
    main.relay_second()
    norm_part.relay_second()
    out_part.begin_second()
    out_part.relay_first()
    norm_part.end()
    span = share * 4
    gains[...] = jnp.concatenate([norms[n].astype(F32)[:, :span] for n in range(32)], axis=1)
    for copy in z_copies:
        copy.wait_recv()
    for copy in own_copies:
        copy.wait()
    main.end()
    row = lax.broadcasted_iota(jnp.int32, (512, 512), 0)
    col = lax.broadcasted_iota(jnp.int32, (512, 512), 1)
    wanted = (row % 64 // 2) * MAIN + (row % 2) * 8 + row // 64
    moved = matmul((wanted == col).astype(BF16), whole_all[:, 2 * model + 256 : late]).astype(BF16)
    for k in range(8):
        extra[:, k * 512 : (k + 1) * 512] = moved[k * 64 : (k + 1) * 64]
    params[...] = both_cols(eye(128), whole_all[:, 2 * model : 2 * model + 128], extra[:, small : small + 128])
    kept_copies = [
        pltpu.make_async_copy(kept, out, k_sems.at[n])
        for n, (kept, out) in enumerate(((whole_all, whole_hbm), (seq, seq_hbm), (extra, extra_hbm)))
    ]
    for copy in kept_copies[1:]:
        copy.start()
    xs[0:8] = jnp.zeros((8, inner), F32)
    marks[0:8] = jnp.zeros((8, 128), F32)
    gain = gains[0:1, :]

    pairs = (
        (normed, normed_hbm), (x_low, x_low_hbm), (u_out, u_hbm), (gate_z, gate_hbm), (proj, proj_hbm),
        (dt_lin, lin_hbm), (y_out, y_hbm), (gated, gated_hbm), (starts, starts_hbm),
    )

    def saved_copy(n, b):
        kept, out = pairs[n]
        size = kept.shape[0] // 4
        rows = pl.ds(pl.multiple_of(b * size, size), size)
        return pltpu.make_async_copy(kept.at[rows], out.at[rows], s_sems.at[n, b])

    def proj_copy(b, k):
        at = k * 4 + b
        return remote(own.at[b], landing.at[k, b], p_send.at[at], p_recv.at[at], z_peers[k])

    def stage_one(b, carry):
        start = pl.multiple_of(b * block, block)
        rows = pl.ds(start, block)
        values = seq[rows, :model].astype(F32)
        scale = lax.rsqrt(jnp.mean(values * values, axis=-1, keepdims=True) + EPS)
        low = (values * scale * gain).astype(BF16)
        normed[rows, :] = low
        gate_z[rows, :] = both_cols(low, whole_all[:, model : 2 * model], extra[:, model : 2 * model])
        x = both_cols(low, whole_all[:, :model], extra[:, :model]).astype(BF16)
        x_low[rows, :] = x
        after = pl.ds(pl.multiple_of(8 + start, 8), block)
        xs[after, :] = x.astype(F32)
        now = seq[rows, model:].astype(F32)
        marks[after, :] = now
        lines_x, lines_m = xs[pl.ds(start, block + 8), :], marks[pl.ds(start, block + 8), :]
        mask = 1.0 - now
        total = params[124:125, :] + params[123:124, :] * x.astype(F32)
        for back in (1, 2, 3):
            past = lines_x[8 - back : 8 - back + block]
            total = total + params[123 - back : 124 - back, :] * past * across(mask, inner)
            if back < 3:
                mask = mask * (1.0 - lines_m[8 - back : 8 - back + block])
        u_out[rows, :] = total
        convolved = total * jax.nn.sigmoid(total)
        conv[rows, :] = convolved
        conv_low = convolved.astype(BF16)
        share = matmul(conv_low[:, :512], whole_all[:, 2 * model : 2 * model + 128]) + matmul(
            conv_low[:, 512:], extra[:, small : small + 128]
        )
        own[b] = share.astype(BF16)
        for k in (1, 0, 2):
            proj_copy(b, k).start()
        for n in range(4):
            saved_copy(n, b).start()
        return carry

    lax.fori_loop(0, 4, stage_one, 0)
    out_part.relay_second()
    out_part.end()
    kept_copies[0].start()
    a = jnp.exp(params[104:120, :]) * (-LOG2E)
    half = states // 2

    quarter = block // 4

    def part_copy(b, k):
        rows = pl.ds(pl.multiple_of(lax.rem(h + 1 + k, 4) * quarter, quarter), quarter)
        at = k * 4 + b
        return remote(branch.at[b, rows], came.at[k, b], b_send.at[at], b_recv.at[at], z_peers[k])

    def whole_copy(b, sender):
        return remote(quarters.at[b], owned.at[sender], q_send.at[b], q_recv.at[sender], (e, r, b))

    def sum_up(b):
        rows = pl.ds(pl.multiple_of(h * quarter, quarter), quarter)
        for k in range(3):
            part_copy(b, k).wait_recv()
        total = branch[b, rows, :].astype(F32)
        for k in range(3):
            total = total + came[k, b].astype(F32)
        quarters[b] = total.astype(BF16)

        @pl.when(b != h)
        def send():
            whole_copy(b, lax.rem(h - b + 4, 4) - 1).start()

    def stage_two(b, state):
        start = pl.multiple_of(b * block, block)
        rows = pl.ds(start, block)
        for k in range(3):
            proj_copy(b, k).wait_recv()
        sums = (
            own[b].astype(F32) + landing[0, b].astype(F32) + landing[1, b].astype(F32) + landing[2, b].astype(F32)
        )
        proj[rows, :] = sums
        lin = both_cols(sums.astype(BF16), whole_all[:, 2 * model + 128 : 2 * model + 256], extra[:, small + 128 : small + 256])
        lin = lin + params[125:126, :]
        dt_lin[rows, :] = lin
        dt = jax.nn.softplus(lin)
        convolved = conv[rows, :]
        dtm[...] = dt + across(STOP * marks[pl.ds(pl.multiple_of(8 + start, 8), block), :], inner)
        dtx[...] = dt * convolved
        turned = sums.T
        b_all, c_all = turned[72:88], turned[88:104]

        def chunk(i, h_now):
            starts[b * lines + i] = h_now
            shift = lax.rem(block - i * STEP, block)
            b_now, c_now = pltpu.roll(b_all, shift, 1), pltpu.roll(c_all, shift, 1)
            rows_m, rows_x = (ref[pl.ds(pl.multiple_of(i * STEP, STEP), STEP), :] for ref in (dtm, dtx))
            for j in range(STEP):
                decay = jnp.exp2(a * rows_m[j : j + 1])
                h_now = decay * h_now + b_now[:, j : j + 1] * rows_x[j : j + 1]
                p = c_now[:, j : j + 1] * h_now
                put_rows(parts, j, p[:half] + p[half:])
            here = pl.ds(pl.multiple_of(start + i * STEP, STEP), STEP)
            y_out[here, :] = summed_groups(parts, half, inner)
            return h_now

        state = lax.fori_loop(0, lines, chunk, state)
        y = y_out[rows, :] + params[126:127, :] * convolved
        y_out[rows, :] = y
        z = gate_z[rows, :]
        low = (y * z * jax.nn.sigmoid(z)).astype(BF16)
        gated[rows, :] = low
        out = matmul(low[:, :512], whole_all[:, late:]) + matmul(low[:, 512:], extra[:, 2 * model : small])
        branch[b] = out.astype(BF16)

        for k in (1, 0, 2):
            part_copy(b, k).start()

        @pl.when(b > 0)
        def earlier():
            sum_up(b - 1)

        for n in range(4, 9):
            saved_copy(n, b).start()
        return state

    lax.fori_loop(0, 4, stage_two, jnp.zeros((states, inner), F32))
    sum_up(3)
    for k in range(3):
        whole_copy(0, k).wait_recv()
    mine = pl.ds(pl.multiple_of(h * block, block), block)
    hidden[...] = seq[mine, :model].astype(F32)
    for k in range(4):
        rows = pl.ds(pl.multiple_of(lax.rem(h + k, 4) * quarter, quarter), quarter)
        piece = owned[k - 1] if k else quarters[h]
        hidden[rows, :] += piece.astype(F32)
    hid = hidden[...]
    scale = lax.rsqrt(jnp.mean(hid * hid, axis=-1, keepdims=True) + EPS)
    moe_low = (hid * scale * gains[1:2, :]).astype(BF16)
    moe_out[...] = moe_low
    logits = outer_cols(moe_low, gains[...].astype(BF16))
    lane = lax.broadcasted_iota(jnp.int32, logits.shape, 1)
    real = (lane >= 2) & (lane < 2 + experts)
    logits = jnp.where(real, logits, -1e30)
    powers = jnp.exp(logits - jnp.max(logits, axis=-1, keepdims=True))
    shares = powers / jnp.sum(powers, axis=-1, keepdims=True)
    probs[...] = shares
    pick_main, top, low_half, onehot = slot_picks(routes[...], experts)
    gate = jnp.sum(shares * onehot, axis=-1, keepdims=True)
    grad_eo = (gate * cotangent[...].astype(F32)).astype(BF16)
    shape = (experts, MAIN, model)
    slots[:, :, :model] = matmul(pick_main, moe_low).astype(BF16).reshape(shape)
    slots[:, :, model : 2 * model] = matmul(pick_main, grad_eo).astype(BF16).reshape(shape)
    slots[:, :, 2 * model :] = (matmul(top, moe_low) + matmul(low_half, grad_eo)).astype(BF16).reshape(shape)
    for n in range(9):
        for b in range(4):
            saved_copy(n, b).wait()
    for copy in kept_copies:
        copy.wait()
    for part in (main, out_part, norm_part):
        part.sent()
    for copy in n_copies + z_copies:
        copy.wait_send()
    for b in range(4):
        for k in range(3):
            proj_copy(b, k).wait_send()
            part_copy(b, k).wait_send()

        @pl.when(b != h)
        def sent():
            whole_copy(b, 0).wait_send()


def layer_kernel(*refs):
    ins, up_down, saved = refs[:16], refs[16:18], refs[18:30]
    params, gains, output, grad_hidden, norm_out, up_out, down_out, ring_up, ring_down = refs[30:39]
    hidden, slots, moe_low, probs, *scratch = refs[39:]
    forward_scratch, expert_scratch = scratch[:FORWARD_SCRATCH], scratch[FORWARD_SCRATCH:]
    forward_part((*ins, *saved, params, gains, hidden, slots, moe_low, probs, *forward_scratch))
    expert_part(
        (
            slots, *up_down, hidden, ins[15], moe_low, probs, ins[14], gains, output, grad_hidden, norm_out, up_out,
            down_out, ring_up, ring_down, *expert_scratch,
        )
    )


def mixer_and_experts(arrays, up, down, inner, states, experts):
    tokens = arrays[12]
    block, model = tokens.shape
    length, hidden = 4 * block, up.shape[1]
    width, lines = 3 * model + 768, MAIN
    S, V = jax.ShapeDtypeStruct, pltpu.VMEM
    saved = [
        ((length, model), BF16), ((length, inner), BF16), ((length, inner), F32), ((length, inner), F32),
        ((length, 128), F32), ((length, inner), F32), ((length, inner), F32), ((length, inner), BF16),
        ((length // STEP, states, inner), F32),
    ]
    eighths = [(4, one.shape[0] // 8, one.shape[1]) for one in (up, down)]
    outs = (
        S((512, width), BF16), S((length, model + 128), BF16), S((64, 4096), BF16), *[S(*one) for one in saved],
        S((128, inner), F32), S((MAIN, model), F32), S((block, model), BF16), S((block, model), F32),
        S((MAIN, model), F32), S(up.shape, BF16), S(down.shape, BF16), *[S(size, BF16) for size in eighths],
    )
    eight = DMA((8,))
    forward_scratch = [
            V((MAIN, width), BF16), V((MAIN, 128), BF16), V((block, model + 128), BF16), V((512, width), BF16),
            V((32, MAIN, 128), BF16), V((length, model + 128), BF16), V((64, 4096), BF16),
            V((3, MAIN, 128), BF16), V((MAIN, 128), BF16),
            DMA((3,)), DMA((3,)), DMA((3,)), DMA((3,)), DMA((3,)),
            DMA((31,)), DMA((31,)), DMA((31,)), DMA((31,)), DMA((31,)), DMA((31,)),
            DMA((3,)), DMA((9, 4)),
            *[V(*one) for one in saved],
            V((length + 8, inner), F32), V((length + 8, 128), F32), V((length, inner), F32), V((block, inner), F32),
            V((block, inner), F32), V((-(-inner // 128), STEP * states // 2, 128), F32), V((4, block, 128), BF16),
            V((3, 4, block, 128), BF16), V((4, block, model), BF16), V((3, 4, block // 4, model), BF16),
            DMA((12,)), DMA((12,)), DMA((12,)), DMA((12,)), V((4, block // 4, model), BF16),
            V((3, block // 4, model), BF16), DMA((4,)), DMA((3,)),
    ]
    slot_lines = (lines, 3 * model)
    expert_scratch = [
        V(up.shape, BF16), V(down.shape, BF16), V(up.shape, BF16), V(down.shape, BF16), DMA((4,)), DMA((2, 4)), DMA((2, 4)),
        V((experts, *slot_lines), BF16), V((4, experts, *slot_lines), BF16), V((4, experts, *slot_lines), BF16),
        V((256, hidden), BF16), V((256, hidden), BF16), V((4, 256, hidden), BF16), V((4, 256, hidden), BF16),
        V((8, *slot_lines), BF16), V((8, *slot_lines), BF16), V((4, *slot_lines), BF16), V((4, *slot_lines), BF16),
        V((8, *slot_lines), BF16), *[eight] * 16,
    ]
    assert len(forward_scratch) == FORWARD_SCRATCH
    return pl.pallas_call(
        layer_kernel,
        out_shape=outs,
        in_specs=[IN_VMEM] * 16 + [ANY] * 2,
        out_specs=(*[ANY] * 12, *[IN_VMEM] * 5, ANY, ANY, IN_VMEM, IN_VMEM),
        scratch_shapes=[
            V((block, model), F32), V((experts, *slot_lines), BF16), V((block, model), BF16), V((block, MAIN), F32),
            *forward_scratch, *expert_scratch,
        ],
        compiler_params=pltpu.CompilerParams(
            collective_id=1, has_side_effects=True, vmem_limit_bytes=62 << 20
        ),
        name="mixer_and_experts",
    )(*arrays, up, down)


class Flow:
    ORDER = (2, 1, 3, 0)

    def __init__(self, turn, source, out, pairs, halves, fours, lines, ends, send, recv):
        self.source, self.out, self.pairs, self.halves = source, out, pairs, halves
        self.fours, self.lines, self.ends, self.send, self.recv = fours, lines, ends, send, recv
        e, r, h = places()
        self.c = lax.rem(e, 2)
        y = e // 2
        self.turn = self.c if turn is None else turn
        self.mate_turn = 1 - self.c if turn is None else turn
        self.f0 = y * (1 - self.turn) + r * self.turn
        self.s0 = r * (1 - self.turn) + y * self.turn
        self.mate_s0 = r * (1 - self.mate_turn) + y * self.mate_turn
        self.mate, self.first, self.second_peers = mixer_peers(self.turn)

    def copy(self, src, dst, at, peer):
        return remote(src, dst, self.send.at[at], self.recv.at[at], peer)

    def mate_copy(self, n, f):
        s = lax.rem(self.mate_s0 + self.ORDER[n], 4)
        block = block_at(1 - self.c, f, s, self.mate_turn)
        return self.copy(self.source.at[block], self.pairs.at[n, f], n * 4 + f, self.mate)

    def second_copy(self, n):
        return self.copy(self.halves.at[n], self.fours.at[n], 16 + n, self.second_peers[self.ORDER[n] - 1])

    def first_copy(self, n):
        return self.copy(self.lines.at[n], self.ends.at[n], 19 + n, self.first[self.ORDER[n] - 1])

    def begin(self):
        for n in range(4):
            for f in range(4):
                self.mate_copy(n, f).start()

    def second(self):
        for n, k in enumerate(self.ORDER):
            s = lax.rem(self.s0 + k, 4)
            for f in range(4):
                self.mate_copy(n, f).wait_recv()
                total = self.source[block_at(self.c, f, s, self.turn)].astype(F32) + self.pairs[n, f].astype(F32)
                self.halves[n, f] = total.astype(BF16)
            if k:
                self.second_copy(n).start()

    def third(self):
        for n in range(3):
            self.second_copy(n).wait_recv()
        for n, k in enumerate(self.ORDER):
            f = lax.rem(self.f0 + k, 4)
            line = self.halves[3, f].astype(F32)
            for m in range(3):
                line = line + self.fours[m, f].astype(F32)
            if k:
                self.lines[n] = line.astype(BF16)
                self.first_copy(n).start()
            else:
                self.out[...] = line

    def finish(self):
        for n in range(3):
            self.first_copy(n).wait_recv()
        self.out[...] = (
            self.out[...] + self.ends[0].astype(F32) + self.ends[1].astype(F32) + self.ends[2].astype(F32)
        )

    def end(self):
        for n in range(4):
            for f in range(4):
                self.mate_copy(n, f).wait_send()
        for n in range(3):
            self.second_copy(n).wait_send()
            self.first_copy(n).wait_send()


def flow_scratch(width):
    return [
        pltpu.VMEM((32, MAIN, width), BF16), pltpu.VMEM((MAIN, width), F32), pltpu.VMEM((4, 4, MAIN, width), BF16),
        pltpu.VMEM((4, 4, MAIN, width), BF16), pltpu.VMEM((3, 4, MAIN, width), BF16),
        pltpu.VMEM((3, MAIN, width), BF16), pltpu.VMEM((3, MAIN, width), BF16), DMA((22,)), DMA((22,)),
    ]


def mixer_back_kernel(*refs):
    (
        grad_hidden, seq_all, whole_in, gains, norm_in, normed_in, x_low_in, u_all, gate_all, proj_in, lin_all, y_all,
        gated_in, starts_in, params, extra_in, g_up, g_down, came_up, came_down,
        grad_tokens, grad_in, grad_out, grad_x, grad_dt, by_channel, by_feature, all_up, all_down,
        seq_own, seq_marks, whole, normed, x_low, u_in, gate_z, proj, dt_lin, y_in, gated, starts, extra, in_sems,
        ghs, gus, marks, dts, dtm, dtx, conv, s1, s2, gdl, ggate, gx, gp_all,
        conv_low, held, decays, parts_1, parts_2, lanes_b, lanes_c, state, g_rate, rows_sum, own, landing, branch, came,
        a_send, a_recv, p_send, p_recv, b_send, b_recv, x_send, x_recv, x_local,
        e_slots_up, e_own_up, e_sums_up, total_up, e_slots_down, e_own_down, e_sums_down, total_down,
        y_send, y_recv, y_local, own_tile, tiles, z_send, z_recv, *flow_refs, gain_sum,
    ) = refs
    e, r, h = places()
    block, model = grad_hidden.shape
    inner, states = u_in.shape[1], starts.shape[1]
    lines, half, small = block // STEP, states // 2, 3 * model
    owners = 32
    z_peers = hid_peers()
    mate, first, second = mixer_peers()
    hail([mate] + first + second + z_peers)
    mine = pl.ds(pl.multiple_of(h * block, block), block)
    loads = [
        (lin_all, dt_lin), (u_all, u_in), (gate_all, gate_z), (y_all, y_in), (seq_all.at[:, model:], seq_marks),
        (proj_in, proj), (starts_in, starts), (whole_in, whole), (extra_in, extra), (x_low_in, x_low),
        (gated_in, gated), (normed_in, normed), (seq_all.at[mine, :model], seq_own),
    ]
    loads = [pltpu.make_async_copy(a, b, in_sems.at[n]) for n, (a, b) in enumerate(loads)]
    for copy in loads:
        copy.start()
    sums = [
        RowsSum(g_up, came_up, e_slots_up, e_own_up, e_sums_up, total_up, y_send.at[0], y_recv.at[0], y_local.at[0]),
        RowsSum(
            g_down, came_down, e_slots_down, e_own_down, e_sums_down, total_down, y_send.at[1], y_recv.at[1], y_local.at[1]
        ),
    ]
    rings = [
        RowsGather(part, whole_grad, x_send.at[n], x_recv.at[n], x_local.at[n])
        for n, (part, whole_grad) in enumerate(((total_up, all_up), (total_down, all_down)))
    ]
    for ring in sums:
        for n in (4, 0, 1, 2, 3):
            ring.load(n).start()
    ghs[h] = grad_hidden[...].astype(BF16)
    pl.semaphore_wait(pltpu.get_barrier_semaphore(), 10)
    right, left, middle = lax.rem(h + 1, 4), lax.rem(h + 3, 4), block // 2
    passed = (ghs.at[left, :middle], ghs.at[right, middle:])
    gh_copies = [
        remote(ghs.at[h], ghs.at[h], a_send.at[0], a_recv.at[0], (e, r, right)),
        remote(ghs.at[h], ghs.at[h], a_send.at[1], a_recv.at[1], (e, r, left)),
        remote(passed[0], passed[0], a_send.at[2], a_recv.at[2], (e, r, right)),
        remote(passed[1], passed[1], a_send.at[3], a_recv.at[3], (e, r, left)),
    ]
    for k in range(2):
        gh_copies[k].start()
    for ring in sums:
        ring.pass_on()
    flow_early, flow_in, flow_rest = [
        Flow(1 if n == 0 else None, *flow_refs[9 * n : 9 * n + 9]) for n in range(3)
    ]
    state[...] = jnp.zeros_like(state)
    g_rate[...] = jnp.zeros_like(g_rate)
    rows_sum[...] = jnp.zeros_like(rows_sum)
    gain_sum[...] = jnp.zeros_like(gain_sum)
    gus[512:520] = jnp.zeros((8, inner), F32)
    a = jnp.exp(params[104:120, :]) * (-LOG2E)
    for copy in loads[:5]:
        copy.wait()
    marks[0:512] = seq_marks[...].astype(F32)
    marks[512:520] = jnp.zeros((8, 128), F32)

    def prepare(b, carry):
        rows = pl.ds(pl.multiple_of(b * block, block), block)
        lin = dt_lin[rows, :]
        dt = jax.nn.softplus(lin)
        dt_lin[rows, :] = jax.nn.sigmoid(lin)
        u_now = u_in[rows, :]
        convolved = u_now * jax.nn.sigmoid(u_now)
        conv[rows, :] = convolved
        conv_low[rows, :] = convolved.astype(BF16)
        dts[rows, :] = dt
        dtm[rows, :] = dt + across(STOP * marks[rows, :], inner)
        dtx[rows, :] = dt * convolved
        z = gate_z[rows, :]
        sig = jax.nn.sigmoid(z)
        gate_z[rows, :] = z * sig
        y_in[rows, :] = y_in[rows, :] * (sig * (1.0 + z * (1.0 - sig)))
        return carry

    lax.fori_loop(0, 4, prepare, 0)
    for k in range(2):
        gh_copies[k].wait_recv()
        gh_copies[2 + k].start()
    for copy in loads[5:]:
        copy.wait()

    def spots(shape, axis):
        return lax.broadcasted_iota(jnp.int32, shape, axis)

    tall = (block * states, 128)
    ones = jnp.ones((128, 128), BF16)

    extras = []

    def weight(left, right, target, at, size):
        main = inner_rows(left[:, :512], right)
        target[:, :, at : at + size] = main.astype(BF16).reshape(owners, MAIN, size)
        extras.append(inner_rows(left[:, 512:], right).astype(BF16))

    for copy in gh_copies[2:]:
        copy.wait_recv()
    gh_rows, low_norm = ghs[...].reshape(4 * block, model), normed[...]
    gg = both_cols(gh_rows, whole[:, 2 * model + 768 :], extra[:, 2 * model : small])
    gate_z[...] = gg * gate_z[...]
    ggate[...] = (gg * y_in[...]).astype(BF16)
    weight(gated[...], gh_rows, flow_early.source, 0, model)
    weight(ggate[...], low_norm, flow_early.source, model, model)
    flow_early.begin()
    for ring, gather in zip(sums, rings):
        ring.finish()
        gather.begin()

    def proj_copy(b, k):
        at = k * 4 + b
        return remote(own.at[b], landing.at[k, b], p_send.at[at], p_recv.at[at], z_peers[k])

    def branch_copy(b, sender):
        return remote(branch.at[b], came.at[sender], b_send.at[b], b_recv.at[sender], (e, r, b))

    def stage_a(b):
        start = pl.multiple_of(b * block, block)
        rows = pl.ds(start, block)
        turned = proj[rows, :].T
        b_all, c_all = turned[72:88], turned[88:104]

        gy_now = gate_z[rows, :]

        def chunk(step, u):
            i = lines - 1 - step
            hh = starts[b * lines + i]
            held[0] = hh
            shift = lax.rem(block - i * STEP, block)
            b_now, c_now = pltpu.roll(b_all, shift, 1), pltpu.roll(c_all, shift, 1)
            there = pl.ds(pl.multiple_of(start + i * STEP, STEP), STEP)
            rows_m, rows_x, rows_g, rows_t = (ref[there, :] for ref in (dtm, dtx, gate_z, dts))
            for j in range(STEP):
                decay = jnp.exp2(a * rows_m[j : j + 1])
                hh = decay * hh + b_now[:, j : j + 1] * rows_x[j : j + 1]
                decays[j] = decay
                held[j + 1] = hh
            for j in range(STEP - 1, -1, -1):
                gy_row = rows_g[j : j + 1]
                g = c_now[:, j : j + 1] * gy_row + u
                u = decays[j] * g
                q = u * held[j]
                g_rate[...] += q * rows_t[j : j + 1]
                w = q * a
                put_rows(parts_2, j, w[:half] + w[half:])
                w = g * b_now[:, j : j + 1]
                put_rows(parts_1, j, w[:half] + w[half:])
                at = pl.ds(pl.multiple_of((i * STEP + j) * states, states), states)
                lanes_b[at, :] = over_lanes(g * rows_x[j : j + 1]).astype(BF16)
                lanes_c[at, :] = over_lanes(held[j + 1] * gy_row).astype(BF16)
            here = pl.ds(pl.multiple_of(i * STEP, STEP), STEP)
            s1[here, :] = summed_groups(parts_1, half, inner)
            s2[here, :] = summed_groups(parts_2, half, inner)
            return u

        state[...] = lax.fori_loop(0, lines, chunk, state[...])
        convolved = conv[rows, :]
        grad_lin = dt_lin[rows, :] * (convolved * s1[...] + s2[...] * (1.0 / LOG2E))
        low = grad_lin.astype(BF16)
        gdl[rows, :] = low
        rows_sum[5:6, :] += jnp.sum(grad_lin, axis=0, keepdims=True)
        rows_sum[6:7, :] += jnp.sum(gy_now * convolved, axis=0, keepdims=True)
        dts[rows, :] = params[126:127, :] * gy_now + dts[rows, :] * s1[...]
        at_state = spots(tall, 0) % states
        spread = jnp.where(spots(tall, 1) - 72 == at_state, matmul(lanes_b[...], ones), 0.0) + jnp.where(
            spots(tall, 1) - 88 == at_state, matmul(lanes_c[...], ones), 0.0
        )
        share = spread.reshape(block, states, 128).sum(axis=1)
        share = share + matmul(low[:, :512], whole[:, 2 * model + 128 : 2 * model + 256])
        share = share + matmul(low[:, 512:], extra[:, small + 128 : small + 256])
        own[b] = share.astype(BF16)
        for k in (1, 0, 2):
            proj_copy(b, k).start()

    def stage_b(b):
        start = pl.multiple_of(b * block, block)
        rows = pl.ds(start, block)
        for k in range(3):
            proj_copy(b, k).wait_recv()
        gp = (
            own[b].astype(F32) + landing[0, b].astype(F32) + landing[1, b].astype(F32) + landing[2, b].astype(F32)
        ).astype(BF16)
        gp_all[rows, :] = gp
        u_now = u_in[rows, :]
        sig = jax.nn.sigmoid(u_now)
        gu = dts[rows, :] + both_cols(gp, whole[:, 2 * model : 2 * model + 128], extra[:, small : small + 128])
        gu = gu * (sig * (1.0 + u_now * (1.0 - sig)))
        gus[rows, :] = gu
        lines_g, lines_m = gus[pl.ds(start, block + 8), :], marks[pl.ds(start, block + 8), :]
        x = x_low[rows, :].astype(F32)
        total = params[123:124, :] * gu
        rows_sum[3:4, :] += jnp.sum(gu * x, axis=0, keepdims=True)
        rows_sum[4:5, :] += jnp.sum(gu, axis=0, keepdims=True)
        mask = jnp.ones((block, 128), F32)
        for ahead in (1, 2, 3):
            mask = mask * (1.0 - lines_m[ahead : ahead + block])
            moved = lines_g[ahead : ahead + block] * across(mask, inner)
            total = total + params[123 - ahead : 124 - ahead, :] * moved
            rows_sum[3 - ahead : 4 - ahead, :] += jnp.sum(moved * x, axis=0, keepdims=True)
        low = total.astype(BF16)
        gx[rows, :] = low
        gate = ggate[rows, :]
        out = (
            matmul(low[:, :512], whole[:, :model])
            + matmul(low[:, 512:], extra[:, :model])
            + matmul(gate[:, :512], whole[:, model : 2 * model])
            + matmul(gate[:, 512:], extra[:, model : 2 * model])
        )
        branch[b] = out.astype(BF16)

        @pl.when(b != h)
        def send():
            branch_copy(b, lax.rem(h - b + 4, 4) - 1).start()

        gain_sum[...] += jnp.sum(out * normed[rows, :].astype(F32), axis=0, keepdims=True)

    def step(n, carry):
        stage_a(3 - n)

        @pl.when(n == 3)
        def early_third():
            flow_early.third()

        @pl.when(n > 0)
        def later():
            stage_b(4 - n)

        @pl.when(n == 0)
        def pass_on():
            flow_early.second()

        @pl.when(n == 2)
        def early():
            for ring in rings:
                ring.forward()

        return carry

    lax.fori_loop(0, 4, step, 0)

    flow_early.finish()
    weight(gdl[...], proj[...].astype(BF16), flow_rest.source, 128, 128)
    known = inner_rows(gx[block:], normed[block:])
    stage_b(0)
    total = known + inner_rows(gx[:block], normed[:block])
    flow_in.source[...] = total[:512].astype(BF16).reshape(owners, MAIN, model)
    extras.append(total[512:].astype(BF16))
    flow_in.begin()
    ends = jnp.concatenate(
        [jnp.zeros((104, inner), F32), g_rate[...] * (a * (1.0 / LOG2E)), rows_sum[...]], axis=0
    ).astype(BF16)
    low_conv, low_gp, unit = conv_low[...], gp_all[...], eye(128)
    main = inner_rows(low_conv[:, :512], low_gp) + inner_rows(ends[:, :512], unit)
    flow_rest.source[:, :, :128] = main.astype(BF16).reshape(owners, MAIN, 128)
    last = (inner_rows(low_conv[:, 512:], low_gp) + inner_rows(ends[:, 512:], unit)).astype(BF16)
    lines_e = jnp.concatenate(
        [extras[3], extras[1], extras[0], last, extras[2], jnp.zeros((64, 4096 - small - 256), BF16)], axis=1
    )
    stacked = jnp.concatenate([lines_e[:, k * 512 : (k + 1) * 512] for k in range(8)], axis=0)
    row, col = spots((512, 512), 0), spots((512, 512), 1)
    wanted = (col % 64 // 2) * MAIN + (col % 2) * 8 + col // 64
    flow_rest.source[:, :, 256:768] = (
        matmul((wanted == row).astype(BF16), stacked).astype(BF16).reshape(owners, MAIN, 512)
    )
    span = model // owners
    tile = norm_in[...] + jnp.where(spots(norm_in.shape, 0) == 0, gain_sum[...] / gains[0:1, :], 0.0)
    for n in range(owners):
        piece = tile[:, n * span : (n + 1) * span]
        piece = jnp.concatenate([piece, jnp.zeros((MAIN, 128 - span), F32)], axis=1)
        flow_rest.source[n, :, 768:] = piece.astype(BF16)
    flow_rest.begin()
    flow_in.second()
    flow_rest.second()
    flow_in.third()
    flow_rest.third()
    for ring in sums + rings:
        ring.end()
    for k in range(3):
        branch_copy(0, k).wait_recv()
    grad_n = branch[h].astype(F32) + came[0].astype(F32) + came[1].astype(F32) + came[2].astype(F32)
    values = seq_own[...].astype(F32)
    scale = lax.rsqrt(jnp.mean(values * values, axis=-1, keepdims=True) + EPS)
    scaled = grad_n * gains[0:1, :]
    inside = jnp.mean(scaled * values, axis=-1, keepdims=True)
    grad_tokens[...] = grad_hidden[...] + scale * scaled - values * (scale * scale * scale * inside)
    flow_rest.finish()
    rest = flow_rest.out[...]
    own_tile[...] = rest[:, 768:].astype(BF16)
    z_copies = [remote(own_tile, tiles.at[k], z_send.at[k], z_recv.at[k], z_peers[k]) for k in range(3)]
    for copy in z_copies:
        copy.start()
    flow_in.finish()
    rank, wide = grad_dt.shape[1], grad_x.shape[1]
    extra_rows = [
        jnp.concatenate([rest[n * 8 + k : n * 8 + k + 1, 256:768] for k in range(8)], axis=1) for n in range(2)
    ]

    def full(main, at, size):
        return jnp.concatenate([main, *[line[:, at : at + size] for line in extra_rows]], axis=0)

    grad_in[:, 0, :] = full(flow_in.out[...], 0, model)
    grad_in[:, 1, :] = full(flow_early.out[:, model:], model, model)
    grad_out[...] = full(flow_early.out[:, :model], 2 * model, model)
    small_sum = full(rest[:, :256], small, 256)
    grad_x[...] = small_sum[:, :wide]
    grad_dt[...] = small_sum[:, 128 : 128 + rank]
    channels = jnp.concatenate([small_sum[:, :128], jnp.zeros((110, 128), F32)], axis=0)
    by_channel[...] = channels.T[104:128, : grad_out.shape[0]]
    for copy in z_copies:
        copy.wait_recv()
    tile = rest[:, 768:] + tiles[0].astype(F32) + tiles[1].astype(F32) + tiles[2].astype(F32)
    share = by_feature.shape[1]
    by_feature[...] = pltpu.roll(tile, lax.rem(128 - h * share, 128), 1)[:, :share]
    for flow in (flow_early, flow_in, flow_rest):
        flow.end()
    for copy in gh_copies + z_copies:
        copy.wait_send()
    for b in range(4):
        for k in range(3):
            proj_copy(b, k).wait_send()

        @pl.when(b != h)
        def sent():
            branch_copy(b, 0).wait_send()


def mixer_backward(grad_hidden, seq, whole, gains, norm_in, saved, expert_grads, own, wide, rank):
    normed, x_low, u, gate_z, proj, dt_lin, y, gated, starts, params, extra = saved
    block, model = grad_hidden.shape
    tokens, inner = u.shape
    states = starts.shape[1]
    S = jax.ShapeDtypeStruct
    g_up, g_down, came_up, came_down = expert_grads

    def like(array):
        return pltpu.VMEM(array.shape, array.dtype)

    line, low = pltpu.VMEM((block, inner), F32), pltpu.VMEM((tokens, inner), BF16)
    tall = pltpu.VMEM((tokens, inner), F32)
    return pl.pallas_call(
        mixer_back_kernel,
        out_shape=(
            S((block, model), F32), S((own, 2, model), F32), S((own, model), F32), S((own, wide), F32),
            S((own, rank), F32), S((24, own), F32), S((MAIN, model // 128), F32), S(g_up.shape, BF16),
            S(g_down.shape, BF16),
        ),
        in_specs=[IN_VMEM, ANY, ANY, IN_VMEM, IN_VMEM, *[ANY] * 9, IN_VMEM, *[ANY] * 5],
        out_specs=(*[IN_VMEM] * 7, ANY, ANY),
        scratch_shapes=[
            pltpu.VMEM((block, model), BF16), pltpu.VMEM((tokens, 128), BF16), like(whole), like(normed), like(x_low),
            like(u), like(gate_z), like(proj), like(dt_lin), like(y), like(gated), like(starts), like(extra),
            DMA((13,)),
            pltpu.VMEM((4, block, model), BF16),
            pltpu.VMEM((tokens + 8, inner), F32),
            pltpu.VMEM((tokens + 8, 128), F32),
            tall, tall, tall, tall, line, line,
            low, low, low,
            pltpu.VMEM((tokens, 128), BF16),
            low,
            pltpu.VMEM((STEP + 1, states, inner), F32),
            pltpu.VMEM((STEP, states, inner), F32),
            pltpu.VMEM((-(-inner // 128), STEP * states // 2, 128), F32),
            pltpu.VMEM((-(-inner // 128), STEP * states // 2, 128), F32),
            pltpu.VMEM((block * states, 128), BF16),
            pltpu.VMEM((block * states, 128), BF16),
            pltpu.VMEM((states, inner), F32),
            pltpu.VMEM((states, inner), F32),
            pltpu.VMEM((8, inner), F32),
            pltpu.VMEM((4, block, 128), BF16),
            pltpu.VMEM((3, 4, block, 128), BF16),
            pltpu.VMEM((4, block, model), BF16),
            pltpu.VMEM((3, block, model), BF16),
            DMA((4,)), DMA((4,)), DMA((12,)), DMA((12,)), DMA((4,)), DMA((3,)),
            DMA((2, 4)), DMA((2, 4)), DMA((2,)),
            like(came_up), like(came_up), like(came_up), pltpu.VMEM((g_up.shape[0] // 4, g_up.shape[1]), BF16),
            like(came_down), like(came_down), like(came_down), pltpu.VMEM((g_down.shape[0] // 4, g_down.shape[1]), BF16),
            DMA((2, 2)), DMA((2, 2)), DMA((2, 5)),
            pltpu.VMEM((MAIN, 128), BF16), pltpu.VMEM((3, MAIN, 128), BF16), DMA((3,)), DMA((3,)),
            *flow_scratch(2 * model), *flow_scratch(model), *flow_scratch(896),
            pltpu.VMEM((1, model), F32),
        ],
        compiler_params=pltpu.CompilerParams(
            collective_id=5, has_side_effects=True, vmem_limit_bytes=62 << 20
        ),
        name="mixer_backward",
    )(
        grad_hidden, seq, whole, gains, norm_in, normed, x_low, u, gate_z, proj, dt_lin, y, gated, starts, params, extra,
        g_up, g_down, came_up, came_down,
    )


def finish_kernel(*refs):
    (
        channel, feature, up_in, down_in, in_0, in_1, in_2, in_3, in_4, in_5, up, down, result, tokens, grad_in, grad_out, grad_x, grad_dt,
        decay, taps, conv_bias, dt_bias, skip, gain_one, gain_two, router, low_up, low_down, high_up, high_down, *kept, sems,
        k_sems,
    ) = refs
    straight_in = (in_0, in_1, in_2, in_3, in_4, in_5)
    straight_out = (result, tokens, grad_in, grad_out, grad_x, grad_dt)
    parts = 8
    loads = []
    for q in range(parts):
        for n, (a, b) in enumerate(((up_in, low_up), (down_in, low_down))):
            size = a.shape[0] // parts
            rows = pl.ds(q * size, size)
            loads.append(pltpu.make_async_copy(a.at[rows, :], b.at[rows, :], sems.at[n, q]))
            loads[-1].start()
    moves = []
    for n, (a, b, c) in enumerate(zip(straight_in, kept, straight_out)):
        moves.append((pltpu.make_async_copy(a, b, k_sems.at[0, n]), pltpu.make_async_copy(b, c, k_sems.at[1, n])))
        moves[-1][0].start()
    lines = channel[...]
    decay[...] = lines[0:16]
    taps[...] = lines[16:20]
    conv_bias[...] = lines[20:21]
    dt_bias[...] = lines[21:22]
    skip[...] = lines[22:23]
    lines = feature[...]
    gain_one[...] = lines[0:1]
    gain_two[...] = lines[1:2]
    router[...] = lines[2:10]
    stores = []
    for q in range(parts):
        for n, (a, b, c) in enumerate(((low_up, high_up, up), (low_down, high_down, down))):
            size = a.shape[0] // parts
            rows = pl.ds(q * size, size)
            loads[2 * q + n].wait()
            b[rows, :] = a[rows, :].astype(F32)
            stores.append(pltpu.make_async_copy(b.at[rows, :], c.at[rows, :], sems.at[2 + n, q]))
            stores[-1].start()
    for a, b in moves:
        a.wait()
        b.start()
    for copy in stores:
        copy.wait()
    for a, b in moves:
        b.wait()


def finished(output, tokens, grad_in, grad_out, grad_x, grad_dt, channel, feature, low_up, low_down):
    S, own, share = jax.ShapeDtypeStruct, channel.shape[1], feature.shape[1]
    straight = (output, tokens, grad_in, grad_out, grad_x, grad_dt)
    outs = [S(low_up.shape, F32), S(low_down.shape, F32), *[S(a.shape, a.dtype) for a in straight]]
    outs += [S((n, own), F32) for n in (16, 4, 1, 1, 1)] + [S((n, share), F32) for n in (1, 1, 8)]
    up, down, *rest = pl.pallas_call(
        finish_kernel,
        out_shape=outs,
        in_specs=[IN_VMEM] * 2 + [ANY] * 8,
        out_specs=[ANY] * 8 + [IN_VMEM] * 8,
        scratch_shapes=[
            pltpu.VMEM(low_up.shape, BF16), pltpu.VMEM(low_down.shape, BF16), pltpu.VMEM(low_up.shape, F32),
            pltpu.VMEM(low_down.shape, F32), *[pltpu.VMEM(a.shape, a.dtype) for a in straight], DMA((4, 8)), DMA((2, 6)),
        ],
        compiler_params=pltpu.CompilerParams(vmem_limit_bytes=62 << 20),
        name="finish",
    )(channel, feature, low_up, low_down, *straight)
    return *rest, up, down


def shards(
    tokens, resets, routes, cotangent, mixer_gain, in_proj, conv_kernel, conv_bias, x_proj, dt_proj,
    dt_bias, log_decay, skip_gain, out_proj, moe_gain, router, up_proj, down_proj,
):
    model, own, experts = tokens.shape[1], conv_bias.shape[0], router.shape[1]
    rank, states = dt_proj.shape[0], log_decay.shape[0]
    inner = lax.axis_size("expert") * lax.axis_size("rows") * own
    route_row = routes.reshape(1, -1)
    arrays = (
        in_proj.transpose(2, 1, 0), out_proj, x_proj.T, dt_proj.T, log_decay, conv_kernel, conv_bias[None],
        dt_bias[None], skip_gain[None], mixer_gain[None], moe_gain[None], router.T, tokens, resets[None], route_row,
        cotangent,
    )
    whole, sequence, extra, *rest = mixer_and_experts(arrays, up_proj[0], down_proj[0], inner, states, experts)
    saved, (params, gains, output, grad_hidden, norm_grads, *expert_grads) = rest[:9], rest[9:]
    results = mixer_backward(
        grad_hidden, sequence, whole, gains, norm_grads, (*saved, params, extra), expert_grads, own,
        rank + 2 * states, rank,
    )
    (
        output, grad_tokens, grad_in, grad_out, grad_x, grad_dt, grad_decay, grad_taps, grad_conv_bias, grad_dt_bias,
        grad_skip, grad_gain_one, grad_gain_two, grad_router, grad_up_sum, grad_down_sum,
    ) = finished(output, *results)
    return (
        output,
        grad_tokens,
        grad_gain_one[0],
        grad_in.transpose(2, 1, 0),
        grad_taps,
        grad_conv_bias[0],
        grad_x.T,
        grad_dt.T,
        grad_dt_bias[0],
        grad_decay,
        grad_skip[0],
        grad_out,
        grad_gain_two[0],
        grad_router.T,
        grad_up_sum[None],
        grad_down_sum[None],
    )


def solution(mesh):
    every = ("expert", "rows", "hid")
    in_specs = (
        P(every, None), P(every), P(every, None), P(every, None), P(every), P(None, None, every),
        P(None, every), P(every), P(None, every), P(None, every), P(every), P(None, every), P(every),
        P(every, None), P(every), P(every, None), P("expert", None, "hid"), P("expert", "hid", None),
    )
    out_specs = (
        P(every, None), P(every, None), P(every), P(None, None, every), P(None, every), P(every),
        P(None, every), P(None, every), P(every), P(None, every), P(every), P(every, None), P(every),
        P(every, None), P("expert", None, "hid"), P("expert", "hid", None),
    )
    return jax.shard_map(shards, mesh=mesh, in_specs=in_specs, out_specs=out_specs, check_vma=False)
```

```python
from functools import partial

import jax
import jax.numpy as jnp
from jax import lax
from jax.experimental import pallas as pl
from jax.experimental.pallas import tpu as pltpu
from jax.sharding import PartitionSpec as P

EPS = 1e-05
LOG2E = 1.4426950408889634
STOP = 1e6
STEP = 16
FORWARD_SCRATCH = 49
MAIN = 16
EXTRA = 512
GELU_C = 0.7978845608028654
F32 = jnp.float32
BF16 = jnp.bfloat16


def matmul(first_op, second_op):
    return jnp.dot(first_op, second_op, preferred_element_type=F32)


def inner_rows(first_op, second_op):
    return lax.dot_general(
        first_op, second_op, (((0,), (0,)), ((), ())), preferred_element_type=F32
    )


def outer_cols(first_op, second_op):
    return lax.dot_general(
        first_op, second_op, (((1,), (1,)), ((), ())), preferred_element_type=F32
    )


def rms_norm(values, gain):
    return values * lax.rsqrt(jnp.mean(values * values, axis=-1, keepdims=True) + EPS) * gain


def over_lanes(v):
    whole = v.shape[1] // 128
    total = v[:, :128]
    for k in range(1, whole):
        total = total + v[:, k * 128 : (k + 1) * 128]
    rest = v.shape[1] - whole * 128
    if rest:
        blank = jnp.zeros((v.shape[0], 128 - rest), F32)
        total = total + jnp.concatenate([v[:, whole * 128 :], blank], axis=1)
    return total


MESH = pl.DeviceIdType.MESH
ANY = pl.BlockSpec(memory_space=pl.ANY)
IN_VMEM = pl.BlockSpec(memory_space=pltpu.VMEM)
DMA = pltpu.SemaphoreType.DMA


def put_rows(parts, j, values):
    count, width = values.shape
    for k in range(parts.shape[0]):
        size = min(128, width - 128 * k)
        parts[k, j * count : (j + 1) * count, :size] = values[:, 128 * k : 128 * k + size]


def summed_groups(parts, count, width):
    groups = parts.shape[1] // count
    columns = []
    for k in range(parts.shape[0]):
        total = parts[k, pl.ds(0, groups, stride=count), :]
        for n in range(1, count):
            total = total + parts[k, pl.ds(n, groups, stride=count), :]
        columns.append(total[:, : min(128, width - 128 * k)])
    return jnp.concatenate(columns, axis=1)


def places():
    return lax.axis_index("expert"), lax.axis_index("rows"), lax.axis_index("hid")


def hail(peers):
    barrier = pltpu.get_barrier_semaphore()
    for peer in peers:
        pl.semaphore_signal(barrier, inc=1, device_id=peer, device_id_type=MESH)


def greet(peers):
    hail(peers)
    pl.semaphore_wait(pltpu.get_barrier_semaphore(), len(peers))


def remote(src, dst, send_sem, recv_sem, peer):
    return pltpu.make_async_remote_copy(
        src_ref=src, dst_ref=dst, send_sem=send_sem, recv_sem=recv_sem, device_id=peer,
        device_id_type=MESH,
    )


def hid_peers():
    e, r, h = places()
    return [(e, r, lax.rem(h + k, 4)) for k in (1, 2, 3)]


def mixer_peers(turn=None):
    e, r, h = places()
    c = lax.rem(e, 2)
    t = c if turn is None else turn
    mate = (e + 1 - 2 * c, r, h)
    first = [(lax.rem(e + 2 * k * (1 - t), 8), lax.rem(r + k * t, 4), h) for k in (1, 2, 3)]
    second = [(lax.rem(e + 2 * k * t, 8), lax.rem(r + k * (1 - t), 4), h) for k in (1, 2, 3)]
    return mate, first, second


def block_at(c, f, s, turn=None):
    t = c if turn is None else turn
    y = f * (1 - t) + s * t
    x = s * (1 - t) + f * t
    return (2 * y + c) * 4 + x


class RowsPlace:
    def __init__(self, size):
        e, r, h = places()
        self.r, self.size = r, size
        self.right, self.left, self.across = lax.rem(r + 1, 4), lax.rem(r + 3, 4), lax.rem(r + 2, 4)
        self.to_right, self.to_left = (e, self.right, h), (e, self.left, h)

    def rows(self, quarter, part, parts=1):
        return pl.ds(pl.multiple_of((2 * quarter + part) * self.size, self.size), parts * self.size)


class RowsSpread(RowsPlace):
    def __init__(self, source, slots, send, recv):
        super().__init__(slots.shape[1])
        self.source, self.slots, self.send, self.recv = source, slots, send, recv

    def copy(self, n):
        plan = (
            (self.across, 0, 0, self.to_right),
            (self.across, 1, 1, self.to_left),
            (self.right, 1, 2, self.to_right),
            (self.left, 0, 3, self.to_left),
        )
        quarter, half, at, peer = plan[n]
        part = self.source.at[self.rows(quarter, half)]
        return remote(part, self.slots.at[at], self.send.at[n], self.recv.at[n], peer)

    def begin(self):
        for n in range(4):
            self.copy(n).start()

    def end(self):
        for n in range(4):
            self.copy(n).wait_recv()
            self.copy(n).wait_send()


class RowsSum(RowsPlace):
    def __init__(self, source, came, slots, own, sums, total, send, recv, local):
        super().__init__(sums.shape[1])
        self.source, self.came, self.slots, self.own, self.sums, self.total = source, came, slots, own, sums, total
        self.send, self.recv, self.local = send, recv, local

    def load(self, n):
        if n == 4:
            return pltpu.make_async_copy(self.came, self.slots, self.local.at[4])
        quarter, half = ((self.right, 0), (self.left, 1), (self.r, 0), (self.r, 1))[n]
        return pltpu.make_async_copy(self.source.at[self.rows(quarter, half)], self.own.at[n], self.local.at[n])

    def copy(self, n):
        return remote(
            self.sums.at[n], self.sums.at[2 + n], self.send.at[n], self.recv.at[n], (self.to_right, self.to_left)[n]
        )

    def pass_on(self):
        for n in (4, 0, 1):
            self.load(n).wait()
        for n in (0, 1):
            self.sums[n] = (self.slots[n].astype(F32) + self.own[n].astype(F32)).astype(BF16)
            self.copy(n).start()

    def finish(self):
        for n in (2, 3):
            self.load(n).wait()
        for n in (0, 1):
            self.copy(n).wait_recv()
            total = (
                self.own[2 + n].astype(F32) + self.slots[3 - n].astype(F32) + self.sums[2 + n].astype(F32)
            )
            self.total[n * self.size : (n + 1) * self.size, :] = total.astype(BF16)

    def end(self):
        for n in (0, 1):
            self.copy(n).wait_send()


class RowsGather(RowsPlace):
    def __init__(self, quarter, target, send, recv, local):
        super().__init__(quarter.shape[0] // 2)
        self.quarter, self.target, self.send, self.recv, self.local = quarter, target, send, recv, local

    def copy(self, n):
        out = self.target
        plan = (
            (lambda: self.quarter, self.rows(self.r, 0, 2), self.to_right),
            (lambda: self.quarter, self.rows(self.r, 0, 2), self.to_left),
            (lambda: out.at[self.rows(self.left, 0)], self.rows(self.left, 0), self.to_right),
            (lambda: out.at[self.rows(self.right, 1)], self.rows(self.right, 1), self.to_left),
        )
        part, rows, peer = plan[n]
        return remote(part(), out.at[rows], self.send.at[n], self.recv.at[n], peer)

    def own(self):
        return pltpu.make_async_copy(self.quarter, self.target.at[self.rows(self.r, 0, 2)], self.local)

    def begin(self):
        for n in (0, 1):
            self.copy(n).start()
        self.own().start()

    def forward(self):
        for n in (0, 1):
            self.copy(n).wait_recv()
            self.copy(2 + n).start()

    def end(self):
        for n in (2, 3):
            self.copy(n).wait_recv()
        self.own().wait()
        for n in range(4):
            self.copy(n).wait_send()


def gelu_pair(pre, grad):
    square = pre * pre
    t = jnp.tanh(GELU_C * pre * (1.0 + 0.044715 * square))
    up = 0.5 * (1.0 + t)
    slope = up + 0.5 * pre * (1.0 - t * t) * (GELU_C * (1.0 + 3 * 0.044715 * square))
    return pre * up, slope * grad


def expert_part(refs):
    (
        slots, up_in, down_in, hid_in, cotangent, moe_low, probs, routes, gains, output, grad_hidden, norm_out,
        up_out, down_out, ring_up, ring_down, g_up, g_down, up, down, m_sems, x_send, x_recv, back, held, results,
        hid_out, pre_out, hid_w, pre_w, from_left, from_right, half_left, half_right, sums, d_send, d_recv, r_send,
        r_recv, l_send, l_recv, f_send, f_recv, c_send, c_recv, k_send, k_recv, h_send, h_recv, b_send, b_recv,
    ) = refs
    e, r, h = places()
    moves = (
        (up_in, up), (down_in, down), (g_up, up_out), (g_down, down_out),
    )
    moves = [pltpu.make_async_copy(a, b, m_sems.at[n]) for n, (a, b) in enumerate(moves)]
    for move in moves[:2]:
        move.start()
    model, hidden = up.shape
    right, left, across = lax.rem(h + 1, 4), lax.rem(h + 3, 4), lax.rem(h + 2, 4)
    to_right, to_left = (e, r, right), (e, r, left)
    y, c = e // 2, lax.rem(e, 2)
    target = [2 * lax.rem(y + k // 2, 4) + lax.rem(c + k, 2) for k in range(8)]
    source = [2 * lax.rem(y + 4 - k // 2, 4) + lax.rem(c + k, 2) for k in range(8)]
    to_expert = [(one, r, h) for one in target]
    to_source = [(one, r, h) for one in source]
    via_right, via_left = (4, 3, 2, 0), (5, 7, 6, 1)
    sums_up = RowsSpread(g_up, ring_up, x_send.at[0], x_recv.at[0])
    sums_down = RowsSpread(g_down, ring_down, x_send.at[1], x_recv.at[1])

    held[h, e] = slots[e]
    d_copies = [None] * 8
    for n in (1, 2, 6, 3, 7, 4, 5):
        d_copies[n] = remote(slots.at[target[n]], held.at[h, e], d_send.at[n], d_recv.at[n], to_expert[n])
        d_copies[n].start()

    def along(buf, where, k, send, recv, peer):
        block = buf.at[where, source[k]]
        copy = remote(block, block, send.at[k], recv.at[k], peer)
        copy.start()
        return copy

    r_copies, l_copies = [None] * 8, [None] * 8
    for n in (0, 1, 2, 6, 3, 7, 4, 5):
        if n:
            d_copies[n].wait_recv()
        r_copies[n] = along(held, h, n, r_send, r_recv, to_right)
        l_copies[n] = along(held, h, n, l_send, l_recv, to_left)

    half = 128

    def worked(where):
        lines = held[where]
        main_x = lines[:, :, :model].reshape(half, model)
        main_g = lines[:, :, model : 2 * model].reshape(half, model)
        extra = lines[:, :, 2 * model :].reshape(half, model)
        rows_x = jnp.concatenate([main_x, extra], axis=0)
        rows_g = jnp.concatenate([main_g, extra], axis=0)

        def first_layer(i, carry):
            cols = pl.ds(pl.multiple_of(i * 256, 256), 256)
            pre = matmul(rows_x, up[:, cols])
            grad = outer_cols(rows_g, down[cols, :])
            hid_m, pre_m = gelu_pair(pre[:half], grad[:half])
            pre_e = pre[half:].reshape(8, 2, 8, 256)[:, 0]
            grad_e = grad[half:].reshape(8, 2, 8, 256)[:, 1]
            hid_e, gpre_e = gelu_pair(pre_e, grad_e)
            none = jnp.zeros_like(hid_e)

            def stacked(a, b):
                return jnp.stack([a, b], axis=1).reshape(half, 256).astype(BF16)

            hid_m, pre_m = hid_m.astype(BF16), pre_m.astype(BF16)
            hid_out[:half, cols] = hid_m
            pre_out[:half, cols] = pre_m
            hid_w[where, :half, cols] = hid_m
            pre_w[where, :half, cols] = pre_m
            hid_out[half:, cols] = stacked(hid_e, none)
            pre_out[half:, cols] = stacked(none, gpre_e)
            hid_w[where, half:, cols] = stacked(none, hid_e)
            pre_w[where, half:, cols] = stacked(gpre_e, none)
            return carry

        lax.fori_loop(0, hidden // 256, first_layer, 0)

        def second_layer(i, carry):
            at = pl.multiple_of(i * 384, 384)
            cols = pl.ds(at, 384)
            share = matmul(hid_out[...], down[:, cols])
            grad = outer_cols(pre_out[...], up[cols, :])
            shape = (8, 16, 384)
            results[where, :, :, cols] = share[:half].astype(BF16).reshape(shape)
            results[where, :, :, pl.ds(model + at, 384)] = grad[:half].astype(BF16).reshape(shape)
            results[where, :, :, pl.ds(2 * model + at, 384)] = (share[half:] + grad[half:]).astype(BF16).reshape(shape)
            return carry

        lax.fori_loop(0, model // 384, second_layer, 0)

    moves[0].wait()
    moves[1].wait()
    worked(h)
    f_copies = [None] * 8
    for a, b in ((0, 1), (2, 6), (3, 7), (4, 5)):
        r_copies[a].wait_recv()
        f_copies[a] = along(held, left, a, f_send, f_recv, to_right)
        l_copies[b].wait_recv()
        f_copies[b] = along(held, right, b, f_send, f_recv, to_left)
    for n in via_left:
        r_copies[n].wait_recv()
    worked(left)
    c_copies = [None] * 8
    k_copies = [None] * 8

    def toward_right(n):
        block = results.at[right, source[n]]
        c_copies[n] = remote(block, from_left.at[n], c_send.at[n], c_recv.at[n], to_right)
        c_copies[n].start()

    def toward_left(n):
        block = results.at[left, source[n]]
        k_copies[n] = remote(block, from_right.at[n], k_send.at[n], k_recv.at[n], to_left)
        k_copies[n].start()

    for n in via_right:
        toward_left(n)
    for n in via_right:
        l_copies[n].wait_recv()
    worked(right)
    for n in via_left:
        toward_right(n)
    for n in range(8):
        f_copies[n].wait_recv()
    worked(across)
    h_copies = [None] * 8
    for at in range(4):
        for n, landing, peer in ((via_right[at], half_left, to_right), (via_left[at], half_right, to_left)):
            block = results.at[across, source[n]]
            h_copies[n] = remote(block, landing.at[at], h_send.at[n], h_recv.at[n], peer)
            h_copies[n].start()

    def weight_grads(i, carry):
        cols = pl.ds(pl.multiple_of(i * 128, 128), 128)
        total = jnp.zeros((128, hidden), F32)
        for lanes, kept, out in ((0, pre_w, g_up),):
            x_main = held[:, :, :, pl.ds(pl.multiple_of(i * 128, 128), 128)].reshape(4, half, 128)
            x_extra = held[:, :, :, pl.ds(pl.multiple_of(2 * model + i * 128, 128), 128)].reshape(4, half, 128)
            rows = jnp.concatenate([x_main, x_extra], axis=1).reshape(8 * half, 128)
            total = inner_rows(rows, kept[...].reshape(8 * half, hidden))
            out[cols, :] = total.astype(BF16)
        g_main = held[:, :, :, pl.ds(pl.multiple_of(model + i * 128, 128), 128)].reshape(4, half, 128)
        rows = jnp.concatenate([g_main, x_extra], axis=1).reshape(8 * half, 128)
        g_down[:, cols] = inner_rows(hid_w[...].reshape(8 * half, hidden), rows).astype(BF16)
        return carry

    lax.fori_loop(0, model // 128, weight_grads, 0)

    for ring in (sums_up, sums_down):
        ring.begin()
    moves[2].start()
    moves[3].start()
    for at in range(4):
        n = via_right[at]
        h_copies[n].wait_recv()
        results[right, source[n]] = (results[right, source[n]].astype(F32) + half_left[at].astype(F32)).astype(BF16)
        toward_right(n)
        n = via_left[at]
        h_copies[n].wait_recv()
        results[left, source[n]] = (results[left, source[n]].astype(F32) + half_right[at].astype(F32)).astype(BF16)
        toward_left(n)
    b_copies = []
    for n in (4, 5, 3, 7, 2, 6, 1, 0):
        c_copies[n].wait_recv()
        k_copies[n].wait_recv()
        total = results[h, source[n]].astype(F32) + from_left[n].astype(F32) + from_right[n].astype(F32)
        if n:
            sums[n] = total.astype(BF16)
            copy = remote(sums.at[n], back.at[e], b_send.at[n], b_recv.at[n], to_source[n])
            copy.start()
            b_copies.append(copy)
        else:
            back[e] = total.astype(BF16)
    for copy in b_copies:
        copy.wait_recv()
    main, top, low_half, onehot = slot_picks(routes[...], slots.shape[0])
    lines = back[...].reshape(128, 3 * model)
    shares = probs[...]
    gate = jnp.sum(shares * onehot, axis=-1, keepdims=True)
    hid, grad_output, low = hid_in[...], cotangent[...].astype(F32), moe_low[...]
    expert_out = inner_rows(main, lines[:, :model]) + inner_rows(top, lines[:, 2 * model :])
    output[...] = (hid + gate * expert_out).astype(BF16)
    grad_gate = jnp.sum(grad_output * expert_out, axis=-1, keepdims=True)
    grad_logits = (gate * grad_gate * (onehot - shares)).astype(BF16)
    grad_moe = inner_rows(main, lines[:, model : 2 * model]) + inner_rows(low_half, lines[:, 2 * model :])
    grad_moe = grad_moe + matmul(grad_logits, gains[...].astype(BF16))
    scale = lax.rsqrt(jnp.mean(hid * hid, axis=-1, keepdims=True) + EPS)
    scaled = grad_moe * gains[1:2, :]
    inside = jnp.mean(scaled * hid, axis=-1, keepdims=True)
    grad_hidden[...] = grad_output + scale * scaled - hid * (scale * scale * scale * inside)
    grad_gain = jnp.sum(grad_moe * hid * scale, axis=0, keepdims=True)
    at = lax.broadcasted_iota(jnp.int32, norm_out.shape, 0)
    norm_out[...] = inner_rows(grad_logits, low) + jnp.where(at == 1, grad_gain, 0.0)
    for ring in (sums_up, sums_down):
        ring.end()
    moves[2].wait()
    moves[3].wait()
    for copy in d_copies[1:] + r_copies + l_copies + f_copies + c_copies + k_copies + h_copies + b_copies:
        copy.wait_send()


def across(tile, width):
    whole = width // 128
    return jnp.concatenate([tile] * whole + [tile[:, : width - 128 * whole]], axis=1)


def eye(size):
    at = [lax.broadcasted_iota(jnp.int32, (size, size), axis) for axis in (0, 1)]
    return (at[0] == at[1]).astype(BF16)


def both_cols(lines, main, extra):
    return jnp.concatenate([outer_cols(lines, main), outer_cols(lines, extra)], axis=1)


class Gather:
    def __init__(self, source, place, send, recv):
        self.source, self.place, self.send, self.recv = source, place, send, recv
        e, r, h = places()
        self.c = lax.rem(e, 2)
        y = e // 2
        self.f0 = y * (1 - self.c) + r * self.c
        self.s0 = r * (1 - self.c) + y * self.c
        self.own = e * 4 + r
        self.mate, self.first, self.second = mixer_peers()

    def copy(self, at, peer, block=None):
        target = self.place(self.own if block is None else block)
        return remote(self.source if block is None else target, target, self.send.at[at], self.recv.at[at], peer)

    def came(self, k, j=None):
        s = self.s0 if j is None else lax.rem(self.s0 + 3 - j, 4)
        return block_at(self.c, lax.rem(self.f0 + 4 - k, 4), s)

    def begin(self):
        for k in (1, 0, 2):
            self.copy(k, self.first[k]).start()

    def begin_second(self):
        for j in (1, 0, 2):
            self.copy(3 + j, self.second[j]).start()
        self.copy(15, self.mate).start()

    def relay_first(self):
        for k in range(3):
            self.copy(k, self.first[k]).wait_recv()
            block = self.came(k + 1)
            for j in (1, 0, 2):
                self.copy(6 + 3 * k + j, self.second[j], block).start()
            self.copy(16 + k, self.mate, block).start()

    def relay_second(self):
        for k in range(4):
            for j in range(3):
                self.copy(3 + 3 * k + j, self.second[j]).wait_recv()
                self.copy(19 + 3 * k + j, self.mate, self.came(k, j)).start()

    def end(self):
        for at in range(15, 31):
            self.copy(at, self.mate).wait_recv()

    def sent(self):
        for at in range(31):
            self.copy(at, self.mate).wait_send()


def slot_picks(route, experts, states=16):
    count = route.shape[1]
    line = lax.broadcasted_iota(jnp.int32, (states, count), 0)
    chosen = jnp.where(line - 2 == route, 1.0, 0.0)
    earlier = lax.broadcasted_iota(jnp.int32, (count, count), 0) <= lax.broadcasted_iota(jnp.int32, (count, count), 1)
    counts = matmul(chosen.astype(BF16), jnp.where(earlier, 1.0, 0.0).astype(BF16))
    within = jnp.sum(chosen * (counts - 1.0), axis=0, keepdims=True).astype(jnp.int32)
    slot = lax.broadcasted_iota(jnp.int32, (experts * MAIN, count), 0)
    line, expert = slot % MAIN, slot // MAIN
    here = expert == route

    def of(found):
        return jnp.where(found, 1.0, 0.0).astype(BF16)

    main = of(here & (within == line))
    top = of(here & (line < 8) & (within == line + 16))
    low = of(here & (line >= 8) & (within == line + 8))
    column = jnp.broadcast_to(route.astype(F32), (count, count)).T[:, :states]
    place = lax.broadcasted_iota(jnp.int32, (count, states), 1) - 2
    onehot = jnp.where(place.astype(F32) == column, 1.0, 0.0)
    return main, top, low, onehot


def other_core_peers():
    e, r, h = places()
    c = lax.rem(e, 2)
    return [(2 * lax.rem(e // 2 + k, 4) + 1 - c, r, h) for k in (1, 2, 3)]


def forward_part(refs):
    (
        in_lines, out_lines, x_cols, dt_cols, decay_in, taps_in, conv_bias, dt_bias, skip, gain_one, gain_two,
        router, tokens, resets, routes, cotangent,
        whole_hbm, seq_hbm, extra_hbm, normed_hbm, x_low_hbm, u_hbm, gate_hbm, proj_hbm, lin_hbm, y_hbm, gated_hbm,
        starts_hbm, params, gains, hidden, slots, moe_out, probs,
        pack, norm, line, whole_all, norms, seq, extra, tiles, total, local_sems, z_send, z_recv, n_send, n_recv,
        w_send, w_recv, v_send, v_recv, o_send, o_recv, k_sems, s_sems,
        normed, x_low, u_out, gate_z, proj, dt_lin, y_out, gated, starts,
        xs, marks, conv, dtm, dtx, parts, own, landing, branch, came, p_send, p_recv, b_send, b_recv, quarters, owned, q_send, q_recv,
    ) = refs
    e, r, h = places()
    block, model = tokens.shape
    inner, states, experts = u_out.shape[1], starts.shape[1], router.shape[0]
    lines, small = block // STEP, 3 * model
    channels, share = in_lines.shape[0], gain_one.shape[1]

    z_peers = hid_peers()
    mate, first, second = mixer_peers()
    hail([mate] + first + second + z_peers + other_core_peers())

    def wide(a):
        return a[...].astype(F32)

    line[:, :model] = tokens[...]
    line[:, model:] = jnp.broadcast_to(wide(resets), (block, 128)).T.astype(BF16)
    columns = jnp.concatenate(
        [
            wide(decay_in), wide(taps_in), wide(conv_bias), wide(dt_bias), wide(skip),
            jnp.zeros((105, channels), F32),
        ],
        axis=0,
    )
    columns = jnp.concatenate([columns, jnp.zeros((128, 128 - channels), F32)], axis=1).T[:channels, :24]
    tail = jnp.concatenate(
        [
            jnp.concatenate([wide(x_cols), columns], axis=1),
            jnp.concatenate([wide(dt_cols), jnp.zeros((channels, 128 - dt_cols.shape[1]), F32)], axis=1),
        ],
        axis=1,
    )
    in_float = wide(in_lines)
    both = jnp.concatenate([in_float[:, 0], in_float[:, 1], wide(out_lines), tail], axis=1)
    pack[:, : 2 * model] = both[:MAIN, : 2 * model].astype(BF16)
    pack[:, 2 * model : 2 * model + 256] = both[:MAIN, small:].astype(BF16)
    pack[:, 2 * model + 768 :] = both[:MAIN, 2 * model : small].astype(BF16)
    last = jnp.concatenate([both[MAIN:], jnp.zeros((channels - MAIN, 4096 - small - 256), F32)], axis=1)
    last = [last[n : n + 1, k * EXTRA : (k + 1) * EXTRA] for n in range(2) for k in range(8)]
    pack[:, 2 * model + 256 : 2 * model + 768] = jnp.concatenate(last, axis=0).astype(BF16)
    tile = jnp.concatenate([wide(gain_one), wide(gain_two), wide(router), jnp.zeros((6, share), F32)], axis=0)
    tile = jnp.concatenate([tile, jnp.zeros((MAIN, 128 - share), F32)], axis=1)
    norm[...] = pltpu.roll(tile, h * share, 1).astype(BF16)
    pl.semaphore_wait(pltpu.get_barrier_semaphore(), 13)
    mine = pl.ds(pl.multiple_of(h * block, block), block)
    late = 2 * model + 768

    def owner_rows(n):
        return pl.ds(pl.multiple_of(n * MAIN, MAIN), MAIN)

    main = Gather(pack.at[:, :late], lambda n: whole_all.at[owner_rows(n), :late], w_send, w_recv)
    out_part = Gather(pack.at[:, late:], lambda n: whole_all.at[owner_rows(n), late:], o_send, o_recv)
    norm_part = Gather(total, lambda n: norms.at[n], v_send, v_recv)
    n_copies = [remote(norm, tiles.at[k], n_send.at[k], n_recv.at[k], z_peers[k]) for k in range(3)]
    z_copies = [remote(line, seq.at[mine], z_send.at[k], z_recv.at[k], z_peers[k]) for k in range(3)]
    own_copies = [
        pltpu.make_async_copy(pack, whole_all.at[owner_rows(main.own)], local_sems.at[0]),
        pltpu.make_async_copy(line, seq.at[mine], local_sems.at[1]),
    ]
    for copy in n_copies:
        copy.start()
    main.begin()
    main.begin_second()
    for n in (1, 0, 2):
        z_copies[n].start()
    for copy in own_copies:
        copy.start()
    for copy in n_copies:
        copy.wait_recv()
    total[...] = norm[...] + tiles[0] + tiles[1] + tiles[2]
    norms[main.own] = total[...]
    norm_part.begin()
    norm_part.begin_second()
    main.relay_first()
    norm_part.relay_first()
    out_part.begin()
    main.relay_second()
    norm_part.relay_second()
    out_part.begin_second()
    out_part.relay_first()
    norm_part.end()
    span = share * 4
    gains[...] = jnp.concatenate([norms[n].astype(F32)[:, :span] for n in range(32)], axis=1)
    for copy in z_copies:
        copy.wait_recv()
    for copy in own_copies:
        copy.wait()
    main.end()
    row = lax.broadcasted_iota(jnp.int32, (512, 512), 0)
    col = lax.broadcasted_iota(jnp.int32, (512, 512), 1)
    wanted = (row % 64 // 2) * MAIN + (row % 2) * 8 + row // 64
    moved = matmul((wanted == col).astype(BF16), whole_all[:, 2 * model + 256 : late]).astype(BF16)
    for k in range(8):
        extra[:, k * 512 : (k + 1) * 512] = moved[k * 64 : (k + 1) * 64]
    params[...] = both_cols(eye(128), whole_all[:, 2 * model : 2 * model + 128], extra[:, small : small + 128])
    kept_copies = [
        pltpu.make_async_copy(kept, out, k_sems.at[n])
        for n, (kept, out) in enumerate(((whole_all, whole_hbm), (seq, seq_hbm), (extra, extra_hbm)))
    ]
    for copy in kept_copies[1:]:
        copy.start()
    xs[0:8] = jnp.zeros((8, inner), F32)
    marks[0:8] = jnp.zeros((8, 128), F32)
    gain = gains[0:1, :]

    pairs = (
        (normed, normed_hbm), (x_low, x_low_hbm), (u_out, u_hbm), (gate_z, gate_hbm), (proj, proj_hbm),
        (dt_lin, lin_hbm), (y_out, y_hbm), (gated, gated_hbm), (starts, starts_hbm),
    )

    def saved_copy(n, b):
        kept, out = pairs[n]
        size = kept.shape[0] // 4
        rows = pl.ds(pl.multiple_of(b * size, size), size)
        return pltpu.make_async_copy(kept.at[rows], out.at[rows], s_sems.at[n, b])

    def proj_copy(b, k):
        at = k * 4 + b
        return remote(own.at[b], landing.at[k, b], p_send.at[at], p_recv.at[at], z_peers[k])

    def normalize(b, carry):
        rows = pl.ds(pl.multiple_of(b * block, block), block)
        values = seq[rows, :model].astype(F32)
        scale = lax.rsqrt(jnp.mean(values * values, axis=-1, keepdims=True) + EPS)
        low = (values * scale * gain).astype(BF16)
        normed[rows, :] = low
        return carry

    lax.fori_loop(0, 4, normalize, 0)
    x_low[...] = both_cols(normed[...], whole_all[:, :model], extra[:, :model]).astype(BF16)
    gate_z[...] = both_cols(normed[...], whole_all[:, model : 2 * model], extra[:, model : 2 * model])

    def stage_one(b, carry):
        start = pl.multiple_of(b * block, block)
        rows = pl.ds(start, block)
        x = x_low[rows, :]
        after = pl.ds(pl.multiple_of(8 + start, 8), block)
        xs[after, :] = x.astype(F32)
        now = seq[rows, model:].astype(F32)
        marks[after, :] = now
        lines_x, lines_m = xs[pl.ds(start, block + 8), :], marks[pl.ds(start, block + 8), :]
        mask = 1.0 - now
        total = params[124:125, :] + params[123:124, :] * x.astype(F32)
        for back in (1, 2, 3):
            past = lines_x[8 - back : 8 - back + block]
            total = total + params[123 - back : 124 - back, :] * past * across(mask, inner)
            if back < 3:
                mask = mask * (1.0 - lines_m[8 - back : 8 - back + block])
        u_out[rows, :] = total
        convolved = total * jax.nn.sigmoid(total)
        conv[rows, :] = convolved
        conv_low = convolved.astype(BF16)
        share = matmul(conv_low[:, :512], whole_all[:, 2 * model : 2 * model + 128]) + matmul(
            conv_low[:, 512:], extra[:, small : small + 128]
        )
        own[b] = share.astype(BF16)
        for k in (1, 0, 2):
            proj_copy(b, k).start()
        for n in range(4):
            saved_copy(n, b).start()
        return carry

    lax.fori_loop(0, 4, stage_one, 0)
    out_part.relay_second()
    out_part.end()
    kept_copies[0].start()
    a = jnp.exp(params[104:120, :]) * (-LOG2E)
    half = states // 2

    quarter = block // 4

    def part_copy(b, k):
        rows = pl.ds(pl.multiple_of(lax.rem(h + 1 + k, 4) * quarter, quarter), quarter)
        at = k * 4 + b
        return remote(branch.at[b, rows], came.at[k, b], b_send.at[at], b_recv.at[at], z_peers[k])

    def whole_copy(b, sender):
        return remote(quarters.at[b], owned.at[sender], q_send.at[b], q_recv.at[sender], (e, r, b))

    def sum_up(b):
        rows = pl.ds(pl.multiple_of(h * quarter, quarter), quarter)
        for k in range(3):
            part_copy(b, k).wait_recv()
        total = branch[b, rows, :].astype(F32)
        for k in range(3):
            total = total + came[k, b].astype(F32)
        quarters[b] = total.astype(BF16)

        @pl.when(b != h)
        def send():
            whole_copy(b, lax.rem(h - b + 4, 4) - 1).start()

    def stage_two(b, state):
        start = pl.multiple_of(b * block, block)
        rows = pl.ds(start, block)
        for k in range(3):
            proj_copy(b, k).wait_recv()
        sums = (
            own[b].astype(F32) + landing[0, b].astype(F32) + landing[1, b].astype(F32) + landing[2, b].astype(F32)
        )
        proj[rows, :] = sums
        lin = both_cols(sums.astype(BF16), whole_all[:, 2 * model + 128 : 2 * model + 256], extra[:, small + 128 : small + 256])
        lin = lin + params[125:126, :]
        dt_lin[rows, :] = lin
        dt = jax.nn.softplus(lin)
        convolved = conv[rows, :]
        dtm[...] = dt + across(STOP * marks[pl.ds(pl.multiple_of(8 + start, 8), block), :], inner)
        dtx[...] = dt * convolved
        turned = sums.T
        b_all, c_all = turned[72:88], turned[88:104]

        def chunk(i, h_now):
            starts[b * lines + i] = h_now
            shift = lax.rem(block - i * STEP, block)
            b_now, c_now = pltpu.roll(b_all, shift, 1), pltpu.roll(c_all, shift, 1)
            rows_m, rows_x = (ref[pl.ds(pl.multiple_of(i * STEP, STEP), STEP), :] for ref in (dtm, dtx))
            for j in range(STEP):
                decay = jnp.exp2(a * rows_m[j : j + 1])
                h_now = decay * h_now + b_now[:, j : j + 1] * rows_x[j : j + 1]
                p = c_now[:, j : j + 1] * h_now
                put_rows(parts, j, p[:half] + p[half:])
            here = pl.ds(pl.multiple_of(start + i * STEP, STEP), STEP)
            y_out[here, :] = summed_groups(parts, half, inner)
            return h_now

        state = lax.fori_loop(0, lines, chunk, state)
        y = y_out[rows, :] + params[126:127, :] * convolved
        y_out[rows, :] = y
        z = gate_z[rows, :]
        low = (y * z * jax.nn.sigmoid(z)).astype(BF16)
        gated[rows, :] = low
        out = matmul(low[:, :512], whole_all[:, late:]) + matmul(low[:, 512:], extra[:, 2 * model : small])
        branch[b] = out.astype(BF16)

        for k in (1, 0, 2):
            part_copy(b, k).start()

        @pl.when(b > 0)
        def earlier():
            sum_up(b - 1)

        for n in range(4, 9):
            saved_copy(n, b).start()
        return state

    lax.fori_loop(0, 4, stage_two, jnp.zeros((states, inner), F32))
    sum_up(3)
    for k in range(3):
        whole_copy(0, k).wait_recv()
    mine = pl.ds(pl.multiple_of(h * block, block), block)
    hidden[...] = seq[mine, :model].astype(F32)
    for k in range(4):
        rows = pl.ds(pl.multiple_of(lax.rem(h + k, 4) * quarter, quarter), quarter)
        piece = owned[k - 1] if k else quarters[h]
        hidden[rows, :] += piece.astype(F32)
    hid = hidden[...]
    scale = lax.rsqrt(jnp.mean(hid * hid, axis=-1, keepdims=True) + EPS)
    moe_low = (hid * scale * gains[1:2, :]).astype(BF16)
    moe_out[...] = moe_low
    logits = outer_cols(moe_low, gains[...].astype(BF16))
    lane = lax.broadcasted_iota(jnp.int32, logits.shape, 1)
    real = (lane >= 2) & (lane < 2 + experts)
    logits = jnp.where(real, logits, -1e30)
    powers = jnp.exp(logits - jnp.max(logits, axis=-1, keepdims=True))
    shares = powers / jnp.sum(powers, axis=-1, keepdims=True)
    probs[...] = shares
    pick_main, top, low_half, onehot = slot_picks(routes[...], experts)
    gate = jnp.sum(shares * onehot, axis=-1, keepdims=True)
    grad_eo = (gate * cotangent[...].astype(F32)).astype(BF16)
    shape = (experts, MAIN, model)
    slots[:, :, :model] = matmul(pick_main, moe_low).astype(BF16).reshape(shape)
    slots[:, :, model : 2 * model] = matmul(pick_main, grad_eo).astype(BF16).reshape(shape)
    slots[:, :, 2 * model :] = (matmul(top, moe_low) + matmul(low_half, grad_eo)).astype(BF16).reshape(shape)
    for n in range(9):
        for b in range(4):
            saved_copy(n, b).wait()
    for copy in kept_copies:
        copy.wait()
    for part in (main, out_part, norm_part):
        part.sent()
    for copy in n_copies + z_copies:
        copy.wait_send()
    for b in range(4):
        for k in range(3):
            proj_copy(b, k).wait_send()
            part_copy(b, k).wait_send()

        @pl.when(b != h)
        def sent():
            whole_copy(b, 0).wait_send()


def layer_kernel(*refs):
    ins, up_down, saved = refs[:16], refs[16:18], refs[18:30]
    params, gains, output, grad_hidden, norm_out, up_out, down_out, ring_up, ring_down = refs[30:39]
    hidden, slots, moe_low, probs, *scratch = refs[39:]
    forward_scratch, expert_scratch = scratch[:FORWARD_SCRATCH], scratch[FORWARD_SCRATCH:]
    forward_part((*ins, *saved, params, gains, hidden, slots, moe_low, probs, *forward_scratch))
    expert_part(
        (
            slots, *up_down, hidden, ins[15], moe_low, probs, ins[14], gains, output, grad_hidden, norm_out, up_out,
            down_out, ring_up, ring_down, *expert_scratch,
        )
    )


def mixer_and_experts(arrays, up, down, inner, states, experts):
    tokens = arrays[12]
    block, model = tokens.shape
    length, hidden = 4 * block, up.shape[1]
    width, lines = 3 * model + 768, MAIN
    S, V = jax.ShapeDtypeStruct, pltpu.VMEM
    saved = [
        ((length, model), BF16), ((length, inner), BF16), ((length, inner), F32), ((length, inner), F32),
        ((length, 128), F32), ((length, inner), F32), ((length, inner), F32), ((length, inner), BF16),
        ((length // STEP, states, inner), F32),
    ]
    eighths = [(4, one.shape[0] // 8, one.shape[1]) for one in (up, down)]
    outs = (
        S((512, width), BF16), S((length, model + 128), BF16), S((64, 4096), BF16), *[S(*one) for one in saved],
        S((128, inner), F32), S((MAIN, model), F32), S((block, model), BF16), S((block, model), F32),
        S((MAIN, model), F32), S(up.shape, BF16), S(down.shape, BF16), *[S(size, BF16) for size in eighths],
    )
    eight = DMA((8,))
    forward_scratch = [
            V((MAIN, width), BF16), V((MAIN, 128), BF16), V((block, model + 128), BF16), V((512, width), BF16),
            V((32, MAIN, 128), BF16), V((length, model + 128), BF16), V((64, 4096), BF16),
            V((3, MAIN, 128), BF16), V((MAIN, 128), BF16),
            DMA((3,)), DMA((3,)), DMA((3,)), DMA((3,)), DMA((3,)),
            DMA((31,)), DMA((31,)), DMA((31,)), DMA((31,)), DMA((31,)), DMA((31,)),
            DMA((3,)), DMA((9, 4)),
            *[V(*one) for one in saved],
            V((length + 8, inner), F32), V((length + 8, 128), F32), V((length, inner), F32), V((block, inner), F32),
            V((block, inner), F32), V((-(-inner // 128), STEP * states // 2, 128), F32), V((4, block, 128), BF16),
            V((3, 4, block, 128), BF16), V((4, block, model), BF16), V((3, 4, block // 4, model), BF16),
            DMA((12,)), DMA((12,)), DMA((12,)), DMA((12,)), V((4, block // 4, model), BF16),
            V((3, block // 4, model), BF16), DMA((4,)), DMA((3,)),
    ]
    slot_lines = (lines, 3 * model)
    expert_scratch = [
        V(up.shape, BF16), V(down.shape, BF16), V(up.shape, BF16), V(down.shape, BF16), DMA((4,)), DMA((2, 4)), DMA((2, 4)),
        V((experts, *slot_lines), BF16), V((4, experts, *slot_lines), BF16), V((4, experts, *slot_lines), BF16),
        V((256, hidden), BF16), V((256, hidden), BF16), V((4, 256, hidden), BF16), V((4, 256, hidden), BF16),
        V((8, *slot_lines), BF16), V((8, *slot_lines), BF16), V((4, *slot_lines), BF16), V((4, *slot_lines), BF16),
        V((8, *slot_lines), BF16), *[eight] * 16,
    ]
    assert len(forward_scratch) == FORWARD_SCRATCH
    return pl.pallas_call(
        layer_kernel,
        out_shape=outs,
        in_specs=[IN_VMEM] * 16 + [ANY] * 2,
        out_specs=(*[ANY] * 12, *[IN_VMEM] * 5, ANY, ANY, IN_VMEM, IN_VMEM),
        scratch_shapes=[
            V((block, model), F32), V((experts, *slot_lines), BF16), V((block, model), BF16), V((block, MAIN), F32),
            *forward_scratch, *expert_scratch,
        ],
        compiler_params=pltpu.CompilerParams(
            collective_id=1, has_side_effects=True, vmem_limit_bytes=62 << 20
        ),
        name="mixer_and_experts",
    )(*arrays, up, down)


class Flow:
    ORDER = (2, 1, 3, 0)

    def __init__(self, turn, source, out, pairs, halves, fours, lines, ends, send, recv):
        self.source, self.out, self.pairs, self.halves = source, out, pairs, halves
        self.fours, self.lines, self.ends, self.send, self.recv = fours, lines, ends, send, recv
        e, r, h = places()
        self.c = lax.rem(e, 2)
        y = e // 2
        self.turn = self.c if turn is None else turn
        self.mate_turn = 1 - self.c if turn is None else turn
        self.f0 = y * (1 - self.turn) + r * self.turn
        self.s0 = r * (1 - self.turn) + y * self.turn
        self.mate_s0 = r * (1 - self.mate_turn) + y * self.mate_turn
        self.mate, self.first, self.second_peers = mixer_peers(self.turn)

    def copy(self, src, dst, at, peer):
        return remote(src, dst, self.send.at[at], self.recv.at[at], peer)

    def mate_copy(self, n, f):
        s = lax.rem(self.mate_s0 + self.ORDER[n], 4)
        block = block_at(1 - self.c, f, s, self.mate_turn)
        return self.copy(self.source.at[block], self.pairs.at[n, f], n * 4 + f, self.mate)

    def second_copy(self, n):
        return self.copy(self.halves.at[n], self.fours.at[n], 16 + n, self.second_peers[self.ORDER[n] - 1])

    def first_copy(self, n):
        return self.copy(self.lines.at[n], self.ends.at[n], 19 + n, self.first[self.ORDER[n] - 1])

    def begin(self):
        for n in range(4):
            for f in range(4):
                self.mate_copy(n, f).start()

    def second(self):
        for n, k in enumerate(self.ORDER):
            s = lax.rem(self.s0 + k, 4)
            for f in range(4):
                self.mate_copy(n, f).wait_recv()
                total = self.source[block_at(self.c, f, s, self.turn)].astype(F32) + self.pairs[n, f].astype(F32)
                self.halves[n, f] = total.astype(BF16)
            if k:
                self.second_copy(n).start()

    def third(self):
        for n in range(3):
            self.second_copy(n).wait_recv()
        for n, k in enumerate(self.ORDER):
            f = lax.rem(self.f0 + k, 4)
            line = self.halves[3, f].astype(F32)
            for m in range(3):
                line = line + self.fours[m, f].astype(F32)
            if k:
                self.lines[n] = line.astype(BF16)
                self.first_copy(n).start()
            else:
                self.out[...] = line

    def finish(self):
        for n in range(3):
            self.first_copy(n).wait_recv()
        self.out[...] = (
            self.out[...] + self.ends[0].astype(F32) + self.ends[1].astype(F32) + self.ends[2].astype(F32)
        )

    def end(self):
        for n in range(4):
            for f in range(4):
                self.mate_copy(n, f).wait_send()
        for n in range(3):
            self.second_copy(n).wait_send()
            self.first_copy(n).wait_send()


def flow_scratch(width):
    return [
        pltpu.VMEM((32, MAIN, width), BF16), pltpu.VMEM((MAIN, width), F32), pltpu.VMEM((4, 4, MAIN, width), BF16),
        pltpu.VMEM((4, 4, MAIN, width), BF16), pltpu.VMEM((3, 4, MAIN, width), BF16),
        pltpu.VMEM((3, MAIN, width), BF16), pltpu.VMEM((3, MAIN, width), BF16), DMA((22,)), DMA((22,)),
    ]


def mixer_back_kernel(*refs):
    (
        grad_hidden, seq_all, whole_in, gains, norm_in, normed_in, x_low_in, u_all, gate_all, proj_in, lin_all, y_all,
        gated_in, starts_in, params, extra_in, g_up, g_down, came_up, came_down,
        grad_tokens, grad_in, grad_out, grad_x, grad_dt, by_channel, by_feature, all_up, all_down,
        seq_own, seq_marks, whole, normed, x_low, u_in, gate_z, proj, dt_lin, y_in, gated, starts, extra, in_sems,
        ghs, gus, marks, dts, dtm, dtx, conv, s1, s2, gdl, ggate, gx, gp_all,
        conv_low, held, decays, parts_1, parts_2, lanes_b, lanes_c, state, g_rate, rows_sum, own, landing, branch, came,
        a_send, a_recv, p_send, p_recv, b_send, b_recv, quarters, owned, q_send, q_recv, x_send, x_recv, x_local,
        e_slots_up, e_own_up, e_sums_up, total_up, e_slots_down, e_own_down, e_sums_down, total_down,
        y_send, y_recv, y_local, own_tile, tiles, z_send, z_recv, *flow_refs, gain_sum,
    ) = refs
    e, r, h = places()
    block, model = grad_hidden.shape
    inner, states = u_in.shape[1], starts.shape[1]
    lines, half, small = block // STEP, states // 2, 3 * model
    owners = 32
    z_peers = hid_peers()
    mate, first, second = mixer_peers()
    hail([mate] + first + second + z_peers)
    mine = pl.ds(pl.multiple_of(h * block, block), block)
    loads = [
        (lin_all, dt_lin), (u_all, u_in), (gate_all, gate_z), (y_all, y_in), (seq_all.at[:, model:], seq_marks),
        (proj_in, proj), (starts_in, starts), (whole_in, whole), (extra_in, extra), (x_low_in, x_low),
        (gated_in, gated), (normed_in, normed), (seq_all.at[mine, :model], seq_own),
    ]
    loads = [pltpu.make_async_copy(a, b, in_sems.at[n]) for n, (a, b) in enumerate(loads)]
    for copy in loads:
        copy.start()
    sums = [
        RowsSum(g_up, came_up, e_slots_up, e_own_up, e_sums_up, total_up, y_send.at[0], y_recv.at[0], y_local.at[0]),
        RowsSum(
            g_down, came_down, e_slots_down, e_own_down, e_sums_down, total_down, y_send.at[1], y_recv.at[1], y_local.at[1]
        ),
    ]
    rings = [
        RowsGather(part, whole_grad, x_send.at[n], x_recv.at[n], x_local.at[n])
        for n, (part, whole_grad) in enumerate(((total_up, all_up), (total_down, all_down)))
    ]
    for ring in sums:
        for n in (4, 0, 1, 2, 3):
            ring.load(n).start()
    ghs[h] = grad_hidden[...].astype(BF16)
    pl.semaphore_wait(pltpu.get_barrier_semaphore(), 10)
    right, left, middle = lax.rem(h + 1, 4), lax.rem(h + 3, 4), block // 2
    passed = (ghs.at[left, :middle], ghs.at[right, middle:])
    gh_copies = [
        remote(ghs.at[h], ghs.at[h], a_send.at[0], a_recv.at[0], (e, r, right)),
        remote(ghs.at[h], ghs.at[h], a_send.at[1], a_recv.at[1], (e, r, left)),
        remote(passed[0], passed[0], a_send.at[2], a_recv.at[2], (e, r, right)),
        remote(passed[1], passed[1], a_send.at[3], a_recv.at[3], (e, r, left)),
    ]
    for k in range(2):
        gh_copies[k].start()
    for ring in sums:
        ring.pass_on()
    flow_early, flow_in, flow_rest = [
        Flow(1 if n == 0 else None, *flow_refs[9 * n : 9 * n + 9]) for n in range(3)
    ]
    state[...] = jnp.zeros_like(state)
    g_rate[...] = jnp.zeros_like(g_rate)
    rows_sum[...] = jnp.zeros_like(rows_sum)
    gain_sum[...] = jnp.zeros_like(gain_sum)
    gus[512:520] = jnp.zeros((8, inner), F32)
    a = jnp.exp(params[104:120, :]) * (-LOG2E)
    for copy in loads[:5]:
        copy.wait()
    marks[0:512] = seq_marks[...].astype(F32)
    marks[512:520] = jnp.zeros((8, 128), F32)

    def prepare(b, carry):
        rows = pl.ds(pl.multiple_of(b * block, block), block)
        lin = dt_lin[rows, :]
        dt = jax.nn.softplus(lin)
        dt_lin[rows, :] = jax.nn.sigmoid(lin)
        u_now = u_in[rows, :]
        convolved = u_now * jax.nn.sigmoid(u_now)
        conv[rows, :] = convolved
        conv_low[rows, :] = convolved.astype(BF16)
        dts[rows, :] = dt
        dtm[rows, :] = dt + across(STOP * marks[rows, :], inner)
        dtx[rows, :] = dt * convolved
        z = gate_z[rows, :]
        sig = jax.nn.sigmoid(z)
        gate_z[rows, :] = z * sig
        y_in[rows, :] = y_in[rows, :] * (sig * (1.0 + z * (1.0 - sig)))
        return carry

    lax.fori_loop(0, 4, prepare, 0)
    for k in range(2):
        gh_copies[k].wait_recv()
        gh_copies[2 + k].start()
    for copy in loads[5:]:
        copy.wait()

    def spots(shape, axis):
        return lax.broadcasted_iota(jnp.int32, shape, axis)

    tall = (block * states, 128)
    ones = jnp.ones((128, 128), BF16)

    extras = []

    def weight(left, right, target, at, size):
        main = inner_rows(left[:, :512], right)
        target[:, :, at : at + size] = main.astype(BF16).reshape(owners, MAIN, size)
        extras.append(inner_rows(left[:, 512:], right).astype(BF16))

    for copy in gh_copies[2:]:
        copy.wait_recv()
    gh_rows, low_norm = ghs[...].reshape(4 * block, model), normed[...]
    gg = both_cols(gh_rows, whole[:, 2 * model + 768 :], extra[:, 2 * model : small])
    gate_z[...] = gg * gate_z[...]
    ggate[...] = (gg * y_in[...]).astype(BF16)
    weight(gated[...], gh_rows, flow_early.source, 0, model)
    weight(ggate[...], low_norm, flow_early.source, model, model)
    flow_early.begin()
    for ring, gather in zip(sums, rings):
        ring.finish()
        gather.begin()

    def proj_copy(b, k):
        at = k * 4 + b
        return remote(own.at[b], landing.at[k, b], p_send.at[at], p_recv.at[at], z_peers[k])

    quarter = block // 4

    def part_copy(b, k):
        rows = pl.ds(pl.multiple_of(lax.rem(h + 1 + k, 4) * quarter, quarter), quarter)
        at = k * 4 + b
        return remote(branch.at[b, rows], came.at[k, b], b_send.at[at], b_recv.at[at], z_peers[k])

    def whole_copy(b, sender):
        return remote(quarters.at[b], owned.at[sender], q_send.at[b], q_recv.at[sender], (e, r, b))

    def sum_up(b):
        rows = pl.ds(pl.multiple_of(h * quarter, quarter), quarter)
        for k in range(3):
            part_copy(b, k).wait_recv()
        total = branch[b, rows, :].astype(F32)
        for k in range(3):
            total = total + came[k, b].astype(F32)
        quarters[b] = total.astype(BF16)

        @pl.when(b != h)
        def send():
            whole_copy(b, lax.rem(h - b + 4, 4) - 1).start()

    def stage_a(b):
        start = pl.multiple_of(b * block, block)
        rows = pl.ds(start, block)
        turned = proj[rows, :].T
        b_all, c_all = turned[72:88], turned[88:104]

        gy_now = gate_z[rows, :]

        def chunk(step, u):
            i = lines - 1 - step
            hh = starts[b * lines + i]
            held[0] = hh
            shift = lax.rem(block - i * STEP, block)
            b_now, c_now = pltpu.roll(b_all, shift, 1), pltpu.roll(c_all, shift, 1)
            there = pl.ds(pl.multiple_of(start + i * STEP, STEP), STEP)
            rows_m, rows_x, rows_g, rows_t = (ref[there, :] for ref in (dtm, dtx, gate_z, dts))
            for j in range(STEP):
                decay = jnp.exp2(a * rows_m[j : j + 1])
                hh = decay * hh + b_now[:, j : j + 1] * rows_x[j : j + 1]
                decays[j] = decay
                held[j + 1] = hh
            for j in range(STEP - 1, -1, -1):
                gy_row = rows_g[j : j + 1]
                g = c_now[:, j : j + 1] * gy_row + u
                u = decays[j] * g
                q = u * held[j]
                g_rate[...] += q * rows_t[j : j + 1]
                w = q * a
                put_rows(parts_2, j, w[:half] + w[half:])
                w = g * b_now[:, j : j + 1]
                put_rows(parts_1, j, w[:half] + w[half:])
                at = pl.ds(pl.multiple_of((i * STEP + j) * states, states), states)
                lanes_b[at, :] = over_lanes(g * rows_x[j : j + 1]).astype(BF16)
                lanes_c[at, :] = over_lanes(held[j + 1] * gy_row).astype(BF16)
            here = pl.ds(pl.multiple_of(i * STEP, STEP), STEP)
            s1[here, :] = summed_groups(parts_1, half, inner)
            s2[here, :] = summed_groups(parts_2, half, inner)
            return u

        state[...] = lax.fori_loop(0, lines, chunk, state[...])
        convolved = conv[rows, :]
        grad_lin = dt_lin[rows, :] * (convolved * s1[...] + s2[...] * (1.0 / LOG2E))
        low = grad_lin.astype(BF16)
        gdl[rows, :] = low
        rows_sum[5:6, :] += jnp.sum(grad_lin, axis=0, keepdims=True)
        rows_sum[6:7, :] += jnp.sum(gy_now * convolved, axis=0, keepdims=True)
        dts[rows, :] = params[126:127, :] * gy_now + dts[rows, :] * s1[...]
        at_state = spots(tall, 0) % states
        spread = jnp.where(spots(tall, 1) - 72 == at_state, matmul(lanes_b[...], ones), 0.0) + jnp.where(
            spots(tall, 1) - 88 == at_state, matmul(lanes_c[...], ones), 0.0
        )
        share = spread.reshape(block, states, 128).sum(axis=1)
        share = share + matmul(low[:, :512], whole[:, 2 * model + 128 : 2 * model + 256])
        share = share + matmul(low[:, 512:], extra[:, small + 128 : small + 256])
        own[b] = share.astype(BF16)
        for k in (1, 0, 2):
            proj_copy(b, k).start()

    def stage_b(b):
        start = pl.multiple_of(b * block, block)
        rows = pl.ds(start, block)
        for k in range(3):
            proj_copy(b, k).wait_recv()
        gp = (
            own[b].astype(F32) + landing[0, b].astype(F32) + landing[1, b].astype(F32) + landing[2, b].astype(F32)
        ).astype(BF16)
        gp_all[rows, :] = gp
        u_now = u_in[rows, :]
        sig = jax.nn.sigmoid(u_now)
        gu = dts[rows, :] + both_cols(gp, whole[:, 2 * model : 2 * model + 128], extra[:, small : small + 128])
        gu = gu * (sig * (1.0 + u_now * (1.0 - sig)))
        gus[rows, :] = gu
        lines_g, lines_m = gus[pl.ds(start, block + 8), :], marks[pl.ds(start, block + 8), :]
        x = x_low[rows, :].astype(F32)
        total = params[123:124, :] * gu
        rows_sum[3:4, :] += jnp.sum(gu * x, axis=0, keepdims=True)
        rows_sum[4:5, :] += jnp.sum(gu, axis=0, keepdims=True)
        mask = jnp.ones((block, 128), F32)
        for ahead in (1, 2, 3):
            mask = mask * (1.0 - lines_m[ahead : ahead + block])
            moved = lines_g[ahead : ahead + block] * across(mask, inner)
            total = total + params[123 - ahead : 124 - ahead, :] * moved
            rows_sum[3 - ahead : 4 - ahead, :] += jnp.sum(moved * x, axis=0, keepdims=True)
        low = total.astype(BF16)
        gx[rows, :] = low
        gate = ggate[rows, :]
        out = (
            matmul(low[:, :512], whole[:, :model])
            + matmul(low[:, 512:], extra[:, :model])
            + matmul(gate[:, :512], whole[:, model : 2 * model])
            + matmul(gate[:, 512:], extra[:, model : 2 * model])
        )
        branch[b] = out.astype(BF16)

        for k in (1, 0, 2):
            part_copy(b, k).start()
        gain_sum[...] += jnp.sum(out * normed[rows, :].astype(F32), axis=0, keepdims=True)

    def step(n, carry):
        stage_a(3 - n)

        @pl.when(n == 3)
        def early_third():
            flow_early.third()

        @pl.when(n > 0)
        def later():
            stage_b(4 - n)

        @pl.when(n > 1)
        def sum_earlier():
            sum_up(5 - n)

        @pl.when(n == 0)
        def pass_on():
            flow_early.second()

        @pl.when(n == 2)
        def early():
            for ring in rings:
                ring.forward()

        return carry

    lax.fori_loop(0, 4, step, 0)

    flow_early.finish()
    sum_up(1)
    weight(gdl[...], proj[...].astype(BF16), flow_rest.source, 128, 128)
    known = inner_rows(gx[block:], normed[block:])
    stage_b(0)
    tile = norm_in[...] + jnp.where(spots(norm_in.shape, 0) == 0, gain_sum[...] / gains[0:1, :], 0.0)
    own_tile[...] = tile.astype(BF16)
    z_copies = [remote(own_tile, tiles.at[k], z_send.at[k], z_recv.at[k], z_peers[k]) for k in range(3)]
    for copy in z_copies:
        copy.start()
    total = known + inner_rows(gx[:block], normed[:block])
    flow_in.source[...] = total[:512].astype(BF16).reshape(owners, MAIN, model)
    extras.append(total[512:].astype(BF16))
    flow_in.begin()
    ends = jnp.concatenate(
        [jnp.zeros((104, inner), F32), g_rate[...] * (a * (1.0 / LOG2E)), rows_sum[...]], axis=0
    ).astype(BF16)
    low_conv, low_gp, unit = conv_low[...], gp_all[...], eye(128)
    main = inner_rows(low_conv[:, :512], low_gp) + inner_rows(ends[:, :512], unit)
    flow_rest.source[:, :, :128] = main.astype(BF16).reshape(owners, MAIN, 128)
    last = (inner_rows(low_conv[:, 512:], low_gp) + inner_rows(ends[:, 512:], unit)).astype(BF16)
    lines_e = jnp.concatenate(
        [extras[3], extras[1], extras[0], last, extras[2], jnp.zeros((64, 4096 - small - 256), BF16)], axis=1
    )
    stacked = jnp.concatenate([lines_e[:, k * 512 : (k + 1) * 512] for k in range(8)], axis=0)
    row, col = spots((512, 512), 0), spots((512, 512), 1)
    wanted = (col % 64 // 2) * MAIN + (col % 2) * 8 + col // 64
    flow_rest.source[:, :, 256:768] = (
        matmul((wanted == row).astype(BF16), stacked).astype(BF16).reshape(owners, MAIN, 512)
    )
    span = model // owners
    for copy in z_copies:
        copy.wait_recv()
    tile = tile + tiles[0].astype(F32) + tiles[1].astype(F32) + tiles[2].astype(F32)
    for n in range(owners):
        piece = tile[:, n * span : (n + 1) * span]
        piece = jnp.concatenate([piece, jnp.zeros((MAIN, 128 - span), F32)], axis=1)
        flow_rest.source[n, :, 768:] = piece.astype(BF16)
    flow_rest.begin()
    flow_in.second()
    flow_rest.second()
    sum_up(0)
    flow_in.third()
    flow_rest.third()
    for ring in sums + rings:
        ring.end()
    for k in range(3):
        whole_copy(0, k).wait_recv()
    for k in range(4):
        rows = pl.ds(pl.multiple_of(lax.rem(h + k, 4) * quarter, quarter), quarter)
        piece = owned[k - 1] if k else quarters[h]
        grad_tokens[rows, :] = piece.astype(F32)
    grad_n = grad_tokens[...]
    values = seq_own[...].astype(F32)
    scale = lax.rsqrt(jnp.mean(values * values, axis=-1, keepdims=True) + EPS)
    scaled = grad_n * gains[0:1, :]
    inside = jnp.mean(scaled * values, axis=-1, keepdims=True)
    grad_tokens[...] = grad_hidden[...] + scale * scaled - values * (scale * scale * scale * inside)
    flow_rest.finish()
    rest = flow_rest.out[...]
    flow_in.finish()
    rank, wide = grad_dt.shape[1], grad_x.shape[1]
    extra_rows = [
        jnp.concatenate([rest[n * 8 + k : n * 8 + k + 1, 256:768] for k in range(8)], axis=1) for n in range(2)
    ]

    def full(main, at, size):
        return jnp.concatenate([main, *[line[:, at : at + size] for line in extra_rows]], axis=0)

    grad_in[:, 0, :] = full(flow_in.out[...], 0, model)
    grad_in[:, 1, :] = full(flow_early.out[:, model:], model, model)
    grad_out[...] = full(flow_early.out[:, :model], 2 * model, model)
    small_sum = full(rest[:, :256], small, 256)
    grad_x[...] = small_sum[:, :wide]
    grad_dt[...] = small_sum[:, 128 : 128 + rank]
    channels = jnp.concatenate([small_sum[:, :128], jnp.zeros((110, 128), F32)], axis=0)
    by_channel[...] = channels.T[104:128, : grad_out.shape[0]]
    share = by_feature.shape[1]
    by_feature[...] = pltpu.roll(rest[:, 768:], lax.rem(128 - h * share, 128), 1)[:, :share]
    for flow in (flow_early, flow_in, flow_rest):
        flow.end()
    for copy in gh_copies + z_copies:
        copy.wait_send()
    for b in range(4):
        for k in range(3):
            proj_copy(b, k).wait_send()
            part_copy(b, k).wait_send()

        @pl.when(b != h)
        def sent():
            whole_copy(b, 0).wait_send()


def mixer_backward(grad_hidden, seq, whole, gains, norm_in, saved, expert_grads, own, wide, rank):
    normed, x_low, u, gate_z, proj, dt_lin, y, gated, starts, params, extra = saved
    block, model = grad_hidden.shape
    tokens, inner = u.shape
    states = starts.shape[1]
    S = jax.ShapeDtypeStruct
    g_up, g_down, came_up, came_down = expert_grads

    def like(array):
        return pltpu.VMEM(array.shape, array.dtype)

    line, low = pltpu.VMEM((block, inner), F32), pltpu.VMEM((tokens, inner), BF16)
    tall = pltpu.VMEM((tokens, inner), F32)
    return pl.pallas_call(
        mixer_back_kernel,
        out_shape=(
            S((block, model), F32), S((own, 2, model), F32), S((own, model), F32), S((own, wide), F32),
            S((own, rank), F32), S((24, own), F32), S((MAIN, model // 128), F32), S(g_up.shape, BF16),
            S(g_down.shape, BF16),
        ),
        in_specs=[IN_VMEM, ANY, ANY, IN_VMEM, IN_VMEM, *[ANY] * 9, IN_VMEM, *[ANY] * 5],
        out_specs=(*[IN_VMEM] * 7, ANY, ANY),
        scratch_shapes=[
            pltpu.VMEM((block, model), BF16), pltpu.VMEM((tokens, 128), BF16), like(whole), like(normed), like(x_low),
            like(u), like(gate_z), like(proj), like(dt_lin), like(y), like(gated), like(starts), like(extra),
            DMA((13,)),
            pltpu.VMEM((4, block, model), BF16),
            pltpu.VMEM((tokens + 8, inner), F32),
            pltpu.VMEM((tokens + 8, 128), F32),
            tall, tall, tall, tall, line, line,
            low, low, low,
            pltpu.VMEM((tokens, 128), BF16),
            low,
            pltpu.VMEM((STEP + 1, states, inner), F32),
            pltpu.VMEM((STEP, states, inner), F32),
            pltpu.VMEM((-(-inner // 128), STEP * states // 2, 128), F32),
            pltpu.VMEM((-(-inner // 128), STEP * states // 2, 128), F32),
            pltpu.VMEM((block * states, 128), BF16),
            pltpu.VMEM((block * states, 128), BF16),
            pltpu.VMEM((states, inner), F32),
            pltpu.VMEM((states, inner), F32),
            pltpu.VMEM((8, inner), F32),
            pltpu.VMEM((4, block, 128), BF16),
            pltpu.VMEM((3, 4, block, 128), BF16),
            pltpu.VMEM((4, block, model), BF16),
            pltpu.VMEM((3, 4, block // 4, model), BF16),
            DMA((4,)), DMA((4,)), DMA((12,)), DMA((12,)), DMA((12,)), DMA((12,)),
            pltpu.VMEM((4, block // 4, model), BF16), pltpu.VMEM((3, block // 4, model), BF16), DMA((4,)), DMA((3,)),
            DMA((2, 4)), DMA((2, 4)), DMA((2,)),
            like(came_up), like(came_up), like(came_up), pltpu.VMEM((g_up.shape[0] // 4, g_up.shape[1]), BF16),
            like(came_down), like(came_down), like(came_down), pltpu.VMEM((g_down.shape[0] // 4, g_down.shape[1]), BF16),
            DMA((2, 2)), DMA((2, 2)), DMA((2, 5)),
            pltpu.VMEM((MAIN, model), BF16), pltpu.VMEM((3, MAIN, model), BF16), DMA((3,)), DMA((3,)),
            *flow_scratch(2 * model), *flow_scratch(model), *flow_scratch(896),
            pltpu.VMEM((1, model), F32),
        ],
        compiler_params=pltpu.CompilerParams(
            collective_id=5, has_side_effects=True, vmem_limit_bytes=62 << 20
        ),
        name="mixer_backward",
    )(
        grad_hidden, seq, whole, gains, norm_in, normed, x_low, u, gate_z, proj, dt_lin, y, gated, starts, params, extra,
        g_up, g_down, came_up, came_down,
    )


def finish_kernel(*refs):
    (
        channel, feature, up_in, down_in, in_0, in_1, in_2, in_3, in_4, in_5, up, down, result, tokens, grad_in, grad_out, grad_x, grad_dt,
        decay, taps, conv_bias, dt_bias, skip, gain_one, gain_two, router, low_up, low_down, high_up, high_down, *kept, sems,
        k_sems,
    ) = refs
    straight_in = (in_0, in_1, in_2, in_3, in_4, in_5)
    straight_out = (result, tokens, grad_in, grad_out, grad_x, grad_dt)
    parts = 8
    loads = []
    for q in range(parts):
        for n, (a, b) in enumerate(((up_in, low_up), (down_in, low_down))):
            size = a.shape[0] // parts
            rows = pl.ds(q * size, size)
            loads.append(pltpu.make_async_copy(a.at[rows, :], b.at[rows, :], sems.at[n, q]))
            loads[-1].start()
    moves = []
    for n, (a, b, c) in enumerate(zip(straight_in, kept, straight_out)):
        moves.append((pltpu.make_async_copy(a, b, k_sems.at[0, n]), pltpu.make_async_copy(b, c, k_sems.at[1, n])))
        moves[-1][0].start()
    lines = channel[...]
    decay[...] = lines[0:16]
    taps[...] = lines[16:20]
    conv_bias[...] = lines[20:21]
    dt_bias[...] = lines[21:22]
    skip[...] = lines[22:23]
    lines = feature[...]
    gain_one[...] = lines[0:1]
    gain_two[...] = lines[1:2]
    router[...] = lines[2:10]
    stores = []
    for q in range(parts):
        for n, (a, b, c) in enumerate(((low_up, high_up, up), (low_down, high_down, down))):
            size = a.shape[0] // parts
            rows = pl.ds(q * size, size)
            loads[2 * q + n].wait()
            b[rows, :] = a[rows, :].astype(F32)
            stores.append(pltpu.make_async_copy(b.at[rows, :], c.at[rows, :], sems.at[2 + n, q]))
            stores[-1].start()
    for a, b in moves:
        a.wait()
        b.start()
    for copy in stores:
        copy.wait()
    for a, b in moves:
        b.wait()


def finished(output, tokens, grad_in, grad_out, grad_x, grad_dt, channel, feature, low_up, low_down):
    S, own, share = jax.ShapeDtypeStruct, channel.shape[1], feature.shape[1]
    straight = (output, tokens, grad_in, grad_out, grad_x, grad_dt)
    outs = [S(low_up.shape, F32), S(low_down.shape, F32), *[S(a.shape, a.dtype) for a in straight]]
    outs += [S((n, own), F32) for n in (16, 4, 1, 1, 1)] + [S((n, share), F32) for n in (1, 1, 8)]
    up, down, *rest = pl.pallas_call(
        finish_kernel,
        out_shape=outs,
        in_specs=[IN_VMEM] * 2 + [ANY] * 8,
        out_specs=[ANY] * 8 + [IN_VMEM] * 8,
        scratch_shapes=[
            pltpu.VMEM(low_up.shape, BF16), pltpu.VMEM(low_down.shape, BF16), pltpu.VMEM(low_up.shape, F32),
            pltpu.VMEM(low_down.shape, F32), *[pltpu.VMEM(a.shape, a.dtype) for a in straight], DMA((4, 8)), DMA((2, 6)),
        ],
        compiler_params=pltpu.CompilerParams(vmem_limit_bytes=62 << 20),
        name="finish",
    )(channel, feature, low_up, low_down, *straight)
    return *rest, up, down


def shards(
    tokens, resets, routes, cotangent, mixer_gain, in_proj, conv_kernel, conv_bias, x_proj, dt_proj,
    dt_bias, log_decay, skip_gain, out_proj, moe_gain, router, up_proj, down_proj,
):
    model, own, experts = tokens.shape[1], conv_bias.shape[0], router.shape[1]
    rank, states = dt_proj.shape[0], log_decay.shape[0]
    inner = lax.axis_size("expert") * lax.axis_size("rows") * own
    route_row = routes.reshape(1, -1)
    arrays = (
        in_proj.transpose(2, 1, 0), out_proj, x_proj.T, dt_proj.T, log_decay, conv_kernel, conv_bias[None],
        dt_bias[None], skip_gain[None], mixer_gain[None], moe_gain[None], router.T, tokens, resets[None], route_row,
        cotangent,
    )
    whole, sequence, extra, *rest = mixer_and_experts(arrays, up_proj[0], down_proj[0], inner, states, experts)
    saved, (params, gains, output, grad_hidden, norm_grads, *expert_grads) = rest[:9], rest[9:]
    results = mixer_backward(
        grad_hidden, sequence, whole, gains, norm_grads, (*saved, params, extra), expert_grads, own,
        rank + 2 * states, rank,
    )
    (
        output, grad_tokens, grad_in, grad_out, grad_x, grad_dt, grad_decay, grad_taps, grad_conv_bias, grad_dt_bias,
        grad_skip, grad_gain_one, grad_gain_two, grad_router, grad_up_sum, grad_down_sum,
    ) = finished(output, *results)
    return (
        output,
        grad_tokens,
        grad_gain_one[0],
        grad_in.transpose(2, 1, 0),
        grad_taps,
        grad_conv_bias[0],
        grad_x.T,
        grad_dt.T,
        grad_dt_bias[0],
        grad_decay,
        grad_skip[0],
        grad_out,
        grad_gain_two[0],
        grad_router.T,
        grad_up_sum[None],
        grad_down_sum[None],
    )


def solution(mesh):
    every = ("expert", "rows", "hid")
    in_specs = (
        P(every, None), P(every), P(every, None), P(every, None), P(every), P(None, None, every),
        P(None, every), P(every), P(None, every), P(None, every), P(every), P(None, every), P(every),
        P(every, None), P(every), P(every, None), P("expert", None, "hid"), P("expert", "hid", None),
    )
    out_specs = (
        P(every, None), P(every, None), P(every), P(None, None, every), P(None, every), P(every),
        P(None, every), P(None, every), P(every), P(None, every), P(every), P(every, None), P(every),
        P(every, None), P("expert", None, "hid"), P("expert", "hid", None),
    )
    return jax.shard_map(shards, mesh=mesh, in_specs=in_specs, out_specs=out_specs, check_vma=False)
```

```python
from functools import partial

import jax
import jax.numpy as jnp
from jax import lax
from jax.experimental import pallas as pl
from jax.experimental.pallas import tpu as pltpu
from jax.sharding import PartitionSpec as P

EPS = 1e-05
LOG2E = 1.4426950408889634
STOP = 1e6
STEP = 16
FORWARD_SCRATCH = 49
MAIN = 16
EXTRA = 512
GELU_C = 0.7978845608028654
F32 = jnp.float32
BF16 = jnp.bfloat16


def matmul(first_op, second_op):
    return jnp.dot(first_op, second_op, preferred_element_type=F32)


def inner_rows(first_op, second_op):
    return lax.dot_general(
        first_op, second_op, (((0,), (0,)), ((), ())), preferred_element_type=F32
    )


def outer_cols(first_op, second_op):
    return lax.dot_general(
        first_op, second_op, (((1,), (1,)), ((), ())), preferred_element_type=F32
    )


def rms_norm(values, gain):
    return values * lax.rsqrt(jnp.mean(values * values, axis=-1, keepdims=True) + EPS) * gain


def over_lanes(v):
    whole = v.shape[1] // 128
    total = v[:, :128]
    for k in range(1, whole):
        total = total + v[:, k * 128 : (k + 1) * 128]
    rest = v.shape[1] - whole * 128
    if rest:
        blank = jnp.zeros((v.shape[0], 128 - rest), F32)
        total = total + jnp.concatenate([v[:, whole * 128 :], blank], axis=1)
    return total


MESH = pl.DeviceIdType.MESH
ANY = pl.BlockSpec(memory_space=pl.ANY)
IN_VMEM = pl.BlockSpec(memory_space=pltpu.VMEM)
DMA = pltpu.SemaphoreType.DMA


def put_rows(parts, j, values):
    count, width = values.shape
    for k in range(parts.shape[0]):
        size = min(128, width - 128 * k)
        parts[k, j * count : (j + 1) * count, :size] = values[:, 128 * k : 128 * k + size]


def summed_groups(parts, count, width):
    groups = parts.shape[1] // count
    columns = []
    for k in range(parts.shape[0]):
        total = parts[k, pl.ds(0, groups, stride=count), :]
        for n in range(1, count):
            total = total + parts[k, pl.ds(n, groups, stride=count), :]
        columns.append(total[:, : min(128, width - 128 * k)])
    return jnp.concatenate(columns, axis=1)


def places():
    return lax.axis_index("expert"), lax.axis_index("rows"), lax.axis_index("hid")


def hail(peers):
    barrier = pltpu.get_barrier_semaphore()
    for peer in peers:
        pl.semaphore_signal(barrier, inc=1, device_id=peer, device_id_type=MESH)


def greet(peers):
    hail(peers)
    pl.semaphore_wait(pltpu.get_barrier_semaphore(), len(peers))


def remote(src, dst, send_sem, recv_sem, peer):
    return pltpu.make_async_remote_copy(
        src_ref=src, dst_ref=dst, send_sem=send_sem, recv_sem=recv_sem, device_id=peer,
        device_id_type=MESH,
    )


def hid_peers():
    e, r, h = places()
    return [(e, r, lax.rem(h + k, 4)) for k in (1, 2, 3)]


def mixer_peers(turn=None):
    e, r, h = places()
    c = lax.rem(e, 2)
    t = c if turn is None else turn
    mate = (e + 1 - 2 * c, r, h)
    first = [(lax.rem(e + 2 * k * (1 - t), 8), lax.rem(r + k * t, 4), h) for k in (1, 2, 3)]
    second = [(lax.rem(e + 2 * k * t, 8), lax.rem(r + k * (1 - t), 4), h) for k in (1, 2, 3)]
    return mate, first, second


def block_at(c, f, s, turn=None):
    t = c if turn is None else turn
    y = f * (1 - t) + s * t
    x = s * (1 - t) + f * t
    return (2 * y + c) * 4 + x


class RowsPlace:
    def __init__(self, size):
        e, r, h = places()
        self.r, self.size = r, size
        self.right, self.left, self.across = lax.rem(r + 1, 4), lax.rem(r + 3, 4), lax.rem(r + 2, 4)
        self.to_right, self.to_left = (e, self.right, h), (e, self.left, h)

    def rows(self, quarter, part, parts=1):
        return pl.ds(pl.multiple_of((2 * quarter + part) * self.size, self.size), parts * self.size)


class RowsSpread(RowsPlace):
    def __init__(self, source, slots, send, recv):
        super().__init__(slots.shape[1])
        self.source, self.slots, self.send, self.recv = source, slots, send, recv

    def copy(self, n):
        plan = (
            (self.across, 0, 0, self.to_right),
            (self.across, 1, 1, self.to_left),
            (self.right, 1, 2, self.to_right),
            (self.left, 0, 3, self.to_left),
        )
        quarter, half, at, peer = plan[n]
        part = self.source.at[self.rows(quarter, half)]
        return remote(part, self.slots.at[at], self.send.at[n], self.recv.at[n], peer)

    def begin(self):
        for n in range(4):
            self.copy(n).start()

    def end(self):
        for n in range(4):
            self.copy(n).wait_recv()
            self.copy(n).wait_send()


class RowsSum(RowsPlace):
    def __init__(self, source, came, slots, own, sums, total, send, recv, local):
        super().__init__(sums.shape[1])
        self.source, self.came, self.slots, self.own, self.sums, self.total = source, came, slots, own, sums, total
        self.send, self.recv, self.local = send, recv, local

    def load(self, n):
        if n == 4:
            return pltpu.make_async_copy(self.came, self.slots, self.local.at[4])
        quarter, half = ((self.right, 0), (self.left, 1), (self.r, 0), (self.r, 1))[n]
        return pltpu.make_async_copy(self.source.at[self.rows(quarter, half)], self.own.at[n], self.local.at[n])

    def copy(self, n):
        return remote(
            self.sums.at[n], self.sums.at[2 + n], self.send.at[n], self.recv.at[n], (self.to_right, self.to_left)[n]
        )

    def pass_on(self):
        for n in (4, 0, 1):
            self.load(n).wait()
        for n in (0, 1):
            self.sums[n] = (self.slots[n].astype(F32) + self.own[n].astype(F32)).astype(BF16)
            self.copy(n).start()

    def finish(self):
        for n in (2, 3):
            self.load(n).wait()
        for n in (0, 1):
            self.copy(n).wait_recv()
            total = (
                self.own[2 + n].astype(F32) + self.slots[3 - n].astype(F32) + self.sums[2 + n].astype(F32)
            )
            self.total[n * self.size : (n + 1) * self.size, :] = total.astype(BF16)

    def end(self):
        for n in (0, 1):
            self.copy(n).wait_send()


class RowsGather(RowsPlace):
    def __init__(self, quarter, target, send, recv, local):
        super().__init__(quarter.shape[0] // 2)
        self.quarter, self.target, self.send, self.recv, self.local = quarter, target, send, recv, local

    def copy(self, n):
        out = self.target
        plan = (
            (lambda: self.quarter, self.rows(self.r, 0, 2), self.to_right),
            (lambda: self.quarter, self.rows(self.r, 0, 2), self.to_left),
            (lambda: out.at[self.rows(self.left, 0)], self.rows(self.left, 0), self.to_right),
            (lambda: out.at[self.rows(self.right, 1)], self.rows(self.right, 1), self.to_left),
        )
        part, rows, peer = plan[n]
        return remote(part(), out.at[rows], self.send.at[n], self.recv.at[n], peer)

    def own(self):
        return pltpu.make_async_copy(self.quarter, self.target.at[self.rows(self.r, 0, 2)], self.local)

    def begin(self):
        for n in (0, 1):
            self.copy(n).start()
        self.own().start()

    def forward(self):
        for n in (0, 1):
            self.copy(n).wait_recv()
            self.copy(2 + n).start()

    def end(self):
        for n in (2, 3):
            self.copy(n).wait_recv()
        self.own().wait()
        for n in range(4):
            self.copy(n).wait_send()


def gelu_pair(pre, grad):
    square = pre * pre
    t = jnp.tanh(GELU_C * pre * (1.0 + 0.044715 * square))
    up = 0.5 * (1.0 + t)
    slope = up + 0.5 * pre * (1.0 - t * t) * (GELU_C * (1.0 + 3 * 0.044715 * square))
    return pre * up, slope * grad


def expert_part(refs):
    (
        slots, up_in, down_in, hid_in, cotangent, moe_low, probs, routes, gains, output, grad_hidden, norm_out,
        up_out, down_out, ring_up, ring_down, g_up, g_down, up, down, m_sems, x_send, x_recv, back, held, results,
        hid_out, pre_out, hid_w, pre_w, from_left, from_right, half_left, half_right, sums, d_send, d_recv, r_send,
        r_recv, l_send, l_recv, f_send, f_recv, c_send, c_recv, k_send, k_recv, h_send, h_recv, b_send, b_recv,
    ) = refs
    e, r, h = places()
    moves = (
        (up_in, up), (down_in, down), (g_up, up_out), (g_down, down_out),
    )
    moves = [pltpu.make_async_copy(a, b, m_sems.at[n]) for n, (a, b) in enumerate(moves)]
    for move in moves[:2]:
        move.start()
    model, hidden = up.shape
    right, left, across = lax.rem(h + 1, 4), lax.rem(h + 3, 4), lax.rem(h + 2, 4)
    to_right, to_left = (e, r, right), (e, r, left)
    y, c = e // 2, lax.rem(e, 2)
    target = [2 * lax.rem(y + k // 2, 4) + lax.rem(c + k, 2) for k in range(8)]
    source = [2 * lax.rem(y + 4 - k // 2, 4) + lax.rem(c + k, 2) for k in range(8)]
    to_expert = [(one, r, h) for one in target]
    to_source = [(one, r, h) for one in source]
    via_right, via_left = (4, 3, 2, 0), (5, 7, 6, 1)
    sums_up = RowsSpread(g_up, ring_up, x_send.at[0], x_recv.at[0])
    sums_down = RowsSpread(g_down, ring_down, x_send.at[1], x_recv.at[1])

    held[h, e] = slots[e]
    d_copies = [None] * 8
    for n in (1, 2, 6, 3, 7, 4, 5):
        d_copies[n] = remote(slots.at[target[n]], held.at[h, e], d_send.at[n], d_recv.at[n], to_expert[n])
        d_copies[n].start()

    def along(buf, where, k, send, recv, peer):
        block = buf.at[where, source[k]]
        copy = remote(block, block, send.at[k], recv.at[k], peer)
        copy.start()
        return copy

    r_copies, l_copies = [None] * 8, [None] * 8
    for n in (0, 1, 2, 6, 3, 7, 4, 5):
        if n:
            d_copies[n].wait_recv()
        r_copies[n] = along(held, h, n, r_send, r_recv, to_right)
        l_copies[n] = along(held, h, n, l_send, l_recv, to_left)

    half = 128

    def worked(where):
        lines = held[where]
        main_x = lines[:, :, :model].reshape(half, model)
        main_g = lines[:, :, model : 2 * model].reshape(half, model)
        extra = lines[:, :, 2 * model :].reshape(half, model)
        rows_x = jnp.concatenate([main_x, extra], axis=0)
        rows_g = jnp.concatenate([main_g, extra], axis=0)

        def first_layer(i, carry):
            cols = pl.ds(pl.multiple_of(i * 256, 256), 256)
            pre = matmul(rows_x, up[:, cols])
            grad = outer_cols(rows_g, down[cols, :])
            hid_m, pre_m = gelu_pair(pre[:half], grad[:half])
            pre_e = pre[half:].reshape(8, 2, 8, 256)[:, 0]
            grad_e = grad[half:].reshape(8, 2, 8, 256)[:, 1]
            hid_e, gpre_e = gelu_pair(pre_e, grad_e)
            none = jnp.zeros_like(hid_e)

            def stacked(a, b):
                return jnp.stack([a, b], axis=1).reshape(half, 256).astype(BF16)

            hid_m, pre_m = hid_m.astype(BF16), pre_m.astype(BF16)
            hid_out[:half, cols] = hid_m
            pre_out[:half, cols] = pre_m
            hid_w[where, :half, cols] = hid_m
            pre_w[where, :half, cols] = pre_m
            hid_out[half:, cols] = stacked(hid_e, none)
            pre_out[half:, cols] = stacked(none, gpre_e)
            hid_w[where, half:, cols] = stacked(none, hid_e)
            pre_w[where, half:, cols] = stacked(gpre_e, none)
            return carry

        lax.fori_loop(0, hidden // 256, first_layer, 0)

        def second_layer(i, carry):
            at = pl.multiple_of(i * 384, 384)
            cols = pl.ds(at, 384)
            share = matmul(hid_out[...], down[:, cols])
            grad = outer_cols(pre_out[...], up[cols, :])
            shape = (8, 16, 384)
            results[where, :, :, cols] = share[:half].astype(BF16).reshape(shape)
            results[where, :, :, pl.ds(model + at, 384)] = grad[:half].astype(BF16).reshape(shape)
            results[where, :, :, pl.ds(2 * model + at, 384)] = (share[half:] + grad[half:]).astype(BF16).reshape(shape)
            return carry

        lax.fori_loop(0, model // 384, second_layer, 0)

    moves[0].wait()
    moves[1].wait()
    worked(h)
    f_copies = [None] * 8
    for a, b in ((0, 1), (2, 6), (3, 7), (4, 5)):
        r_copies[a].wait_recv()
        f_copies[a] = along(held, left, a, f_send, f_recv, to_right)
        l_copies[b].wait_recv()
        f_copies[b] = along(held, right, b, f_send, f_recv, to_left)
    for n in via_left:
        r_copies[n].wait_recv()
    worked(left)
    c_copies = [None] * 8
    k_copies = [None] * 8

    def toward_right(n):
        block = results.at[right, source[n]]
        c_copies[n] = remote(block, from_left.at[n], c_send.at[n], c_recv.at[n], to_right)
        c_copies[n].start()

    def toward_left(n):
        block = results.at[left, source[n]]
        k_copies[n] = remote(block, from_right.at[n], k_send.at[n], k_recv.at[n], to_left)
        k_copies[n].start()

    for n in via_right:
        toward_left(n)
    for n in via_right:
        l_copies[n].wait_recv()
    worked(right)
    for n in via_left:
        toward_right(n)
    for n in range(8):
        f_copies[n].wait_recv()
    worked(across)
    h_copies = [None] * 8
    for at in range(4):
        for n, landing, peer in ((via_right[at], half_left, to_right), (via_left[at], half_right, to_left)):
            block = results.at[across, source[n]]
            h_copies[n] = remote(block, landing.at[at], h_send.at[n], h_recv.at[n], peer)
            h_copies[n].start()

    def weight_grads(i, carry):
        cols = pl.ds(pl.multiple_of(i * 128, 128), 128)
        total = jnp.zeros((128, hidden), F32)
        for lanes, kept, out in ((0, pre_w, g_up),):
            x_main = held[:, :, :, pl.ds(pl.multiple_of(i * 128, 128), 128)].reshape(4, half, 128)
            x_extra = held[:, :, :, pl.ds(pl.multiple_of(2 * model + i * 128, 128), 128)].reshape(4, half, 128)
            rows = jnp.concatenate([x_main, x_extra], axis=1).reshape(8 * half, 128)
            total = inner_rows(rows, kept[...].reshape(8 * half, hidden))
            out[cols, :] = total.astype(BF16)
        g_main = held[:, :, :, pl.ds(pl.multiple_of(model + i * 128, 128), 128)].reshape(4, half, 128)
        rows = jnp.concatenate([g_main, x_extra], axis=1).reshape(8 * half, 128)
        g_down[:, cols] = inner_rows(hid_w[...].reshape(8 * half, hidden), rows).astype(BF16)
        return carry

    lax.fori_loop(0, model // 128, weight_grads, 0)

    for ring in (sums_up, sums_down):
        ring.begin()
    moves[2].start()
    moves[3].start()
    for at in range(4):
        n = via_right[at]
        h_copies[n].wait_recv()
        results[right, source[n]] = (results[right, source[n]].astype(F32) + half_left[at].astype(F32)).astype(BF16)
        toward_right(n)
        n = via_left[at]
        h_copies[n].wait_recv()
        results[left, source[n]] = (results[left, source[n]].astype(F32) + half_right[at].astype(F32)).astype(BF16)
        toward_left(n)
    b_copies = []
    for n in (4, 5, 3, 7, 2, 6, 1, 0):
        c_copies[n].wait_recv()
        k_copies[n].wait_recv()
        total = results[h, source[n]].astype(F32) + from_left[n].astype(F32) + from_right[n].astype(F32)
        if n:
            sums[n] = total.astype(BF16)
            copy = remote(sums.at[n], back.at[e], b_send.at[n], b_recv.at[n], to_source[n])
            copy.start()
            b_copies.append(copy)
        else:
            back[e] = total.astype(BF16)
    for copy in b_copies:
        copy.wait_recv()
    main, top, low_half, onehot = slot_picks(routes[...], slots.shape[0])
    lines = back[...].reshape(128, 3 * model)
    shares = probs[...]
    gate = jnp.sum(shares * onehot, axis=-1, keepdims=True)
    hid, grad_output, low = hid_in[...], cotangent[...].astype(F32), moe_low[...]
    expert_out = inner_rows(main, lines[:, :model]) + inner_rows(top, lines[:, 2 * model :])
    output[...] = (hid + gate * expert_out).astype(BF16)
    grad_gate = jnp.sum(grad_output * expert_out, axis=-1, keepdims=True)
    grad_logits = (gate * grad_gate * (onehot - shares)).astype(BF16)
    grad_moe = inner_rows(main, lines[:, model : 2 * model]) + inner_rows(low_half, lines[:, 2 * model :])
    grad_moe = grad_moe + matmul(grad_logits, gains[...].astype(BF16))
    scale = lax.rsqrt(jnp.mean(hid * hid, axis=-1, keepdims=True) + EPS)
    scaled = grad_moe * gains[1:2, :]
    inside = jnp.mean(scaled * hid, axis=-1, keepdims=True)
    grad_hidden[...] = grad_output + scale * scaled - hid * (scale * scale * scale * inside)
    grad_gain = jnp.sum(grad_moe * hid * scale, axis=0, keepdims=True)
    at = lax.broadcasted_iota(jnp.int32, norm_out.shape, 0)
    norm_out[...] = inner_rows(grad_logits, low) + jnp.where(at == 1, grad_gain, 0.0)
    for ring in (sums_up, sums_down):
        ring.end()
    moves[2].wait()
    moves[3].wait()
    for copy in d_copies[1:] + r_copies + l_copies + f_copies + c_copies + k_copies + h_copies + b_copies:
        copy.wait_send()


def across(tile, width):
    whole = width // 128
    return jnp.concatenate([tile] * whole + [tile[:, : width - 128 * whole]], axis=1)


def eye(size):
    at = [lax.broadcasted_iota(jnp.int32, (size, size), axis) for axis in (0, 1)]
    return (at[0] == at[1]).astype(BF16)


def both_cols(lines, main, extra):
    return jnp.concatenate([outer_cols(lines, main), outer_cols(lines, extra)], axis=1)


class Gather:
    def __init__(self, source, place, send, recv):
        self.source, self.place, self.send, self.recv = source, place, send, recv
        e, r, h = places()
        self.c = lax.rem(e, 2)
        y = e // 2
        self.f0 = y * (1 - self.c) + r * self.c
        self.s0 = r * (1 - self.c) + y * self.c
        self.own = e * 4 + r
        self.mate, self.first, self.second = mixer_peers()

    def copy(self, at, peer, block=None):
        target = self.place(self.own if block is None else block)
        return remote(self.source if block is None else target, target, self.send.at[at], self.recv.at[at], peer)

    def came(self, k, j=None):
        s = self.s0 if j is None else lax.rem(self.s0 + 3 - j, 4)
        return block_at(self.c, lax.rem(self.f0 + 4 - k, 4), s)

    def begin(self):
        for k in (1, 0, 2):
            self.copy(k, self.first[k]).start()

    def begin_second(self):
        for j in (1, 0, 2):
            self.copy(3 + j, self.second[j]).start()
        self.copy(15, self.mate).start()

    def relay_first(self):
        for k in range(3):
            self.copy(k, self.first[k]).wait_recv()
            block = self.came(k + 1)
            for j in (1, 0, 2):
                self.copy(6 + 3 * k + j, self.second[j], block).start()
            self.copy(16 + k, self.mate, block).start()

    def relay_second(self):
        for k in range(4):
            for j in range(3):
                self.copy(3 + 3 * k + j, self.second[j]).wait_recv()
                self.copy(19 + 3 * k + j, self.mate, self.came(k, j)).start()

    def end(self):
        for at in range(15, 31):
            self.copy(at, self.mate).wait_recv()

    def sent(self):
        for at in range(31):
            self.copy(at, self.mate).wait_send()


def slot_picks(route, experts, states=16):
    count = route.shape[1]
    line = lax.broadcasted_iota(jnp.int32, (states, count), 0)
    chosen = jnp.where(line - 2 == route, 1.0, 0.0)
    earlier = lax.broadcasted_iota(jnp.int32, (count, count), 0) <= lax.broadcasted_iota(jnp.int32, (count, count), 1)
    counts = matmul(chosen.astype(BF16), jnp.where(earlier, 1.0, 0.0).astype(BF16))
    within = jnp.sum(chosen * (counts - 1.0), axis=0, keepdims=True).astype(jnp.int32)
    slot = lax.broadcasted_iota(jnp.int32, (experts * MAIN, count), 0)
    line, expert = slot % MAIN, slot // MAIN
    here = expert == route

    def of(found):
        return jnp.where(found, 1.0, 0.0).astype(BF16)

    main = of(here & (within == line))
    top = of(here & (line < 8) & (within == line + 16))
    low = of(here & (line >= 8) & (within == line + 8))
    column = jnp.broadcast_to(route.astype(F32), (count, count)).T[:, :states]
    place = lax.broadcasted_iota(jnp.int32, (count, states), 1) - 2
    onehot = jnp.where(place.astype(F32) == column, 1.0, 0.0)
    return main, top, low, onehot


def other_core_peers():
    e, r, h = places()
    c = lax.rem(e, 2)
    return [(2 * lax.rem(e // 2 + k, 4) + 1 - c, r, h) for k in (1, 2, 3)]


def forward_part(refs):
    (
        in_lines, out_lines, x_cols, dt_cols, decay_in, taps_in, conv_bias, dt_bias, skip, gain_one, gain_two,
        router, tokens, resets, routes, cotangent,
        whole_hbm, seq_hbm, extra_hbm, normed_hbm, x_low_hbm, u_hbm, gate_hbm, proj_hbm, lin_hbm, y_hbm, gated_hbm,
        starts_hbm, params, gains, hidden, slots, moe_out, probs,
        pack, norm, line, whole_all, norms, seq, extra, tiles, total, local_sems, z_send, z_recv, n_send, n_recv,
        w_send, w_recv, v_send, v_recv, o_send, o_recv, k_sems, s_sems,
        normed, x_low, u_out, gate_z, proj, dt_lin, y_out, gated, starts,
        xs, marks, conv, dtm, dtx, parts, own, landing, branch, came, p_send, p_recv, b_send, b_recv, quarters, owned, q_send, q_recv,
    ) = refs
    e, r, h = places()
    block, model = tokens.shape
    inner, states, experts = u_out.shape[1], starts.shape[1], router.shape[0]
    lines, small = block // STEP, 3 * model
    channels, share = in_lines.shape[0], gain_one.shape[1]

    z_peers = hid_peers()
    mate, first, second = mixer_peers()
    hail([mate] + first + second + z_peers + other_core_peers())

    def wide(a):
        return a[...].astype(F32)

    line[:, :model] = tokens[...]
    line[:, model:] = jnp.broadcast_to(wide(resets), (block, 128)).T.astype(BF16)
    columns = jnp.concatenate(
        [
            wide(decay_in), wide(taps_in), wide(conv_bias), wide(dt_bias), wide(skip),
            jnp.zeros((105, channels), F32),
        ],
        axis=0,
    )
    columns = jnp.concatenate([columns, jnp.zeros((128, 128 - channels), F32)], axis=1).T[:channels, :24]
    tail = jnp.concatenate(
        [
            jnp.concatenate([wide(x_cols), columns], axis=1),
            jnp.concatenate([wide(dt_cols), jnp.zeros((channels, 128 - dt_cols.shape[1]), F32)], axis=1),
        ],
        axis=1,
    )
    in_float = wide(in_lines)
    both = jnp.concatenate([in_float[:, 0], in_float[:, 1], wide(out_lines), tail], axis=1)
    pack[:, : 2 * model] = both[:MAIN, : 2 * model].astype(BF16)
    pack[:, 2 * model : 2 * model + 256] = both[:MAIN, small:].astype(BF16)
    pack[:, 2 * model + 768 :] = both[:MAIN, 2 * model : small].astype(BF16)
    last = jnp.concatenate([both[MAIN:], jnp.zeros((channels - MAIN, 4096 - small - 256), F32)], axis=1)
    last = [last[n : n + 1, k * EXTRA : (k + 1) * EXTRA] for n in range(2) for k in range(8)]
    pack[:, 2 * model + 256 : 2 * model + 768] = jnp.concatenate(last, axis=0).astype(BF16)
    tile = jnp.concatenate([wide(gain_one), wide(gain_two), wide(router), jnp.zeros((6, share), F32)], axis=0)
    tile = jnp.concatenate([tile, jnp.zeros((MAIN, 128 - share), F32)], axis=1)
    norm[...] = pltpu.roll(tile, h * share, 1).astype(BF16)
    pl.semaphore_wait(pltpu.get_barrier_semaphore(), 13)
    mine = pl.ds(pl.multiple_of(h * block, block), block)
    late = 2 * model + 768

    def owner_rows(n):
        return pl.ds(pl.multiple_of(n * MAIN, MAIN), MAIN)

    main = Gather(pack.at[:, :late], lambda n: whole_all.at[owner_rows(n), :late], w_send, w_recv)
    out_part = Gather(pack.at[:, late:], lambda n: whole_all.at[owner_rows(n), late:], o_send, o_recv)
    norm_part = Gather(total, lambda n: norms.at[n], v_send, v_recv)
    n_copies = [remote(norm, tiles.at[k], n_send.at[k], n_recv.at[k], z_peers[k]) for k in range(3)]
    z_copies = [remote(line, seq.at[mine], z_send.at[k], z_recv.at[k], z_peers[k]) for k in range(3)]
    own_copies = [
        pltpu.make_async_copy(pack, whole_all.at[owner_rows(main.own)], local_sems.at[0]),
        pltpu.make_async_copy(line, seq.at[mine], local_sems.at[1]),
    ]
    for copy in n_copies:
        copy.start()
    main.begin()
    main.begin_second()
    for n in (1, 0, 2):
        z_copies[n].start()
    for copy in own_copies:
        copy.start()
    for copy in n_copies:
        copy.wait_recv()
    total[...] = norm[...] + tiles[0] + tiles[1] + tiles[2]
    norms[main.own] = total[...]
    norm_part.begin()
    norm_part.begin_second()
    main.relay_first()
    norm_part.relay_first()
    out_part.begin()
    main.relay_second()
    norm_part.relay_second()
    out_part.begin_second()
    out_part.relay_first()
    norm_part.end()
    span = share * 4
    gains[...] = jnp.concatenate([norms[n].astype(F32)[:, :span] for n in range(32)], axis=1)
    for copy in z_copies:
        copy.wait_recv()
    for copy in own_copies:
        copy.wait()
    gain = gains[0:1, :]

    def normalize(b, carry):
        rows = pl.ds(pl.multiple_of(b * block, block), block)
        values = seq[rows, :model].astype(F32)
        scale = lax.rsqrt(jnp.mean(values * values, axis=-1, keepdims=True) + EPS)
        low = (values * scale * gain).astype(BF16)
        normed[rows, :] = low
        return carry

    lax.fori_loop(0, 4, normalize, 0)
    main.end()
    row = lax.broadcasted_iota(jnp.int32, (512, 512), 0)
    col = lax.broadcasted_iota(jnp.int32, (512, 512), 1)
    wanted = (row % 64 // 2) * MAIN + (row % 2) * 8 + row // 64
    moved = matmul((wanted == col).astype(BF16), whole_all[:, 2 * model + 256 : late]).astype(BF16)
    for k in range(8):
        extra[:, k * 512 : (k + 1) * 512] = moved[k * 64 : (k + 1) * 64]
    params[...] = both_cols(eye(128), whole_all[:, 2 * model : 2 * model + 128], extra[:, small : small + 128])
    kept_copies = [
        pltpu.make_async_copy(kept, out, k_sems.at[n])
        for n, (kept, out) in enumerate(((whole_all, whole_hbm), (seq, seq_hbm), (extra, extra_hbm)))
    ]
    for copy in kept_copies[1:]:
        copy.start()
    xs[0:8] = jnp.zeros((8, inner), F32)
    marks[0:8] = jnp.zeros((8, 128), F32)

    pairs = (
        (normed, normed_hbm), (x_low, x_low_hbm), (u_out, u_hbm), (gate_z, gate_hbm), (proj, proj_hbm),
        (dt_lin, lin_hbm), (y_out, y_hbm), (gated, gated_hbm), (starts, starts_hbm),
    )

    def saved_copy(n, b):
        kept, out = pairs[n]
        size = kept.shape[0] // 4
        rows = pl.ds(pl.multiple_of(b * size, size), size)
        return pltpu.make_async_copy(kept.at[rows], out.at[rows], s_sems.at[n, b])

    def proj_copy(b, k):
        at = k * 4 + b
        return remote(own.at[b], landing.at[k, b], p_send.at[at], p_recv.at[at], z_peers[k])

    x_low[...] = both_cols(normed[...], whole_all[:, :model], extra[:, :model]).astype(BF16)
    gate_z[...] = both_cols(normed[...], whole_all[:, model : 2 * model], extra[:, model : 2 * model])

    def stage_one(b, carry):
        start = pl.multiple_of(b * block, block)
        rows = pl.ds(start, block)
        x = x_low[rows, :]
        after = pl.ds(pl.multiple_of(8 + start, 8), block)
        xs[after, :] = x.astype(F32)
        now = seq[rows, model:].astype(F32)
        marks[after, :] = now
        lines_x, lines_m = xs[pl.ds(start, block + 8), :], marks[pl.ds(start, block + 8), :]
        mask = 1.0 - now
        total = params[124:125, :] + params[123:124, :] * x.astype(F32)
        for back in (1, 2, 3):
            past = lines_x[8 - back : 8 - back + block]
            total = total + params[123 - back : 124 - back, :] * past * across(mask, inner)
            if back < 3:
                mask = mask * (1.0 - lines_m[8 - back : 8 - back + block])
        u_out[rows, :] = total
        convolved = total * jax.nn.sigmoid(total)
        conv[rows, :] = convolved
        conv_low = convolved.astype(BF16)
        share = matmul(conv_low[:, :512], whole_all[:, 2 * model : 2 * model + 128]) + matmul(
            conv_low[:, 512:], extra[:, small : small + 128]
        )
        own[b] = share.astype(BF16)
        for k in (1, 0, 2):
            proj_copy(b, k).start()
        for n in range(4):
            saved_copy(n, b).start()
        return carry

    lax.fori_loop(0, 4, stage_one, 0)
    out_part.relay_second()
    out_part.end()
    kept_copies[0].start()
    a = jnp.exp(params[104:120, :]) * (-LOG2E)
    half = states // 2

    quarter = block // 4

    def part_copy(b, k):
        rows = pl.ds(pl.multiple_of(lax.rem(h + 1 + k, 4) * quarter, quarter), quarter)
        at = k * 4 + b
        return remote(branch.at[b, rows], came.at[k, b], b_send.at[at], b_recv.at[at], z_peers[k])

    def whole_copy(b, sender):
        return remote(quarters.at[b], owned.at[sender], q_send.at[b], q_recv.at[sender], (e, r, b))

    def sum_up(b):
        rows = pl.ds(pl.multiple_of(h * quarter, quarter), quarter)
        for k in range(3):
            part_copy(b, k).wait_recv()
        total = branch[b, rows, :].astype(F32)
        for k in range(3):
            total = total + came[k, b].astype(F32)
        quarters[b] = total.astype(BF16)

        @pl.when(b != h)
        def send():
            whole_copy(b, lax.rem(h - b + 4, 4) - 1).start()

    def stage_two(b, state):
        start = pl.multiple_of(b * block, block)
        rows = pl.ds(start, block)
        for k in range(3):
            proj_copy(b, k).wait_recv()
        sums = (
            own[b].astype(F32) + landing[0, b].astype(F32) + landing[1, b].astype(F32) + landing[2, b].astype(F32)
        )
        proj[rows, :] = sums
        lin = both_cols(sums.astype(BF16), whole_all[:, 2 * model + 128 : 2 * model + 256], extra[:, small + 128 : small + 256])
        lin = lin + params[125:126, :]
        dt_lin[rows, :] = lin
        dt = jax.nn.softplus(lin)
        convolved = conv[rows, :]
        dtm[...] = dt + across(STOP * marks[pl.ds(pl.multiple_of(8 + start, 8), block), :], inner)
        dtx[...] = dt * convolved
        turned = sums.T
        b_all, c_all = turned[72:88], turned[88:104]

        def chunk(i, h_now):
            starts[b * lines + i] = h_now
            shift = lax.rem(block - i * STEP, block)
            b_now, c_now = pltpu.roll(b_all, shift, 1), pltpu.roll(c_all, shift, 1)
            rows_m, rows_x = (ref[pl.ds(pl.multiple_of(i * STEP, STEP), STEP), :] for ref in (dtm, dtx))
            for j in range(STEP):
                decay = jnp.exp2(a * rows_m[j : j + 1])
                h_now = decay * h_now + b_now[:, j : j + 1] * rows_x[j : j + 1]
                p = c_now[:, j : j + 1] * h_now
                put_rows(parts, j, p[:half] + p[half:])
            here = pl.ds(pl.multiple_of(start + i * STEP, STEP), STEP)
            y_out[here, :] = summed_groups(parts, half, inner)
            return h_now

        state = lax.fori_loop(0, lines, chunk, state)
        y = y_out[rows, :] + params[126:127, :] * convolved
        y_out[rows, :] = y
        z = gate_z[rows, :]
        low = (y * z * jax.nn.sigmoid(z)).astype(BF16)
        gated[rows, :] = low
        out = matmul(low[:, :512], whole_all[:, late:]) + matmul(low[:, 512:], extra[:, 2 * model : small])
        branch[b] = out.astype(BF16)

        for k in (1, 0, 2):
            part_copy(b, k).start()

        @pl.when(b > 0)
        def earlier():
            sum_up(b - 1)

        for n in range(4, 9):
            saved_copy(n, b).start()
        return state

    lax.fori_loop(0, 4, stage_two, jnp.zeros((states, inner), F32))
    sum_up(3)
    for k in range(3):
        whole_copy(0, k).wait_recv()
    mine = pl.ds(pl.multiple_of(h * block, block), block)
    hidden[...] = seq[mine, :model].astype(F32)
    for k in range(4):
        rows = pl.ds(pl.multiple_of(lax.rem(h + k, 4) * quarter, quarter), quarter)
        piece = owned[k - 1] if k else quarters[h]
        hidden[rows, :] += piece.astype(F32)
    hid = hidden[...]
    scale = lax.rsqrt(jnp.mean(hid * hid, axis=-1, keepdims=True) + EPS)
    moe_low = (hid * scale * gains[1:2, :]).astype(BF16)
    moe_out[...] = moe_low
    logits = outer_cols(moe_low, gains[...].astype(BF16))
    lane = lax.broadcasted_iota(jnp.int32, logits.shape, 1)
    real = (lane >= 2) & (lane < 2 + experts)
    logits = jnp.where(real, logits, -1e30)
    powers = jnp.exp(logits - jnp.max(logits, axis=-1, keepdims=True))
    shares = powers / jnp.sum(powers, axis=-1, keepdims=True)
    probs[...] = shares
    pick_main, top, low_half, onehot = slot_picks(routes[...], experts)
    gate = jnp.sum(shares * onehot, axis=-1, keepdims=True)
    grad_eo = (gate * cotangent[...].astype(F32)).astype(BF16)
    shape = (experts, MAIN, model)
    slots[:, :, :model] = matmul(pick_main, moe_low).astype(BF16).reshape(shape)
    slots[:, :, model : 2 * model] = matmul(pick_main, grad_eo).astype(BF16).reshape(shape)
    slots[:, :, 2 * model :] = (matmul(top, moe_low) + matmul(low_half, grad_eo)).astype(BF16).reshape(shape)
    for n in range(9):
        for b in range(4):
            saved_copy(n, b).wait()
    for copy in kept_copies:
        copy.wait()
    for part in (main, out_part, norm_part):
        part.sent()
    for copy in n_copies + z_copies:
        copy.wait_send()
    for b in range(4):
        for k in range(3):
            proj_copy(b, k).wait_send()
            part_copy(b, k).wait_send()

        @pl.when(b != h)
        def sent():
            whole_copy(b, 0).wait_send()


def layer_kernel(*refs):
    ins, up_down, saved = refs[:16], refs[16:18], refs[18:30]
    params, gains, output, grad_hidden, norm_out, up_out, down_out, ring_up, ring_down = refs[30:39]
    hidden, slots, moe_low, probs, *scratch = refs[39:]
    forward_scratch, expert_scratch = scratch[:FORWARD_SCRATCH], scratch[FORWARD_SCRATCH:]
    forward_part((*ins, *saved, params, gains, hidden, slots, moe_low, probs, *forward_scratch))
    expert_part(
        (
            slots, *up_down, hidden, ins[15], moe_low, probs, ins[14], gains, output, grad_hidden, norm_out, up_out,
            down_out, ring_up, ring_down, *expert_scratch,
        )
    )


def mixer_and_experts(arrays, up, down, inner, states, experts):
    tokens = arrays[12]
    block, model = tokens.shape
    length, hidden = 4 * block, up.shape[1]
    width, lines = 3 * model + 768, MAIN
    S, V = jax.ShapeDtypeStruct, pltpu.VMEM
    saved = [
        ((length, model), BF16), ((length, inner), BF16), ((length, inner), F32), ((length, inner), F32),
        ((length, 128), F32), ((length, inner), F32), ((length, inner), F32), ((length, inner), BF16),
        ((length // STEP, states, inner), F32),
    ]
    eighths = [(4, one.shape[0] // 8, one.shape[1]) for one in (up, down)]
    outs = (
        S((512, width), BF16), S((length, model + 128), BF16), S((64, 4096), BF16), *[S(*one) for one in saved],
        S((128, inner), F32), S((MAIN, model), F32), S((block, model), BF16), S((block, model), F32),
        S((MAIN, model), F32), S(up.shape, BF16), S(down.shape, BF16), *[S(size, BF16) for size in eighths],
    )
    eight = DMA((8,))
    forward_scratch = [
            V((MAIN, width), BF16), V((MAIN, 128), BF16), V((block, model + 128), BF16), V((512, width), BF16),
            V((32, MAIN, 128), BF16), V((length, model + 128), BF16), V((64, 4096), BF16),
            V((3, MAIN, 128), BF16), V((MAIN, 128), BF16),
            DMA((3,)), DMA((3,)), DMA((3,)), DMA((3,)), DMA((3,)),
            DMA((31,)), DMA((31,)), DMA((31,)), DMA((31,)), DMA((31,)), DMA((31,)),
            DMA((3,)), DMA((9, 4)),
            *[V(*one) for one in saved],
            V((length + 8, inner), F32), V((length + 8, 128), F32), V((length, inner), F32), V((block, inner), F32),
            V((block, inner), F32), V((-(-inner // 128), STEP * states // 2, 128), F32), V((4, block, 128), BF16),
            V((3, 4, block, 128), BF16), V((4, block, model), BF16), V((3, 4, block // 4, model), BF16),
            DMA((12,)), DMA((12,)), DMA((12,)), DMA((12,)), V((4, block // 4, model), BF16),
            V((3, block // 4, model), BF16), DMA((4,)), DMA((3,)),
    ]
    slot_lines = (lines, 3 * model)
    expert_scratch = [
        V(up.shape, BF16), V(down.shape, BF16), V(up.shape, BF16), V(down.shape, BF16), DMA((4,)), DMA((2, 4)), DMA((2, 4)),
        V((experts, *slot_lines), BF16), V((4, experts, *slot_lines), BF16), V((4, experts, *slot_lines), BF16),
        V((256, hidden), BF16), V((256, hidden), BF16), V((4, 256, hidden), BF16), V((4, 256, hidden), BF16),
        V((8, *slot_lines), BF16), V((8, *slot_lines), BF16), V((4, *slot_lines), BF16), V((4, *slot_lines), BF16),
        V((8, *slot_lines), BF16), *[eight] * 16,
    ]
    assert len(forward_scratch) == FORWARD_SCRATCH
    return pl.pallas_call(
        layer_kernel,
        out_shape=outs,
        in_specs=[IN_VMEM] * 16 + [ANY] * 2,
        out_specs=(*[ANY] * 12, *[IN_VMEM] * 5, ANY, ANY, IN_VMEM, IN_VMEM),
        scratch_shapes=[
            V((block, model), F32), V((experts, *slot_lines), BF16), V((block, model), BF16), V((block, MAIN), F32),
            *forward_scratch, *expert_scratch,
        ],
        compiler_params=pltpu.CompilerParams(
            collective_id=1, has_side_effects=True, vmem_limit_bytes=62 << 20
        ),
        name="mixer_and_experts",
    )(*arrays, up, down)


class Flow:
    ORDER = (2, 1, 3, 0)

    def __init__(self, turn, source, out, pairs, halves, fours, lines, ends, send, recv):
        self.source, self.out, self.pairs, self.halves = source, out, pairs, halves
        self.fours, self.lines, self.ends, self.send, self.recv = fours, lines, ends, send, recv
        e, r, h = places()
        self.c = lax.rem(e, 2)
        y = e // 2
        self.turn = self.c if turn is None else turn
        self.mate_turn = 1 - self.c if turn is None else turn
        self.f0 = y * (1 - self.turn) + r * self.turn
        self.s0 = r * (1 - self.turn) + y * self.turn
        self.mate_s0 = r * (1 - self.mate_turn) + y * self.mate_turn
        self.mate, self.first, self.second_peers = mixer_peers(self.turn)

    def copy(self, src, dst, at, peer):
        return remote(src, dst, self.send.at[at], self.recv.at[at], peer)

    def mate_copy(self, n, f):
        s = lax.rem(self.mate_s0 + self.ORDER[n], 4)
        block = block_at(1 - self.c, f, s, self.mate_turn)
        return self.copy(self.source.at[block], self.pairs.at[n, f], n * 4 + f, self.mate)

    def second_copy(self, n):
        return self.copy(self.halves.at[n], self.fours.at[n], 16 + n, self.second_peers[self.ORDER[n] - 1])

    def first_copy(self, n):
        return self.copy(self.lines.at[n], self.ends.at[n], 19 + n, self.first[self.ORDER[n] - 1])

    def begin(self):
        for n in range(4):
            for f in range(4):
                self.mate_copy(n, f).start()

    def second(self):
        for n, k in enumerate(self.ORDER):
            s = lax.rem(self.s0 + k, 4)
            for f in range(4):
                self.mate_copy(n, f).wait_recv()
                total = self.source[block_at(self.c, f, s, self.turn)].astype(F32) + self.pairs[n, f].astype(F32)
                self.halves[n, f] = total.astype(BF16)
            if k:
                self.second_copy(n).start()

    def third(self):
        for n in range(3):
            self.second_copy(n).wait_recv()
        for n, k in enumerate(self.ORDER):
            f = lax.rem(self.f0 + k, 4)
            line = self.halves[3, f].astype(F32)
            for m in range(3):
                line = line + self.fours[m, f].astype(F32)
            if k:
                self.lines[n] = line.astype(BF16)
                self.first_copy(n).start()
            else:
                self.out[...] = line

    def finish(self):
        for n in range(3):
            self.first_copy(n).wait_recv()
        self.out[...] = (
            self.out[...] + self.ends[0].astype(F32) + self.ends[1].astype(F32) + self.ends[2].astype(F32)
        )

    def end(self):
        for n in range(4):
            for f in range(4):
                self.mate_copy(n, f).wait_send()
        for n in range(3):
            self.second_copy(n).wait_send()
            self.first_copy(n).wait_send()


def flow_scratch(width):
    return [
        pltpu.VMEM((32, MAIN, width), BF16), pltpu.VMEM((MAIN, width), F32), pltpu.VMEM((4, 4, MAIN, width), BF16),
        pltpu.VMEM((4, 4, MAIN, width), BF16), pltpu.VMEM((3, 4, MAIN, width), BF16),
        pltpu.VMEM((3, MAIN, width), BF16), pltpu.VMEM((3, MAIN, width), BF16), DMA((22,)), DMA((22,)),
    ]


def mixer_back_kernel(*refs):
    (
        grad_hidden, seq_all, whole_in, gains, norm_in, normed_in, x_low_in, u_all, gate_all, proj_in, lin_all, y_all,
        gated_in, starts_in, params, extra_in, g_up, g_down, came_up, came_down,
        grad_tokens, grad_in, grad_out, grad_x, grad_dt, by_channel, by_feature, all_up, all_down,
        seq_own, seq_marks, whole, normed, x_low, u_in, gate_z, proj, dt_lin, y_in, gated, starts, extra, in_sems,
        ghs, gus, marks, dts, dtm, dtx, conv, s1, s2, gdl, ggate, gx, gp_all,
        conv_low, held, decays, parts_1, parts_2, lanes_b, lanes_c, state, g_rate, rows_sum, own, landing, branch, came,
        a_send, a_recv, p_send, p_recv, b_send, b_recv, quarters, owned, q_send, q_recv, x_send, x_recv, x_local,
        e_slots_up, e_own_up, e_sums_up, total_up, e_slots_down, e_own_down, e_sums_down, total_down,
        y_send, y_recv, y_local, own_tile, tiles, z_send, z_recv, *flow_refs, gain_sum,
    ) = refs
    e, r, h = places()
    block, model = grad_hidden.shape
    inner, states = u_in.shape[1], starts.shape[1]
    lines, half, small = block // STEP, states // 2, 3 * model
    owners = 32
    z_peers = hid_peers()
    mate, first, second = mixer_peers()
    hail([mate] + first + second + z_peers)
    mine = pl.ds(pl.multiple_of(h * block, block), block)
    loads = [
        (lin_all, dt_lin), (u_all, u_in), (gate_all, gate_z), (y_all, y_in), (seq_all.at[:, model:], seq_marks),
        (proj_in, proj), (starts_in, starts), (whole_in, whole), (extra_in, extra), (x_low_in, x_low),
        (gated_in, gated), (normed_in, normed), (seq_all.at[mine, :model], seq_own),
    ]
    loads = [pltpu.make_async_copy(a, b, in_sems.at[n]) for n, (a, b) in enumerate(loads)]
    for copy in loads:
        copy.start()
    sums = [
        RowsSum(g_up, came_up, e_slots_up, e_own_up, e_sums_up, total_up, y_send.at[0], y_recv.at[0], y_local.at[0]),
        RowsSum(
            g_down, came_down, e_slots_down, e_own_down, e_sums_down, total_down, y_send.at[1], y_recv.at[1], y_local.at[1]
        ),
    ]
    rings = [
        RowsGather(part, whole_grad, x_send.at[n], x_recv.at[n], x_local.at[n])
        for n, (part, whole_grad) in enumerate(((total_up, all_up), (total_down, all_down)))
    ]
    for ring in sums:
        for n in (4, 0, 1, 2, 3):
            ring.load(n).start()
    ghs[h] = grad_hidden[...].astype(BF16)
    pl.semaphore_wait(pltpu.get_barrier_semaphore(), 10)
    right, left, middle = lax.rem(h + 1, 4), lax.rem(h + 3, 4), block // 2
    passed = (ghs.at[left, :middle], ghs.at[right, middle:])
    gh_copies = [
        remote(ghs.at[h], ghs.at[h], a_send.at[0], a_recv.at[0], (e, r, right)),
        remote(ghs.at[h], ghs.at[h], a_send.at[1], a_recv.at[1], (e, r, left)),
        remote(passed[0], passed[0], a_send.at[2], a_recv.at[2], (e, r, right)),
        remote(passed[1], passed[1], a_send.at[3], a_recv.at[3], (e, r, left)),
    ]
    for k in range(2):
        gh_copies[k].start()
    for ring in sums:
        ring.pass_on()
    flow_early, flow_in, flow_rest = [
        Flow(1 if n == 0 else None, *flow_refs[9 * n : 9 * n + 9]) for n in range(3)
    ]
    state[...] = jnp.zeros_like(state)
    g_rate[...] = jnp.zeros_like(g_rate)
    rows_sum[...] = jnp.zeros_like(rows_sum)
    gain_sum[...] = jnp.zeros_like(gain_sum)
    gus[512:520] = jnp.zeros((8, inner), F32)
    a = jnp.exp(params[104:120, :]) * (-LOG2E)
    for copy in loads[:5]:
        copy.wait()
    marks[0:512] = seq_marks[...].astype(F32)
    marks[512:520] = jnp.zeros((8, 128), F32)

    def prepare(b, carry):
        rows = pl.ds(pl.multiple_of(b * block, block), block)
        lin = dt_lin[rows, :]
        dt = jax.nn.softplus(lin)
        dt_lin[rows, :] = jax.nn.sigmoid(lin)
        u_now = u_in[rows, :]
        convolved = u_now * jax.nn.sigmoid(u_now)
        conv[rows, :] = convolved
        conv_low[rows, :] = convolved.astype(BF16)
        dts[rows, :] = dt
        dtm[rows, :] = dt + across(STOP * marks[rows, :], inner)
        dtx[rows, :] = dt * convolved
        z = gate_z[rows, :]
        sig = jax.nn.sigmoid(z)
        gate_z[rows, :] = z * sig
        y_in[rows, :] = y_in[rows, :] * (sig * (1.0 + z * (1.0 - sig)))
        return carry

    lax.fori_loop(0, 4, prepare, 0)
    for k in range(2):
        gh_copies[k].wait_recv()
        gh_copies[2 + k].start()
    for copy in loads[5:]:
        copy.wait()

    def spots(shape, axis):
        return lax.broadcasted_iota(jnp.int32, shape, axis)

    tall = (block * states, 128)
    ones = jnp.ones((128, 128), BF16)

    extras = []

    def weight(left, right, target, at, size):
        main = inner_rows(left[:, :512], right)
        target[:, :, at : at + size] = main.astype(BF16).reshape(owners, MAIN, size)
        extras.append(inner_rows(left[:, 512:], right).astype(BF16))

    for copy in gh_copies[2:]:
        copy.wait_recv()
    gh_rows, low_norm = ghs[...].reshape(4 * block, model), normed[...]
    gg = both_cols(gh_rows, whole[:, 2 * model + 768 :], extra[:, 2 * model : small])
    gate_z[...] = gg * gate_z[...]
    ggate[...] = (gg * y_in[...]).astype(BF16)
    weight(gated[...], gh_rows, flow_early.source, 0, model)
    weight(ggate[...], low_norm, flow_early.source, model, model)
    flow_early.begin()
    for ring, gather in zip(sums, rings):
        ring.finish()
        gather.begin()

    def proj_copy(b, k):
        at = k * 4 + b
        return remote(own.at[b], landing.at[k, b], p_send.at[at], p_recv.at[at], z_peers[k])

    quarter = block // 4

    def part_copy(b, k):
        rows = pl.ds(pl.multiple_of(lax.rem(h + 1 + k, 4) * quarter, quarter), quarter)
        at = k * 4 + b
        return remote(branch.at[b, rows], came.at[k, b], b_send.at[at], b_recv.at[at], z_peers[k])

    def whole_copy(b, sender):
        return remote(quarters.at[b], owned.at[sender], q_send.at[b], q_recv.at[sender], (e, r, b))

    def sum_up(b):
        rows = pl.ds(pl.multiple_of(h * quarter, quarter), quarter)
        for k in range(3):
            part_copy(b, k).wait_recv()
        total = branch[b, rows, :].astype(F32)
        for k in range(3):
            total = total + came[k, b].astype(F32)
        quarters[b] = total.astype(BF16)

        @pl.when(b != h)
        def send():
            whole_copy(b, lax.rem(h - b + 4, 4) - 1).start()

    def stage_a(b):
        start = pl.multiple_of(b * block, block)
        rows = pl.ds(start, block)
        turned = proj[rows, :].T
        b_all, c_all = turned[72:88], turned[88:104]

        gy_now = gate_z[rows, :]

        def chunk(step, u):
            i = lines - 1 - step
            hh = starts[b * lines + i]
            held[0] = hh
            shift = lax.rem(block - i * STEP, block)
            b_now, c_now = pltpu.roll(b_all, shift, 1), pltpu.roll(c_all, shift, 1)
            there = pl.ds(pl.multiple_of(start + i * STEP, STEP), STEP)
            rows_m, rows_x, rows_g, rows_t = (ref[there, :] for ref in (dtm, dtx, gate_z, dts))
            for j in range(STEP):
                decay = jnp.exp2(a * rows_m[j : j + 1])
                hh = decay * hh + b_now[:, j : j + 1] * rows_x[j : j + 1]
                decays[j] = decay
                held[j + 1] = hh
            for j in range(STEP - 1, -1, -1):
                gy_row = rows_g[j : j + 1]
                g = c_now[:, j : j + 1] * gy_row + u
                u = decays[j] * g
                q = u * held[j]
                g_rate[...] += q * rows_t[j : j + 1]
                w = q * a
                put_rows(parts_2, j, w[:half] + w[half:])
                w = g * b_now[:, j : j + 1]
                put_rows(parts_1, j, w[:half] + w[half:])
                at = pl.ds(pl.multiple_of((i * STEP + j) * states, states), states)
                lanes_b[at, :] = over_lanes(g * rows_x[j : j + 1]).astype(BF16)
                lanes_c[at, :] = over_lanes(held[j + 1] * gy_row).astype(BF16)
            here = pl.ds(pl.multiple_of(i * STEP, STEP), STEP)
            s1[here, :] = summed_groups(parts_1, half, inner)
            s2[here, :] = summed_groups(parts_2, half, inner)
            return u

        state[...] = lax.fori_loop(0, lines, chunk, state[...])
        convolved = conv[rows, :]
        grad_lin = dt_lin[rows, :] * (convolved * s1[...] + s2[...] * (1.0 / LOG2E))
        low = grad_lin.astype(BF16)
        gdl[rows, :] = low
        rows_sum[5:6, :] += jnp.sum(grad_lin, axis=0, keepdims=True)
        rows_sum[6:7, :] += jnp.sum(gy_now * convolved, axis=0, keepdims=True)
        dts[rows, :] = params[126:127, :] * gy_now + dts[rows, :] * s1[...]
        at_state = spots(tall, 0) % states
        spread = jnp.where(spots(tall, 1) - 72 == at_state, matmul(lanes_b[...], ones), 0.0) + jnp.where(
            spots(tall, 1) - 88 == at_state, matmul(lanes_c[...], ones), 0.0
        )
        share = spread.reshape(block, states, 128).sum(axis=1)
        share = share + matmul(low[:, :512], whole[:, 2 * model + 128 : 2 * model + 256])
        share = share + matmul(low[:, 512:], extra[:, small + 128 : small + 256])
        own[b] = share.astype(BF16)
        for k in (1, 0, 2):
            proj_copy(b, k).start()

    def stage_b(b):
        start = pl.multiple_of(b * block, block)
        rows = pl.ds(start, block)
        for k in range(3):
            proj_copy(b, k).wait_recv()
        gp = (
            own[b].astype(F32) + landing[0, b].astype(F32) + landing[1, b].astype(F32) + landing[2, b].astype(F32)
        ).astype(BF16)
        gp_all[rows, :] = gp
        u_now = u_in[rows, :]
        sig = jax.nn.sigmoid(u_now)
        gu = dts[rows, :] + both_cols(gp, whole[:, 2 * model : 2 * model + 128], extra[:, small : small + 128])
        gu = gu * (sig * (1.0 + u_now * (1.0 - sig)))
        gus[rows, :] = gu
        lines_g, lines_m = gus[pl.ds(start, block + 8), :], marks[pl.ds(start, block + 8), :]
        x = x_low[rows, :].astype(F32)
        total = params[123:124, :] * gu
        rows_sum[3:4, :] += jnp.sum(gu * x, axis=0, keepdims=True)
        rows_sum[4:5, :] += jnp.sum(gu, axis=0, keepdims=True)
        mask = jnp.ones((block, 128), F32)
        for ahead in (1, 2, 3):
            mask = mask * (1.0 - lines_m[ahead : ahead + block])
            moved = lines_g[ahead : ahead + block] * across(mask, inner)
            total = total + params[123 - ahead : 124 - ahead, :] * moved
            rows_sum[3 - ahead : 4 - ahead, :] += jnp.sum(moved * x, axis=0, keepdims=True)
        low = total.astype(BF16)
        gx[rows, :] = low
        gate = ggate[rows, :]
        out = (
            matmul(low[:, :512], whole[:, :model])
            + matmul(low[:, 512:], extra[:, :model])
            + matmul(gate[:, :512], whole[:, model : 2 * model])
            + matmul(gate[:, 512:], extra[:, model : 2 * model])
        )
        branch[b] = out.astype(BF16)

        for k in (1, 0, 2):
            part_copy(b, k).start()
        gain_sum[...] += jnp.sum(out * normed[rows, :].astype(F32), axis=0, keepdims=True)

    def step(n, carry):
        stage_a(3 - n)

        @pl.when(n == 3)
        def early_third():
            flow_early.third()

        @pl.when(n > 0)
        def later():
            stage_b(4 - n)

        @pl.when(n > 1)
        def sum_earlier():
            sum_up(5 - n)

        @pl.when(n == 0)
        def pass_on():
            flow_early.second()

        @pl.when(n == 2)
        def early():
            for ring in rings:
                ring.forward()

        return carry

    lax.fori_loop(0, 4, step, 0)

    flow_early.finish()
    sum_up(1)
    weight(gdl[...], proj[...].astype(BF16), flow_rest.source, 128, 128)
    known = inner_rows(gx[block:], normed[block:])
    stage_b(0)
    tile = norm_in[...] + jnp.where(spots(norm_in.shape, 0) == 0, gain_sum[...] / gains[0:1, :], 0.0)
    own_tile[...] = tile.astype(BF16)
    z_copies = [remote(own_tile, tiles.at[k], z_send.at[k], z_recv.at[k], z_peers[k]) for k in range(3)]
    for copy in z_copies:
        copy.start()
    total = known + inner_rows(gx[:block], normed[:block])
    flow_in.source[...] = total[:512].astype(BF16).reshape(owners, MAIN, model)
    extras.append(total[512:].astype(BF16))
    flow_in.begin()
    ends = jnp.concatenate(
        [jnp.zeros((104, inner), F32), g_rate[...] * (a * (1.0 / LOG2E)), rows_sum[...]], axis=0
    ).astype(BF16)
    low_conv, low_gp, unit = conv_low[...], gp_all[...], eye(128)
    main = inner_rows(low_conv[:, :512], low_gp) + inner_rows(ends[:, :512], unit)
    flow_rest.source[:, :, :128] = main.astype(BF16).reshape(owners, MAIN, 128)
    last = (inner_rows(low_conv[:, 512:], low_gp) + inner_rows(ends[:, 512:], unit)).astype(BF16)
    lines_e = jnp.concatenate(
        [extras[3], extras[1], extras[0], last, extras[2], jnp.zeros((64, 4096 - small - 256), BF16)], axis=1
    )
    stacked = jnp.concatenate([lines_e[:, k * 512 : (k + 1) * 512] for k in range(8)], axis=0)
    row, col = spots((512, 512), 0), spots((512, 512), 1)
    wanted = (col % 64 // 2) * MAIN + (col % 2) * 8 + col // 64
    flow_rest.source[:, :, 256:768] = (
        matmul((wanted == row).astype(BF16), stacked).astype(BF16).reshape(owners, MAIN, 512)
    )
    span = model // owners
    for copy in z_copies:
        copy.wait_recv()
    tile = tile + tiles[0].astype(F32) + tiles[1].astype(F32) + tiles[2].astype(F32)
    for n in range(owners):
        piece = tile[:, n * span : (n + 1) * span]
        piece = jnp.concatenate([piece, jnp.zeros((MAIN, 128 - span), F32)], axis=1)
        flow_rest.source[n, :, 768:] = piece.astype(BF16)
    flow_rest.begin()
    flow_in.second()
    flow_rest.second()
    sum_up(0)
    flow_in.third()
    flow_rest.third()
    for ring in sums + rings:
        ring.end()
    for k in range(3):
        whole_copy(0, k).wait_recv()
    for k in range(4):
        rows = pl.ds(pl.multiple_of(lax.rem(h + k, 4) * quarter, quarter), quarter)
        piece = owned[k - 1] if k else quarters[h]
        grad_tokens[rows, :] = piece.astype(F32)
    grad_n = grad_tokens[...]
    values = seq_own[...].astype(F32)
    scale = lax.rsqrt(jnp.mean(values * values, axis=-1, keepdims=True) + EPS)
    scaled = grad_n * gains[0:1, :]
    inside = jnp.mean(scaled * values, axis=-1, keepdims=True)
    grad_tokens[...] = grad_hidden[...] + scale * scaled - values * (scale * scale * scale * inside)
    flow_rest.finish()
    rest = flow_rest.out[...]
    flow_in.finish()
    rank, wide = grad_dt.shape[1], grad_x.shape[1]
    extra_rows = [
        jnp.concatenate([rest[n * 8 + k : n * 8 + k + 1, 256:768] for k in range(8)], axis=1) for n in range(2)
    ]

    def full(main, at, size):
        return jnp.concatenate([main, *[line[:, at : at + size] for line in extra_rows]], axis=0)

    grad_in[:, 0, :] = full(flow_in.out[...], 0, model)
    grad_in[:, 1, :] = full(flow_early.out[:, model:], model, model)
    grad_out[...] = full(flow_early.out[:, :model], 2 * model, model)
    small_sum = full(rest[:, :256], small, 256)
    grad_x[...] = small_sum[:, :wide]
    grad_dt[...] = small_sum[:, 128 : 128 + rank]
    channels = jnp.concatenate([small_sum[:, :128], jnp.zeros((110, 128), F32)], axis=0)
    by_channel[...] = channels.T[104:128, : grad_out.shape[0]]
    share = by_feature.shape[1]
    by_feature[...] = pltpu.roll(rest[:, 768:], lax.rem(128 - h * share, 128), 1)[:, :share]
    for flow in (flow_early, flow_in, flow_rest):
        flow.end()
    for copy in gh_copies + z_copies:
        copy.wait_send()
    for b in range(4):
        for k in range(3):
            proj_copy(b, k).wait_send()
            part_copy(b, k).wait_send()

        @pl.when(b != h)
        def sent():
            whole_copy(b, 0).wait_send()


def mixer_backward(grad_hidden, seq, whole, gains, norm_in, saved, expert_grads, own, wide, rank):
    normed, x_low, u, gate_z, proj, dt_lin, y, gated, starts, params, extra = saved
    block, model = grad_hidden.shape
    tokens, inner = u.shape
    states = starts.shape[1]
    S = jax.ShapeDtypeStruct
    g_up, g_down, came_up, came_down = expert_grads

    def like(array):
        return pltpu.VMEM(array.shape, array.dtype)

    line, low = pltpu.VMEM((block, inner), F32), pltpu.VMEM((tokens, inner), BF16)
    tall = pltpu.VMEM((tokens, inner), F32)
    return pl.pallas_call(
        mixer_back_kernel,
        out_shape=(
            S((block, model), F32), S((own, 2, model), F32), S((own, model), F32), S((own, wide), F32),
            S((own, rank), F32), S((24, own), F32), S((MAIN, model // 128), F32), S(g_up.shape, BF16),
            S(g_down.shape, BF16),
        ),
        in_specs=[IN_VMEM, ANY, ANY, IN_VMEM, IN_VMEM, *[ANY] * 9, IN_VMEM, *[ANY] * 5],
        out_specs=(*[IN_VMEM] * 7, ANY, ANY),
        scratch_shapes=[
            pltpu.VMEM((block, model), BF16), pltpu.VMEM((tokens, 128), BF16), like(whole), like(normed), like(x_low),
            like(u), like(gate_z), like(proj), like(dt_lin), like(y), like(gated), like(starts), like(extra),
            DMA((13,)),
            pltpu.VMEM((4, block, model), BF16),
            pltpu.VMEM((tokens + 8, inner), F32),
            pltpu.VMEM((tokens + 8, 128), F32),
            tall, tall, tall, tall, line, line,
            low, low, low,
            pltpu.VMEM((tokens, 128), BF16),
            low,
            pltpu.VMEM((STEP + 1, states, inner), F32),
            pltpu.VMEM((STEP, states, inner), F32),
            pltpu.VMEM((-(-inner // 128), STEP * states // 2, 128), F32),
            pltpu.VMEM((-(-inner // 128), STEP * states // 2, 128), F32),
            pltpu.VMEM((block * states, 128), BF16),
            pltpu.VMEM((block * states, 128), BF16),
            pltpu.VMEM((states, inner), F32),
            pltpu.VMEM((states, inner), F32),
            pltpu.VMEM((8, inner), F32),
            pltpu.VMEM((4, block, 128), BF16),
            pltpu.VMEM((3, 4, block, 128), BF16),
            pltpu.VMEM((4, block, model), BF16),
            pltpu.VMEM((3, 4, block // 4, model), BF16),
            DMA((4,)), DMA((4,)), DMA((12,)), DMA((12,)), DMA((12,)), DMA((12,)),
            pltpu.VMEM((4, block // 4, model), BF16), pltpu.VMEM((3, block // 4, model), BF16), DMA((4,)), DMA((3,)),
            DMA((2, 4)), DMA((2, 4)), DMA((2,)),
            like(came_up), like(came_up), like(came_up), pltpu.VMEM((g_up.shape[0] // 4, g_up.shape[1]), BF16),
            like(came_down), like(came_down), like(came_down), pltpu.VMEM((g_down.shape[0] // 4, g_down.shape[1]), BF16),
            DMA((2, 2)), DMA((2, 2)), DMA((2, 5)),
            pltpu.VMEM((MAIN, model), BF16), pltpu.VMEM((3, MAIN, model), BF16), DMA((3,)), DMA((3,)),
            *flow_scratch(2 * model), *flow_scratch(model), *flow_scratch(896),
            pltpu.VMEM((1, model), F32),
        ],
        compiler_params=pltpu.CompilerParams(
            collective_id=5, has_side_effects=True, vmem_limit_bytes=62 << 20
        ),
        name="mixer_backward",
    )(
        grad_hidden, seq, whole, gains, norm_in, normed, x_low, u, gate_z, proj, dt_lin, y, gated, starts, params, extra,
        g_up, g_down, came_up, came_down,
    )


def finish_kernel(*refs):
    (
        channel, feature, up_in, down_in, in_0, in_1, in_2, in_3, in_4, in_5, up, down, result, tokens, grad_in, grad_out, grad_x, grad_dt,
        decay, taps, conv_bias, dt_bias, skip, gain_one, gain_two, router, low_up, low_down, high_up, high_down, *kept, sems,
        k_sems,
    ) = refs
    straight_in = (in_0, in_1, in_2, in_3, in_4, in_5)
    straight_out = (result, tokens, grad_in, grad_out, grad_x, grad_dt)
    parts = 8
    loads = []
    for q in range(parts):
        for n, (a, b) in enumerate(((up_in, low_up), (down_in, low_down))):
            size = a.shape[0] // parts
            rows = pl.ds(q * size, size)
            loads.append(pltpu.make_async_copy(a.at[rows, :], b.at[rows, :], sems.at[n, q]))
            loads[-1].start()
    moves = []
    for n, (a, b, c) in enumerate(zip(straight_in, kept, straight_out)):
        moves.append((pltpu.make_async_copy(a, b, k_sems.at[0, n]), pltpu.make_async_copy(b, c, k_sems.at[1, n])))
        moves[-1][0].start()
    lines = channel[...]
    decay[...] = lines[0:16]
    taps[...] = lines[16:20]
    conv_bias[...] = lines[20:21]
    dt_bias[...] = lines[21:22]
    skip[...] = lines[22:23]
    lines = feature[...]
    gain_one[...] = lines[0:1]
    gain_two[...] = lines[1:2]
    router[...] = lines[2:10]
    stores = []
    for q in range(parts):
        for n, (a, b, c) in enumerate(((low_up, high_up, up), (low_down, high_down, down))):
            size = a.shape[0] // parts
            rows = pl.ds(q * size, size)
            loads[2 * q + n].wait()
            b[rows, :] = a[rows, :].astype(F32)
            stores.append(pltpu.make_async_copy(b.at[rows, :], c.at[rows, :], sems.at[2 + n, q]))
            stores[-1].start()
    for a, b in moves:
        a.wait()
        b.start()
    for copy in stores:
        copy.wait()
    for a, b in moves:
        b.wait()


def finished(output, tokens, grad_in, grad_out, grad_x, grad_dt, channel, feature, low_up, low_down):
    S, own, share = jax.ShapeDtypeStruct, channel.shape[1], feature.shape[1]
    straight = (output, tokens, grad_in, grad_out, grad_x, grad_dt)
    outs = [S(low_up.shape, F32), S(low_down.shape, F32), *[S(a.shape, a.dtype) for a in straight]]
    outs += [S((n, own), F32) for n in (16, 4, 1, 1, 1)] + [S((n, share), F32) for n in (1, 1, 8)]
    up, down, *rest = pl.pallas_call(
        finish_kernel,
        out_shape=outs,
        in_specs=[IN_VMEM] * 2 + [ANY] * 8,
        out_specs=[ANY] * 8 + [IN_VMEM] * 8,
        scratch_shapes=[
            pltpu.VMEM(low_up.shape, BF16), pltpu.VMEM(low_down.shape, BF16), pltpu.VMEM(low_up.shape, F32),
            pltpu.VMEM(low_down.shape, F32), *[pltpu.VMEM(a.shape, a.dtype) for a in straight], DMA((4, 8)), DMA((2, 6)),
        ],
        compiler_params=pltpu.CompilerParams(vmem_limit_bytes=62 << 20),
        name="finish",
    )(channel, feature, low_up, low_down, *straight)
    return *rest, up, down


def shards(
    tokens, resets, routes, cotangent, mixer_gain, in_proj, conv_kernel, conv_bias, x_proj, dt_proj,
    dt_bias, log_decay, skip_gain, out_proj, moe_gain, router, up_proj, down_proj,
):
    model, own, experts = tokens.shape[1], conv_bias.shape[0], router.shape[1]
    rank, states = dt_proj.shape[0], log_decay.shape[0]
    inner = lax.axis_size("expert") * lax.axis_size("rows") * own
    route_row = routes.reshape(1, -1)
    arrays = (
        in_proj.transpose(2, 1, 0), out_proj, x_proj.T, dt_proj.T, log_decay, conv_kernel, conv_bias[None],
        dt_bias[None], skip_gain[None], mixer_gain[None], moe_gain[None], router.T, tokens, resets[None], route_row,
        cotangent,
    )
    whole, sequence, extra, *rest = mixer_and_experts(arrays, up_proj[0], down_proj[0], inner, states, experts)
    saved, (params, gains, output, grad_hidden, norm_grads, *expert_grads) = rest[:9], rest[9:]
    results = mixer_backward(
        grad_hidden, sequence, whole, gains, norm_grads, (*saved, params, extra), expert_grads, own,
        rank + 2 * states, rank,
    )
    (
        output, grad_tokens, grad_in, grad_out, grad_x, grad_dt, grad_decay, grad_taps, grad_conv_bias, grad_dt_bias,
        grad_skip, grad_gain_one, grad_gain_two, grad_router, grad_up_sum, grad_down_sum,
    ) = finished(output, *results)
    return (
        output,
        grad_tokens,
        grad_gain_one[0],
        grad_in.transpose(2, 1, 0),
        grad_taps,
        grad_conv_bias[0],
        grad_x.T,
        grad_dt.T,
        grad_dt_bias[0],
        grad_decay,
        grad_skip[0],
        grad_out,
        grad_gain_two[0],
        grad_router.T,
        grad_up_sum[None],
        grad_down_sum[None],
    )


def solution(mesh):
    every = ("expert", "rows", "hid")
    in_specs = (
        P(every, None), P(every), P(every, None), P(every, None), P(every), P(None, None, every),
        P(None, every), P(every), P(None, every), P(None, every), P(every), P(None, every), P(every),
        P(every, None), P(every), P(every, None), P("expert", None, "hid"), P("expert", "hid", None),
    )
    out_specs = (
        P(every, None), P(every, None), P(every), P(None, None, every), P(None, every), P(every),
        P(None, every), P(None, every), P(every), P(None, every), P(every), P(every, None), P(every),
        P(every, None), P("expert", None, "hid"), P("expert", "hid", None),
    )
    return jax.shard_map(shards, mesh=mesh, in_specs=in_specs, out_specs=out_specs, check_vma=False)
```
